32 devices in a mesh: groups: 2 (over x), row: 16 (over z, y, core).
Axes of the slice: x: 2, y: 2, z: 4, core: 2. Of those that a mesh axis runs over, the one named last changes fastest.
Arguments:
- object_field: float32 [2, 1280, 32768], P(None, ('groups', 'row')), parts along dimension 1, may hold values from -5 to 5
- probe: bfloat16 [4, 512, 512], P('groups'), parts along dimension 0, may hold values from -5 to 5
- amplitude: bfloat16 [32, 512, 512], P(('groups', 'row')), parts along dimension 0, may hold values from 0.25 to 2.5
- row_offsets: int32 [32], P('groups'), parts along dimension 0, may hold values from 0 to 128
- col_offsets: int32 [32], P('groups'), parts along dimension 0, may hold values from 0 to 32256
- dealing: int32 [32], P('groups'), parts along dimension 0, may hold values from 0 to 15, each once
Outputs:
- object_grad: float32 [2, 1280, 32768], P(None, ('groups', 'row')), parts along dimension 1
- probe_grad: float32 [4, 512, 512], P('groups'), parts along dimension 0
The draws below stay inside these ranges and needn't reach their ends.
There are 2 independent parts, one for each index of `groups`. The reference program is written for one: setup_inputs(seed, part) draws one part's arguments, and reference() takes and returns one part's arrays. A program takes and returns all parts, laid end to end along the dimension named above; each array names one. Nothing has to cross between parts.
Inputs may be any that keep to these rules, and one draw needn't show every extreme that they name: dealing holds every scan position exactly once.
All inputs are finite; a program needn't handle non-finite values.
Results may differ from the reference program's by a relative error of at most 0.012.
The reference program's roundings to bfloat16 on the way count: a program that leaves them out, or rounds other values in their place, can miss the bound.
Values may be sent and summed in bfloat16 or wider, within the bound.
No kernel may reach another device: no remote copies, remote signals or barrier semaphores. Data moves between devices by JAX's collectives and lax.ppermute only.
A program may use at most 128 MiB of HBM per device.

```python
import math
import jax
import jax.numpy as jnp
from jax import lax

PROBE = 512
OBJ_ROWS = 640
OBJ_COLS = 32768
POSITIONS = 16


def with_ends(result, rng, low, top_value):
    place = [jax.random.randint(jax.random.fold_in(rng, axis), (), 0, length) for axis, length in enumerate(result.shape)]
    longest = result.shape.index(max(result.shape))
    beside = place[:longest] + [(place[longest] + 1) % result.shape[longest]] + place[longest + 1:]
    return result.at[tuple(place)].set(low).at[tuple(beside)].set(top_value)


def shard_levels(key, extent, shards, least, high):
    level = 1.0
    for position, shards_of in shards:
        heights = jax.random.uniform(jax.random.fold_in(jax.random.fold_in(key, 6), position), (shards_of,), jnp.float32, least / len(shards), high / len(shards))
        level = level * jnp.repeat(jnp.exp(heights), extent[position] // shards_of).reshape((-1,) + (1,) * (len(extent) - 1 - position))
    return level


def centred(stream_key, dims, spread, limit, shards=(), held_as=jnp.bfloat16):
    entries = spread * jax.random.normal(stream_key, dims, jnp.float32)
    if shards:
        entries = entries * shard_levels(stream_key, dims, shards, -0.22, 0.18)
    return jnp.clip(entries, -limit, limit).astype(held_as)


def setup_inputs(seed: int = 0, part: int = 0) -> dict:
    arg_keys = jax.random.split(jax.random.key(seed), 7)
    part_splits = jax.random.split(jax.random.fold_in(arg_keys[6], part), 7)
    object_field = centred(part_splits[0], (2, OBJ_ROWS, OBJ_COLS), 0.7, 5.0, ((1, 16),), jnp.float32)
    probe = centred(part_splits[1], (2, PROBE, PROBE), 0.7, 5.0)
    amplitude = jnp.clip(jnp.exp(math.log(2.5) - 2.3025851 * jax.random.uniform(part_splits[2], (POSITIONS, PROBE, PROBE), jnp.float32) ** shard_levels(part_splits[2], (POSITIONS, PROBE, PROBE), ((0, 16),), -0.2, 0.2)), 0.25, 2.5).astype(jnp.bfloat16)
    row_offsets = with_ends(jax.random.randint(part_splits[3], (POSITIONS,), 0, OBJ_ROWS - PROBE + 1), jax.random.fold_in(part_splits[3], 1), 0, OBJ_ROWS - PROBE).astype(jnp.int32)
    col_offsets = with_ends(jax.random.randint(part_splits[4], (POSITIONS,), 0, OBJ_COLS - PROBE + 1), jax.random.fold_in(part_splits[4], 1), 0, OBJ_COLS - PROBE).astype(jnp.int32)
    dealing = jax.random.permutation(part_splits[5], POSITIONS).astype(jnp.int32)
    return dict(object_field=object_field, probe=probe, amplitude=amplitude, row_offsets=row_offsets, col_offsets=col_offsets, dealing=dealing)


MAG_FLOOR = 0.25

def dft_tables(order):
    indices = jnp.arange(order, dtype=jnp.int32)
    phases = indices[:, None] * indices[None, :] % order
    angles = phases.astype(jnp.float32) * (2.0 * math.pi / order)
    factor = 1.0 / math.sqrt(order)
    real_part = jnp.cos(angles) * factor
    imag_part = -jnp.sin(angles) * factor
    right_table = jnp.block([[real_part, imag_part], [-imag_part, real_part]]).astype(jnp.bfloat16)
    left_table = jnp.block([[real_part, -imag_part], [imag_part, real_part]]).astype(jnp.bfloat16)
    return (right_table, left_table)

def slot_terms(patch_cells, probe, measured, right_table, left_table):
    order = probe.shape[1]
    patch_wide = patch_cells.astype(jnp.float32)
    probe_wide = probe.astype(jnp.float32)
    wave_real = probe_wide[0] * patch_wide[0] - probe_wide[1] * patch_wide[1]
    wave_imag = probe_wide[0] * patch_wide[1] + probe_wide[1] * patch_wide[0]
    wave_cells = jnp.concatenate([wave_real, wave_imag], axis=1).astype(jnp.bfloat16)
    half_done = jnp.dot(wave_cells, right_table, preferred_element_type=jnp.float32).astype(jnp.bfloat16)
    stacked = jnp.concatenate([half_done[:, :order], half_done[:, order:]], axis=0)
    far_field = jnp.dot(left_table, stacked, preferred_element_type=jnp.float32)
    far_real = far_field[:order]
    far_imag = far_field[order:]
    magnitude = jnp.sqrt(far_real * far_real + far_imag * far_imag)
    shrink = 1.0 - measured.astype(jnp.float32) / jnp.maximum(magnitude, MAG_FLOOR)
    resid_cells = jnp.concatenate([far_real * shrink, far_imag * shrink], axis=1).astype(jnp.bfloat16)
    turned = jnp.dot(resid_cells, left_table, preferred_element_type=jnp.float32).astype(jnp.bfloat16)
    turned_rows = jnp.concatenate([turned[:, :order], turned[:, order:]], axis=0)
    back_field = jnp.dot(right_table, turned_rows, preferred_element_type=jnp.float32)
    back_real = back_field[:order]
    back_imag = back_field[order:]
    object_term = jnp.stack([probe_wide[0] * back_real + probe_wide[1] * back_imag, probe_wide[0] * back_imag - probe_wide[1] * back_real])
    probe_term = jnp.stack([patch_wide[0] * back_real + patch_wide[1] * back_imag, patch_wide[0] * back_imag - patch_wide[1] * back_real])
    return (object_term, probe_term)

def reference(object_field, probe, amplitude, row_offsets, col_offsets, dealing):
    right_table, left_table = dft_tables(PROBE)
    slot_rows = row_offsets[dealing].astype(jnp.int32)
    slot_cols = col_offsets[dealing].astype(jnp.int32)
    zero_index = jnp.zeros((), jnp.int32)

    def scan_step(running, entry_item):
        object_total, probe_total = running
        first_row, first_col, measured = entry_item
        patch_cells = lax.dynamic_slice(object_field, (zero_index, first_row, first_col), (2, PROBE, PROBE)).astype(jnp.bfloat16)
        object_term, probe_term = slot_terms(patch_cells, probe, measured, right_table, left_table)
        window = lax.dynamic_slice(object_total, (zero_index, first_row, first_col), (2, PROBE, PROBE))
        object_total = lax.dynamic_update_slice(object_total, window + object_term, (zero_index, first_row, first_col))
        return ((object_total, probe_total + probe_term), None)
    start_state = (jnp.zeros((2, OBJ_ROWS, OBJ_COLS), jnp.float32), jnp.zeros((2, PROBE, PROBE), jnp.float32))
    final_state, unused = lax.scan(scan_step, start_state, (slot_rows, slot_cols, amplitude))
    object_grad, probe_total = final_state
    return (object_grad, probe_total * (1.0 / POSITIONS))
```

```python
import functools
import math

import jax
import jax.numpy as jnp
import numpy as np
from jax import lax
from jax.experimental import pallas as pl
from jax.experimental.pallas import tpu as pltpu
from jax.sharding import PartitionSpec as P

MAG_FLOOR = 0.25
LANES = 128
SUBLANES = 8
SMEM = pl.BlockSpec(memory_space=pltpu.SMEM)
VMEM = pl.BlockSpec(memory_space=pltpu.VMEM)
ANY = pl.BlockSpec(memory_space=pl.ANY)


def dft_tables(order):
    indices = np.arange(order, dtype=np.int32)
    phases = indices[:, None] * indices[None, :] % order
    angles = phases.astype(np.float32) * np.float32(2.0 * math.pi / order)
    factor = np.float32(1.0 / math.sqrt(order))
    real_part = np.cos(angles) * factor
    imag_part = -np.sin(angles) * factor
    right_table = np.block([[real_part, imag_part], [-imag_part, real_part]])
    left_table = np.block([[real_part, -imag_part], [imag_part, real_part]])
    return right_table.astype(jnp.bfloat16), left_table.astype(jnp.bfloat16)


def window_start(column, order, tile_cols):
    span = order + LANES
    base = jnp.minimum(column // LANES, (tile_cols - span) // LANES) * LANES
    return pl.multiple_of(base, LANES), column - base


def rows_from(ref, start, count):
    aligned = pl.multiple_of(start // SUBLANES * SUBLANES, SUBLANES)
    rest = start - aligned
    width = ref.shape[-1]
    blocks = ref[pl.ds(aligned, count + SUBLANES), :].reshape(-1, SUBLANES, width)
    turned = pltpu.roll(blocks, lax.rem(SUBLANES - rest, SUBLANES), 1)
    sub = lax.broadcasted_iota(jnp.int32, (1, SUBLANES, width), 1)
    picked = jnp.where(sub < SUBLANES - rest, turned[:-1], turned[1:])
    return picked.reshape(count, width)


def fetch_kernel(order, dealing, cols, tile, out, held, sems):
    slots, tile_rows = out.shape[0], out.shape[1]
    tile_cols = tile.shape[2]
    span = order + LANES

    def copy(slot):
        base, _ = window_start(cols[dealing[slot]], order, tile_cols)
        return pltpu.make_async_copy(tile.at[:, :, pl.ds(base, span)], held.at[slot], sems.at[slot])

    @pl.loop(0, slots)
    def _(slot):
        copy(slot).start()

    lane = lax.broadcasted_iota(jnp.int32, (tile_rows, LANES), 1)

    @pl.loop(0, slots)
    def _(slot):
        copy(slot).wait()
        _, offset = window_start(cols[dealing[slot]], order, tile_cols)
        shift = lax.rem(LANES - lax.rem(offset, LANES), LANES)
        for part in range(2):
            turned = [
                pltpu.roll(held[slot, part, :, b * LANES : (b + 1) * LANES], shift, 1)
                for b in range(span // LANES)
            ]
            for b in range(order // LANES):
                first = part * order + b * LANES
                cells = jnp.where(lane < LANES - offset, turned[b], turned[b + 1])
                out[slot, :, first : first + LANES] = cells.astype(out.dtype)


def fetch_windows(tile, dealing, cols, order):
    slots, tile_rows, tile_cols = dealing.shape[0], tile.shape[1], tile.shape[2]
    span = order + LANES

    return pl.pallas_call(
        functools.partial(fetch_kernel, order),
        out_shape=jax.ShapeDtypeStruct((slots, tile_rows, 2 * order), jnp.bfloat16),
        in_specs=[SMEM, SMEM, ANY],
        out_specs=VMEM,
        scratch_shapes=[
            pltpu.VMEM((slots, 2, tile_rows, span), jnp.float32),
            pltpu.SemaphoreType.DMA((slots,)),
        ],
        compiler_params=pltpu.CompilerParams(vmem_limit_bytes=24 * 2**20),
        cost_estimate=pl.CostEstimate(flops=0, bytes_accessed=6 * 2**20, transcendentals=0),
        name="fetch",
    )(dealing, cols, tile)


def slot_kernel(
    dealing, rows, cells, probe, measured, right, left,
    terms, kept, sent, empty,
    wide, patch, wave, half, resid, turned, padded, mine, zeros, sem,
):
    order = probe.shape[1]
    total_rows = cells.shape[0]
    reach = total_rows - order
    me = lax.axis_index("row")
    first_row = rows[dealing[me]]
    step = 64
    tile = 256

    zeros[...] = jnp.zeros_like(zeros)
    fills = []
    for b in range(empty.shape[2] // zeros.shape[2]):
        fill = pltpu.make_async_copy(
            zeros, empty.at[:, :, b * zeros.shape[2] : (b + 1) * zeros.shape[2]], sem.at[b]
        )
        fill.start()
        fills.append(fill)

    wide[0:total_rows, :] = cells[...].astype(jnp.float32)
    wide[total_rows:, :] = jnp.zeros((SUBLANES, 2 * order), jnp.float32)
    padded[0:reach, :] = jnp.zeros((reach, 2 * order), jnp.float32)
    padded[reach + order :, :] = jnp.zeros((reach + SUBLANES, 2 * order), jnp.float32)

    @pl.loop(0, order // step)
    def _(i):
        place = pl.ds(pl.multiple_of(i * step, step), step)
        found = rows_from(wide, first_row + i * step, step)
        patch[place, :] = found.astype(patch.dtype)
        real, imag = found[:, :order], found[:, order:]
        probe_real = probe[0, place, :].astype(jnp.float32)
        probe_imag = probe[1, place, :].astype(jnp.float32)
        wave[place, :order] = (probe_real * real - probe_imag * imag).astype(wave.dtype)
        wave[place, order:] = (probe_real * imag + probe_imag * real).astype(wave.dtype)

    def dot(a, b):
        return jnp.dot(a, b, preferred_element_type=jnp.float32)

    for first in range(0, order, tile):
        here = slice(first, first + tile)
        there = slice(order + first, order + first + tile)
        half[:order, here] = dot(wave[...], right[:, here]).astype(half.dtype)
        half[order:, here] = dot(wave[...], right[:, there]).astype(half.dtype)
    for first in range(0, order, tile):
        here = slice(first, first + tile)
        there = slice(order + first, order + first + tile)
        for top in range(0, order, tile):
            line = slice(top, top + tile)
            real = dot(left[line, :], half[:, here])
            imag = dot(left[order + top : order + top + tile, :], half[:, here])
            inverse = jnp.minimum(lax.rsqrt(real * real + imag * imag), 1.0 / MAG_FLOOR)
            shrink = 1.0 - measured[0, line, here].astype(jnp.float32) * inverse
            resid[line, here] = (real * shrink).astype(resid.dtype)
            resid[line, there] = (imag * shrink).astype(resid.dtype)
    for first in range(0, order, tile):
        here = slice(first, first + tile)
        there = slice(order + first, order + first + tile)
        turned[:order, here] = dot(resid[...], left[:, here]).astype(turned.dtype)
        turned[order:, here] = dot(resid[...], left[:, there]).astype(turned.dtype)
    for first in range(0, order, tile):
        here = slice(first, first + tile)
        there = slice(order + first, order + first + tile)
        for top in range(0, order, tile):
            line = slice(top, top + tile)
            real = dot(right[line, :], turned[:, here])
            imag = dot(right[order + top : order + top + tile, :], turned[:, here])
            probe_real = probe[0, line, here].astype(jnp.float32)
            probe_imag = probe[1, line, here].astype(jnp.float32)
            down = slice(reach + top, reach + top + tile)
            padded[down, here] = probe_real * real + probe_imag * imag
            padded[down, there] = probe_real * imag - probe_imag * real
            patch_real = patch[line, here].astype(jnp.float32)
            patch_imag = patch[line, there].astype(jnp.float32)
            mine[line, here] = patch_real * real + patch_imag * imag
            mine[line, there] = patch_real * imag - patch_imag * real

    @pl.loop(0, total_rows // step)
    def _(i):
        place = pl.ds(pl.multiple_of(i * step, step), step)
        terms[place, :] = rows_from(padded, reach - first_row + i * step, step).astype(terms.dtype)

    count = kept.shape[0]
    side = lax.rem(me, 2)
    kept[...] = mine[pl.ds(pl.multiple_of(side * count, count), count), :]
    sent[...] = mine[pl.ds(pl.multiple_of((1 - side) * count, count), count), :].astype(sent.dtype)
    for fill in fills:
        fill.wait()


def slot_terms(cells, probe, measured, dealing, rows, tile_rows, tile_cols):
    order = probe.shape[1]
    total_rows = cells.shape[0]
    right, left = dft_tables(order)
    wide_cols = 2 * order
    fill_cols = 2048
    bf16, f32 = jnp.bfloat16, jnp.float32
    return pl.pallas_call(
        slot_kernel,
        out_shape=(
            jax.ShapeDtypeStruct((total_rows, wide_cols), bf16),
            jax.ShapeDtypeStruct((order // 2, wide_cols), f32),
            jax.ShapeDtypeStruct((order // 2, wide_cols), bf16),
            jax.ShapeDtypeStruct((2, tile_rows, tile_cols), f32),
        ),
        in_specs=[SMEM, SMEM, VMEM, VMEM, VMEM, VMEM, VMEM],
        out_specs=(VMEM, VMEM, VMEM, ANY),
        scratch_shapes=[
            pltpu.VMEM((total_rows + SUBLANES, wide_cols), f32),
            pltpu.VMEM((order, wide_cols), bf16),
            pltpu.VMEM((order, wide_cols), bf16),
            pltpu.VMEM((wide_cols, order), bf16),
            pltpu.VMEM((order, wide_cols), bf16),
            pltpu.VMEM((wide_cols, order), bf16),
            pltpu.VMEM((2 * total_rows - order + SUBLANES, wide_cols), f32),
            pltpu.VMEM((order, wide_cols), f32),
            pltpu.VMEM((2, tile_rows, fill_cols), f32),
            pltpu.SemaphoreType.DMA((tile_cols // fill_cols,)),
        ],
        compiler_params=pltpu.CompilerParams(vmem_limit_bytes=40 * 2**20),
        cost_estimate=pl.CostEstimate(
            flops=8 * 2 * order**3 * 2, bytes_accessed=20 * 2**20, transcendentals=order * order
        ),
        name="slot",
    )(dealing, rows, cells, probe, measured, jnp.asarray(right), jnp.asarray(left))


def block_places(dealing, cols, order, tile_cols):
    base, _ = window_start(cols[dealing], order, tile_cols)
    count = (order + LANES) // LANES
    blocks = (base[:, None] // LANES + jnp.arange(count, dtype=jnp.int32)[None, :]).reshape(-1)
    same = blocks[:, None] == blocks[None, :]
    return blocks, jnp.argmax(same, axis=1).astype(jnp.int32)


def place_kernel(order, dealing, cols, blocks, owners, terms, empty, out, totals, sems):
    del empty
    slots, tile_rows = terms.shape[0], terms.shape[1]
    tile_cols = out.shape[2]
    count = (order + LANES) // LANES
    totals[...] = jnp.zeros_like(totals)
    lane = lax.broadcasted_iota(jnp.int32, (tile_rows, LANES), 1)

    @pl.loop(0, slots)
    def _(slot):
        _, offset = window_start(cols[dealing[slot]], order, tile_cols)
        shift = lax.rem(offset, LANES)
        for part in range(2):
            turned = []
            for b in range(count - 1):
                first = part * order + b * LANES
                turned.append(pltpu.roll(terms[slot, :, first : first + LANES].astype(jnp.float32), shift, 1))
            nothing = jnp.zeros_like(turned[0])
            for b in range(count):
                before = turned[b - 1] if b else nothing
                after = turned[b] if b < count - 1 else nothing
                owner = owners[slot * count + b]
                totals[owner, part] += jnp.where(lane < offset, before, after)

    def copy(number):
        place = pl.multiple_of(blocks[number] * LANES, LANES)
        return pltpu.make_async_copy(totals.at[number], out.at[:, :, pl.ds(place, LANES)], sems.at[number])

    @pl.loop(0, slots * count)
    def _(number):
        @pl.when(owners[number] == number)
        def _():
            copy(number).start()

    @pl.loop(0, slots * count)
    def _(number):
        @pl.when(owners[number] == number)
        def _():
            copy(number).wait()


def place_windows(terms, empty, dealing, cols, order):

    slots, tile_rows = terms.shape[0], terms.shape[1]
    tile_cols = empty.shape[2]
    count = (order + LANES) // LANES
    blocks, owners = block_places(dealing, cols, order, tile_cols)
    return pl.pallas_call(
        functools.partial(place_kernel, order),
        out_shape=jax.ShapeDtypeStruct(empty.shape, empty.dtype),
        in_specs=[SMEM, SMEM, SMEM, SMEM, VMEM, ANY],
        out_specs=ANY,
        scratch_shapes=[
            pltpu.VMEM((slots * count, 2, tile_rows, LANES), jnp.float32),
            pltpu.SemaphoreType.DMA((slots * count,)),
        ],
        input_output_aliases={5: 0},
        compiler_params=pltpu.CompilerParams(vmem_limit_bytes=24 * 2**20),
        cost_estimate=pl.CostEstimate(flops=0, bytes_accessed=6 * 2**20, transcendentals=0),
        name="place",
    )(dealing, cols, blocks, owners, terms, empty)


def strides(devices):
    steps, stride = [], 1
    while stride < devices:
        radix = 4 if len(steps) >= 2 and (devices // stride) % 4 == 0 else 2
        steps.append((stride, radix))
        stride *= radix
    return steps


def turn(x, stride, radix, distance, devices):
    pairs = []
    for d in range(devices):
        digit = d // stride % radix
        pairs.append((d, d + ((digit + distance) % radix - digit) * stride))
    return lax.ppermute(x, "row", pairs)


def sum_probe(kept, sent, devices, scale):
    me = lax.axis_index("row")
    steps = strides(devices)
    total = kept + turn(sent, 1, 2, 1, devices).astype(jnp.float32)
    for stride, radix in steps[1:]:
        digit = me // stride % radix
        count = total.shape[0] // radix
        own = lax.dynamic_slice_in_dim(total, digit * count, count)
        for distance in range(1, radix):
            other = lax.rem(digit + distance, radix)
            share = lax.dynamic_slice_in_dim(total, other * count, count).astype(jnp.bfloat16)
            own = own + turn(share, stride, radix, distance, devices).astype(jnp.float32)
        total = own
    whole = (total * scale).astype(jnp.bfloat16)
    for stride, radix in reversed(steps):
        digit = me // stride % radix
        shares = [whole] + [turn(whole, stride, radix, distance, devices) for distance in range(1, radix)]
        order = [lax.rem(digit - k + radix, radix) for k in range(radix)]
        rows = []
        for k in range(radix):
            piece = shares[0]
            for d in range(1, radix):
                piece = jnp.where(order[k] == d, shares[d], piece)
            rows.append(piece)
        whole = jnp.concatenate(rows, axis=0)
    return whole


def body(object_field, probe, amplitude, row_offsets, col_offsets, dealing):
    order = probe.shape[1]
    devices = lax.axis_size("row")
    own_rows, tile_cols = object_field.shape[1], object_field.shape[2]
    tile_rows = -(-own_rows // SUBLANES) * SUBLANES
    spare = tile_rows - own_rows
    if spare:
        object_field = jnp.pad(object_field, ((0, 0), (0, spare), (0, 0)))
    pieces = fetch_windows(object_field, dealing, col_offsets, order)
    strips = lax.all_to_all(pieces, "row", split_axis=0, concat_axis=0, tiled=True)
    cells = strips[:, :own_rows].reshape(devices * own_rows, 2 * order)
    terms, kept, sent, empty = slot_terms(
        cells, probe, amplitude, dealing, row_offsets, tile_rows, tile_cols
    )
    outgoing = terms.reshape(devices, own_rows, 2 * order)
    if spare:
        outgoing = jnp.pad(outgoing, ((0, 0), (0, spare), (0, 0)))
    arrived = lax.all_to_all(outgoing, "row", split_axis=0, concat_axis=0, tiled=True)
    whole = sum_probe(kept, sent, devices, 1.0 / dealing.shape[0]).astype(jnp.float32)
    probe_grad = jnp.stack([whole[:, :order], whole[:, order:]])
    object_grad = place_windows(arrived, empty, dealing, col_offsets, order)
    if spare:
        object_grad = object_grad[:, :own_rows]
    return (object_grad, probe_grad)


def solution(mesh):
    return jax.shard_map(
        body,
        mesh=mesh,
        in_specs=(
            P(None, ("groups", "row"), None),
            P("groups", None, None),
            P(("groups", "row"), None, None),
            P("groups"),
            P("groups"),
            P("groups"),
        ),
        out_specs=(P(None, ("groups", "row"), None), P("groups", None, None)),
        check_vma=False,
    )
```

```python
import functools
import math

import jax
import jax.numpy as jnp
import numpy as np
from jax import lax
from jax.experimental import pallas as pl
from jax.experimental.pallas import tpu as pltpu
from jax.sharding import PartitionSpec as P

MAG_FLOOR = 0.25
LANES = 128
SUBLANES = 8
SMEM = pl.BlockSpec(memory_space=pltpu.SMEM)
VMEM = pl.BlockSpec(memory_space=pltpu.VMEM)
ANY = pl.BlockSpec(memory_space=pl.ANY)


def dft_tables(order):
    indices = np.arange(order, dtype=np.int32)
    phases = indices[:, None] * indices[None, :] % order
    angles = phases.astype(np.float32) * np.float32(2.0 * math.pi / order)
    factor = np.float32(1.0 / math.sqrt(order))
    real_part = np.cos(angles) * factor
    imag_part = -np.sin(angles) * factor
    right_table = np.block([[real_part, imag_part], [-imag_part, real_part]])
    left_table = np.block([[real_part, -imag_part], [imag_part, real_part]])
    return right_table.astype(jnp.bfloat16), left_table.astype(jnp.bfloat16)


def window_start(column, order, tile_cols):
    span = order + LANES
    base = jnp.minimum(column // LANES, (tile_cols - span) // LANES) * LANES
    return pl.multiple_of(base, LANES), column - base


def rows_from(ref, start, count):
    aligned = pl.multiple_of(start // SUBLANES * SUBLANES, SUBLANES)
    rest = start - aligned
    width = ref.shape[-1]
    blocks = ref[pl.ds(aligned, count + SUBLANES), :].reshape(-1, SUBLANES, width)
    turned = pltpu.roll(blocks, lax.rem(SUBLANES - rest, SUBLANES), 1)
    sub = lax.broadcasted_iota(jnp.int32, (1, SUBLANES, width), 1)
    picked = jnp.where(sub < SUBLANES - rest, turned[:-1], turned[1:])
    return picked.reshape(count, width)


def fetch_kernel(order, dealing, cols, tile, out, held, sems):
    slots, tile_rows = out.shape[0], out.shape[1]
    tile_cols = tile.shape[2]
    span = order + LANES

    def copy(slot):
        base, _ = window_start(cols[dealing[slot]], order, tile_cols)
        return pltpu.make_async_copy(tile.at[:, :, pl.ds(base, span)], held.at[slot], sems.at[slot])

    @pl.loop(0, slots)
    def _(slot):
        copy(slot).start()

    lane = lax.broadcasted_iota(jnp.int32, (tile_rows, LANES), 1)

    @pl.loop(0, slots, unroll=2)
    def _(slot):
        copy(slot).wait()
        _, offset = window_start(cols[dealing[slot]], order, tile_cols)
        shift = lax.rem(LANES - lax.rem(offset, LANES), LANES)
        for part in range(2):
            turned = [
                pltpu.roll(held[slot, part, :, b * LANES : (b + 1) * LANES], shift, 1)
                for b in range(span // LANES)
            ]
            for b in range(order // LANES):
                first = part * order + b * LANES
                cells = jnp.where(lane < LANES - offset, turned[b], turned[b + 1])
                out[slot, :, first : first + LANES] = cells.astype(out.dtype)


def fetch_windows(tile, dealing, cols, order):
    slots, tile_rows, tile_cols = dealing.shape[0], tile.shape[1], tile.shape[2]
    span = order + LANES

    return pl.pallas_call(
        functools.partial(fetch_kernel, order),
        out_shape=jax.ShapeDtypeStruct((slots, tile_rows, 2 * order), jnp.bfloat16),
        in_specs=[SMEM, SMEM, ANY],
        out_specs=VMEM,
        scratch_shapes=[
            pltpu.VMEM((slots, 2, tile_rows, span), jnp.float32),
            pltpu.SemaphoreType.DMA((slots,)),
        ],
        compiler_params=pltpu.CompilerParams(vmem_limit_bytes=56 * 2**20),
        cost_estimate=pl.CostEstimate(flops=0, bytes_accessed=6 * 2**20, transcendentals=0),
        name="fetch",
    )(dealing, cols, tile)


def slot_kernel(
    dealing, rows, cells, probe, measured, right, left,
    terms, kept, sent, empty,
    wide, patch, wave, half, resid, turned, padded, mine, zeros, sem,
):
    order = probe.shape[1]
    total_rows = cells.shape[0]
    reach = total_rows - order
    me = lax.axis_index("row")
    first_row = rows[dealing[me]]
    step = 64
    tile = 256

    zeros[...] = jnp.zeros_like(zeros)
    fills = []
    for b in range(empty.shape[2] // zeros.shape[2]):
        fill = pltpu.make_async_copy(
            zeros, empty.at[:, :, b * zeros.shape[2] : (b + 1) * zeros.shape[2]], sem.at[b]
        )
        fill.start()
        fills.append(fill)

    wide[0:total_rows, :] = cells[...].astype(jnp.float32)
    wide[total_rows:, :] = jnp.zeros((SUBLANES, 2 * order), jnp.float32)
    padded[0:reach, :] = jnp.zeros((reach, 2 * order), jnp.float32)
    padded[reach + order :, :] = jnp.zeros((reach + SUBLANES, 2 * order), jnp.float32)

    @pl.loop(0, order // step)
    def _(i):
        place = pl.ds(pl.multiple_of(i * step, step), step)
        found = rows_from(wide, first_row + i * step, step)
        patch[place, :] = found.astype(patch.dtype)
        real, imag = found[:, :order], found[:, order:]
        probe_real = probe[0, place, :].astype(jnp.float32)
        probe_imag = probe[1, place, :].astype(jnp.float32)
        wave[place, :order] = (probe_real * real - probe_imag * imag).astype(wave.dtype)
        wave[place, order:] = (probe_real * imag + probe_imag * real).astype(wave.dtype)

    def dot(a, b):
        return jnp.dot(a, b, preferred_element_type=jnp.float32)

    for first in range(0, order, tile):
        here = slice(first, first + tile)
        there = slice(order + first, order + first + tile)
        half[:order, here] = dot(wave[...], right[:, here]).astype(half.dtype)
        half[order:, here] = dot(wave[...], right[:, there]).astype(half.dtype)
    for first in range(0, order, tile):
        here = slice(first, first + tile)
        there = slice(order + first, order + first + tile)
        for top in range(0, order, tile):
            line = slice(top, top + tile)
            real = dot(left[line, :], half[:, here])
            imag = dot(left[order + top : order + top + tile, :], half[:, here])
            inverse = jnp.minimum(lax.rsqrt(real * real + imag * imag), 1.0 / MAG_FLOOR)
            shrink = 1.0 - measured[0, line, here].astype(jnp.float32) * inverse
            resid[line, here] = (real * shrink).astype(resid.dtype)
            resid[line, there] = (imag * shrink).astype(resid.dtype)
    for first in range(0, order, tile):
        here = slice(first, first + tile)
        there = slice(order + first, order + first + tile)
        turned[:order, here] = dot(resid[...], left[:, here]).astype(turned.dtype)
        turned[order:, here] = dot(resid[...], left[:, there]).astype(turned.dtype)
    for first in range(0, order, tile):
        here = slice(first, first + tile)
        there = slice(order + first, order + first + tile)
        for top in range(0, order, tile):
            line = slice(top, top + tile)
            real = dot(right[line, :], turned[:, here])
            imag = dot(right[order + top : order + top + tile, :], turned[:, here])
            probe_real = probe[0, line, here].astype(jnp.float32)
            probe_imag = probe[1, line, here].astype(jnp.float32)
            down = slice(reach + top, reach + top + tile)
            padded[down, here] = probe_real * real + probe_imag * imag
            padded[down, there] = probe_real * imag - probe_imag * real
            patch_real = patch[line, here].astype(jnp.float32)
            patch_imag = patch[line, there].astype(jnp.float32)
            mine[line, here] = patch_real * real + patch_imag * imag
            mine[line, there] = patch_real * imag - patch_imag * real

    @pl.loop(0, total_rows // step)
    def _(i):
        place = pl.ds(pl.multiple_of(i * step, step), step)
        terms[place, :] = rows_from(padded, reach - first_row + i * step, step).astype(terms.dtype)

    count = kept.shape[0]
    side = lax.rem(me, 2)
    kept[...] = mine[pl.ds(pl.multiple_of(side * count, count), count), :]
    sent[...] = mine[pl.ds(pl.multiple_of((1 - side) * count, count), count), :].astype(sent.dtype)
    for fill in fills:
        fill.wait()


def slot_terms(cells, probe, measured, dealing, rows, tile_rows, tile_cols):
    order = probe.shape[1]
    total_rows = cells.shape[0]
    right, left = dft_tables(order)
    wide_cols = 2 * order
    fill_cols = 2048
    bf16, f32 = jnp.bfloat16, jnp.float32
    return pl.pallas_call(
        slot_kernel,
        out_shape=(
            jax.ShapeDtypeStruct((total_rows, wide_cols), bf16),
            jax.ShapeDtypeStruct((order // 2, wide_cols), f32),
            jax.ShapeDtypeStruct((order // 2, wide_cols), bf16),
            jax.ShapeDtypeStruct((2, tile_rows, tile_cols), f32),
        ),
        in_specs=[SMEM, SMEM, VMEM, VMEM, VMEM, VMEM, VMEM],
        out_specs=(VMEM, VMEM, VMEM, ANY),
        scratch_shapes=[
            pltpu.VMEM((total_rows + SUBLANES, wide_cols), f32),
            pltpu.VMEM((order, wide_cols), bf16),
            pltpu.VMEM((order, wide_cols), bf16),
            pltpu.VMEM((wide_cols, order), bf16),
            pltpu.VMEM((order, wide_cols), bf16),
            pltpu.VMEM((wide_cols, order), bf16),
            pltpu.VMEM((2 * total_rows - order + SUBLANES, wide_cols), f32),
            pltpu.VMEM((order, wide_cols), f32),
            pltpu.VMEM((2, tile_rows, fill_cols), f32),
            pltpu.SemaphoreType.DMA((tile_cols // fill_cols,)),
        ],
        compiler_params=pltpu.CompilerParams(vmem_limit_bytes=40 * 2**20),
        cost_estimate=pl.CostEstimate(
            flops=8 * 2 * order**3 * 2, bytes_accessed=20 * 2**20, transcendentals=order * order
        ),
        name="slot",
    )(dealing, rows, cells, probe, measured, jnp.asarray(right), jnp.asarray(left))


def block_places(dealing, cols, order, tile_cols):
    base, _ = window_start(cols[dealing], order, tile_cols)
    count = (order + LANES) // LANES
    blocks = (base[:, None] // LANES + jnp.arange(count, dtype=jnp.int32)[None, :]).reshape(-1)
    same = blocks[:, None] == blocks[None, :]
    return blocks, jnp.argmax(same, axis=1).astype(jnp.int32)


def place_kernel(order, dealing, cols, blocks, owners, terms, empty, out, totals, sems):
    del empty
    slots, tile_rows = terms.shape[0], terms.shape[1]
    tile_cols = out.shape[2]
    count = (order + LANES) // LANES
    totals[...] = jnp.zeros_like(totals)
    lane = lax.broadcasted_iota(jnp.int32, (tile_rows, LANES), 1)

    @pl.loop(0, slots, unroll=2)
    def _(slot):
        _, offset = window_start(cols[dealing[slot]], order, tile_cols)
        shift = lax.rem(offset, LANES)
        for part in range(2):
            turned = []
            for b in range(count - 1):
                first = part * order + b * LANES
                turned.append(pltpu.roll(terms[slot, :, first : first + LANES].astype(jnp.float32), shift, 1))
            nothing = jnp.zeros_like(turned[0])
            for b in range(count):
                before = turned[b - 1] if b else nothing
                after = turned[b] if b < count - 1 else nothing
                owner = owners[slot * count + b]
                totals[owner, part] += jnp.where(lane < offset, before, after)

    def copy(number):
        place = pl.multiple_of(blocks[number] * LANES, LANES)
        return pltpu.make_async_copy(totals.at[number], out.at[:, :, pl.ds(place, LANES)], sems.at[number])

    @pl.loop(0, slots * count)
    def _(number):
        @pl.when(owners[number] == number)
        def _():
            copy(number).start()

    @pl.loop(0, slots * count)
    def _(number):
        @pl.when(owners[number] == number)
        def _():
            copy(number).wait()


def place_windows(terms, empty, dealing, cols, order):

    slots, tile_rows = terms.shape[0], terms.shape[1]
    tile_cols = empty.shape[2]
    count = (order + LANES) // LANES
    blocks, owners = block_places(dealing, cols, order, tile_cols)
    return pl.pallas_call(
        functools.partial(place_kernel, order),
        out_shape=jax.ShapeDtypeStruct(empty.shape, empty.dtype),
        in_specs=[SMEM, SMEM, SMEM, SMEM, VMEM, ANY],
        out_specs=ANY,
        scratch_shapes=[
            pltpu.VMEM((slots * count, 2, tile_rows, LANES), jnp.float32),
            pltpu.SemaphoreType.DMA((slots * count,)),
        ],
        input_output_aliases={5: 0},
        compiler_params=pltpu.CompilerParams(vmem_limit_bytes=24 * 2**20),
        cost_estimate=pl.CostEstimate(flops=0, bytes_accessed=6 * 2**20, transcendentals=0),
        name="place",
    )(dealing, cols, blocks, owners, terms, empty)


def strides(devices):
    steps, stride = [], 1
    while stride < devices:
        radix = 4 if len(steps) >= 2 and (devices // stride) % 4 == 0 else 2
        steps.append((stride, radix))
        stride *= radix
    return steps


def turn(x, stride, radix, distance, devices):
    pairs = []
    for d in range(devices):
        digit = d // stride % radix
        pairs.append((d, d + ((digit + distance) % radix - digit) * stride))
    return lax.ppermute(x, "row", pairs)


def sum_probe(kept, sent, devices, scale):
    me = lax.axis_index("row")
    steps = strides(devices)
    total = kept + turn(sent, 1, 2, 1, devices).astype(jnp.float32)
    for stride, radix in steps[1:]:
        digit = me // stride % radix
        count = total.shape[0] // radix
        own = lax.dynamic_slice_in_dim(total, digit * count, count)
        for distance in range(1, radix):
            other = lax.rem(digit + distance, radix)
            share = lax.dynamic_slice_in_dim(total, other * count, count).astype(jnp.bfloat16)
            own = own + turn(share, stride, radix, distance, devices).astype(jnp.float32)
        total = own
    whole = (total * scale).astype(jnp.bfloat16)
    for stride, radix in reversed(steps):
        digit = me // stride % radix
        shares = [whole] + [turn(whole, stride, radix, distance, devices) for distance in range(1, radix)]
        order = [lax.rem(digit - k + radix, radix) for k in range(radix)]
        rows = []
        for k in range(radix):
            piece = shares[0]
            for d in range(1, radix):
                piece = jnp.where(order[k] == d, shares[d], piece)
            rows.append(piece)
        whole = jnp.concatenate(rows, axis=0)
    return whole


def body(object_field, probe, amplitude, row_offsets, col_offsets, dealing):
    order = probe.shape[1]
    devices = lax.axis_size("row")
    own_rows, tile_cols = object_field.shape[1], object_field.shape[2]
    tile_rows = -(-own_rows // SUBLANES) * SUBLANES
    spare = tile_rows - own_rows
    if spare:
        object_field = jnp.pad(object_field, ((0, 0), (0, spare), (0, 0)))
    pieces = fetch_windows(object_field, dealing, col_offsets, order)
    strips = lax.all_to_all(pieces, "row", split_axis=0, concat_axis=0, tiled=True)
    cells = strips[:, :own_rows].reshape(devices * own_rows, 2 * order)
    terms, kept, sent, empty = slot_terms(
        cells, probe, amplitude, dealing, row_offsets, tile_rows, tile_cols
    )
    outgoing = terms.reshape(devices, own_rows, 2 * order)
    if spare:
        outgoing = jnp.pad(outgoing, ((0, 0), (0, spare), (0, 0)))
    arrived = lax.all_to_all(outgoing, "row", split_axis=0, concat_axis=0, tiled=True)
    rounds = jnp.minimum(dealing[0] + 1, 1)
    _, whole = lax.while_loop(
        lambda state: state[0] < rounds,
        lambda state: (state[0] + 1, sum_probe(kept, sent, devices, 1.0 / dealing.shape[0])),
        (jnp.zeros((), jnp.int32), jnp.zeros((order, 2 * order), jnp.bfloat16)),
    )
    whole = whole.astype(jnp.float32)
    probe_grad = jnp.stack([whole[:, :order], whole[:, order:]])
    object_grad = place_windows(arrived, empty, dealing, col_offsets, order)
    if spare:
        object_grad = object_grad[:, :own_rows]
    return (object_grad, probe_grad)


def solution(mesh):
    return jax.shard_map(
        body,
        mesh=mesh,
        in_specs=(
            P(None, ("groups", "row"), None),
            P("groups", None, None),
            P(("groups", "row"), None, None),
            P("groups"),
            P("groups"),
            P("groups"),
        ),
        out_specs=(P(None, ("groups", "row"), None), P("groups", None, None)),
        check_vma=False,
    )
```

```python
import functools
import math

import jax
import jax.numpy as jnp
import numpy as np
from jax import lax
from jax.experimental import pallas as pl
from jax.experimental.pallas import tpu as pltpu
from jax.sharding import PartitionSpec as P

MAG_FLOOR = 0.25
LANES = 128
SUBLANES = 8
SMEM = pl.BlockSpec(memory_space=pltpu.SMEM)
VMEM = pl.BlockSpec(memory_space=pltpu.VMEM)
ANY = pl.BlockSpec(memory_space=pl.ANY)


def dft_tables(order):
    indices = np.arange(order, dtype=np.int32)
    phases = indices[:, None] * indices[None, :] % order
    angles = phases.astype(np.float32) * np.float32(2.0 * math.pi / order)
    factor = np.float32(1.0 / math.sqrt(order))
    real_part = np.cos(angles) * factor
    imag_part = -np.sin(angles) * factor
    right_table = np.block([[real_part, imag_part], [-imag_part, real_part]])
    left_table = np.block([[real_part, -imag_part], [imag_part, real_part]])
    return right_table.astype(jnp.bfloat16), left_table.astype(jnp.bfloat16)


def window_start(column, order, tile_cols):
    span = order + LANES
    base = jnp.minimum(column // LANES, (tile_cols - span) // LANES) * LANES
    return pl.multiple_of(base, LANES), column - base


def rows_from(ref, start, count):
    aligned = pl.multiple_of(start // SUBLANES * SUBLANES, SUBLANES)
    rest = start - aligned
    width = ref.shape[-1]
    blocks = ref[pl.ds(aligned, count + SUBLANES), :].reshape(-1, SUBLANES, width)
    turned = pltpu.roll(blocks, lax.rem(SUBLANES - rest, SUBLANES), 1)
    sub = lax.broadcasted_iota(jnp.int32, (1, SUBLANES, width), 1)
    picked = jnp.where(sub < SUBLANES - rest, turned[:-1], turned[1:])
    return picked.reshape(count, width)


def fetch_kernel(order, dealing, cols, tile, out, held, sems):
    slots, tile_rows = out.shape[0], out.shape[1]
    tile_cols = tile.shape[2]
    span = order + LANES

    def copy(slot):
        base, _ = window_start(cols[dealing[slot]], order, tile_cols)
        return pltpu.make_async_copy(tile.at[:, :, pl.ds(base, span)], held.at[slot], sems.at[slot])

    @pl.loop(0, slots)
    def _(slot):
        copy(slot).start()

    lane = lax.broadcasted_iota(jnp.int32, (tile_rows, LANES), 1)

    @pl.loop(0, slots, unroll=2)
    def _(slot):
        copy(slot).wait()
        _, offset = window_start(cols[dealing[slot]], order, tile_cols)
        shift = lax.rem(LANES - lax.rem(offset, LANES), LANES)
        for part in range(2):
            turned = [
                pltpu.roll(held[slot, part, :, b * LANES : (b + 1) * LANES], shift, 1)
                for b in range(span // LANES)
            ]
            for b in range(order // LANES):
                first = part * order + b * LANES
                cells = jnp.where(lane < LANES - offset, turned[b], turned[b + 1])
                out[slot, :, first : first + LANES] = cells.astype(out.dtype)


def fetch_windows(tile, dealing, cols, order):
    slots, tile_rows, tile_cols = dealing.shape[0], tile.shape[1], tile.shape[2]
    span = order + LANES

    return pl.pallas_call(
        functools.partial(fetch_kernel, order),
        out_shape=jax.ShapeDtypeStruct((slots, tile_rows, 2 * order), jnp.bfloat16),
        in_specs=[SMEM, SMEM, ANY],
        out_specs=VMEM,
        scratch_shapes=[
            pltpu.VMEM((slots, 2, tile_rows, span), jnp.float32),
            pltpu.SemaphoreType.DMA((slots,)),
        ],
        compiler_params=pltpu.CompilerParams(vmem_limit_bytes=56 * 2**20),
        cost_estimate=pl.CostEstimate(flops=0, bytes_accessed=6 * 2**20, transcendentals=0),
        name="fetch",
    )(dealing, cols, tile)


def slot_kernel(
    chunks, dealing, rows, cells, probe, measured, right_table, left_table,
    *rest,
):
    backs, (empty, wide, wave, half, resid, turned, padded, zeros, right, left, sem, table_sem) = (
        rest[: len(chunks)], rest[len(chunks) :]
    )
    order = probe.shape[1]
    total_rows = cells.shape[0]
    reach = total_rows - order
    me = lax.axis_index("row")
    first_row = rows[dealing[me]]
    step = 64
    tile = 256

    right_copy = pltpu.make_async_copy(right_table, right, table_sem.at[0])
    left_copy = pltpu.make_async_copy(left_table, left, table_sem.at[1])
    right_copy.start()
    left_copy.start()
    zeros[...] = jnp.zeros_like(zeros)
    fills = []
    for b in range(empty.shape[2] // zeros.shape[2]):
        fill = pltpu.make_async_copy(
            zeros, empty.at[:, :, b * zeros.shape[2] : (b + 1) * zeros.shape[2]], sem.at[b]
        )
        fill.start()
        fills.append(fill)

    wide[0:total_rows, :] = cells[...].astype(jnp.float32)
    wide[total_rows:, :] = jnp.zeros((SUBLANES, 2 * order), jnp.float32)
    padded[0:reach, :] = jnp.zeros((reach, 2 * order), jnp.float32)
    padded[reach + order :, :] = jnp.zeros((reach + SUBLANES, 2 * order), jnp.float32)

    @pl.loop(0, order // step)
    def _(i):
        place = pl.ds(pl.multiple_of(i * step, step), step)
        found = rows_from(wide, first_row + i * step, step)
        real, imag = found[:, :order], found[:, order:]
        probe_real = probe[0, place, :].astype(jnp.float32)
        probe_imag = probe[1, place, :].astype(jnp.float32)
        wave[place, :order] = (probe_real * real - probe_imag * imag).astype(wave.dtype)
        wave[place, order:] = (probe_real * imag + probe_imag * real).astype(wave.dtype)

    def dot(a, b):
        return jnp.dot(a, b, preferred_element_type=jnp.float32)

    right_copy.wait()
    for first in range(0, order, tile):
        here = slice(first, first + tile)
        there = slice(order + first, order + first + tile)
        half[:order, here] = dot(wave[...], right[:, here]).astype(half.dtype)
        half[order:, here] = dot(wave[...], right[:, there]).astype(half.dtype)
    left_copy.wait()
    for first in range(0, order, tile):
        here = slice(first, first + tile)
        there = slice(order + first, order + first + tile)
        for top in range(0, order, tile):
            line = slice(top, top + tile)
            real = dot(left[line, :], half[:, here])
            imag = dot(left[order + top : order + top + tile, :], half[:, here])
            inverse = jnp.minimum(lax.rsqrt(real * real + imag * imag), 1.0 / MAG_FLOOR)
            shrink = 1.0 - measured[0, line, here].astype(jnp.float32) * inverse
            resid[line, here] = (real * shrink).astype(resid.dtype)
            resid[line, there] = (imag * shrink).astype(resid.dtype)
    for first in range(0, order, tile):
        here = slice(first, first + tile)
        there = slice(order + first, order + first + tile)
        turned[:order, here] = dot(resid[...], left[:, here]).astype(turned.dtype)
        turned[order:, here] = dot(resid[...], left[:, there]).astype(turned.dtype)
    for first in range(0, order, tile):
        here = slice(first, first + tile)
        there = slice(order + first, order + first + tile)
        padded[reach : reach + order, here] = dot(right[:order, :], turned[:, here])
        padded[reach : reach + order, there] = dot(right[order:, :], turned[:, here])

    @pl.loop(0, total_rows // step)
    def _(i):
        place = pl.ds(pl.multiple_of(i * step, step), step)
        moved = rows_from(padded, reach - first_row + i * step, step).astype(jnp.bfloat16)
        for back, (low, high) in zip(backs, chunks):
            back[place, : high - low] = moved[:, low:high]
            back[place, high - low :] = moved[:, order + low : order + high]

    for fill in fills:
        fill.wait()


def slot_backs(cells, probe, measured, dealing, rows, tile_rows, tile_cols, chunks):
    order = probe.shape[1]
    total_rows = cells.shape[0]
    right, left = dft_tables(order)
    wide_cols = 2 * order
    fill_cols = 2048
    bf16, f32 = jnp.bfloat16, jnp.float32
    *backs, empty = pl.pallas_call(
        functools.partial(slot_kernel, chunks),
        out_shape=tuple(
            jax.ShapeDtypeStruct((total_rows, 2 * (high - low)), bf16) for low, high in chunks
        )
        + (jax.ShapeDtypeStruct((2, tile_rows, tile_cols), f32),),
        in_specs=[SMEM, SMEM, VMEM, VMEM, VMEM, ANY, ANY],
        out_specs=(VMEM,) * len(chunks) + (ANY,),
        scratch_shapes=[
            pltpu.VMEM((total_rows + SUBLANES, wide_cols), f32),
            pltpu.VMEM((order, wide_cols), bf16),
            pltpu.VMEM((wide_cols, order), bf16),
            pltpu.VMEM((order, wide_cols), bf16),
            pltpu.VMEM((wide_cols, order), bf16),
            pltpu.VMEM((2 * total_rows - order + SUBLANES, wide_cols), f32),
            pltpu.VMEM((2, tile_rows, fill_cols), f32),
            pltpu.VMEM((wide_cols, wide_cols), bf16),
            pltpu.VMEM((wide_cols, wide_cols), bf16),
            pltpu.SemaphoreType.DMA((tile_cols // fill_cols,)),
            pltpu.SemaphoreType.DMA((2,)),
        ],
        compiler_params=pltpu.CompilerParams(vmem_limit_bytes=40 * 2**20),
        cost_estimate=pl.CostEstimate(
            flops=8 * 2 * order**3 * 2, bytes_accessed=20 * 2**20, transcendentals=order * order
        ),
        name="slot",
    )(dealing, rows, cells, probe, measured, jnp.asarray(right), jnp.asarray(left))
    return backs, empty


def partial_kernel(reach, own_rows, shifts, low, dealing, rows, pieces, back, *out):
    *parts, total = out
    slots, tile_rows = back.shape[0], back.shape[1]
    width = back.shape[2] // 2
    order = pieces.shape[2] // 2
    count = tile_rows // SUBLANES
    total[...] = jnp.zeros_like(total)
    sub = lax.broadcasted_iota(jnp.int32, (1, SUBLANES, 2 * width), 1)
    nothing = jnp.zeros((1, SUBLANES, 2 * width), jnp.float32)

    @pl.loop(0, slots, unroll=2)
    def _(slot):
        start = (shifts - 1) * own_rows - rows[dealing[slot]]
        aligned = pl.multiple_of(start // SUBLANES * SUBLANES, SUBLANES)
        rest = start - aligned
        patch_real = pieces[slot, :, low : low + width].astype(jnp.float32)
        patch_imag = pieces[slot, :, order + low : order + low + width].astype(jnp.float32)
        real = back[slot, :, :width].astype(jnp.float32)
        imag = back[slot, :, width:].astype(jnp.float32)
        terms = jnp.concatenate(
            [patch_real * real + patch_imag * imag, patch_real * imag - patch_imag * real], axis=1
        )
        turned = pltpu.roll(terms.reshape(count, SUBLANES, 2 * width), rest, 1)
        before = jnp.concatenate([nothing, turned], axis=0)
        after = jnp.concatenate([turned, nothing], axis=0)
        moved = jnp.where(sub < rest, before, after).reshape(tile_rows + SUBLANES, 2 * width)
        total[pl.ds(aligned, tile_rows + SUBLANES), :] += moved

    for e, part in enumerate(parts):
        part[...] = total[e * own_rows : (e + 1) * own_rows, :].astype(part.dtype)


def probe_partials(pieces, back, dealing, rows, own_rows, reach, shifts, low, dtypes):
    tile_rows, wide = back.shape[1], back.shape[2]
    return pl.pallas_call(
        functools.partial(partial_kernel, reach, own_rows, shifts, low),
        out_shape=tuple(jax.ShapeDtypeStruct((own_rows, wide), dtype) for dtype in dtypes),
        in_specs=[SMEM, SMEM, VMEM, VMEM],
        out_specs=(VMEM,) * len(dtypes),
        scratch_shapes=[pltpu.VMEM((shifts * own_rows + tile_rows + SUBLANES, wide), jnp.float32)],
        compiler_params=pltpu.CompilerParams(vmem_limit_bytes=16 * 2**20),
        cost_estimate=pl.CostEstimate(flops=0, bytes_accessed=4 * 2**20, transcendentals=0),
        name="partial",
    )(dealing, rows, pieces, back)


def block_places(dealing, cols, order, tile_cols):
    base, _ = window_start(cols[dealing], order, tile_cols)
    count = (order + LANES) // LANES
    blocks = (base[:, None] // LANES + jnp.arange(count, dtype=jnp.int32)[None, :]).reshape(-1)
    same = blocks[:, None] == blocks[None, :]
    return blocks, jnp.argmax(same, axis=1).astype(jnp.int32)


def place_kernel(
    order, own_rows, top, chunks, dealing, rows, cols, blocks, owners, probe, *rest
):
    backs, (empty, out, totals, spread, sems) = rest[: len(chunks)], rest[len(chunks) :]
    del empty
    slots, tile_rows = backs[0].shape[0], backs[0].shape[1]
    count = (order + LANES) // LANES
    me = lax.axis_index("row")
    spread[0:top, :] = jnp.zeros((top, 2 * order), jnp.float32)
    spread[top : top + order, :order] = probe[0].astype(jnp.float32)
    spread[top : top + order, order:] = probe[1].astype(jnp.float32)
    spread[top + order :, :] = jnp.zeros((spread.shape[0] - top - order, 2 * order), jnp.float32)
    totals[...] = jnp.zeros_like(totals)
    lane = lax.broadcasted_iota(jnp.int32, (tile_rows, LANES), 1)

    @pl.loop(0, slots, unroll=2)
    def _(slot):
        _, offset = window_start(cols[dealing[slot]], order, out.shape[2])
        shift = lax.rem(offset, LANES)
        around = rows_from(spread, top + me * own_rows - rows[dealing[slot]], tile_rows)
        turned = [[], []]
        for back, (low, high) in zip(backs, chunks):
            for first in range(low, high, LANES):
                here = slice(first - low, first - low + LANES)
                there = slice(high - low + first - low, high - low + first - low + LANES)
                real = back[slot, :, here].astype(jnp.float32)
                imag = back[slot, :, there].astype(jnp.float32)
                probe_real = around[:, first : first + LANES]
                probe_imag = around[:, order + first : order + first + LANES]
                turned[0].append(pltpu.roll(probe_real * real + probe_imag * imag, shift, 1))
                turned[1].append(pltpu.roll(probe_real * imag - probe_imag * real, shift, 1))
        nothing = jnp.zeros((tile_rows, LANES), jnp.float32)
        for b in range(count):
            owner = owners[slot * count + b]
            for part in range(2):
                before = turned[part][b - 1] if b else nothing
                after = turned[part][b] if b < count - 1 else nothing
                totals[owner, part] += jnp.where(lane < offset, before, after)

    def copy(number):
        place = pl.multiple_of(blocks[number] * LANES, LANES)
        return pltpu.make_async_copy(totals.at[number], out.at[:, :, pl.ds(place, LANES)], sems.at[number])

    @pl.loop(0, slots * count)
    def _(number):
        @pl.when(owners[number] == number)
        def _():
            copy(number).start()

    @pl.loop(0, slots * count)
    def _(number):
        @pl.when(owners[number] == number)
        def _():
            copy(number).wait()


def place_windows(backs, empty, probe, dealing, rows, cols, own_rows, total_rows, chunks):
    order = probe.shape[1]
    slots, tile_rows = backs[0].shape[0], backs[0].shape[1]
    tile_cols = empty.shape[2]
    count = (order + LANES) // LANES
    blocks, owners = block_places(dealing, cols, order, tile_cols)
    top = -(-(total_rows - order) // SUBLANES) * SUBLANES
    spread_rows = -(-(top + total_rows) // SUBLANES) * SUBLANES + tile_rows + SUBLANES
    return pl.pallas_call(
        functools.partial(place_kernel, order, own_rows, top, chunks),
        out_shape=jax.ShapeDtypeStruct(empty.shape, empty.dtype),
        in_specs=[SMEM, SMEM, SMEM, SMEM, SMEM, VMEM] + [VMEM] * len(backs) + [ANY],
        out_specs=ANY,
        scratch_shapes=[
            pltpu.VMEM((slots * count, 2, tile_rows, LANES), jnp.float32),
            pltpu.VMEM((spread_rows, 2 * order), jnp.float32),
            pltpu.SemaphoreType.DMA((slots * count,)),
        ],
        input_output_aliases={6 + len(backs): 0},
        compiler_params=pltpu.CompilerParams(vmem_limit_bytes=24 * 2**20),
        cost_estimate=pl.CostEstimate(flops=0, bytes_accessed=6 * 2**20, transcendentals=0),
        name="place",
    )(dealing, rows, cols, blocks, owners, probe, *backs, empty)


def strides(devices):
    steps, stride = [], 1
    while stride < devices:
        radix = 4 if len(steps) >= 2 and (devices // stride) % 4 == 0 else 2
        steps.append((stride, radix))
        stride *= radix
    return steps


def turn(x, stride, radix, distance, devices):
    pairs = []
    for d in range(devices):
        digit = d // stride % radix
        pairs.append((d, d + ((digit + distance) % radix - digit) * stride))
    return lax.ppermute(x, "row", pairs)


def join(whole, devices):
    me = lax.axis_index("row")
    rows, width = whole.shape
    for axis, (stride, radix) in enumerate(reversed(strides(devices))):
        digit = me // stride % radix
        shares = [whole] + [turn(whole, stride, radix, distance, devices) for distance in range(1, radix)]
        pieces = []
        for k in range(radix):
            distance = lax.rem(digit - k + radix, radix)
            piece = shares[0]
            for d in range(1, radix):
                piece = jnp.where(distance == d, shares[d], piece)
            pieces.append(piece)
        whole = jnp.stack(pieces, axis=axis)
    return whole.reshape(devices * rows, width)


def sum_probe(pieces, back, dealing, rows, own_rows, reach, low, devices):
    order = pieces.shape[2] // 2
    scale = 1.0 / dealing.shape[0]
    shifts = -(-reach // own_rows) + 1
    held = -(-order // own_rows)
    middle = (shifts - 1) // 2
    own = shifts - 1 - middle
    direct = shifts <= 8
    dtypes = [jnp.bfloat16 if direct and e != own else jnp.float32 for e in range(shifts)]
    parts = probe_partials(pieces, back, dealing, rows, own_rows, reach, shifts, low, dtypes)
    if direct:
        total = parts[own]
        for e in range(shifts):
            if e != own:
                pairs = [
                    (d, d - shifts + 1 + e + middle)
                    for d in range(devices)
                    if 0 <= d - shifts + 1 + e < held
                ]
                total = total + lax.ppermute(parts[e], "row", pairs).astype(jnp.float32)
        whole = join((total * scale).astype(jnp.bfloat16), devices)
        first = middle * own_rows
    else:
        spread = jnp.zeros(((devices + shifts) * own_rows, back.shape[2]), jnp.float32)
        start = lax.axis_index("row") * own_rows
        spread = lax.dynamic_update_slice(spread, jnp.concatenate(parts, axis=0), (start, 0))
        first = (shifts - 1) * own_rows
        whole = lax.psum(spread, "row") * scale
    return whole[first : first + order].astype(jnp.float32)


def body(object_field, probe, amplitude, row_offsets, col_offsets, dealing):
    order = probe.shape[1]
    devices = lax.axis_size("row")
    own_rows, tile_cols = object_field.shape[1], object_field.shape[2]
    total_rows = devices * own_rows
    tile_rows = -(-own_rows // SUBLANES) * SUBLANES
    spare = tile_rows - own_rows
    cut = order // LANES * 3 // 4 * LANES
    chunks = ((0, cut), (cut, order))
    if spare:
        object_field = jnp.pad(object_field, ((0, 0), (0, spare), (0, 0)))
    pieces = fetch_windows(object_field, dealing, col_offsets, order)
    strips = lax.all_to_all(pieces, "row", split_axis=0, concat_axis=0, tiled=True)
    cells = strips[:, :own_rows].reshape(total_rows, 2 * order)
    backs, empty = slot_backs(
        cells, probe, amplitude, dealing, row_offsets, tile_rows, tile_cols, chunks
    )
    arrived, sums = [], []
    for back, (low, high) in zip(backs, chunks):
        outgoing = back.reshape(devices, own_rows, 2 * (high - low))
        if spare:
            outgoing = jnp.pad(outgoing, ((0, 0), (0, spare), (0, 0)))
        arrived.append(lax.all_to_all(outgoing, "row", split_axis=0, concat_axis=0, tiled=True))
    for here, (low, high) in zip(arrived, chunks):
        sums.append(
            sum_probe(pieces, here, dealing, row_offsets, own_rows, total_rows - order, low, devices)
        )
    widths = [high - low for low, high in chunks]
    probe_grad = jnp.stack(
        [
            jnp.concatenate([total[:, :width] for total, width in zip(sums, widths)], axis=1),
            jnp.concatenate([total[:, width:] for total, width in zip(sums, widths)], axis=1),
        ]
    )
    object_grad = place_windows(
        arrived, empty, probe, dealing, row_offsets, col_offsets, own_rows, total_rows, chunks
    )
    if spare:
        object_grad = object_grad[:, :own_rows]
    return (object_grad, probe_grad)


def solution(mesh):
    return jax.shard_map(
        body,
        mesh=mesh,
        in_specs=(
            P(None, ("groups", "row"), None),
            P("groups", None, None),
            P(("groups", "row"), None, None),
            P("groups"),
            P("groups"),
            P("groups"),
        ),
        out_specs=(P(None, ("groups", "row"), None), P("groups", None, None)),
        check_vma=False,
    )
```

```python
import functools
import math

import jax
import jax.numpy as jnp
import numpy as np
from jax import lax
from jax.experimental import pallas as pl
from jax.experimental.pallas import tpu as pltpu
from jax.sharding import PartitionSpec as P

MAG_FLOOR = 0.25
LANES = 128
SUBLANES = 8
SMEM = pl.BlockSpec(memory_space=pltpu.SMEM)
VMEM = pl.BlockSpec(memory_space=pltpu.VMEM)
ANY = pl.BlockSpec(memory_space=pl.ANY)


def dft_tables(order):
    indices = np.arange(order, dtype=np.int32)
    phases = indices[:, None] * indices[None, :] % order
    angles = phases.astype(np.float32) * np.float32(2.0 * math.pi / order)
    factor = np.float32(1.0 / math.sqrt(order))
    real_part = np.cos(angles) * factor
    imag_part = -np.sin(angles) * factor
    right_table = np.block([[real_part, imag_part], [-imag_part, real_part]])
    left_table = np.block([[real_part, -imag_part], [imag_part, real_part]])
    return right_table.astype(jnp.bfloat16), left_table.astype(jnp.bfloat16)


def window_start(column, order, tile_cols):
    span = order + LANES
    base = jnp.minimum(column // LANES, (tile_cols - span) // LANES) * LANES
    return pl.multiple_of(base, LANES), column - base


def rows_from(ref, start, count):
    aligned = pl.multiple_of(start // SUBLANES * SUBLANES, SUBLANES)
    rest = start - aligned
    width = ref.shape[-1]
    blocks = ref[pl.ds(aligned, count + SUBLANES), :].reshape(-1, SUBLANES, width)
    turned = pltpu.roll(blocks, lax.rem(SUBLANES - rest, SUBLANES), 1)
    sub = lax.broadcasted_iota(jnp.int32, (1, SUBLANES, width), 1)
    picked = jnp.where(sub < SUBLANES - rest, turned[:-1], turned[1:])
    return picked.reshape(count, width)


def partner(k, paired):
    return lax.bitwise_xor(lax.axis_index("row"), k) if paired else k


def fetch_kernel(order, paired, dealing, cols, tile, *rest):
    *outs, held, sems = rest
    tile_rows, tile_cols = tile.shape[1], tile.shape[2]
    span = order + LANES
    copies, offsets = [], []
    for k in range(len(outs)):
        base, offset = window_start(cols[dealing[partner(k, paired)]], order, tile_cols)
        copy = pltpu.make_async_copy(tile.at[:, :, pl.ds(base, span)], held.at[k], sems.at[k])
        copy.start()
        copies.append(copy)
        offsets.append(offset)
    lane = lax.broadcasted_iota(jnp.int32, (tile_rows, LANES), 1)
    for k, out in enumerate(outs):
        copies[k].wait()
        offset = offsets[k]
        shift = lax.rem(LANES - lax.rem(offset, LANES), LANES)
        for part in range(2):
            turned = [
                pltpu.roll(held[k, part, :, b * LANES : (b + 1) * LANES], shift, 1)
                for b in range(span // LANES)
            ]
            for b in range(order // LANES):
                first = part * order + b * LANES
                cells = jnp.where(lane < LANES - offset, turned[b], turned[b + 1])
                out[:, first : first + LANES] = cells.astype(out.dtype)


def fetch_windows(tile, dealing, cols, order, paired):
    slots, tile_rows = dealing.shape[0], tile.shape[1]
    span = order + LANES
    return pl.pallas_call(
        functools.partial(fetch_kernel, order, paired),
        out_shape=(jax.ShapeDtypeStruct((tile_rows, 2 * order), jnp.bfloat16),) * slots,
        in_specs=[SMEM, SMEM, ANY],
        out_specs=(VMEM,) * slots,
        scratch_shapes=[
            pltpu.VMEM((slots, 2, tile_rows, span), jnp.float32),
            pltpu.SemaphoreType.DMA((slots,)),
        ],
        compiler_params=pltpu.CompilerParams(vmem_limit_bytes=54 * 2**20),
        cost_estimate=pl.CostEstimate(flops=0, bytes_accessed=6 * 2**20, transcendentals=0),
        name="fetch",
    )(dealing, cols, tile)


def exchange(items, paired):
    if paired:
        devices = len(items)
        return [items[0]] + [
            lax.ppermute(items[k], "row", [(d, d ^ k) for d in range(devices)])
            for k in range(1, devices)
        ]
    arrived = lax.all_to_all(jnp.stack(items), "row", split_axis=0, concat_axis=0, tiled=True)
    return [arrived[k] for k in range(len(items))]


def slot_kernel(slots, own_rows, paired, dealing, rows, probe, measured, right_table, left_table, *rest):
    cells, backs = rest[:slots], rest[slots : 2 * slots]
    empty, wide, wave, half, resid, turned, padded, zeros, right, left, sem, table_sem = rest[2 * slots :]
    order = probe.shape[1]
    total_rows = slots * own_rows
    reach = total_rows - order
    me = lax.axis_index("row")
    first_row = rows[dealing[me]]
    step = 64
    tile = 256

    right_copy = pltpu.make_async_copy(right_table, right, table_sem.at[0])
    left_copy = pltpu.make_async_copy(left_table, left, table_sem.at[1])
    right_copy.start()
    left_copy.start()
    zeros[...] = jnp.zeros_like(zeros)
    fills = []
    for b in range(empty.shape[2] // zeros.shape[2]):
        fill = pltpu.make_async_copy(
            zeros, empty.at[:, :, b * zeros.shape[2] : (b + 1) * zeros.shape[2]], sem.at[b]
        )
        fill.start()
        fills.append(fill)

    for k, cell in enumerate(cells):
        place = partner(k, paired) * own_rows
        if own_rows % SUBLANES == 0:
            place = pl.multiple_of(place, SUBLANES)
        wide[pl.ds(place, own_rows), :] = cell[:own_rows, :].astype(jnp.float32)
    wide[total_rows:, :] = jnp.zeros((SUBLANES, 2 * order), jnp.float32)
    padded[0:reach, :] = jnp.zeros((reach, 2 * order), jnp.float32)
    below = padded.shape[0] - reach - order
    padded[reach + order :, :] = jnp.zeros((below, 2 * order), jnp.float32)

    @pl.loop(0, order // step)
    def _(i):
        place = pl.ds(pl.multiple_of(i * step, step), step)
        found = rows_from(wide, first_row + i * step, step)
        real, imag = found[:, :order], found[:, order:]
        probe_real = probe[0, place, :].astype(jnp.float32)
        probe_imag = probe[1, place, :].astype(jnp.float32)
        wave[place, :order] = (probe_real * real - probe_imag * imag).astype(wave.dtype)
        wave[place, order:] = (probe_real * imag + probe_imag * real).astype(wave.dtype)

    def dot(a, b):
        return jnp.dot(a, b, preferred_element_type=jnp.float32)

    right_copy.wait()
    for first in range(0, order, tile):
        here = slice(first, first + tile)
        there = slice(order + first, order + first + tile)
        half[:order, here] = dot(wave[...], right[:, here]).astype(half.dtype)
        half[order:, here] = dot(wave[...], right[:, there]).astype(half.dtype)
    left_copy.wait()
    for first in range(0, order, tile):
        here = slice(first, first + tile)
        there = slice(order + first, order + first + tile)
        for top in range(0, order, tile):
            line = slice(top, top + tile)
            real = dot(left[line, :], half[:, here])
            imag = dot(left[order + top : order + top + tile, :], half[:, here])
            inverse = jnp.minimum(lax.rsqrt(real * real + imag * imag), 1.0 / MAG_FLOOR)
            shrink = 1.0 - measured[0, line, here].astype(jnp.float32) * inverse
            resid[line, here] = (real * shrink).astype(resid.dtype)
            resid[line, there] = (imag * shrink).astype(resid.dtype)
    for first in range(0, order, tile):
        here = slice(first, first + tile)
        there = slice(order + first, order + first + tile)
        turned[:order, here] = dot(resid[...], left[:, here]).astype(turned.dtype)
        turned[order:, here] = dot(resid[...], left[:, there]).astype(turned.dtype)
    for first in range(0, order, tile):
        here = slice(first, first + tile)
        there = slice(order + first, order + first + tile)
        padded[reach : reach + order, here] = dot(right[:order, :], turned[:, here])
        padded[reach : reach + order, there] = dot(right[order:, :], turned[:, here])

    for k, back in enumerate(backs):
        start = reach - first_row + partner(k, paired) * own_rows
        back[...] = rows_from(padded, start, back.shape[0]).astype(back.dtype)

    for fill in fills:
        fill.wait()


def slot_backs(cells, probe, measured, dealing, rows, own_rows, tile_cols, paired):
    order = probe.shape[1]
    slots, tile_rows = len(cells), cells[0].shape[0]
    total_rows = slots * own_rows
    right, left = dft_tables(order)
    wide_cols = 2 * order
    fill_cols = 2048
    bf16, f32 = jnp.bfloat16, jnp.float32
    *backs, empty = pl.pallas_call(
        functools.partial(slot_kernel, slots, own_rows, paired),
        out_shape=(jax.ShapeDtypeStruct((tile_rows, wide_cols), bf16),) * slots
        + (jax.ShapeDtypeStruct((2, tile_rows, tile_cols), f32),),
        in_specs=[SMEM, SMEM, VMEM, VMEM, ANY, ANY] + [VMEM] * slots,
        out_specs=(VMEM,) * slots + (ANY,),
        scratch_shapes=[
            pltpu.VMEM((total_rows + SUBLANES, wide_cols), f32),
            pltpu.VMEM((order, wide_cols), bf16),
            pltpu.VMEM((wide_cols, order), bf16),
            pltpu.VMEM((order, wide_cols), bf16),
            pltpu.VMEM((wide_cols, order), bf16),
            pltpu.VMEM((2 * total_rows - order + tile_rows + SUBLANES, wide_cols), f32),
            pltpu.VMEM((2, tile_rows, fill_cols), f32),
            pltpu.VMEM((wide_cols, wide_cols), bf16),
            pltpu.VMEM((wide_cols, wide_cols), bf16),
            pltpu.SemaphoreType.DMA((tile_cols // fill_cols,)),
            pltpu.SemaphoreType.DMA((2,)),
        ],
        compiler_params=pltpu.CompilerParams(vmem_limit_bytes=40 * 2**20),
        cost_estimate=pl.CostEstimate(
            flops=8 * 2 * order**3 * 2, bytes_accessed=20 * 2**20, transcendentals=order * order
        ),
        name="slot",
    )(dealing, rows, probe, measured, jnp.asarray(right), jnp.asarray(left), *cells)
    return backs, empty


def partial_kernel(slots, own_rows, shifts, paired, dealing, rows, *rest):
    pieces, backs, (*parts, total) = rest[:slots], rest[slots : 2 * slots], rest[2 * slots :]
    tile_rows, width = backs[0].shape
    order = width // 2
    count = tile_rows // SUBLANES
    total[...] = jnp.zeros_like(total)
    sub = lax.broadcasted_iota(jnp.int32, (1, SUBLANES, width), 1)
    nothing = jnp.zeros((1, SUBLANES, width), jnp.float32)
    for k in range(slots):
        start = (shifts - 1) * own_rows - rows[dealing[partner(k, paired)]]
        aligned = pl.multiple_of(start // SUBLANES * SUBLANES, SUBLANES)
        rest_rows = start - aligned
        patch_real = pieces[k][:, :order].astype(jnp.float32)
        patch_imag = pieces[k][:, order:].astype(jnp.float32)
        real = backs[k][:, :order].astype(jnp.float32)
        imag = backs[k][:, order:].astype(jnp.float32)
        terms = jnp.concatenate(
            [patch_real * real + patch_imag * imag, patch_real * imag - patch_imag * real], axis=1
        )
        turned = pltpu.roll(terms.reshape(count, SUBLANES, width), rest_rows, 1)
        before = jnp.concatenate([nothing, turned], axis=0)
        after = jnp.concatenate([turned, nothing], axis=0)
        moved = jnp.where(sub < rest_rows, before, after).reshape(tile_rows + SUBLANES, width)
        total[pl.ds(aligned, tile_rows + SUBLANES), :] += moved

    for e, part in enumerate(parts):
        part[...] = total[e * own_rows : (e + 1) * own_rows, :].astype(part.dtype)


def probe_partials(pieces, backs, dealing, rows, own_rows, shifts, dtypes, paired):
    slots, (tile_rows, width) = len(backs), backs[0].shape
    return pl.pallas_call(
        functools.partial(partial_kernel, slots, own_rows, shifts, paired),
        out_shape=tuple(jax.ShapeDtypeStruct((own_rows, width), dtype) for dtype in dtypes),
        in_specs=[SMEM, SMEM] + [VMEM] * (2 * slots),
        out_specs=(VMEM,) * len(dtypes),
        scratch_shapes=[pltpu.VMEM((shifts * own_rows + tile_rows + SUBLANES, width), jnp.float32)],
        compiler_params=pltpu.CompilerParams(vmem_limit_bytes=16 * 2**20),
        cost_estimate=pl.CostEstimate(flops=0, bytes_accessed=4 * 2**20, transcendentals=0),
        name="partial",
    )(dealing, rows, *pieces, *backs)


def block_places(dealing, cols, order, tile_cols):
    base, _ = window_start(cols[dealing], order, tile_cols)
    count = (order + LANES) // LANES
    blocks = (base[:, None] // LANES + jnp.arange(count, dtype=jnp.int32)[None, :]).reshape(-1)
    same = blocks[:, None] == blocks[None, :]
    return blocks, jnp.argmax(same, axis=1).astype(jnp.int32)


def place_kernel(
    slots, order, own_rows, top, paired, dealing, rows, cols, blocks, owners, probe, *rest
):
    backs, (empty, out, totals, spread, sems) = rest[:slots], rest[slots:]
    del empty
    tile_rows = backs[0].shape[0]
    count = (order + LANES) // LANES
    me = lax.axis_index("row")
    spread[0:top, :] = jnp.zeros((top, 2 * order), jnp.float32)
    spread[top : top + order, :order] = probe[0].astype(jnp.float32)
    spread[top : top + order, order:] = probe[1].astype(jnp.float32)
    spread[top + order :, :] = jnp.zeros((spread.shape[0] - top - order, 2 * order), jnp.float32)
    totals[...] = jnp.zeros_like(totals)
    lane = lax.broadcasted_iota(jnp.int32, (tile_rows, LANES), 1)
    nothing = jnp.zeros((tile_rows, LANES), jnp.float32)

    for k, back in enumerate(backs):
        slot = partner(k, paired)
        _, offset = window_start(cols[dealing[slot]], order, out.shape[2])
        shift = lax.rem(offset, LANES)
        around = rows_from(spread, top + me * own_rows - rows[dealing[slot]], tile_rows)
        turned = [[], []]
        for first in range(0, order, LANES):
            here = slice(first, first + LANES)
            there = slice(order + first, order + first + LANES)
            real = back[:, here].astype(jnp.float32)
            imag = back[:, there].astype(jnp.float32)
            probe_real, probe_imag = around[:, here], around[:, there]
            turned[0].append(pltpu.roll(probe_real * real + probe_imag * imag, shift, 1))
            turned[1].append(pltpu.roll(probe_real * imag - probe_imag * real, shift, 1))
        for b in range(count):
            owner = owners[slot * count + b]
            for part in range(2):
                before = turned[part][b - 1] if b else nothing
                after = turned[part][b] if b < count - 1 else nothing
                totals[owner, part] += jnp.where(lane < offset, before, after)

    def copy(number):
        place = pl.multiple_of(blocks[number] * LANES, LANES)
        return pltpu.make_async_copy(totals.at[number], out.at[:, :, pl.ds(place, LANES)], sems.at[number])

    @pl.loop(0, slots * count)
    def _(number):
        @pl.when(owners[number] == number)
        def _():
            copy(number).start()

    @pl.loop(0, slots * count)
    def _(number):
        @pl.when(owners[number] == number)
        def _():
            copy(number).wait()


def place_windows(backs, empty, probe, dealing, rows, cols, own_rows, paired):
    order = probe.shape[1]
    slots, tile_rows = len(backs), backs[0].shape[0]
    total_rows = slots * own_rows
    tile_cols = empty.shape[2]
    count = (order + LANES) // LANES
    blocks, owners = block_places(dealing, cols, order, tile_cols)
    top = -(-(total_rows - order) // SUBLANES) * SUBLANES
    spread_rows = -(-(top + total_rows) // SUBLANES) * SUBLANES + tile_rows + SUBLANES
    return pl.pallas_call(
        functools.partial(place_kernel, slots, order, own_rows, top, paired),
        out_shape=jax.ShapeDtypeStruct(empty.shape, empty.dtype),
        in_specs=[SMEM, SMEM, SMEM, SMEM, SMEM, VMEM] + [VMEM] * slots + [ANY],
        out_specs=ANY,
        scratch_shapes=[
            pltpu.VMEM((slots * count, 2, tile_rows, LANES), jnp.float32),
            pltpu.VMEM((spread_rows, 2 * order), jnp.float32),
            pltpu.SemaphoreType.DMA((slots * count,)),
        ],
        input_output_aliases={6 + slots: 0},
        compiler_params=pltpu.CompilerParams(vmem_limit_bytes=24 * 2**20),
        cost_estimate=pl.CostEstimate(flops=0, bytes_accessed=6 * 2**20, transcendentals=0),
        name="place",
    )(dealing, rows, cols, blocks, owners, probe, *backs, empty)


def strides(devices):
    steps, stride = [], 1
    while stride < devices:
        radix = 4 if len(steps) >= 2 and (devices // stride) % 4 == 0 else 2
        steps.append((stride, radix))
        stride *= radix
    return steps


def turn(x, stride, radix, distance, devices):
    pairs = []
    for d in range(devices):
        digit = d // stride % radix
        pairs.append((d, d + ((digit + distance) % radix - digit) * stride))
    return lax.ppermute(x, "row", pairs)


def join(whole, devices):
    me = lax.axis_index("row")
    rows, width = whole.shape
    for axis, (stride, radix) in enumerate(reversed(strides(devices))):
        digit = me // stride % radix
        shares = [whole] + [turn(whole, stride, radix, distance, devices) for distance in range(1, radix)]
        pieces = []
        for k in range(radix):
            distance = lax.rem(digit - k + radix, radix)
            piece = shares[0]
            for d in range(1, radix):
                piece = jnp.where(distance == d, shares[d], piece)
            pieces.append(piece)
        whole = jnp.stack(pieces, axis=axis)
    return whole.reshape(devices * rows, width)


def sum_probe(pieces, backs, dealing, rows, own_rows, reach, paired):
    devices, width = len(backs), backs[0].shape[1]
    order = width // 2
    scale = 1.0 / dealing.shape[0]
    shifts = -(-reach // own_rows) + 1
    held = -(-order // own_rows)
    middle = (shifts - 1) // 2
    own = shifts - 1 - middle
    direct = shifts <= 8
    dtypes = [jnp.bfloat16 if direct and e != own else jnp.float32 for e in range(shifts)]
    parts = probe_partials(pieces, backs, dealing, rows, own_rows, shifts, dtypes, paired)
    if direct:
        total = parts[own]
        for e in range(shifts):
            if e != own:
                pairs = [
                    (d, d - shifts + 1 + e + middle)
                    for d in range(devices)
                    if 0 <= d - shifts + 1 + e < held
                ]
                total = total + lax.ppermute(parts[e], "row", pairs).astype(jnp.float32)
        whole = join((total * scale).astype(jnp.bfloat16), devices)
        first = middle * own_rows
    else:
        spread = jnp.zeros(((devices + shifts) * own_rows, width), jnp.float32)
        start = lax.axis_index("row") * own_rows
        spread = lax.dynamic_update_slice(spread, jnp.concatenate(parts, axis=0), (start, 0))
        first = (shifts - 1) * own_rows
        whole = lax.psum(spread, "row") * scale
    return whole[first : first + order].astype(jnp.float32)


def body(object_field, probe, amplitude, row_offsets, col_offsets, dealing):
    order = probe.shape[1]
    devices = lax.axis_size("row")
    own_rows, tile_cols = object_field.shape[1], object_field.shape[2]
    total_rows = devices * own_rows
    tile_rows = -(-own_rows // SUBLANES) * SUBLANES
    spare = tile_rows - own_rows
    paired = devices <= 16 and devices & (devices - 1) == 0
    if spare:
        object_field = jnp.pad(object_field, ((0, 0), (0, spare), (0, 0)))
    pieces = fetch_windows(object_field, dealing, col_offsets, order, paired)
    cells = exchange(pieces, paired)
    backs, empty = slot_backs(
        cells, probe, amplitude, dealing, row_offsets, own_rows, tile_cols, paired
    )
    backs = exchange(backs, paired)
    whole = sum_probe(pieces, backs, dealing, row_offsets, own_rows, total_rows - order, paired)
    probe_grad = jnp.stack([whole[:, :order], whole[:, order:]])
    object_grad = place_windows(
        backs, empty, probe, dealing, row_offsets, col_offsets, own_rows, paired
    )
    if spare:
        object_grad = object_grad[:, :own_rows]
    return (object_grad, probe_grad)


def solution(mesh):
    return jax.shard_map(
        body,
        mesh=mesh,
        in_specs=(
            P(None, ("groups", "row"), None),
            P("groups", None, None),
            P(("groups", "row"), None, None),
            P("groups"),
            P("groups"),
            P("groups"),
        ),
        out_specs=(P(None, ("groups", "row"), None), P("groups", None, None)),
        check_vma=False,
    )
```

```python
import functools
import math

import jax
import jax.numpy as jnp
import numpy as np
from jax import lax
from jax.experimental import pallas as pl
from jax.experimental.pallas import tpu as pltpu
from jax.sharding import PartitionSpec as P

MAG_FLOOR = 0.25
LANES = 128
SUBLANES = 8
SMEM = pl.BlockSpec(memory_space=pltpu.SMEM)
VMEM = pl.BlockSpec(memory_space=pltpu.VMEM)
ANY = pl.BlockSpec(memory_space=pl.ANY)


def dft_tables(order):
    indices = np.arange(order, dtype=np.int32)
    phases = indices[:, None] * indices[None, :] % order
    angles = phases.astype(np.float32) * np.float32(2.0 * math.pi / order)
    factor = np.float32(1.0 / math.sqrt(order))
    real_part = np.cos(angles) * factor
    imag_part = -np.sin(angles) * factor
    right_table = np.block([[real_part, imag_part], [-imag_part, real_part]])
    left_table = np.block([[real_part, -imag_part], [imag_part, real_part]])
    return right_table.astype(jnp.bfloat16), left_table.astype(jnp.bfloat16)


def window_start(column, order, tile_cols):
    span = order + LANES
    base = jnp.minimum(column // LANES, (tile_cols - span) // LANES) * LANES
    return pl.multiple_of(base, LANES), column - base


def rows_from(ref, start, count):
    aligned = pl.multiple_of(start // SUBLANES * SUBLANES, SUBLANES)
    rest = start - aligned
    width = ref.shape[-1]
    blocks = ref[pl.ds(aligned, count + SUBLANES), :].reshape(-1, SUBLANES, width)
    turned = pltpu.roll(blocks, lax.rem(SUBLANES - rest, SUBLANES), 1)
    sub = lax.broadcasted_iota(jnp.int32, (1, SUBLANES, width), 1)
    picked = jnp.where(sub < SUBLANES - rest, turned[:-1], turned[1:])
    return picked.reshape(count, width)


def fetch_kernel(order, dealing, cols, tile, out, held, sems):
    slots, tile_rows = out.shape[0], out.shape[1]
    tile_cols = tile.shape[2]
    span = order + LANES

    def copy(slot):
        base, _ = window_start(cols[dealing[slot]], order, tile_cols)
        return pltpu.make_async_copy(tile.at[:, :, pl.ds(base, span)], held.at[slot], sems.at[slot])

    @pl.loop(0, slots)
    def _(slot):
        copy(slot).start()

    lane = lax.broadcasted_iota(jnp.int32, (tile_rows, LANES), 1)

    @pl.loop(0, slots, unroll=2)
    def _(slot):
        copy(slot).wait()
        _, offset = window_start(cols[dealing[slot]], order, tile_cols)
        shift = lax.rem(LANES - lax.rem(offset, LANES), LANES)
        for part in range(2):
            turned = [
                pltpu.roll(held[slot, part, :, b * LANES : (b + 1) * LANES], shift, 1)
                for b in range(span // LANES)
            ]
            for b in range(order // LANES):
                first = part * order + b * LANES
                cells = jnp.where(lane < LANES - offset, turned[b], turned[b + 1])
                out[slot, :, first : first + LANES] = cells.astype(out.dtype)


def fetch_windows(tile, dealing, cols, order):
    slots, tile_rows, tile_cols = dealing.shape[0], tile.shape[1], tile.shape[2]
    span = order + LANES

    return pl.pallas_call(
        functools.partial(fetch_kernel, order),
        out_shape=jax.ShapeDtypeStruct((slots, tile_rows, 2 * order), jnp.bfloat16),
        in_specs=[SMEM, SMEM, ANY],
        out_specs=VMEM,
        scratch_shapes=[
            pltpu.VMEM((slots, 2, tile_rows, span), jnp.float32),
            pltpu.SemaphoreType.DMA((slots,)),
        ],
        compiler_params=pltpu.CompilerParams(vmem_limit_bytes=56 * 2**20),
        cost_estimate=pl.CostEstimate(flops=0, bytes_accessed=6 * 2**20, transcendentals=0),
        name="fetch",
    )(dealing, cols, tile)


def slot_kernel(
    dealing, rows, cells, probe, measured, right_table, left_table,
    terms, kept, sent, empty,
    wide, patch, wave, half, resid, turned, padded, mine, zeros, right, left, sem, table_sem,
):
    order = probe.shape[1]
    total_rows = cells.shape[0]
    reach = total_rows - order
    me = lax.axis_index("row")
    first_row = rows[dealing[me]]
    step = 64
    tile = 256

    right_copy = pltpu.make_async_copy(right_table, right, table_sem.at[0])
    left_copy = pltpu.make_async_copy(left_table, left, table_sem.at[1])
    right_copy.start()
    left_copy.start()
    zeros[...] = jnp.zeros_like(zeros)
    fills = []
    for b in range(empty.shape[2] // zeros.shape[2]):
        fill = pltpu.make_async_copy(
            zeros, empty.at[:, :, b * zeros.shape[2] : (b + 1) * zeros.shape[2]], sem.at[b]
        )
        fill.start()
        fills.append(fill)

    wide[0:total_rows, :] = cells[...].astype(jnp.float32)
    wide[total_rows:, :] = jnp.zeros((SUBLANES, 2 * order), jnp.float32)
    padded[0:reach, :] = jnp.zeros((reach, 2 * order), jnp.float32)
    padded[reach + order :, :] = jnp.zeros((reach + SUBLANES, 2 * order), jnp.float32)

    @pl.loop(0, order // step)
    def _(i):
        place = pl.ds(pl.multiple_of(i * step, step), step)
        found = rows_from(wide, first_row + i * step, step)
        patch[place, :] = found.astype(patch.dtype)
        real, imag = found[:, :order], found[:, order:]
        probe_real = probe[0, place, :].astype(jnp.float32)
        probe_imag = probe[1, place, :].astype(jnp.float32)
        wave[place, :order] = (probe_real * real - probe_imag * imag).astype(wave.dtype)
        wave[place, order:] = (probe_real * imag + probe_imag * real).astype(wave.dtype)

    def dot(a, b):
        return jnp.dot(a, b, preferred_element_type=jnp.float32)

    right_copy.wait()
    for first in range(0, order, tile):
        here = slice(first, first + tile)
        there = slice(order + first, order + first + tile)
        half[:order, here] = dot(wave[...], right[:, here]).astype(half.dtype)
        half[order:, here] = dot(wave[...], right[:, there]).astype(half.dtype)
    left_copy.wait()
    for first in range(0, order, tile):
        here = slice(first, first + tile)
        there = slice(order + first, order + first + tile)
        for top in range(0, order, tile):
            line = slice(top, top + tile)
            real = dot(left[line, :], half[:, here])
            imag = dot(left[order + top : order + top + tile, :], half[:, here])
            inverse = jnp.minimum(lax.rsqrt(real * real + imag * imag), 1.0 / MAG_FLOOR)
            shrink = 1.0 - measured[0, line, here].astype(jnp.float32) * inverse
            resid[line, here] = (real * shrink).astype(resid.dtype)
            resid[line, there] = (imag * shrink).astype(resid.dtype)
    for first in range(0, order, tile):
        here = slice(first, first + tile)
        there = slice(order + first, order + first + tile)
        turned[:order, here] = dot(resid[...], left[:, here]).astype(turned.dtype)
        turned[order:, here] = dot(resid[...], left[:, there]).astype(turned.dtype)
    for first in range(0, order, tile):
        here = slice(first, first + tile)
        there = slice(order + first, order + first + tile)
        for top in range(0, order, tile):
            line = slice(top, top + tile)
            real = dot(right[line, :], turned[:, here])
            imag = dot(right[order + top : order + top + tile, :], turned[:, here])
            probe_real = probe[0, line, here].astype(jnp.float32)
            probe_imag = probe[1, line, here].astype(jnp.float32)
            down = slice(reach + top, reach + top + tile)
            padded[down, here] = probe_real * real + probe_imag * imag
            padded[down, there] = probe_real * imag - probe_imag * real
            patch_real = patch[line, here].astype(jnp.float32)
            patch_imag = patch[line, there].astype(jnp.float32)
            mine[line, here] = patch_real * real + patch_imag * imag
            mine[line, there] = patch_real * imag - patch_imag * real

    @pl.loop(0, total_rows // step)
    def _(i):
        place = pl.ds(pl.multiple_of(i * step, step), step)
        terms[place, :] = rows_from(padded, reach - first_row + i * step, step).astype(terms.dtype)

    count = kept.shape[0]
    side = lax.rem(me, 2)
    kept[...] = mine[pl.ds(pl.multiple_of(side * count, count), count), :]
    sent[...] = mine[pl.ds(pl.multiple_of((1 - side) * count, count), count), :].astype(sent.dtype)
    for fill in fills:
        fill.wait()


def slot_terms(cells, probe, measured, dealing, rows, tile_rows, tile_cols):
    order = probe.shape[1]
    total_rows = cells.shape[0]
    right, left = dft_tables(order)
    wide_cols = 2 * order
    fill_cols = 2048
    bf16, f32 = jnp.bfloat16, jnp.float32
    return pl.pallas_call(
        slot_kernel,
        out_shape=(
            jax.ShapeDtypeStruct((total_rows, wide_cols), bf16),
            jax.ShapeDtypeStruct((order // 2, wide_cols), f32),
            jax.ShapeDtypeStruct((order // 2, wide_cols), bf16),
            jax.ShapeDtypeStruct((2, tile_rows, tile_cols), f32),
        ),
        in_specs=[SMEM, SMEM, VMEM, VMEM, VMEM, ANY, ANY],
        out_specs=(VMEM, VMEM, VMEM, ANY),
        scratch_shapes=[
            pltpu.VMEM((total_rows + SUBLANES, wide_cols), f32),
            pltpu.VMEM((order, wide_cols), bf16),
            pltpu.VMEM((order, wide_cols), bf16),
            pltpu.VMEM((wide_cols, order), bf16),
            pltpu.VMEM((order, wide_cols), bf16),
            pltpu.VMEM((wide_cols, order), bf16),
            pltpu.VMEM((2 * total_rows - order + SUBLANES, wide_cols), f32),
            pltpu.VMEM((order, wide_cols), f32),
            pltpu.VMEM((2, tile_rows, fill_cols), f32),
            pltpu.VMEM((wide_cols, wide_cols), bf16),
            pltpu.VMEM((wide_cols, wide_cols), bf16),
            pltpu.SemaphoreType.DMA((tile_cols // fill_cols,)),
            pltpu.SemaphoreType.DMA((2,)),
        ],
        compiler_params=pltpu.CompilerParams(vmem_limit_bytes=40 * 2**20),
        cost_estimate=pl.CostEstimate(
            flops=8 * 2 * order**3 * 2, bytes_accessed=20 * 2**20, transcendentals=order * order
        ),
        name="slot",
    )(dealing, rows, cells, probe, measured, jnp.asarray(right), jnp.asarray(left))


def block_places(dealing, cols, order, tile_cols):
    base, _ = window_start(cols[dealing], order, tile_cols)
    count = (order + LANES) // LANES
    blocks = (base[:, None] // LANES + jnp.arange(count, dtype=jnp.int32)[None, :]).reshape(-1)
    same = blocks[:, None] == blocks[None, :]
    return blocks, jnp.argmax(same, axis=1).astype(jnp.int32)


def place_kernel(order, dealing, cols, blocks, owners, terms, empty, out, totals, sems):
    del empty
    slots, tile_rows = terms.shape[0], terms.shape[1]
    tile_cols = out.shape[2]
    count = (order + LANES) // LANES
    totals[...] = jnp.zeros_like(totals)
    lane = lax.broadcasted_iota(jnp.int32, (tile_rows, LANES), 1)

    @pl.loop(0, slots, unroll=2)
    def _(slot):
        _, offset = window_start(cols[dealing[slot]], order, tile_cols)
        shift = lax.rem(offset, LANES)
        for part in range(2):
            turned = []
            for b in range(count - 1):
                first = part * order + b * LANES
                turned.append(pltpu.roll(terms[slot, :, first : first + LANES].astype(jnp.float32), shift, 1))
            nothing = jnp.zeros_like(turned[0])
            for b in range(count):
                before = turned[b - 1] if b else nothing
                after = turned[b] if b < count - 1 else nothing
                owner = owners[slot * count + b]
                totals[owner, part] += jnp.where(lane < offset, before, after)

    def copy(number):
        place = pl.multiple_of(blocks[number] * LANES, LANES)
        return pltpu.make_async_copy(totals.at[number], out.at[:, :, pl.ds(place, LANES)], sems.at[number])

    @pl.loop(0, slots * count)
    def _(number):
        @pl.when(owners[number] == number)
        def _():
            copy(number).start()

    @pl.loop(0, slots * count)
    def _(number):
        @pl.when(owners[number] == number)
        def _():
            copy(number).wait()


def place_windows(terms, empty, dealing, cols, order):

    slots, tile_rows = terms.shape[0], terms.shape[1]
    tile_cols = empty.shape[2]
    count = (order + LANES) // LANES
    blocks, owners = block_places(dealing, cols, order, tile_cols)
    return pl.pallas_call(
        functools.partial(place_kernel, order),
        out_shape=jax.ShapeDtypeStruct(empty.shape, empty.dtype),
        in_specs=[SMEM, SMEM, SMEM, SMEM, VMEM, ANY],
        out_specs=ANY,
        scratch_shapes=[
            pltpu.VMEM((slots * count, 2, tile_rows, LANES), jnp.float32),
            pltpu.SemaphoreType.DMA((slots * count,)),
        ],
        input_output_aliases={5: 0},
        compiler_params=pltpu.CompilerParams(vmem_limit_bytes=24 * 2**20),
        cost_estimate=pl.CostEstimate(flops=0, bytes_accessed=6 * 2**20, transcendentals=0),
        name="place",
    )(dealing, cols, blocks, owners, terms, empty)


def swap_sides(x, devices):
    return lax.ppermute(x, "row", [(d, d ^ 1) for d in range(devices)])


def sum_probe(kept, sent, devices, scale):
    side = lax.rem(lax.axis_index("row"), 2)
    total = (kept + swap_sides(sent, devices).astype(jnp.float32)).astype(jnp.bfloat16)
    groups = [list(range(core, devices, 2)) for core in range(2)]
    total = lax.psum(total, "row", axis_index_groups=groups)
    mine = (total.astype(jnp.float32) * scale).astype(jnp.bfloat16)
    other = swap_sides(mine, devices)
    return jnp.where(side == 0, jnp.concatenate([mine, other]), jnp.concatenate([other, mine]))


def body(object_field, probe, amplitude, row_offsets, col_offsets, dealing):
    order = probe.shape[1]
    devices = lax.axis_size("row")
    own_rows, tile_cols = object_field.shape[1], object_field.shape[2]
    tile_rows = -(-own_rows // SUBLANES) * SUBLANES
    spare = tile_rows - own_rows
    if spare:
        object_field = jnp.pad(object_field, ((0, 0), (0, spare), (0, 0)))
    pieces = fetch_windows(object_field, dealing, col_offsets, order)
    strips = lax.all_to_all(pieces, "row", split_axis=0, concat_axis=0, tiled=True)
    cells = strips[:, :own_rows].reshape(devices * own_rows, 2 * order)
    terms, kept, sent, empty = slot_terms(
        cells, probe, amplitude, dealing, row_offsets, tile_rows, tile_cols
    )
    outgoing = terms.reshape(devices, own_rows, 2 * order)
    if spare:
        outgoing = jnp.pad(outgoing, ((0, 0), (0, spare), (0, 0)))
    arrived = lax.all_to_all(outgoing, "row", split_axis=0, concat_axis=0, tiled=True)
    whole = sum_probe(kept, sent, devices, 1.0 / dealing.shape[0])
    whole = whole.astype(jnp.float32)
    probe_grad = jnp.stack([whole[:, :order], whole[:, order:]])
    object_grad = place_windows(arrived, empty, dealing, col_offsets, order)
    if spare:
        object_grad = object_grad[:, :own_rows]
    return (object_grad, probe_grad)


def solution(mesh):
    return jax.shard_map(
        body,
        mesh=mesh,
        in_specs=(
            P(None, ("groups", "row"), None),
            P("groups", None, None),
            P(("groups", "row"), None, None),
            P("groups"),
            P("groups"),
            P("groups"),
        ),
        out_specs=(P(None, ("groups", "row"), None), P("groups", None, None)),
        check_vma=False,
    )
```

```python
import functools
import math

import jax
import jax.numpy as jnp
import numpy as np
from jax import lax
from jax.experimental import pallas as pl
from jax.experimental.pallas import tpu as pltpu
from jax.sharding import PartitionSpec as P

MAG_FLOOR = 0.25
LANES = 128
SUBLANES = 8
SMEM = pl.BlockSpec(memory_space=pltpu.SMEM)
VMEM = pl.BlockSpec(memory_space=pltpu.VMEM)
ANY = pl.BlockSpec(memory_space=pl.ANY)


def dft_tables(order):
    indices = np.arange(order, dtype=np.int32)
    phases = indices[:, None] * indices[None, :] % order
    angles = phases.astype(np.float32) * np.float32(2.0 * math.pi / order)
    factor = np.float32(1.0 / math.sqrt(order))
    real_part = np.cos(angles) * factor
    imag_part = -np.sin(angles) * factor
    right_table = np.block([[real_part, imag_part], [-imag_part, real_part]])
    left_table = np.block([[real_part, -imag_part], [imag_part, real_part]])
    return right_table.astype(jnp.bfloat16), left_table.astype(jnp.bfloat16)


def window_start(column, order, tile_cols):
    span = order + LANES
    base = jnp.minimum(column // LANES, (tile_cols - span) // LANES) * LANES
    return pl.multiple_of(base, LANES), column - base


def rows_from(ref, start, count):
    aligned = pl.multiple_of(start // SUBLANES * SUBLANES, SUBLANES)
    rest = start - aligned
    width = ref.shape[-1]
    blocks = ref[pl.ds(aligned, count + SUBLANES), :].reshape(-1, SUBLANES, width)
    turned = pltpu.roll(blocks, lax.rem(SUBLANES - rest, SUBLANES), 1)
    sub = lax.broadcasted_iota(jnp.int32, (1, SUBLANES, width), 1)
    picked = jnp.where(sub < SUBLANES - rest, turned[:-1], turned[1:])
    return picked.reshape(count, width)


def partner(k, paired):
    return lax.bitwise_xor(lax.axis_index("row"), k) if paired else k


def fetch_kernel(order, dealing, cols, tile, out, token, held, sems):
    token[0] = dealing[0]
    slots, tile_rows = out.shape[0], out.shape[1]
    tile_cols = tile.shape[2]
    span = order + LANES

    def copy(slot):
        base, _ = window_start(cols[dealing[slot]], order, tile_cols)
        return pltpu.make_async_copy(tile.at[:, :, pl.ds(base, span)], held.at[slot], sems.at[slot])

    @pl.loop(0, slots)
    def _(slot):
        copy(slot).start()

    lane = lax.broadcasted_iota(jnp.int32, (tile_rows, LANES), 1)

    @pl.loop(0, slots, unroll=4)
    def _(slot):
        copy(slot).wait()
        _, offset = window_start(cols[dealing[slot]], order, tile_cols)
        shift = lax.rem(LANES - lax.rem(offset, LANES), LANES)
        for part in range(2):
            turned = [
                pltpu.roll(held[slot, part, :, b * LANES : (b + 1) * LANES], shift, 1)
                for b in range(span // LANES)
            ]
            for b in range(order // LANES):
                first = part * order + b * LANES
                cells = jnp.where(lane < LANES - offset, turned[b], turned[b + 1])
                out[slot, :, first : first + LANES] = cells.astype(out.dtype)


def fetch_windows(tile, dealing, cols, order):
    slots, tile_rows, tile_cols = dealing.shape[0], tile.shape[1], tile.shape[2]
    span = order + LANES

    return pl.pallas_call(
        functools.partial(fetch_kernel, order),
        out_shape=(
            jax.ShapeDtypeStruct((slots, tile_rows, 2 * order), jnp.bfloat16),
            jax.ShapeDtypeStruct((1,), jnp.int32),
        ),
        in_specs=[SMEM, SMEM, ANY],
        out_specs=(VMEM, SMEM),
        scratch_shapes=[
            pltpu.VMEM((slots, 2, tile_rows, span), jnp.float32),
            pltpu.SemaphoreType.DMA((slots,)),
        ],
        compiler_params=pltpu.CompilerParams(vmem_limit_bytes=56 * 2**20),
        cost_estimate=pl.CostEstimate(flops=0, bytes_accessed=6 * 2**20, transcendentals=0),
        name="fetch",
    )(dealing, cols, tile)


def prepare_kernel(order, dealing, cols, token, empty, blocks, owners, table, zeros, sems):
    del token
    count = (order + LANES) // LANES
    slots = dealing.shape[0]
    tile_cols = empty.shape[2]
    width = zeros.shape[2]
    zeros[...] = jnp.zeros_like(zeros)
    fills = []
    for b in range(tile_cols // width):
        fill = pltpu.make_async_copy(zeros, empty.at[:, :, b * width : (b + 1) * width], sems.at[b])
        fill.start()
        fills.append(fill)

    @pl.loop(0, tile_cols // LANES)
    def _(block):
        table[block] = -1

    @pl.loop(0, slots)
    def _(slot):
        base, _ = window_start(cols[dealing[slot]], order, tile_cols)
        for b in range(count):
            number = slot * count + b
            block = base // LANES + b
            blocks[number] = block
            known = table[block]
            owner = jnp.where(known < 0, number, known)
            owners[number] = owner
            table[block] = owner

    for fill in fills:
        fill.wait()


def prepare(dealing, cols, token, tile_shape, order):
    slots = dealing.shape[0]
    numbers = slots * (order + LANES) // LANES
    fill_cols = 2048
    return pl.pallas_call(
        functools.partial(prepare_kernel, order),
        out_shape=(
            jax.ShapeDtypeStruct(tile_shape, jnp.float32),
            jax.ShapeDtypeStruct((numbers,), jnp.int32),
            jax.ShapeDtypeStruct((numbers,), jnp.int32),
        ),
        in_specs=[SMEM, SMEM, SMEM],
        out_specs=(ANY, SMEM, SMEM),
        scratch_shapes=[
            pltpu.SMEM((tile_shape[2] // LANES,), jnp.int32),
            pltpu.VMEM(tile_shape[:2] + (fill_cols,), jnp.float32),
            pltpu.SemaphoreType.DMA((tile_shape[2] // fill_cols,)),
        ],
        compiler_params=pltpu.CompilerParams(vmem_limit_bytes=8 * 2**20),
        cost_estimate=pl.CostEstimate(flops=0, bytes_accessed=11 * 2**20, transcendentals=0),
        name="prepare",
    )(dealing, cols, token)


def exchange(items, paired):
    if paired:
        devices = len(items)
        return [items[0]] + [
            lax.ppermute(items[k], "row", [(d, d ^ k) for d in range(devices)])
            for k in range(1, devices)
        ]
    arrived = lax.all_to_all(jnp.stack(items), "row", split_axis=0, concat_axis=0, tiled=True)
    return [arrived[k] for k in range(len(items))]


def slot_kernel(own_rows, paired, dealing, rows, owners, cells, probe, measured, right_table, left_table, *rest):
    del owners
    *terms, kept, sent = rest[:-11]
    wide, patch, wave, half, resid, turned, padded, mine, right, left, table_sem = rest[-11:]
    order = probe.shape[1]
    total_rows = cells.shape[0]
    reach = total_rows - order
    me = lax.axis_index("row")
    first_row = rows[dealing[me]]
    step = 64
    tile = 256

    right_copy = pltpu.make_async_copy(right_table, right, table_sem.at[0])
    left_copy = pltpu.make_async_copy(left_table, left, table_sem.at[1])
    right_copy.start()
    left_copy.start()
    wide[0:total_rows, :] = cells[...].astype(jnp.float32)
    wide[total_rows:, :] = jnp.zeros((SUBLANES, 2 * order), jnp.float32)
    padded[0:reach, :] = jnp.zeros((reach, 2 * order), jnp.float32)
    below = padded.shape[0] - reach - order
    padded[reach + order :, :] = jnp.zeros((below, 2 * order), jnp.float32)

    @pl.loop(0, order // step)
    def _(i):
        place = pl.ds(pl.multiple_of(i * step, step), step)
        found = rows_from(wide, first_row + i * step, step)
        patch[place, :] = found.astype(patch.dtype)
        real, imag = found[:, :order], found[:, order:]
        probe_real = probe[0, place, :].astype(jnp.float32)
        probe_imag = probe[1, place, :].astype(jnp.float32)
        wave[place, :order] = (probe_real * real - probe_imag * imag).astype(wave.dtype)
        wave[place, order:] = (probe_real * imag + probe_imag * real).astype(wave.dtype)

    def dot(a, b):
        return jnp.dot(a, b, preferred_element_type=jnp.float32)

    right_copy.wait()
    for first in range(0, order, tile):
        here = slice(first, first + tile)
        there = slice(order + first, order + first + tile)
        half[:order, here] = dot(wave[...], right[:, here]).astype(half.dtype)
        half[order:, here] = dot(wave[...], right[:, there]).astype(half.dtype)
    left_copy.wait()
    for first in range(0, order, tile):
        here = slice(first, first + tile)
        there = slice(order + first, order + first + tile)
        for top in range(0, order, tile):
            line = slice(top, top + tile)
            real = dot(left[line, :], half[:, here])
            imag = dot(left[order + top : order + top + tile, :], half[:, here])
            inverse = jnp.minimum(lax.rsqrt(real * real + imag * imag), 1.0 / MAG_FLOOR)
            shrink = 1.0 - measured[0, line, here].astype(jnp.float32) * inverse
            resid[line, here] = (real * shrink).astype(resid.dtype)
            resid[line, there] = (imag * shrink).astype(resid.dtype)
    for first in range(0, order, tile):
        here = slice(first, first + tile)
        there = slice(order + first, order + first + tile)
        turned[:order, here] = dot(resid[...], left[:, here]).astype(turned.dtype)
        turned[order:, here] = dot(resid[...], left[:, there]).astype(turned.dtype)
    for first in range(0, order, tile):
        here = slice(first, first + tile)
        there = slice(order + first, order + first + tile)
        for top in range(0, order, tile):
            line = slice(top, top + tile)
            real = dot(right[line, :], turned[:, here])
            imag = dot(right[order + top : order + top + tile, :], turned[:, here])
            probe_real = probe[0, line, here].astype(jnp.float32)
            probe_imag = probe[1, line, here].astype(jnp.float32)
            down = slice(reach + top, reach + top + tile)
            padded[down, here] = probe_real * real + probe_imag * imag
            padded[down, there] = probe_real * imag - probe_imag * real
            patch_real = patch[line, here].astype(jnp.float32)
            patch_imag = patch[line, there].astype(jnp.float32)
            mine[line, here] = patch_real * real + patch_imag * imag
            mine[line, there] = patch_real * imag - patch_imag * real

    count = kept.shape[0]
    side = lax.rem(me, 2)
    kept[...] = mine[pl.ds(pl.multiple_of(side * count, count), count), :]
    sent[...] = mine[pl.ds(pl.multiple_of((1 - side) * count, count), count), :].astype(sent.dtype)
    for k, term in enumerate(terms):
        start = reach - first_row + partner(k, paired) * own_rows
        term[...] = rows_from(padded, start, term.shape[0]).astype(term.dtype)


def slot_terms(cells, probe, measured, dealing, rows, owners, own_rows, tile_rows, paired):
    order = probe.shape[1]
    total_rows = cells.shape[0]
    slots = total_rows // own_rows
    right, left = dft_tables(order)
    wide_cols = 2 * order
    bf16, f32 = jnp.bfloat16, jnp.float32
    *terms, kept, sent = pl.pallas_call(
        functools.partial(slot_kernel, own_rows, paired),
        out_shape=(jax.ShapeDtypeStruct((tile_rows, wide_cols), bf16),) * slots
        + (
            jax.ShapeDtypeStruct((order // 2, wide_cols), f32),
            jax.ShapeDtypeStruct((order // 2, wide_cols), bf16),
        ),
        in_specs=[SMEM, SMEM, SMEM, VMEM, VMEM, VMEM, ANY, ANY],
        out_specs=(VMEM,) * (slots + 2),
        scratch_shapes=[
            pltpu.VMEM((total_rows + SUBLANES, wide_cols), f32),
            pltpu.VMEM((order, wide_cols), bf16),
            pltpu.VMEM((order, wide_cols), bf16),
            pltpu.VMEM((wide_cols, order), bf16),
            pltpu.VMEM((order, wide_cols), bf16),
            pltpu.VMEM((wide_cols, order), bf16),
            pltpu.VMEM((2 * total_rows - order + tile_rows + SUBLANES, wide_cols), f32),
            pltpu.VMEM((order, wide_cols), f32),
            pltpu.VMEM((wide_cols, wide_cols), bf16),
            pltpu.VMEM((wide_cols, wide_cols), bf16),
            pltpu.SemaphoreType.DMA((2,)),
        ],
        compiler_params=pltpu.CompilerParams(vmem_limit_bytes=40 * 2**20),
        cost_estimate=pl.CostEstimate(
            flops=8 * 2 * order**3 * 2, bytes_accessed=8 * 2**20, transcendentals=order * order
        ),
        name="slot",
    )(dealing, rows, owners, cells, probe, measured, jnp.asarray(right), jnp.asarray(left))
    return terms, kept, sent


def place_kernel(slots, order, paired, dealing, cols, blocks, owners, *rest):
    terms, (empty, out, totals, sems) = rest[:slots], rest[slots:]
    del empty
    tile_rows = terms[0].shape[0]
    count = (order + LANES) // LANES
    totals[...] = jnp.zeros_like(totals)
    lane = lax.broadcasted_iota(jnp.int32, (tile_rows, LANES), 1)
    nothing = jnp.zeros((tile_rows, LANES), jnp.float32)

    for k, term in enumerate(terms):
        slot = partner(k, paired)
        _, offset = window_start(cols[dealing[slot]], order, out.shape[2])
        shift = lax.rem(offset, LANES)
        for part in range(2):
            turned = []
            for b in range(count - 1):
                first = part * order + b * LANES
                turned.append(pltpu.roll(term[:, first : first + LANES].astype(jnp.float32), shift, 1))
            for b in range(count):
                before = turned[b - 1] if b else nothing
                after = turned[b] if b < count - 1 else nothing
                owner = owners[slot * count + b]
                totals[owner, part] += jnp.where(lane < offset, before, after)

    def copy(number):
        place = pl.multiple_of(blocks[number] * LANES, LANES)
        return pltpu.make_async_copy(totals.at[number], out.at[:, :, pl.ds(place, LANES)], sems.at[number])

    @pl.loop(0, slots * count)
    def _(number):
        @pl.when(owners[number] == number)
        def _():
            copy(number).start()

    @pl.loop(0, slots * count)
    def _(number):
        @pl.when(owners[number] == number)
        def _():
            copy(number).wait()


def place_windows(terms, empty, blocks, owners, dealing, cols, order, paired):
    slots, tile_rows = len(terms), terms[0].shape[0]
    count = (order + LANES) // LANES
    return pl.pallas_call(
        functools.partial(place_kernel, slots, order, paired),
        out_shape=jax.ShapeDtypeStruct(empty.shape, empty.dtype),
        in_specs=[SMEM, SMEM, SMEM, SMEM] + [VMEM] * slots + [ANY],
        out_specs=ANY,
        scratch_shapes=[
            pltpu.VMEM((slots * count, 2, tile_rows, LANES), jnp.float32),
            pltpu.SemaphoreType.DMA((slots * count,)),
        ],
        input_output_aliases={4 + slots: 0},
        compiler_params=pltpu.CompilerParams(vmem_limit_bytes=24 * 2**20),
        cost_estimate=pl.CostEstimate(flops=0, bytes_accessed=6 * 2**20, transcendentals=0),
        name="place",
    )(dealing, cols, blocks, owners, *terms, empty)


def strides(devices):
    steps, stride = [], 1
    while stride < devices:
        radix = 4 if len(steps) >= 2 and (devices // stride) % 4 == 0 else 2
        steps.append((stride, radix))
        stride *= radix
    return steps


def swap(x, distance, devices):
    return lax.ppermute(x, "row", [(d, d ^ distance) for d in range(devices)])


def sum_probe(kept, sent, devices, scale):
    me = lax.axis_index("row")
    steps = strides(devices)
    total = kept + swap(sent, 1, devices).astype(jnp.float32)
    for stride, radix in steps[1:]:
        digit = me // stride % radix
        count = total.shape[0] // radix
        own = lax.dynamic_slice_in_dim(total, digit * count, count)
        for k in range(1, radix):
            share = lax.dynamic_slice_in_dim(total, lax.bitwise_xor(digit, k) * count, count)
            own = own + swap(share.astype(jnp.bfloat16), k * stride, devices).astype(jnp.float32)
        total = own
    whole = (total * scale).astype(jnp.bfloat16)
    for stride, radix in reversed(steps):
        digit = me // stride % radix
        shares = [whole] + [swap(whole, k * stride, devices) for k in range(1, radix)]
        pieces = []
        for j in range(radix):
            piece = shares[0]
            for k in range(1, radix):
                piece = jnp.where(lax.bitwise_xor(digit, k) == j, shares[k], piece)
            pieces.append(piece)
        whole = jnp.concatenate(pieces, axis=0)
    return whole


def body(object_field, probe, amplitude, row_offsets, col_offsets, dealing):
    order = probe.shape[1]
    devices = lax.axis_size("row")
    own_rows, tile_cols = object_field.shape[1], object_field.shape[2]
    total_rows = devices * own_rows
    tile_rows = -(-own_rows // SUBLANES) * SUBLANES
    spare = tile_rows - own_rows
    paired = devices <= 16 and devices & (devices - 1) == 0
    if spare:
        object_field = jnp.pad(object_field, ((0, 0), (0, spare), (0, 0)))
    pieces, token = fetch_windows(object_field, dealing, col_offsets, order)
    strips = lax.all_to_all(pieces, "row", split_axis=0, concat_axis=0, tiled=True)
    cells = strips[:, :own_rows].reshape(total_rows, 2 * order)
    empty, blocks, owners = prepare(dealing, col_offsets, token, object_field.shape, order)
    terms, kept, sent = slot_terms(
        cells, probe, amplitude, dealing, row_offsets, owners, own_rows, tile_rows, paired
    )
    terms = exchange(terms, paired)
    whole = sum_probe(kept, sent, devices, 1.0 / dealing.shape[0]).astype(jnp.float32)
    probe_grad = jnp.stack([whole[:, :order], whole[:, order:]])
    object_grad = place_windows(terms, empty, blocks, owners, dealing, col_offsets, order, paired)
    if spare:
        object_grad = object_grad[:, :own_rows]
    return (object_grad, probe_grad)


def solution(mesh):
    return jax.shard_map(
        body,
        mesh=mesh,
        in_specs=(
            P(None, ("groups", "row"), None),
            P("groups", None, None),
            P(("groups", "row"), None, None),
            P("groups"),
            P("groups"),
            P("groups"),
        ),
        out_specs=(P(None, ("groups", "row"), None), P("groups", None, None)),
        check_vma=False,
    )
```

```python
import functools
import math

import jax
import jax.numpy as jnp
import numpy as np
from jax import lax
from jax.experimental import pallas as pl
from jax.experimental.pallas import tpu as pltpu
from jax.sharding import PartitionSpec as P

MAG_FLOOR = 0.25
LANES = 128
SUBLANES = 8
SMEM = pl.BlockSpec(memory_space=pltpu.SMEM)
VMEM = pl.BlockSpec(memory_space=pltpu.VMEM)
ANY = pl.BlockSpec(memory_space=pl.ANY)


def dft_tables(order):
    indices = np.arange(order, dtype=np.int32)
    phases = indices[:, None] * indices[None, :] % order
    angles = phases.astype(np.float32) * np.float32(2.0 * math.pi / order)
    factor = np.float32(1.0 / math.sqrt(order))
    real_part = np.cos(angles) * factor
    imag_part = -np.sin(angles) * factor
    right_table = np.block([[real_part, imag_part], [-imag_part, real_part]])
    left_table = np.block([[real_part, -imag_part], [imag_part, real_part]])
    return right_table.astype(jnp.bfloat16), left_table.astype(jnp.bfloat16)


def window_start(column, order, tile_cols):
    span = order + LANES
    base = jnp.minimum(column // LANES, (tile_cols - span) // LANES) * LANES
    return pl.multiple_of(base, LANES), column - base


def rows_from(ref, start, count):
    aligned = pl.multiple_of(start // SUBLANES * SUBLANES, SUBLANES)
    rest = start - aligned
    width = ref.shape[-1]
    blocks = ref[pl.ds(aligned, count + SUBLANES), :].reshape(-1, SUBLANES, width)
    turned = pltpu.roll(blocks, lax.rem(SUBLANES - rest, SUBLANES), 1)
    sub = lax.broadcasted_iota(jnp.int32, (1, SUBLANES, width), 1)
    picked = jnp.where(sub < SUBLANES - rest, turned[:-1], turned[1:])
    return picked.reshape(count, width)


def fetch_kernel(order, dealing, cols, tile, out, token, held, sems):
    token[0] = dealing[0]
    slots, tile_rows = out.shape[0], out.shape[1]
    tile_cols = tile.shape[2]
    span = order + LANES

    def copy(slot):
        base, _ = window_start(cols[dealing[slot]], order, tile_cols)
        return pltpu.make_async_copy(tile.at[:, :, pl.ds(base, span)], held.at[slot], sems.at[slot])

    @pl.loop(0, slots)
    def _(slot):
        copy(slot).start()

    lane = lax.broadcasted_iota(jnp.int32, (tile_rows, LANES), 1)

    @pl.loop(0, slots, unroll=4)
    def _(slot):
        copy(slot).wait()
        _, offset = window_start(cols[dealing[slot]], order, tile_cols)
        shift = lax.rem(LANES - lax.rem(offset, LANES), LANES)
        for part in range(2):
            turned = [
                pltpu.roll(held[slot, part, :, b * LANES : (b + 1) * LANES], shift, 1)
                for b in range(span // LANES)
            ]
            for b in range(order // LANES):
                first = part * order + b * LANES
                cells = jnp.where(lane < LANES - offset, turned[b], turned[b + 1])
                out[slot, :, first : first + LANES] = cells.astype(out.dtype)


def fetch_windows(tile, dealing, cols, order):
    slots, tile_rows, tile_cols = dealing.shape[0], tile.shape[1], tile.shape[2]
    span = order + LANES

    return pl.pallas_call(
        functools.partial(fetch_kernel, order),
        out_shape=(
            jax.ShapeDtypeStruct((slots, tile_rows, 2 * order), jnp.bfloat16),
            jax.ShapeDtypeStruct((1,), jnp.int32),
        ),
        in_specs=[SMEM, SMEM, ANY],
        out_specs=(VMEM, SMEM),
        scratch_shapes=[
            pltpu.VMEM((slots, 2, tile_rows, span), jnp.float32),
            pltpu.SemaphoreType.DMA((slots,)),
        ],
        compiler_params=pltpu.CompilerParams(vmem_limit_bytes=56 * 2**20),
        cost_estimate=pl.CostEstimate(flops=0, bytes_accessed=6 * 2**20, transcendentals=0),
        name="fetch",
    )(dealing, cols, tile)


def prepare_kernel(order, dealing, cols, token, empty, blocks, owners, table, zeros, sems):
    del token
    count = (order + LANES) // LANES
    slots = dealing.shape[0]
    tile_cols = empty.shape[2]
    width = zeros.shape[2]
    zeros[...] = jnp.zeros_like(zeros)
    fills = []
    for b in range(tile_cols // width):
        fill = pltpu.make_async_copy(zeros, empty.at[:, :, b * width : (b + 1) * width], sems.at[b])
        fill.start()
        fills.append(fill)

    @pl.loop(0, tile_cols // LANES)
    def _(block):
        table[block] = -1

    @pl.loop(0, slots)
    def _(slot):
        base, _ = window_start(cols[dealing[slot]], order, tile_cols)
        for b in range(count):
            number = slot * count + b
            block = base // LANES + b
            blocks[number] = block
            known = table[block]
            owner = jnp.where(known < 0, number, known)
            owners[number] = owner
            table[block] = owner

    for fill in fills:
        fill.wait()


def prepare(dealing, cols, token, tile_shape, order):
    slots = dealing.shape[0]
    numbers = slots * (order + LANES) // LANES
    fill_cols = 2048
    return pl.pallas_call(
        functools.partial(prepare_kernel, order),
        out_shape=(
            jax.ShapeDtypeStruct(tile_shape, jnp.float32),
            jax.ShapeDtypeStruct((numbers,), jnp.int32),
            jax.ShapeDtypeStruct((numbers,), jnp.int32),
        ),
        in_specs=[SMEM, SMEM, SMEM],
        out_specs=(ANY, SMEM, SMEM),
        scratch_shapes=[
            pltpu.SMEM((tile_shape[2] // LANES,), jnp.int32),
            pltpu.VMEM(tile_shape[:2] + (fill_cols,), jnp.float32),
            pltpu.SemaphoreType.DMA((tile_shape[2] // fill_cols,)),
        ],
        compiler_params=pltpu.CompilerParams(vmem_limit_bytes=8 * 2**20),
        cost_estimate=pl.CostEstimate(flops=0, bytes_accessed=11 * 2**20, transcendentals=0),
        name="prepare",
    )(dealing, cols, token)


def slot_kernel(
    dealing, rows, owners, cells, probe, measured, right_table, left_table,
    term, kept, sent,
    wide, patch, wave, half, resid, turned, mine, right, left, table_sem,
):
    del owners
    order = probe.shape[1]
    total_rows = cells.shape[0]
    me = lax.axis_index("row")
    first_row = rows[dealing[me]]
    step = 64
    tile = 256

    right_copy = pltpu.make_async_copy(right_table, right, table_sem.at[0])
    left_copy = pltpu.make_async_copy(left_table, left, table_sem.at[1])
    right_copy.start()
    left_copy.start()
    wide[0:total_rows, :] = cells[...].astype(jnp.float32)
    wide[total_rows:, :] = jnp.zeros((SUBLANES, 2 * order), jnp.float32)
    @pl.loop(0, order // step)
    def _(i):
        place = pl.ds(pl.multiple_of(i * step, step), step)
        found = rows_from(wide, first_row + i * step, step)
        patch[place, :] = found.astype(patch.dtype)
        real, imag = found[:, :order], found[:, order:]
        probe_real = probe[0, place, :].astype(jnp.float32)
        probe_imag = probe[1, place, :].astype(jnp.float32)
        wave[place, :order] = (probe_real * real - probe_imag * imag).astype(wave.dtype)
        wave[place, order:] = (probe_real * imag + probe_imag * real).astype(wave.dtype)

    def dot(a, b):
        return jnp.dot(a, b, preferred_element_type=jnp.float32)

    right_copy.wait()
    for first in range(0, order, tile):
        here = slice(first, first + tile)
        there = slice(order + first, order + first + tile)
        half[:order, here] = dot(wave[...], right[:, here]).astype(half.dtype)
        half[order:, here] = dot(wave[...], right[:, there]).astype(half.dtype)
    left_copy.wait()
    for first in range(0, order, tile):
        here = slice(first, first + tile)
        there = slice(order + first, order + first + tile)
        for top in range(0, order, tile):
            line = slice(top, top + tile)
            real = dot(left[line, :], half[:, here])
            imag = dot(left[order + top : order + top + tile, :], half[:, here])
            inverse = jnp.minimum(lax.rsqrt(real * real + imag * imag), 1.0 / MAG_FLOOR)
            shrink = 1.0 - measured[0, line, here].astype(jnp.float32) * inverse
            resid[line, here] = (real * shrink).astype(resid.dtype)
            resid[line, there] = (imag * shrink).astype(resid.dtype)
    for first in range(0, order, tile):
        here = slice(first, first + tile)
        there = slice(order + first, order + first + tile)
        turned[:order, here] = dot(resid[...], left[:, here]).astype(turned.dtype)
        turned[order:, here] = dot(resid[...], left[:, there]).astype(turned.dtype)
    for first in range(0, order, tile):
        here = slice(first, first + tile)
        there = slice(order + first, order + first + tile)
        for top in range(0, order, tile):
            line = slice(top, top + tile)
            real = dot(right[line, :], turned[:, here])
            imag = dot(right[order + top : order + top + tile, :], turned[:, here])
            probe_real = probe[0, line, here].astype(jnp.float32)
            probe_imag = probe[1, line, here].astype(jnp.float32)
            term[line, here] = (probe_real * real + probe_imag * imag).astype(term.dtype)
            term[line, there] = (probe_real * imag - probe_imag * real).astype(term.dtype)
            patch_real = patch[line, here].astype(jnp.float32)
            patch_imag = patch[line, there].astype(jnp.float32)
            mine[line, here] = patch_real * real + patch_imag * imag
            mine[line, there] = patch_real * imag - patch_imag * real

    count = kept.shape[0]
    side = lax.rem(me, 2)
    kept[...] = mine[pl.ds(pl.multiple_of(side * count, count), count), :]
    sent[...] = mine[pl.ds(pl.multiple_of((1 - side) * count, count), count), :].astype(sent.dtype)

def slot_terms(cells, probe, measured, dealing, rows, owners):
    order = probe.shape[1]
    total_rows = cells.shape[0]
    right, left = dft_tables(order)
    wide_cols = 2 * order
    bf16, f32 = jnp.bfloat16, jnp.float32
    return pl.pallas_call(
        slot_kernel,
        out_shape=(
            jax.ShapeDtypeStruct((order, wide_cols), bf16),
            jax.ShapeDtypeStruct((order // 2, wide_cols), f32),
            jax.ShapeDtypeStruct((order // 2, wide_cols), bf16),
        ),
        in_specs=[SMEM, SMEM, SMEM, VMEM, VMEM, VMEM, ANY, ANY],
        out_specs=(VMEM,) * 3,
        scratch_shapes=[
            pltpu.VMEM((total_rows + SUBLANES, wide_cols), f32),
            pltpu.VMEM((order, wide_cols), bf16),
            pltpu.VMEM((order, wide_cols), bf16),
            pltpu.VMEM((wide_cols, order), bf16),
            pltpu.VMEM((order, wide_cols), bf16),
            pltpu.VMEM((wide_cols, order), bf16),
            pltpu.VMEM((order, wide_cols), f32),
            pltpu.VMEM((wide_cols, wide_cols), bf16),
            pltpu.VMEM((wide_cols, wide_cols), bf16),
            pltpu.SemaphoreType.DMA((2,)),
        ],
        compiler_params=pltpu.CompilerParams(vmem_limit_bytes=54 * 2**20),
        cost_estimate=pl.CostEstimate(
            flops=8 * 2 * order**3 * 2, bytes_accessed=8 * 2**20, transcendentals=order * order
        ),
        name="slot",
    )(dealing, rows, owners, cells, probe, measured, jnp.asarray(right), jnp.asarray(left))


def pack_kernel(reach, own_rows, dealing, rows, term, out, padded):
    order = term.shape[0]
    first_row = rows[dealing[lax.axis_index("row")]]
    below = padded.shape[0] - reach - order
    padded[0:reach, :] = jnp.zeros((reach, padded.shape[1]), jnp.float32)
    padded[reach : reach + order, :] = term[...].astype(jnp.float32)
    padded[reach + order :, :] = jnp.zeros((below, padded.shape[1]), jnp.float32)

    @pl.loop(0, out.shape[0], unroll=2)
    def _(k):
        out[k] = rows_from(padded, reach - first_row + k * own_rows, out.shape[1]).astype(out.dtype)


def pack_rows(term, dealing, rows, slots, own_rows, tile_rows):
    order, width = term.shape
    reach = slots * own_rows - order
    return pl.pallas_call(
        functools.partial(pack_kernel, reach, own_rows),
        out_shape=jax.ShapeDtypeStruct((slots, tile_rows, width), jnp.bfloat16),
        in_specs=[SMEM, SMEM, VMEM],
        out_specs=VMEM,
        scratch_shapes=[pltpu.VMEM((2 * reach + order + tile_rows + SUBLANES, width), jnp.float32)],
        compiler_params=pltpu.CompilerParams(vmem_limit_bytes=16 * 2**20),
        cost_estimate=pl.CostEstimate(flops=0, bytes_accessed=3 * 2**20, transcendentals=0),
        name="pack",
    )(dealing, rows, term)


def place_kernel(order, dealing, cols, blocks, owners, terms, empty, out, totals, sems):
    del empty
    slots, tile_rows = terms.shape[0], terms.shape[1]
    count = (order + LANES) // LANES
    totals[...] = jnp.zeros_like(totals)
    lane = lax.broadcasted_iota(jnp.int32, (tile_rows, LANES), 1)
    nothing = jnp.zeros((tile_rows, LANES), jnp.float32)

    @pl.loop(0, slots, unroll=4)
    def _(slot):
        _, offset = window_start(cols[dealing[slot]], order, out.shape[2])
        shift = lax.rem(offset, LANES)
        for part in range(2):
            turned = []
            for b in range(count - 1):
                first = part * order + b * LANES
                turned.append(pltpu.roll(terms[slot, :, first : first + LANES].astype(jnp.float32), shift, 1))
            for b in range(count):
                before = turned[b - 1] if b else nothing
                after = turned[b] if b < count - 1 else nothing
                owner = owners[slot * count + b]
                totals[owner, part] += jnp.where(lane < offset, before, after)

    def copy(number):
        place = pl.multiple_of(blocks[number] * LANES, LANES)
        return pltpu.make_async_copy(totals.at[number], out.at[:, :, pl.ds(place, LANES)], sems.at[number])

    @pl.loop(0, slots * count)
    def _(number):
        @pl.when(owners[number] == number)
        def _():
            copy(number).start()

    @pl.loop(0, slots * count)
    def _(number):
        @pl.when(owners[number] == number)
        def _():
            copy(number).wait()


def place_windows(terms, empty, blocks, owners, dealing, cols, order):
    slots, tile_rows = terms.shape[0], terms.shape[1]
    count = (order + LANES) // LANES
    return pl.pallas_call(
        functools.partial(place_kernel, order),
        out_shape=jax.ShapeDtypeStruct(empty.shape, empty.dtype),
        in_specs=[SMEM, SMEM, SMEM, SMEM, VMEM, ANY],
        out_specs=ANY,
        scratch_shapes=[
            pltpu.VMEM((slots * count, 2, tile_rows, LANES), jnp.float32),
            pltpu.SemaphoreType.DMA((slots * count,)),
        ],
        input_output_aliases={5: 0},
        compiler_params=pltpu.CompilerParams(vmem_limit_bytes=24 * 2**20),
        cost_estimate=pl.CostEstimate(flops=0, bytes_accessed=6 * 2**20, transcendentals=0),
        name="place",
    )(dealing, cols, blocks, owners, terms, empty)


def strides(devices):
    steps, stride = [], 1
    while stride < devices:
        radix = 4 if len(steps) >= 2 and (devices // stride) % 4 == 0 else 2
        steps.append((stride, radix))
        stride *= radix
    return steps


def swap(x, distance, devices):
    return lax.ppermute(x, "row", [(d, d ^ distance) for d in range(devices)])


def sum_probe(kept, sent, devices):
    me = lax.axis_index("row")
    total = kept + swap(sent, 1, devices).astype(jnp.float32)
    parts = [1 << k for k in range(1, devices.bit_length() - 1)]
    orders = (parts[:1] + parts[:0:-1], parts[1:2] + parts[:1] + parts[2:])
    sets = jnp.split(total, 2)
    for step in range(len(parts)):
        for number, order in enumerate(orders):
            digit = me // order[step] % 2
            count = sets[number].shape[0] // 2
            own = lax.dynamic_slice_in_dim(sets[number], digit * count, count)
            other = lax.dynamic_slice_in_dim(sets[number], (1 - digit) * count, count)
            sets[number] = own + swap(other.astype(jnp.bfloat16), order[step], devices).astype(jnp.float32)
    return jnp.concatenate(sets), orders


def join(whole, orders, devices):
    me = lax.axis_index("row")
    steps = strides(devices)
    count, width = whole.shape[0] // 2, whole.shape[1]
    for stride, radix in reversed(steps):
        digit = me // stride % radix
        shares = [whole] + [swap(whole, k * stride, devices) for k in range(1, radix)]
        pieces = []
        for j in range(radix):
            piece = shares[0]
            for k in range(1, radix):
                piece = jnp.where(lax.bitwise_xor(digit, k) == j, shares[k], piece)
            pieces.append(piece)
        whole = jnp.concatenate(pieces, axis=0)
    axes = []
    for stride, radix in steps:
        axes += [2 * stride, stride] if radix == 4 else [stride]
    whole = whole.reshape([2] * len(axes) + [2, count, width])
    sets = []
    for number, order in enumerate(orders):
        one = lax.index_in_dim(whole, number, len(axes), keepdims=False)
        one = one.transpose([0] + [axes.index(part) for part in order] + [len(axes), len(axes) + 1])
        sets.append(one.reshape(2, -1, width))
    return jnp.concatenate(sets, axis=1).reshape(-1, width)


def body(object_field, probe, amplitude, row_offsets, col_offsets, dealing):
    order = probe.shape[1]
    devices = lax.axis_size("row")
    own_rows, tile_cols = object_field.shape[1], object_field.shape[2]
    total_rows = devices * own_rows
    tile_rows = -(-own_rows // SUBLANES) * SUBLANES
    spare = tile_rows - own_rows
    if spare:
        object_field = jnp.pad(object_field, ((0, 0), (0, spare), (0, 0)))
    pieces, token = fetch_windows(object_field, dealing, col_offsets, order)
    strips = lax.all_to_all(pieces, "row", split_axis=0, concat_axis=0, tiled=True)
    cells = strips[:, :own_rows].reshape(total_rows, 2 * order)
    empty, blocks, owners = prepare(dealing, col_offsets, token, object_field.shape, order)
    term, kept, sent = slot_terms(cells, probe, amplitude, dealing, row_offsets, owners)
    total, orders = sum_probe(kept, sent, devices)
    terms = pack_rows(term, dealing, row_offsets, devices, own_rows, tile_rows)
    terms, total = lax.optimization_barrier((terms, total))
    arrived = lax.all_to_all(terms, "row", split_axis=0, concat_axis=0, tiled=True)
    share = (total * (1.0 / dealing.shape[0])).astype(jnp.bfloat16)
    whole = join(share, orders, devices).astype(jnp.float32)
    probe_grad = jnp.stack([whole[:, :order], whole[:, order:]])
    object_grad = place_windows(arrived, empty, blocks, owners, dealing, col_offsets, order)
    if spare:
        object_grad = object_grad[:, :own_rows]
    return (object_grad, probe_grad)


def solution(mesh):
    return jax.shard_map(
        body,
        mesh=mesh,
        in_specs=(
            P(None, ("groups", "row"), None),
            P("groups", None, None),
            P(("groups", "row"), None, None),
            P("groups"),
            P("groups"),
            P("groups"),
        ),
        out_specs=(P(None, ("groups", "row"), None), P("groups", None, None)),
        check_vma=False,
    )
```

```python
import functools
import math

import jax
import jax.numpy as jnp
import numpy as np
from jax import lax
from jax.experimental import pallas as pl
from jax.experimental.pallas import tpu as pltpu
from jax.sharding import PartitionSpec as P

MAG_FLOOR = 0.25
LANES = 128
SUBLANES = 8
SMEM = pl.BlockSpec(memory_space=pltpu.SMEM)
VMEM = pl.BlockSpec(memory_space=pltpu.VMEM)
ANY = pl.BlockSpec(memory_space=pl.ANY)


def dft_tables(order):
    indices = np.arange(order, dtype=np.int32)
    phases = indices[:, None] * indices[None, :] % order
    angles = phases.astype(np.float32) * np.float32(2.0 * math.pi / order)
    factor = np.float32(1.0 / math.sqrt(order))
    real_part = np.cos(angles) * factor
    imag_part = -np.sin(angles) * factor
    right_table = np.block([[real_part, imag_part], [-imag_part, real_part]])
    left_table = np.block([[real_part, -imag_part], [imag_part, real_part]])
    return right_table.astype(jnp.bfloat16), left_table.astype(jnp.bfloat16)


def window_start(column, order, tile_cols):
    span = order + LANES
    base = jnp.minimum(column // LANES, (tile_cols - span) // LANES) * LANES
    return pl.multiple_of(base, LANES), column - base


def rows_from(ref, start, count):
    aligned = pl.multiple_of(start // SUBLANES * SUBLANES, SUBLANES)
    rest = start - aligned
    width = ref.shape[-1]
    blocks = ref[pl.ds(aligned, count + SUBLANES), :].reshape(-1, SUBLANES, width)
    turned = pltpu.roll(blocks, lax.rem(SUBLANES - rest, SUBLANES), 1)
    sub = lax.broadcasted_iota(jnp.int32, (1, SUBLANES, width), 1)
    picked = jnp.where(sub < SUBLANES - rest, turned[:-1], turned[1:])
    return picked.reshape(count, width)


def fetch_kernel(order, dealing, cols, tile, out, token, held, sems):
    token[0] = dealing[0]
    slots, tile_rows = out.shape[0], out.shape[1]
    tile_cols = tile.shape[2]
    span = order + LANES

    def copy(slot):
        base, _ = window_start(cols[dealing[slot]], order, tile_cols)
        return pltpu.make_async_copy(tile.at[:, :, pl.ds(base, span)], held.at[slot], sems.at[slot])

    @pl.loop(0, slots)
    def _(slot):
        copy(slot).start()

    lane = lax.broadcasted_iota(jnp.int32, (tile_rows, LANES), 1)

    @pl.loop(0, slots, unroll=4)
    def _(slot):
        copy(slot).wait()
        _, offset = window_start(cols[dealing[slot]], order, tile_cols)
        shift = lax.rem(LANES - lax.rem(offset, LANES), LANES)
        for part in range(2):
            turned = [
                pltpu.roll(held[slot, part, :, b * LANES : (b + 1) * LANES], shift, 1)
                for b in range(span // LANES)
            ]
            for b in range(order // LANES):
                first = part * order + b * LANES
                cells = jnp.where(lane < LANES - offset, turned[b], turned[b + 1])
                out[slot, :, first : first + LANES] = cells.astype(out.dtype)


def fetch_windows(tile, dealing, cols, order):
    slots, tile_rows, tile_cols = dealing.shape[0], tile.shape[1], tile.shape[2]
    span = order + LANES

    return pl.pallas_call(
        functools.partial(fetch_kernel, order),
        out_shape=(
            jax.ShapeDtypeStruct((slots, tile_rows, 2 * order), jnp.bfloat16),
            jax.ShapeDtypeStruct((1,), jnp.int32),
        ),
        in_specs=[SMEM, SMEM, ANY],
        out_specs=(VMEM, SMEM),
        scratch_shapes=[
            pltpu.VMEM((slots, 2, tile_rows, span), jnp.float32),
            pltpu.SemaphoreType.DMA((slots,)),
        ],
        compiler_params=pltpu.CompilerParams(vmem_limit_bytes=56 * 2**20),
        cost_estimate=pl.CostEstimate(flops=0, bytes_accessed=6 * 2**20, transcendentals=0),
        name="fetch",
    )(dealing, cols, tile)


def prepare_kernel(
    order, dealing, cols, token, right_table, left_table,
    empty, blocks, owners, right, left,
    table, zeros, sems, table_sems,
):
    del token
    loads = [
        pltpu.make_async_copy(right_table, right, table_sems.at[0]),
        pltpu.make_async_copy(left_table, left, table_sems.at[1]),
    ]
    for load in loads:
        load.start()
    count = (order + LANES) // LANES
    slots = dealing.shape[0]
    tile_cols = empty.shape[2]
    width = zeros.shape[2]
    zeros[...] = jnp.zeros_like(zeros)
    fills = []
    for b in range(tile_cols // width):
        fill = pltpu.make_async_copy(zeros, empty.at[:, :, b * width : (b + 1) * width], sems.at[b])
        fill.start()
        fills.append(fill)

    @pl.loop(0, tile_cols // LANES)
    def _(block):
        table[block] = -1

    @pl.loop(0, slots)
    def _(slot):
        base, _ = window_start(cols[dealing[slot]], order, tile_cols)
        for b in range(count):
            number = slot * count + b
            block = base // LANES + b
            blocks[number] = block
            known = table[block]
            owner = jnp.where(known < 0, number, known)
            owners[number] = owner
            table[block] = owner

    for copy in loads + fills:
        copy.wait()


def prepare(dealing, cols, token, tile_shape, order):
    slots = dealing.shape[0]
    numbers = slots * (order + LANES) // LANES
    fill_cols = 2048
    right, left = dft_tables(order)
    table = jax.ShapeDtypeStruct(right.shape, jnp.bfloat16)
    return pl.pallas_call(
        functools.partial(prepare_kernel, order),
        out_shape=(
            jax.ShapeDtypeStruct(tile_shape, jnp.float32),
            jax.ShapeDtypeStruct((numbers,), jnp.int32),
            jax.ShapeDtypeStruct((numbers,), jnp.int32),
            table,
            table,
        ),
        in_specs=[SMEM, SMEM, SMEM, ANY, ANY],
        out_specs=(ANY, SMEM, SMEM, VMEM, VMEM),
        scratch_shapes=[
            pltpu.SMEM((tile_shape[2] // LANES,), jnp.int32),
            pltpu.VMEM(tile_shape[:2] + (fill_cols,), jnp.float32),
            pltpu.SemaphoreType.DMA((tile_shape[2] // fill_cols,)),
            pltpu.SemaphoreType.DMA((2,)),
        ],
        compiler_params=pltpu.CompilerParams(vmem_limit_bytes=16 * 2**20),
        cost_estimate=pl.CostEstimate(flops=0, bytes_accessed=11 * 2**20, transcendentals=0),
        name="prepare",
    )(dealing, cols, token, jnp.asarray(right), jnp.asarray(left))


def slot_kernel(
    dealing, rows, cells, probe, measured, right, left,
    term, kept, sent,
    wide, patch, wave, half, resid, turned, mine,
):
    order = probe.shape[1]
    total_rows = cells.shape[0]
    me = lax.axis_index("row")
    first_row = rows[dealing[me]]
    step = 64
    tile = 256

    wide[0:total_rows, :] = cells[...].astype(jnp.float32)
    wide[total_rows:, :] = jnp.zeros((SUBLANES, 2 * order), jnp.float32)
    @pl.loop(0, order // step)
    def _(i):
        place = pl.ds(pl.multiple_of(i * step, step), step)
        found = rows_from(wide, first_row + i * step, step)
        patch[place, :] = found.astype(patch.dtype)
        real, imag = found[:, :order], found[:, order:]
        probe_real = probe[0, place, :].astype(jnp.float32)
        probe_imag = probe[1, place, :].astype(jnp.float32)
        wave[place, :order] = (probe_real * real - probe_imag * imag).astype(wave.dtype)
        wave[place, order:] = (probe_real * imag + probe_imag * real).astype(wave.dtype)

    def dot(a, b):
        return jnp.dot(a, b, preferred_element_type=jnp.float32)

    for first in range(0, order, tile):
        here = slice(first, first + tile)
        there = slice(order + first, order + first + tile)
        half[:order, here] = dot(wave[...], right[:, here]).astype(half.dtype)
        half[order:, here] = dot(wave[...], right[:, there]).astype(half.dtype)
    for first in range(0, order, tile):
        here = slice(first, first + tile)
        there = slice(order + first, order + first + tile)
        for top in range(0, order, tile):
            line = slice(top, top + tile)
            real = dot(left[line, :], half[:, here])
            imag = dot(left[order + top : order + top + tile, :], half[:, here])
            inverse = jnp.minimum(lax.rsqrt(real * real + imag * imag), 1.0 / MAG_FLOOR)
            shrink = 1.0 - measured[0, line, here].astype(jnp.float32) * inverse
            resid[line, here] = (real * shrink).astype(resid.dtype)
            resid[line, there] = (imag * shrink).astype(resid.dtype)
    for first in range(0, order, tile):
        here = slice(first, first + tile)
        there = slice(order + first, order + first + tile)
        turned[:order, here] = dot(resid[...], left[:, here]).astype(turned.dtype)
        turned[order:, here] = dot(resid[...], left[:, there]).astype(turned.dtype)
    for first in range(0, order, tile):
        here = slice(first, first + tile)
        there = slice(order + first, order + first + tile)
        for top in range(0, order, tile):
            line = slice(top, top + tile)
            real = dot(right[line, :], turned[:, here])
            imag = dot(right[order + top : order + top + tile, :], turned[:, here])
            probe_real = probe[0, line, here].astype(jnp.float32)
            probe_imag = probe[1, line, here].astype(jnp.float32)
            term[line, here] = (probe_real * real + probe_imag * imag).astype(term.dtype)
            term[line, there] = (probe_real * imag - probe_imag * real).astype(term.dtype)
            patch_real = patch[line, here].astype(jnp.float32)
            patch_imag = patch[line, there].astype(jnp.float32)
            mine[line, here] = patch_real * real + patch_imag * imag
            mine[line, there] = patch_real * imag - patch_imag * real

    count = kept.shape[0]
    side = lax.rem(me, 2)
    kept[...] = mine[pl.ds(pl.multiple_of(side * count, count), count), :]
    sent[...] = mine[pl.ds(pl.multiple_of((1 - side) * count, count), count), :].astype(sent.dtype)

def slot_terms(cells, probe, measured, dealing, rows, right, left):
    order = probe.shape[1]
    total_rows = cells.shape[0]
    wide_cols = 2 * order
    bf16, f32 = jnp.bfloat16, jnp.float32
    return pl.pallas_call(
        slot_kernel,
        out_shape=(
            jax.ShapeDtypeStruct((order, wide_cols), bf16),
            jax.ShapeDtypeStruct((order // 2, wide_cols), f32),
            jax.ShapeDtypeStruct((order // 2, wide_cols), bf16),
        ),
        in_specs=[SMEM, SMEM, VMEM, VMEM, VMEM, VMEM, VMEM],
        out_specs=(VMEM,) * 3,
        scratch_shapes=[
            pltpu.VMEM((total_rows + SUBLANES, wide_cols), f32),
            pltpu.VMEM((order, wide_cols), bf16),
            pltpu.VMEM((order, wide_cols), bf16),
            pltpu.VMEM((wide_cols, order), bf16),
            pltpu.VMEM((order, wide_cols), bf16),
            pltpu.VMEM((wide_cols, order), bf16),
            pltpu.VMEM((order, wide_cols), f32),
        ],
        compiler_params=pltpu.CompilerParams(vmem_limit_bytes=40 * 2**20),
        cost_estimate=pl.CostEstimate(
            flops=8 * 2 * order**3 * 2, bytes_accessed=8 * 2**20, transcendentals=order * order
        ),
        name="slot",
    )(dealing, rows, cells, probe, measured, right, left)


def pack_kernel(reach, own_rows, dealing, rows, term, out, padded):
    order = term.shape[0]
    first_row = rows[dealing[lax.axis_index("row")]]
    below = padded.shape[0] - reach - order
    padded[0:reach, :] = jnp.zeros((reach, padded.shape[1]), jnp.float32)
    padded[reach : reach + order, :] = term[...].astype(jnp.float32)
    padded[reach + order :, :] = jnp.zeros((below, padded.shape[1]), jnp.float32)

    @pl.loop(0, out.shape[0], unroll=2)
    def _(k):
        out[k] = rows_from(padded, reach - first_row + k * own_rows, out.shape[1]).astype(out.dtype)


def pack_rows(term, dealing, rows, slots, own_rows, tile_rows):
    order, width = term.shape
    reach = slots * own_rows - order
    return pl.pallas_call(
        functools.partial(pack_kernel, reach, own_rows),
        out_shape=jax.ShapeDtypeStruct((slots, tile_rows, width), jnp.bfloat16),
        in_specs=[SMEM, SMEM, VMEM],
        out_specs=VMEM,
        scratch_shapes=[pltpu.VMEM((2 * reach + order + tile_rows + SUBLANES, width), jnp.float32)],
        compiler_params=pltpu.CompilerParams(vmem_limit_bytes=16 * 2**20),
        cost_estimate=pl.CostEstimate(flops=0, bytes_accessed=3 * 2**20, transcendentals=0),
        name="pack",
    )(dealing, rows, term)


def place_kernel(order, dealing, cols, blocks, owners, terms, empty, out, totals, sems):
    del empty
    slots, tile_rows = terms.shape[0], terms.shape[1]
    count = (order + LANES) // LANES
    totals[...] = jnp.zeros_like(totals)
    lane = lax.broadcasted_iota(jnp.int32, (tile_rows, LANES), 1)
    nothing = jnp.zeros((tile_rows, LANES), jnp.float32)

    @pl.loop(0, slots, unroll=4)
    def _(slot):
        _, offset = window_start(cols[dealing[slot]], order, out.shape[2])
        shift = lax.rem(offset, LANES)
        for part in range(2):
            turned = []
            for b in range(count - 1):
                first = part * order + b * LANES
                turned.append(pltpu.roll(terms[slot, :, first : first + LANES].astype(jnp.float32), shift, 1))
            for b in range(count):
                before = turned[b - 1] if b else nothing
                after = turned[b] if b < count - 1 else nothing
                owner = owners[slot * count + b]
                totals[owner, part] += jnp.where(lane < offset, before, after)

    def copy(number):
        place = pl.multiple_of(blocks[number] * LANES, LANES)
        return pltpu.make_async_copy(totals.at[number], out.at[:, :, pl.ds(place, LANES)], sems.at[number])

    @pl.loop(0, slots * count)
    def _(number):
        @pl.when(owners[number] == number)
        def _():
            copy(number).start()

    @pl.loop(0, slots * count)
    def _(number):
        @pl.when(owners[number] == number)
        def _():
            copy(number).wait()


def place_windows(terms, empty, blocks, owners, dealing, cols, order):
    slots, tile_rows = terms.shape[0], terms.shape[1]
    count = (order + LANES) // LANES
    return pl.pallas_call(
        functools.partial(place_kernel, order),
        out_shape=jax.ShapeDtypeStruct(empty.shape, empty.dtype),
        in_specs=[SMEM, SMEM, SMEM, SMEM, VMEM, ANY],
        out_specs=ANY,
        scratch_shapes=[
            pltpu.VMEM((slots * count, 2, tile_rows, LANES), jnp.float32),
            pltpu.SemaphoreType.DMA((slots * count,)),
        ],
        input_output_aliases={5: 0},
        compiler_params=pltpu.CompilerParams(vmem_limit_bytes=24 * 2**20),
        cost_estimate=pl.CostEstimate(flops=0, bytes_accessed=6 * 2**20, transcendentals=0),
        name="place",
    )(dealing, cols, blocks, owners, terms, empty)


def strides(devices):
    steps, stride = [], 1
    while stride < devices:
        radix = 4 if len(steps) >= 2 and (devices // stride) % 4 == 0 else 2
        steps.append((stride, radix))
        stride *= radix
    return steps


def swap(x, distance, devices):
    return lax.ppermute(x, "row", [(d, d ^ distance) for d in range(devices)])


def share_index(device, steps):
    index = 0
    for stride, radix in steps[1:]:
        index = index * radix + device // stride % radix
    return index


def share_kernel(steps, kept, met, own, *shares):
    me = lax.axis_index("row")
    count = own.shape[0]

    def rows(device):
        place = pl.ds(pl.multiple_of(share_index(device, steps) * count, count), count)
        return kept[place, :] + met[place, :].astype(jnp.float32)

    own[...] = rows(me)
    for k, share in enumerate(shares, 1):
        share[...] = rows(lax.bitwise_xor(me, 2 * k)).astype(share.dtype)


def sum_probe(kept, sent, devices):
    me = lax.axis_index("row")
    steps = strides(devices)
    met = swap(sent, 1, devices)
    if devices <= 16:
        chips = devices // 2
        count, width = kept.shape[0] // chips, kept.shape[1]
        total, *shares = pl.pallas_call(
            functools.partial(share_kernel, steps),
            out_shape=(jax.ShapeDtypeStruct((count, width), jnp.float32),)
            + (jax.ShapeDtypeStruct((count, width), jnp.bfloat16),) * (chips - 1),
            in_specs=[VMEM, VMEM],
            out_specs=(VMEM,) * chips,
            cost_estimate=pl.CostEstimate(flops=0, bytes_accessed=2 * 2**20, transcendentals=0),
            name="share",
        )(kept, met)
        for k, share in enumerate(shares, 1):
            total = total + swap(share, 2 * k, devices).astype(jnp.float32)
        return total
    total = kept + met.astype(jnp.float32)
    for stride, radix in steps[1:]:
        digit = me // stride % radix
        count = total.shape[0] // radix
        own = lax.dynamic_slice_in_dim(total, digit * count, count)
        for k in range(1, radix):
            share = lax.dynamic_slice_in_dim(total, lax.bitwise_xor(digit, k) * count, count)
            own = own + swap(share.astype(jnp.bfloat16), k * stride, devices).astype(jnp.float32)
        total = own
    return total


def join(whole, devices):
    me = lax.axis_index("row")
    for stride, radix in reversed(strides(devices)):
        digit = me // stride % radix
        shares = [whole] + [swap(whole, k * stride, devices) for k in range(1, radix)]
        pieces = []
        for j in range(radix):
            piece = shares[0]
            for k in range(1, radix):
                piece = jnp.where(lax.bitwise_xor(digit, k) == j, shares[k], piece)
            pieces.append(piece)
        whole = jnp.concatenate(pieces, axis=0)
    return whole


def body(object_field, probe, amplitude, row_offsets, col_offsets, dealing):
    order = probe.shape[1]
    devices = lax.axis_size("row")
    own_rows, tile_cols = object_field.shape[1], object_field.shape[2]
    total_rows = devices * own_rows
    tile_rows = -(-own_rows // SUBLANES) * SUBLANES
    spare = tile_rows - own_rows
    if spare:
        object_field = jnp.pad(object_field, ((0, 0), (0, spare), (0, 0)))
    pieces, token = fetch_windows(object_field, dealing, col_offsets, order)
    strips = lax.all_to_all(pieces, "row", split_axis=0, concat_axis=0, tiled=True)
    cells = strips[:, :own_rows].reshape(total_rows, 2 * order)
    empty, blocks, owners, right, left = prepare(dealing, col_offsets, token, object_field.shape, order)
    term, kept, sent = slot_terms(cells, probe, amplitude, dealing, row_offsets, right, left)
    total = sum_probe(kept, sent, devices)
    terms = pack_rows(term, dealing, row_offsets, devices, own_rows, tile_rows)
    arrived = lax.all_to_all(terms, "row", split_axis=0, concat_axis=0, tiled=True)
    share = (total * (1.0 / dealing.shape[0])).astype(jnp.bfloat16)
    whole = join(share, devices).astype(jnp.float32)
    probe_grad = jnp.stack([whole[:, :order], whole[:, order:]])
    object_grad = place_windows(arrived, empty, blocks, owners, dealing, col_offsets, order)
    if spare:
        object_grad = object_grad[:, :own_rows]
    return (object_grad, probe_grad)


def solution(mesh):
    return jax.shard_map(
        body,
        mesh=mesh,
        in_specs=(
            P(None, ("groups", "row"), None),
            P("groups", None, None),
            P(("groups", "row"), None, None),
            P("groups"),
            P("groups"),
            P("groups"),
        ),
        out_specs=(P(None, ("groups", "row"), None), P("groups", None, None)),
        check_vma=False,
    )
```

```python
import functools
import math

import jax
import jax.numpy as jnp
import numpy as np
from jax import lax
from jax.experimental import pallas as pl
from jax.experimental.pallas import tpu as pltpu
from jax.sharding import PartitionSpec as P

MAG_FLOOR = 0.25
LANES = 128
SUBLANES = 8
SMEM = pl.BlockSpec(memory_space=pltpu.SMEM)
VMEM = pl.BlockSpec(memory_space=pltpu.VMEM)
ANY = pl.BlockSpec(memory_space=pl.ANY)


def dft_tables(order):
    indices = np.arange(order, dtype=np.int32)
    phases = indices[:, None] * indices[None, :] % order
    angles = phases.astype(np.float32) * np.float32(2.0 * math.pi / order)
    factor = np.float32(1.0 / math.sqrt(order))
    real_part = np.cos(angles) * factor
    imag_part = -np.sin(angles) * factor
    right_table = np.block([[real_part, imag_part], [-imag_part, real_part]])
    left_table = np.block([[real_part, -imag_part], [imag_part, real_part]])
    return right_table.astype(jnp.bfloat16), left_table.astype(jnp.bfloat16)


def window_start(column, order, tile_cols):
    span = order + LANES
    base = jnp.minimum(column // LANES, (tile_cols - span) // LANES) * LANES
    return pl.multiple_of(base, LANES), column - base


def rows_from(ref, start, count):
    aligned = pl.multiple_of(start // SUBLANES * SUBLANES, SUBLANES)
    rest = start - aligned
    width = ref.shape[-1]
    blocks = ref[pl.ds(aligned, count + SUBLANES), :].reshape(-1, SUBLANES, width)
    turned = pltpu.roll(blocks, lax.rem(SUBLANES - rest, SUBLANES), 1)
    sub = lax.broadcasted_iota(jnp.int32, (1, SUBLANES, width), 1)
    picked = jnp.where(sub < SUBLANES - rest, turned[:-1], turned[1:])
    return picked.reshape(count, width)


def fetch_kernel(order, dealing, cols, tile, out, token, held, sems):
    token[0] = dealing[0]
    slots, tile_rows = out.shape[0], out.shape[1]
    tile_cols = tile.shape[2]
    span = order + LANES

    def copy(slot):
        base, _ = window_start(cols[dealing[slot]], order, tile_cols)
        return pltpu.make_async_copy(tile.at[:, :, pl.ds(base, span)], held.at[slot], sems.at[slot])

    @pl.loop(0, slots)
    def _(slot):
        copy(slot).start()

    lane = lax.broadcasted_iota(jnp.int32, (tile_rows, LANES), 1)

    @pl.loop(0, slots, unroll=4)
    def _(slot):
        copy(slot).wait()
        _, offset = window_start(cols[dealing[slot]], order, tile_cols)
        shift = lax.rem(LANES - lax.rem(offset, LANES), LANES)
        for part in range(2):
            turned = [
                pltpu.roll(held[slot, part, :, b * LANES : (b + 1) * LANES], shift, 1)
                for b in range(span // LANES)
            ]
            for b in range(order // LANES):
                first = part * order + b * LANES
                cells = jnp.where(lane < LANES - offset, turned[b], turned[b + 1])
                out[slot, :, first : first + LANES] = cells.astype(out.dtype)


def fetch_windows(tile, dealing, cols, order):
    slots, tile_rows, tile_cols = dealing.shape[0], tile.shape[1], tile.shape[2]
    span = order + LANES

    return pl.pallas_call(
        functools.partial(fetch_kernel, order),
        out_shape=(
            jax.ShapeDtypeStruct((slots, tile_rows, 2 * order), jnp.bfloat16),
            jax.ShapeDtypeStruct((1,), jnp.int32),
        ),
        in_specs=[SMEM, SMEM, ANY],
        out_specs=(VMEM, SMEM),
        scratch_shapes=[
            pltpu.VMEM((slots, 2, tile_rows, span), jnp.float32),
            pltpu.SemaphoreType.DMA((slots,)),
        ],
        compiler_params=pltpu.CompilerParams(vmem_limit_bytes=56 * 2**20),
        cost_estimate=pl.CostEstimate(flops=0, bytes_accessed=6 * 2**20, transcendentals=0),
        name="fetch",
    )(dealing, cols, tile)


def prepare_kernel(order, dealing, cols, token, empty, blocks, owners, lasts, table, zeros, sems):
    del token
    count = (order + LANES) // LANES
    slots = dealing.shape[0]
    tile_cols = empty.shape[2]
    width = zeros.shape[2]
    zeros[...] = jnp.zeros_like(zeros)
    fills = []
    for b in range(tile_cols // width):
        fill = pltpu.make_async_copy(zeros, empty.at[:, :, b * width : (b + 1) * width], sems.at[b])
        fill.start()
        fills.append(fill)

    @pl.loop(0, tile_cols // LANES)
    def _(block):
        table[block] = -1

    @pl.loop(0, slots)
    def _(slot):
        base, _ = window_start(cols[dealing[slot]], order, tile_cols)
        for b in range(count):
            number = slot * count + b
            block = base // LANES + b
            blocks[number] = block
            known = table[block]
            owner = jnp.where(known < 0, number, known)
            owners[number] = owner
            table[block] = owner
            lasts[owner] = slot

    for fill in fills:
        fill.wait()


def prepare(dealing, cols, token, tile_shape, order):
    slots = dealing.shape[0]
    numbers = slots * (order + LANES) // LANES
    fill_cols = 2048
    return pl.pallas_call(
        functools.partial(prepare_kernel, order),
        out_shape=(
            jax.ShapeDtypeStruct(tile_shape, jnp.float32),
            jax.ShapeDtypeStruct((numbers,), jnp.int32),
            jax.ShapeDtypeStruct((numbers,), jnp.int32),
            jax.ShapeDtypeStruct((numbers,), jnp.int32),
        ),
        in_specs=[SMEM, SMEM, SMEM],
        out_specs=(ANY, SMEM, SMEM, SMEM),
        scratch_shapes=[
            pltpu.SMEM((tile_shape[2] // LANES,), jnp.int32),
            pltpu.VMEM(tile_shape[:2] + (fill_cols,), jnp.float32),
            pltpu.SemaphoreType.DMA((tile_shape[2] // fill_cols,)),
        ],
        compiler_params=pltpu.CompilerParams(vmem_limit_bytes=8 * 2**20),
        cost_estimate=pl.CostEstimate(flops=0, bytes_accessed=11 * 2**20, transcendentals=0),
        name="prepare",
    )(dealing, cols, token)


def slot_kernel(
    dealing, rows, *rest
):
    sources, (term, kept, sent), rest = rest[:5], rest[5:8], rest[8:]
    (cells, probe, right, measured, left), rest = rest[:5], rest[5:]
    wide, patch, wave, half, resid, turned, mine, sems = rest
    loads = [
        pltpu.make_async_copy(source, held, sems.at[k])
        for k, (source, held) in enumerate(zip(sources, (cells, probe, right, measured, left)))
    ]
    for load in loads:
        load.start()
    order = probe.shape[1]
    total_rows = cells.shape[0]
    me = lax.axis_index("row")
    first_row = rows[dealing[me]]
    step = 64
    tile = 256

    loads[0].wait()
    wide[0:total_rows, :] = cells[...].astype(jnp.float32)
    wide[total_rows:, :] = jnp.zeros((SUBLANES, 2 * order), jnp.float32)
    loads[1].wait()

    @pl.loop(0, order // step)
    def _(i):
        place = pl.ds(pl.multiple_of(i * step, step), step)
        found = rows_from(wide, first_row + i * step, step)
        patch[place, :] = found.astype(patch.dtype)
        real, imag = found[:, :order], found[:, order:]
        probe_real = probe[0, place, :].astype(jnp.float32)
        probe_imag = probe[1, place, :].astype(jnp.float32)
        wave[place, :order] = (probe_real * real - probe_imag * imag).astype(wave.dtype)
        wave[place, order:] = (probe_real * imag + probe_imag * real).astype(wave.dtype)

    def dot(a, b):
        return jnp.dot(a, b, preferred_element_type=jnp.float32)

    loads[2].wait()
    for first in range(0, order, tile):
        here = slice(first, first + tile)
        there = slice(order + first, order + first + tile)
        half[:order, here] = dot(wave[...], right[:, here]).astype(half.dtype)
        half[order:, here] = dot(wave[...], right[:, there]).astype(half.dtype)
    loads[3].wait()
    loads[4].wait()
    for first in range(0, order, tile):
        here = slice(first, first + tile)
        there = slice(order + first, order + first + tile)
        for top in range(0, order, tile):
            line = slice(top, top + tile)
            real = dot(left[line, :], half[:, here])
            imag = dot(left[order + top : order + top + tile, :], half[:, here])
            inverse = jnp.minimum(lax.rsqrt(real * real + imag * imag), 1.0 / MAG_FLOOR)
            shrink = 1.0 - measured[0, line, here].astype(jnp.float32) * inverse
            resid[line, here] = (real * shrink).astype(resid.dtype)
            resid[line, there] = (imag * shrink).astype(resid.dtype)
    for first in range(0, order, tile):
        here = slice(first, first + tile)
        there = slice(order + first, order + first + tile)
        turned[:order, here] = dot(resid[...], left[:, here]).astype(turned.dtype)
        turned[order:, here] = dot(resid[...], left[:, there]).astype(turned.dtype)
    for first in range(0, order, tile):
        here = slice(first, first + tile)
        there = slice(order + first, order + first + tile)
        for top in range(0, order, tile):
            line = slice(top, top + tile)
            real = dot(right[line, :], turned[:, here])
            imag = dot(right[order + top : order + top + tile, :], turned[:, here])
            probe_real = probe[0, line, here].astype(jnp.float32)
            probe_imag = probe[1, line, here].astype(jnp.float32)
            term[line, here] = (probe_real * real + probe_imag * imag).astype(term.dtype)
            term[line, there] = (probe_real * imag - probe_imag * real).astype(term.dtype)
            patch_real = patch[line, here].astype(jnp.float32)
            patch_imag = patch[line, there].astype(jnp.float32)
            mine[line, here] = patch_real * real + patch_imag * imag
            mine[line, there] = patch_real * imag - patch_imag * real

    count = kept.shape[0]
    side = lax.rem(me, 2)
    kept[...] = mine[pl.ds(pl.multiple_of(side * count, count), count), :]
    sent[...] = mine[pl.ds(pl.multiple_of((1 - side) * count, count), count), :].astype(sent.dtype)

def slot_terms(cells, probe, measured, dealing, rows):
    order = probe.shape[1]
    total_rows = cells.shape[0]
    right, left = dft_tables(order)
    wide_cols = 2 * order
    bf16, f32 = jnp.bfloat16, jnp.float32
    sources = (cells, probe, jnp.asarray(right), measured, jnp.asarray(left))
    return pl.pallas_call(
        slot_kernel,
        out_shape=(
            jax.ShapeDtypeStruct((order, wide_cols), bf16),
            jax.ShapeDtypeStruct((order // 2, wide_cols), f32),
            jax.ShapeDtypeStruct((order // 2, wide_cols), bf16),
        ),
        in_specs=[SMEM, SMEM] + [ANY] * len(sources),
        out_specs=(VMEM,) * 3,
        scratch_shapes=[pltpu.VMEM(source.shape, bf16) for source in sources]
        + [
            pltpu.VMEM((total_rows + SUBLANES, wide_cols), f32),
            pltpu.VMEM((order, wide_cols), bf16),
            pltpu.VMEM((order, wide_cols), bf16),
            pltpu.VMEM((wide_cols, order), bf16),
            pltpu.VMEM((order, wide_cols), bf16),
            pltpu.VMEM((wide_cols, order), bf16),
            pltpu.VMEM((order, wide_cols), f32),
            pltpu.SemaphoreType.DMA((len(sources),)),
        ],
        compiler_params=pltpu.CompilerParams(vmem_limit_bytes=54 * 2**20),
        cost_estimate=pl.CostEstimate(
            flops=8 * 2 * order**3 * 2, bytes_accessed=8 * 2**20, transcendentals=order * order
        ),
        name="slot",
    )(dealing, rows, *sources)


def pack_kernel(reach, own_rows, dealing, rows, term, out, padded):
    order = term.shape[0]
    first_row = rows[dealing[lax.axis_index("row")]]
    below = padded.shape[0] - reach - order
    padded[0:reach, :] = jnp.zeros((reach, padded.shape[1]), jnp.float32)
    padded[reach : reach + order, :] = term[...].astype(jnp.float32)
    padded[reach + order :, :] = jnp.zeros((below, padded.shape[1]), jnp.float32)

    @pl.loop(0, out.shape[0], unroll=2)
    def _(k):
        out[k] = rows_from(padded, reach - first_row + k * own_rows, out.shape[1]).astype(out.dtype)


def pack_rows(term, dealing, rows, slots, own_rows, tile_rows):
    order, width = term.shape
    reach = slots * own_rows - order
    return pl.pallas_call(
        functools.partial(pack_kernel, reach, own_rows),
        out_shape=jax.ShapeDtypeStruct((slots, tile_rows, width), jnp.bfloat16),
        in_specs=[SMEM, SMEM, VMEM],
        out_specs=VMEM,
        scratch_shapes=[pltpu.VMEM((2 * reach + order + tile_rows + SUBLANES, width), jnp.float32)],
        compiler_params=pltpu.CompilerParams(vmem_limit_bytes=16 * 2**20),
        cost_estimate=pl.CostEstimate(flops=0, bytes_accessed=3 * 2**20, transcendentals=0),
        name="pack",
    )(dealing, rows, term)


def place_kernel(order, dealing, cols, blocks, owners, lasts, terms, empty, out, totals, sems):
    del empty
    slots, tile_rows = terms.shape[0], terms.shape[1]
    count = (order + LANES) // LANES
    totals[...] = jnp.zeros_like(totals)
    lane = lax.broadcasted_iota(jnp.int32, (tile_rows, LANES), 1)
    nothing = jnp.zeros((tile_rows, LANES), jnp.float32)

    def copy(number):
        place = pl.multiple_of(blocks[number] * LANES, LANES)
        return pltpu.make_async_copy(totals.at[number], out.at[:, :, pl.ds(place, LANES)], sems.at[number])

    @pl.loop(0, slots)
    def _(slot):
        _, offset = window_start(cols[dealing[slot]], order, out.shape[2])
        shift = lax.rem(offset, LANES)
        for part in range(2):
            turned = []
            for b in range(count - 1):
                first = part * order + b * LANES
                turned.append(pltpu.roll(terms[slot, :, first : first + LANES].astype(jnp.float32), shift, 1))
            for b in range(count):
                before = turned[b - 1] if b else nothing
                after = turned[b] if b < count - 1 else nothing
                owner = owners[slot * count + b]
                totals[owner, part] += jnp.where(lane < offset, before, after)
        for b in range(count):
            owner = owners[slot * count + b]

            @pl.when(lasts[owner] == slot)
            def _():
                copy(owner).start()

    @pl.loop(0, slots * count)
    def _(number):
        @pl.when(owners[number] == number)
        def _():
            copy(number).wait()


def place_windows(terms, empty, blocks, owners, lasts, dealing, cols, order):
    slots, tile_rows = terms.shape[0], terms.shape[1]
    count = (order + LANES) // LANES
    return pl.pallas_call(
        functools.partial(place_kernel, order),
        out_shape=jax.ShapeDtypeStruct(empty.shape, empty.dtype),
        in_specs=[SMEM, SMEM, SMEM, SMEM, SMEM, VMEM, ANY],
        out_specs=ANY,
        scratch_shapes=[
            pltpu.VMEM((slots * count, 2, tile_rows, LANES), jnp.float32),
            pltpu.SemaphoreType.DMA((slots * count,)),
        ],
        input_output_aliases={6: 0},
        compiler_params=pltpu.CompilerParams(vmem_limit_bytes=24 * 2**20),
        cost_estimate=pl.CostEstimate(flops=0, bytes_accessed=6 * 2**20, transcendentals=0),
        name="place",
    )(dealing, cols, blocks, owners, lasts, terms, empty)


def strides(devices):
    steps, stride = [], 1
    while stride < devices:
        radix = 4 if len(steps) >= 2 and (devices // stride) % 4 == 0 else 2
        steps.append((stride, radix))
        stride *= radix
    return steps


def swap(x, distance, devices):
    return lax.ppermute(x, "row", [(d, d ^ distance) for d in range(devices)])


def sum_probe(kept, sent, devices):
    me = lax.axis_index("row")
    total = kept + swap(sent, 1, devices).astype(jnp.float32)
    for stride, radix in strides(devices)[1:]:
        digit = me // stride % radix
        count = total.shape[0] // radix
        own = lax.dynamic_slice_in_dim(total, digit * count, count)
        for k in range(1, radix):
            share = lax.dynamic_slice_in_dim(total, lax.bitwise_xor(digit, k) * count, count)
            own = own + swap(share.astype(jnp.bfloat16), k * stride, devices).astype(jnp.float32)
        total = own
    return total


def join(whole, devices):
    me = lax.axis_index("row")
    for stride, radix in reversed(strides(devices)):
        digit = me // stride % radix
        shares = [whole] + [swap(whole, k * stride, devices) for k in range(1, radix)]
        pieces = []
        for j in range(radix):
            piece = shares[0]
            for k in range(1, radix):
                piece = jnp.where(lax.bitwise_xor(digit, k) == j, shares[k], piece)
            pieces.append(piece)
        whole = jnp.concatenate(pieces, axis=0)
    return whole


def body(object_field, probe, amplitude, row_offsets, col_offsets, dealing):
    order = probe.shape[1]
    devices = lax.axis_size("row")
    own_rows, tile_cols = object_field.shape[1], object_field.shape[2]
    total_rows = devices * own_rows
    tile_rows = -(-own_rows // SUBLANES) * SUBLANES
    spare = tile_rows - own_rows
    if spare:
        object_field = jnp.pad(object_field, ((0, 0), (0, spare), (0, 0)))
    pieces, token = fetch_windows(object_field, dealing, col_offsets, order)
    strips = lax.all_to_all(pieces, "row", split_axis=0, concat_axis=0, tiled=True)
    cells = strips[:, :own_rows].reshape(total_rows, 2 * order)
    empty, blocks, owners, lasts = prepare(dealing, col_offsets, token, object_field.shape, order)
    term, kept, sent = slot_terms(cells, probe, amplitude, dealing, row_offsets)
    total = sum_probe(kept, sent, devices)
    terms = pack_rows(term, dealing, row_offsets, devices, own_rows, tile_rows)
    terms, total = lax.optimization_barrier((terms, total))
    arrived = lax.all_to_all(terms, "row", split_axis=0, concat_axis=0, tiled=True)
    share = (total * (1.0 / dealing.shape[0])).astype(jnp.bfloat16)
    whole = join(share, devices).astype(jnp.float32)
    probe_grad = jnp.stack([whole[:, :order], whole[:, order:]])
    object_grad = place_windows(
        arrived, empty, blocks, owners, lasts, dealing, col_offsets, order
    )
    if spare:
        object_grad = object_grad[:, :own_rows]
    return (object_grad, probe_grad)


def solution(mesh):
    return jax.shard_map(
        body,
        mesh=mesh,
        in_specs=(
            P(None, ("groups", "row"), None),
            P("groups", None, None),
            P(("groups", "row"), None, None),
            P("groups"),
            P("groups"),
            P("groups"),
        ),
        out_specs=(P(None, ("groups", "row"), None), P("groups", None, None)),
        check_vma=False,
    )
```

```python
import functools
import math

import jax
import jax.numpy as jnp
import numpy as np
from jax import lax
from jax.experimental import pallas as pl
from jax.experimental.pallas import tpu as pltpu
from jax.sharding import PartitionSpec as P

MAG_FLOOR = 0.25
LANES = 128
SUBLANES = 8
SMEM = pl.BlockSpec(memory_space=pltpu.SMEM)
VMEM = pl.BlockSpec(memory_space=pltpu.VMEM)
ANY = pl.BlockSpec(memory_space=pl.ANY)


def dft_tables(order):
    indices = np.arange(order, dtype=np.int32)
    phases = indices[:, None] * indices[None, :] % order
    angles = phases.astype(np.float32) * np.float32(2.0 * math.pi / order)
    factor = np.float32(1.0 / math.sqrt(order))
    real_part = np.cos(angles) * factor
    imag_part = -np.sin(angles) * factor
    right_table = np.block([[real_part, imag_part], [-imag_part, real_part]])
    left_table = np.block([[real_part, -imag_part], [imag_part, real_part]])
    return right_table.astype(jnp.bfloat16), left_table.astype(jnp.bfloat16)


def window_start(column, order, tile_cols):
    span = order + LANES
    base = jnp.minimum(column // LANES, (tile_cols - span) // LANES) * LANES
    return pl.multiple_of(base, LANES), column - base


def rows_from(ref, start, count):
    aligned = pl.multiple_of(start // SUBLANES * SUBLANES, SUBLANES)
    rest = start - aligned
    width = ref.shape[-1]
    blocks = ref[pl.ds(aligned, count + SUBLANES), :].reshape(-1, SUBLANES, width)
    turned = pltpu.roll(blocks, lax.rem(SUBLANES - rest, SUBLANES), 1)
    sub = lax.broadcasted_iota(jnp.int32, (1, SUBLANES, width), 1)
    picked = jnp.where(sub < SUBLANES - rest, turned[:-1], turned[1:])
    return picked.reshape(count, width)


def fetch_kernel(order, dealing, cols, tile, out, token, held, sems):
    token[0] = dealing[0]
    slots, tile_rows = out.shape[0], out.shape[1]
    tile_cols = tile.shape[2]
    span = order + LANES

    def copy(slot):
        base, _ = window_start(cols[dealing[slot]], order, tile_cols)
        return pltpu.make_async_copy(tile.at[:, :, pl.ds(base, span)], held.at[slot], sems.at[slot])

    @pl.loop(0, slots)
    def _(slot):
        copy(slot).start()

    lane = lax.broadcasted_iota(jnp.int32, (tile_rows, LANES), 1)

    @pl.loop(0, slots, unroll=4)
    def _(slot):
        copy(slot).wait()
        _, offset = window_start(cols[dealing[slot]], order, tile_cols)
        shift = lax.rem(LANES - lax.rem(offset, LANES), LANES)
        for part in range(2):
            turned = [
                pltpu.roll(held[slot, part, :, b * LANES : (b + 1) * LANES], shift, 1)
                for b in range(span // LANES)
            ]
            for b in range(order // LANES):
                first = part * order + b * LANES
                cells = jnp.where(lane < LANES - offset, turned[b], turned[b + 1])
                out[slot, :, first : first + LANES] = cells.astype(out.dtype)


def fetch_windows(tile, dealing, cols, order):
    slots, tile_rows, tile_cols = dealing.shape[0], tile.shape[1], tile.shape[2]
    span = order + LANES

    return pl.pallas_call(
        functools.partial(fetch_kernel, order),
        out_shape=(
            jax.ShapeDtypeStruct((slots, tile_rows, 2 * order), jnp.bfloat16),
            jax.ShapeDtypeStruct((1,), jnp.int32),
        ),
        in_specs=[SMEM, SMEM, ANY],
        out_specs=(VMEM, SMEM),
        scratch_shapes=[
            pltpu.VMEM((slots, 2, tile_rows, span), jnp.float32),
            pltpu.SemaphoreType.DMA((slots,)),
        ],
        compiler_params=pltpu.CompilerParams(vmem_limit_bytes=56 * 2**20),
        cost_estimate=pl.CostEstimate(flops=0, bytes_accessed=6 * 2**20, transcendentals=0),
        name="fetch",
    )(dealing, cols, tile)


def prepare_kernel(order, dealing, cols, token, empty, blocks, owners, table, zeros, sems):
    del token
    count = (order + LANES) // LANES
    slots = dealing.shape[0]
    tile_cols = empty.shape[2]
    width = zeros.shape[2]
    zeros[...] = jnp.zeros_like(zeros)
    fills = []
    for b in range(tile_cols // width):
        fill = pltpu.make_async_copy(zeros, empty.at[:, :, b * width : (b + 1) * width], sems.at[b])
        fill.start()
        fills.append(fill)

    @pl.loop(0, tile_cols // LANES)
    def _(block):
        table[block] = -1

    @pl.loop(0, slots)
    def _(slot):
        base, _ = window_start(cols[dealing[slot]], order, tile_cols)
        for b in range(count):
            number = slot * count + b
            block = base // LANES + b
            blocks[number] = block
            known = table[block]
            owner = jnp.where(known < 0, number, known)
            owners[number] = owner
            table[block] = owner

    for fill in fills:
        fill.wait()


def prepare(dealing, cols, token, tile_shape, order):
    slots = dealing.shape[0]
    numbers = slots * (order + LANES) // LANES
    fill_cols = 2048
    return pl.pallas_call(
        functools.partial(prepare_kernel, order),
        out_shape=(
            jax.ShapeDtypeStruct(tile_shape, jnp.float32),
            jax.ShapeDtypeStruct((numbers,), jnp.int32),
            jax.ShapeDtypeStruct((numbers,), jnp.int32),
        ),
        in_specs=[SMEM, SMEM, SMEM],
        out_specs=(ANY, SMEM, SMEM),
        scratch_shapes=[
            pltpu.SMEM((tile_shape[2] // LANES,), jnp.int32),
            pltpu.VMEM(tile_shape[:2] + (fill_cols,), jnp.float32),
            pltpu.SemaphoreType.DMA((tile_shape[2] // fill_cols,)),
        ],
        compiler_params=pltpu.CompilerParams(vmem_limit_bytes=8 * 2**20),
        cost_estimate=pl.CostEstimate(flops=0, bytes_accessed=110 * 2**20, transcendentals=0),
        name="prepare",
    )(dealing, cols, token)


def slot_kernel(
    dealing, rows, owners, cells, probe, measured, right, left,
    term, kept, sent,
    wide, patch, wave, half, resid, turned, mine,
):
    del owners
    order = probe.shape[1]
    total_rows = cells.shape[0]
    me = lax.axis_index("row")
    first_row = rows[dealing[me]]
    step = 64
    tile = 256

    wide[0:total_rows, :] = cells[...].astype(jnp.float32)
    wide[total_rows:, :] = jnp.zeros((SUBLANES, 2 * order), jnp.float32)
    @pl.loop(0, order // step)
    def _(i):
        place = pl.ds(pl.multiple_of(i * step, step), step)
        found = rows_from(wide, first_row + i * step, step)
        patch[place, :] = found.astype(patch.dtype)
        real, imag = found[:, :order], found[:, order:]
        probe_real = probe[0, place, :].astype(jnp.float32)
        probe_imag = probe[1, place, :].astype(jnp.float32)
        wave[place, :order] = (probe_real * real - probe_imag * imag).astype(wave.dtype)
        wave[place, order:] = (probe_real * imag + probe_imag * real).astype(wave.dtype)

    def dot(a, b):
        return jnp.dot(a, b, preferred_element_type=jnp.float32)

    for first in range(0, order, tile):
        here = slice(first, first + tile)
        there = slice(order + first, order + first + tile)
        half[:order, here] = dot(wave[...], right[:, here]).astype(half.dtype)
        half[order:, here] = dot(wave[...], right[:, there]).astype(half.dtype)
    for first in range(0, order, tile):
        here = slice(first, first + tile)
        there = slice(order + first, order + first + tile)
        for top in range(0, order, tile):
            line = slice(top, top + tile)
            real = dot(left[line, :], half[:, here])
            imag = dot(left[order + top : order + top + tile, :], half[:, here])
            inverse = jnp.minimum(lax.rsqrt(real * real + imag * imag), 1.0 / MAG_FLOOR)
            shrink = 1.0 - measured[0, line, here].astype(jnp.float32) * inverse
            resid[line, here] = (real * shrink).astype(resid.dtype)
            resid[line, there] = (imag * shrink).astype(resid.dtype)
    for first in range(0, order, tile):
        here = slice(first, first + tile)
        there = slice(order + first, order + first + tile)
        turned[:order, here] = dot(resid[...], left[:, here]).astype(turned.dtype)
        turned[order:, here] = dot(resid[...], left[:, there]).astype(turned.dtype)
    for first in range(0, order, tile):
        here = slice(first, first + tile)
        there = slice(order + first, order + first + tile)
        for top in range(0, order, tile):
            line = slice(top, top + tile)
            real = dot(right[line, :], turned[:, here])
            imag = dot(right[order + top : order + top + tile, :], turned[:, here])
            probe_real = probe[0, line, here].astype(jnp.float32)
            probe_imag = probe[1, line, here].astype(jnp.float32)
            term[line, here] = (probe_real * real + probe_imag * imag).astype(term.dtype)
            term[line, there] = (probe_real * imag - probe_imag * real).astype(term.dtype)
            patch_real = patch[line, here].astype(jnp.float32)
            patch_imag = patch[line, there].astype(jnp.float32)
            mine[line, here] = patch_real * real + patch_imag * imag
            mine[line, there] = patch_real * imag - patch_imag * real

    count = kept.shape[0]
    side = lax.rem(me, 2)
    kept[...] = mine[pl.ds(pl.multiple_of(side * count, count), count), :]
    sent[...] = mine[pl.ds(pl.multiple_of((1 - side) * count, count), count), :].astype(sent.dtype)

def slot_terms(cells, probe, measured, dealing, rows, owners):
    order = probe.shape[1]
    total_rows = cells.shape[0]
    wide_cols = 2 * order
    right, left = dft_tables(order)
    bf16, f32 = jnp.bfloat16, jnp.float32
    return pl.pallas_call(
        slot_kernel,
        out_shape=(
            jax.ShapeDtypeStruct((order, wide_cols), bf16),
            jax.ShapeDtypeStruct((order // 2, wide_cols), f32),
            jax.ShapeDtypeStruct((order // 2, wide_cols), bf16),
        ),
        in_specs=[SMEM, SMEM, SMEM, VMEM, VMEM, VMEM, VMEM, VMEM],
        out_specs=(VMEM,) * 3,
        scratch_shapes=[
            pltpu.VMEM((total_rows + SUBLANES, wide_cols), f32),
            pltpu.VMEM((order, wide_cols), bf16),
            pltpu.VMEM((order, wide_cols), bf16),
            pltpu.VMEM((wide_cols, order), bf16),
            pltpu.VMEM((order, wide_cols), bf16),
            pltpu.VMEM((wide_cols, order), bf16),
            pltpu.VMEM((order, wide_cols), f32),
        ],
        compiler_params=pltpu.CompilerParams(vmem_limit_bytes=40 * 2**20),
        cost_estimate=pl.CostEstimate(
            flops=8 * 2 * order**3 * 2, bytes_accessed=8 * 2**20, transcendentals=order * order
        ),
        name="slot",
    )(dealing, rows, owners, cells, probe, measured, jnp.asarray(right), jnp.asarray(left))


def pack_kernel(reach, own_rows, dealing, rows, term, out, padded):
    order = term.shape[0]
    first_row = rows[dealing[lax.axis_index("row")]]
    below = padded.shape[0] - reach - order
    padded[0:reach, :] = jnp.zeros((reach, padded.shape[1]), jnp.float32)
    padded[reach : reach + order, :] = term[...].astype(jnp.float32)
    padded[reach + order :, :] = jnp.zeros((below, padded.shape[1]), jnp.float32)

    @pl.loop(0, out.shape[0], unroll=2)
    def _(k):
        out[k] = rows_from(padded, reach - first_row + k * own_rows, out.shape[1]).astype(out.dtype)


def pack_rows(term, dealing, rows, slots, own_rows, tile_rows):
    order, width = term.shape
    reach = slots * own_rows - order
    return pl.pallas_call(
        functools.partial(pack_kernel, reach, own_rows),
        out_shape=jax.ShapeDtypeStruct((slots, tile_rows, width), jnp.bfloat16),
        in_specs=[SMEM, SMEM, VMEM],
        out_specs=VMEM,
        scratch_shapes=[pltpu.VMEM((2 * reach + order + tile_rows + SUBLANES, width), jnp.float32)],
        compiler_params=pltpu.CompilerParams(vmem_limit_bytes=16 * 2**20),
        cost_estimate=pl.CostEstimate(flops=0, bytes_accessed=3 * 2**20, transcendentals=0),
        name="pack",
    )(dealing, rows, term)


def place_kernel(order, dealing, cols, blocks, owners, terms, empty, out, totals, sems):
    del empty
    slots, tile_rows = terms.shape[0], terms.shape[1]
    count = (order + LANES) // LANES
    totals[...] = jnp.zeros_like(totals)
    lane = lax.broadcasted_iota(jnp.int32, (tile_rows, LANES), 1)
    nothing = jnp.zeros((tile_rows, LANES), jnp.float32)

    @pl.loop(0, slots, unroll=4)
    def _(slot):
        _, offset = window_start(cols[dealing[slot]], order, out.shape[2])
        shift = lax.rem(offset, LANES)
        for part in range(2):
            turned = []
            for b in range(count - 1):
                first = part * order + b * LANES
                turned.append(pltpu.roll(terms[slot, :, first : first + LANES].astype(jnp.float32), shift, 1))
            for b in range(count):
                before = turned[b - 1] if b else nothing
                after = turned[b] if b < count - 1 else nothing
                owner = owners[slot * count + b]
                totals[owner, part] += jnp.where(lane < offset, before, after)

    def copy(number):
        place = pl.multiple_of(blocks[number] * LANES, LANES)
        return pltpu.make_async_copy(totals.at[number], out.at[:, :, pl.ds(place, LANES)], sems.at[number])

    @pl.loop(0, slots * count)
    def _(number):
        @pl.when(owners[number] == number)
        def _():
            copy(number).start()

    @pl.loop(0, slots * count)
    def _(number):
        @pl.when(owners[number] == number)
        def _():
            copy(number).wait()


def place_windows(terms, empty, blocks, owners, dealing, cols, order):
    slots, tile_rows = terms.shape[0], terms.shape[1]
    count = (order + LANES) // LANES
    return pl.pallas_call(
        functools.partial(place_kernel, order),
        out_shape=jax.ShapeDtypeStruct(empty.shape, empty.dtype),
        in_specs=[SMEM, SMEM, SMEM, SMEM, VMEM, ANY],
        out_specs=ANY,
        scratch_shapes=[
            pltpu.VMEM((slots * count, 2, tile_rows, LANES), jnp.float32),
            pltpu.SemaphoreType.DMA((slots * count,)),
        ],
        input_output_aliases={5: 0},
        compiler_params=pltpu.CompilerParams(vmem_limit_bytes=24 * 2**20),
        cost_estimate=pl.CostEstimate(flops=0, bytes_accessed=6 * 2**20, transcendentals=0),
        name="place",
    )(dealing, cols, blocks, owners, terms, empty)


def strides(devices):
    steps, stride = [], 1
    while stride < devices:
        radix = 4 if len(steps) >= 2 and (devices // stride) % 4 == 0 else 2
        steps.append((stride, radix))
        stride *= radix
    return steps


def swap(x, distance, devices):
    return lax.ppermute(x, "row", [(d, d ^ distance) for d in range(devices)])


def sum_probe(kept, sent, devices):
    me = lax.axis_index("row")
    total = kept + swap(sent, 1, devices).astype(jnp.float32)
    for stride, radix in strides(devices)[1:]:
        digit = me // stride % radix
        count = total.shape[0] // radix
        own = lax.dynamic_slice_in_dim(total, digit * count, count)
        for k in range(1, radix):
            share = lax.dynamic_slice_in_dim(total, lax.bitwise_xor(digit, k) * count, count)
            own = own + swap(share.astype(jnp.bfloat16), k * stride, devices).astype(jnp.float32)
        total = own
    return total


def join(whole, devices):
    me = lax.axis_index("row")
    for stride, radix in reversed(strides(devices)):
        digit = me // stride % radix
        shares = [whole] + [swap(whole, k * stride, devices) for k in range(1, radix)]
        pieces = []
        for j in range(radix):
            piece = shares[0]
            for k in range(1, radix):
                piece = jnp.where(lax.bitwise_xor(digit, k) == j, shares[k], piece)
            pieces.append(piece)
        whole = jnp.concatenate(pieces, axis=0)
    return whole


def body(object_field, probe, amplitude, row_offsets, col_offsets, dealing):
    order = probe.shape[1]
    devices = lax.axis_size("row")
    own_rows, tile_cols = object_field.shape[1], object_field.shape[2]
    total_rows = devices * own_rows
    tile_rows = -(-own_rows // SUBLANES) * SUBLANES
    spare = tile_rows - own_rows
    if spare:
        object_field = jnp.pad(object_field, ((0, 0), (0, spare), (0, 0)))
    pieces, token = fetch_windows(object_field, dealing, col_offsets, order)
    strips = lax.all_to_all(pieces, "row", split_axis=0, concat_axis=0, tiled=True)
    cells = strips[:, :own_rows].reshape(total_rows, 2 * order)
    empty, blocks, owners = prepare(dealing, col_offsets, token, object_field.shape, order)
    term, kept, sent = slot_terms(cells, probe, amplitude, dealing, row_offsets, owners)
    total = sum_probe(kept, sent, devices)
    terms = pack_rows(term, dealing, row_offsets, devices, own_rows, tile_rows)
    terms, total = lax.optimization_barrier((terms, total))
    arrived = lax.all_to_all(terms, "row", split_axis=0, concat_axis=0, tiled=True)
    share = (total * (1.0 / dealing.shape[0])).astype(jnp.bfloat16)
    whole = join(share, devices).astype(jnp.float32)
    probe_grad = jnp.stack([whole[:, :order], whole[:, order:]])
    object_grad = place_windows(arrived, empty, blocks, owners, dealing, col_offsets, order)
    if spare:
        object_grad = object_grad[:, :own_rows]
    return (object_grad, probe_grad)


def solution(mesh):
    return jax.shard_map(
        body,
        mesh=mesh,
        in_specs=(
            P(None, ("groups", "row"), None),
            P("groups", None, None),
            P(("groups", "row"), None, None),
            P("groups"),
            P("groups"),
            P("groups"),
        ),
        out_specs=(P(None, ("groups", "row"), None), P("groups", None, None)),
        check_vma=False,
    )
```

```python
import functools
import math

import jax
import jax.numpy as jnp
import numpy as np
from jax import lax
from jax.experimental import pallas as pl
from jax.experimental.pallas import tpu as pltpu
from jax.sharding import PartitionSpec as P

MAG_FLOOR = 0.25
LANES = 128
SUBLANES = 8
SMEM = pl.BlockSpec(memory_space=pltpu.SMEM)
VMEM = pl.BlockSpec(memory_space=pltpu.VMEM)
ANY = pl.BlockSpec(memory_space=pl.ANY)


def dft_tables(order):
    indices = np.arange(order, dtype=np.int32)
    phases = indices[:, None] * indices[None, :] % order
    angles = phases.astype(np.float32) * np.float32(2.0 * math.pi / order)
    factor = np.float32(1.0 / math.sqrt(order))
    real_part = np.cos(angles) * factor
    imag_part = -np.sin(angles) * factor
    right_table = np.block([[real_part, imag_part], [-imag_part, real_part]])
    left_table = np.block([[real_part, -imag_part], [imag_part, real_part]])
    return right_table.astype(jnp.bfloat16), left_table.astype(jnp.bfloat16)


def window_start(column, order, tile_cols):
    span = order + LANES
    base = jnp.minimum(column // LANES, (tile_cols - span) // LANES) * LANES
    return pl.multiple_of(base, LANES), column - base


def rows_from(ref, start, count):
    aligned = pl.multiple_of(start // SUBLANES * SUBLANES, SUBLANES)
    rest = start - aligned
    width = ref.shape[-1]
    blocks = ref[pl.ds(aligned, count + SUBLANES), :].reshape(-1, SUBLANES, width)
    turned = pltpu.roll(blocks, lax.rem(SUBLANES - rest, SUBLANES), 1)
    sub = lax.broadcasted_iota(jnp.int32, (1, SUBLANES, width), 1)
    picked = jnp.where(sub < SUBLANES - rest, turned[:-1], turned[1:])
    return picked.reshape(count, width)


def fetch_kernel(order, dealing, cols, tile, out, token, held, sems):
    token[0] = dealing[0]
    slots, tile_rows = out.shape[0], out.shape[1]
    tile_cols = tile.shape[2]
    span = order + LANES

    def copy(slot):
        base, _ = window_start(cols[dealing[slot]], order, tile_cols)
        return pltpu.make_async_copy(tile.at[:, :, pl.ds(base, span)], held.at[slot], sems.at[slot])

    @pl.loop(0, slots)
    def _(slot):
        copy(slot).start()

    lane = lax.broadcasted_iota(jnp.int32, (tile_rows, LANES), 1)

    @pl.loop(0, slots, unroll=4)
    def _(slot):
        copy(slot).wait()
        _, offset = window_start(cols[dealing[slot]], order, tile_cols)
        shift = lax.rem(LANES - lax.rem(offset, LANES), LANES)
        for part in range(2):
            turned = [
                pltpu.roll(held[slot, part, :, b * LANES : (b + 1) * LANES].astype(out.dtype), shift, 1)
                for b in range(span // LANES)
            ]
            for b in range(order // LANES):
                first = part * order + b * LANES
                cells = jnp.where(lane < LANES - offset, turned[b], turned[b + 1])
                out[slot, :, first : first + LANES] = cells


def fetch_windows(tile, dealing, cols, order):
    slots, tile_rows, tile_cols = dealing.shape[0], tile.shape[1], tile.shape[2]
    span = order + LANES

    return pl.pallas_call(
        functools.partial(fetch_kernel, order),
        out_shape=(
            jax.ShapeDtypeStruct((slots, tile_rows, 2 * order), jnp.bfloat16),
            jax.ShapeDtypeStruct((1,), jnp.int32),
        ),
        in_specs=[SMEM, SMEM, ANY],
        out_specs=(VMEM, SMEM),
        scratch_shapes=[
            pltpu.VMEM((slots, 2, tile_rows, span), jnp.float32),
            pltpu.SemaphoreType.DMA((slots,)),
        ],
        compiler_params=pltpu.CompilerParams(vmem_limit_bytes=56 * 2**20),
        cost_estimate=pl.CostEstimate(flops=0, bytes_accessed=6 * 2**20, transcendentals=0),
        name="fetch",
    )(dealing, cols, tile)


def stock_places(stock, order):
    return (
        stock.at[0:order, 0:order],
        stock.at[0:order, order : 2 * order],
        stock.at[order : 3 * order, :],
        stock.at[3 * order : 4 * order, 0:order],
        stock.at[4 * order : 6 * order, :],
    )


def prepare_kernel(
    order, dealing, cols, token, right, left, probe, measured,
    empty, blocks, owners, stock,
    table, zeros, sems, stock_sems,
):
    del token
    places = stock_places(stock, order)
    sources = (probe.at[0], probe.at[1], right, measured.at[0], left)
    fills = []
    for k, (source, place) in enumerate(zip(sources, places)):
        fill = pltpu.make_async_copy(source, place, stock_sems.at[k])
        fill.start()
        fills.append(fill)
    count = (order + LANES) // LANES
    slots = dealing.shape[0]
    tile_cols = empty.shape[2]
    width = zeros.shape[2]
    zeros[...] = jnp.zeros_like(zeros)
    for b in range(tile_cols // width):
        fill = pltpu.make_async_copy(zeros, empty.at[:, :, b * width : (b + 1) * width], sems.at[b])
        fill.start()
        fills.append(fill)

    @pl.loop(0, tile_cols // LANES)
    def _(block):
        table[block] = -1

    @pl.loop(0, slots)
    def _(slot):
        base, _ = window_start(cols[dealing[slot]], order, tile_cols)
        for b in range(count):
            number = slot * count + b
            block = base // LANES + b
            blocks[number] = block
            known = table[block]
            owner = jnp.where(known < 0, number, known)
            owners[number] = owner
            table[block] = owner

    for fill in fills:
        fill.wait()


def prepare(dealing, cols, token, probe, measured, tile_shape):
    order = probe.shape[1]
    right, left = dft_tables(order)
    slots = dealing.shape[0]
    numbers = slots * (order + LANES) // LANES
    fill_cols = 2048
    return pl.pallas_call(
        functools.partial(prepare_kernel, order),
        out_shape=(
            jax.ShapeDtypeStruct(tile_shape, jnp.float32),
            jax.ShapeDtypeStruct((numbers,), jnp.int32),
            jax.ShapeDtypeStruct((numbers,), jnp.int32),
            jax.ShapeDtypeStruct((28 * order, 2 * order), jnp.bfloat16),
        ),
        in_specs=[SMEM, SMEM, SMEM, ANY, ANY, ANY, ANY],
        out_specs=(ANY, SMEM, SMEM, ANY),
        scratch_shapes=[
            pltpu.SMEM((tile_shape[2] // LANES,), jnp.int32),
            pltpu.VMEM(tile_shape[:2] + (fill_cols,), jnp.float32),
            pltpu.SemaphoreType.DMA((tile_shape[2] // fill_cols,)),
            pltpu.SemaphoreType.DMA((5,)),
        ],
        compiler_params=pltpu.CompilerParams(vmem_limit_bytes=8 * 2**20),
        cost_estimate=pl.CostEstimate(flops=0, bytes_accessed=110 * 2**20, transcendentals=0),
        name="prepare",
    )(dealing, cols, token, jnp.asarray(right), jnp.asarray(left), probe, measured)


def slot_kernel(
    dealing, rows, owners, cells, stock,
    term, kept, sent,
    wide, patch, wave, half, resid, turned, mine, probe, right, measured, left, sems,
):
    del owners
    order = term.shape[0]
    targets = (probe.at[0], probe.at[1], right, measured, left)
    loads = [
        pltpu.make_async_copy(source, target, sems.at[k])
        for k, (source, target) in enumerate(zip(stock_places(stock, order), targets))
    ]
    for load in loads:
        load.start()
    total_rows = cells.shape[0]
    me = lax.axis_index("row")
    first_row = rows[dealing[me]]
    step = 64
    tile = 256

    wide[0:total_rows, :] = cells[...].astype(jnp.float32)
    wide[total_rows:, :] = jnp.zeros((SUBLANES, 2 * order), jnp.float32)
    loads[0].wait()
    loads[1].wait()

    @pl.loop(0, order // step)
    def _(i):
        place = pl.ds(pl.multiple_of(i * step, step), step)
        found = rows_from(wide, first_row + i * step, step)
        patch[place, :] = found.astype(patch.dtype)
        real, imag = found[:, :order], found[:, order:]
        probe_real = probe[0, place, :].astype(jnp.float32)
        probe_imag = probe[1, place, :].astype(jnp.float32)
        wave[place, :order] = (probe_real * real - probe_imag * imag).astype(wave.dtype)
        wave[place, order:] = (probe_real * imag + probe_imag * real).astype(wave.dtype)

    def dot(a, b):
        return jnp.dot(a, b, preferred_element_type=jnp.float32)

    loads[2].wait()
    for first in range(0, order, tile):
        here = slice(first, first + tile)
        there = slice(order + first, order + first + tile)
        half[:order, here] = dot(wave[...], right[:, here]).astype(half.dtype)
        half[order:, here] = dot(wave[...], right[:, there]).astype(half.dtype)
    loads[3].wait()
    loads[4].wait()
    for first in range(0, order, tile):
        here = slice(first, first + tile)
        there = slice(order + first, order + first + tile)
        for top in range(0, order, tile):
            line = slice(top, top + tile)
            real = dot(left[line, :], half[:, here])
            imag = dot(left[order + top : order + top + tile, :], half[:, here])
            inverse = jnp.minimum(lax.rsqrt(real * real + imag * imag), 1.0 / MAG_FLOOR)
            shrink = 1.0 - measured[line, here].astype(jnp.float32) * inverse
            resid[line, here] = (real * shrink).astype(resid.dtype)
            resid[line, there] = (imag * shrink).astype(resid.dtype)
    for first in range(0, order, tile):
        here = slice(first, first + tile)
        there = slice(order + first, order + first + tile)
        turned[:order, here] = dot(resid[...], left[:, here]).astype(turned.dtype)
        turned[order:, here] = dot(resid[...], left[:, there]).astype(turned.dtype)
    for first in range(0, order, tile):
        here = slice(first, first + tile)
        there = slice(order + first, order + first + tile)
        for top in range(0, order, tile):
            line = slice(top, top + tile)
            real = dot(right[line, :], turned[:, here])
            imag = dot(right[order + top : order + top + tile, :], turned[:, here])
            probe_real = probe[0, line, here].astype(jnp.float32)
            probe_imag = probe[1, line, here].astype(jnp.float32)
            term[line, here] = (probe_real * real + probe_imag * imag).astype(term.dtype)
            term[line, there] = (probe_real * imag - probe_imag * real).astype(term.dtype)
            patch_real = patch[line, here].astype(jnp.float32)
            patch_imag = patch[line, there].astype(jnp.float32)
            mine[line, here] = patch_real * real + patch_imag * imag
            mine[line, there] = patch_real * imag - patch_imag * real

    count = kept.shape[0]
    side = lax.rem(me, 2)
    kept[...] = mine[pl.ds(pl.multiple_of(side * count, count), count), :]
    sent[...] = mine[pl.ds(pl.multiple_of((1 - side) * count, count), count), :].astype(sent.dtype)

def slot_terms(cells, stock, dealing, rows, owners, order):
    total_rows = cells.shape[0]
    wide_cols = 2 * order
    bf16, f32 = jnp.bfloat16, jnp.float32
    return pl.pallas_call(
        slot_kernel,
        out_shape=(
            jax.ShapeDtypeStruct((order, wide_cols), bf16),
            jax.ShapeDtypeStruct((order // 2, wide_cols), f32),
            jax.ShapeDtypeStruct((order // 2, wide_cols), bf16),
        ),
        in_specs=[SMEM, SMEM, SMEM, VMEM, ANY],
        out_specs=(VMEM,) * 3,
        scratch_shapes=[
            pltpu.VMEM((total_rows + SUBLANES, wide_cols), f32),
            pltpu.VMEM((order, wide_cols), bf16),
            pltpu.VMEM((order, wide_cols), bf16),
            pltpu.VMEM((wide_cols, order), bf16),
            pltpu.VMEM((order, wide_cols), bf16),
            pltpu.VMEM((wide_cols, order), bf16),
            pltpu.VMEM((order, wide_cols), f32),
            pltpu.VMEM((2, order, order), bf16),
            pltpu.VMEM((wide_cols, wide_cols), bf16),
            pltpu.VMEM((order, order), bf16),
            pltpu.VMEM((wide_cols, wide_cols), bf16),
            pltpu.SemaphoreType.DMA((5,)),
        ],
        compiler_params=pltpu.CompilerParams(vmem_limit_bytes=40 * 2**20),
        cost_estimate=pl.CostEstimate(
            flops=8 * 2 * order**3 * 2, bytes_accessed=8 * 2**20, transcendentals=order * order
        ),
        name="slot",
    )(dealing, rows, owners, cells, stock)


def pack_kernel(reach, own_rows, dealing, rows, term, out, padded):
    order = term.shape[0]
    first_row = rows[dealing[lax.axis_index("row")]]
    below = padded.shape[0] - reach - order
    padded[0:reach, :] = jnp.zeros((reach, padded.shape[1]), jnp.float32)
    padded[reach : reach + order, :] = term[...].astype(jnp.float32)
    padded[reach + order :, :] = jnp.zeros((below, padded.shape[1]), jnp.float32)

    @pl.loop(0, out.shape[0], unroll=2)
    def _(k):
        out[k] = rows_from(padded, reach - first_row + k * own_rows, out.shape[1]).astype(out.dtype)


def pack_rows(term, dealing, rows, slots, own_rows, tile_rows):
    order, width = term.shape
    reach = slots * own_rows - order
    return pl.pallas_call(
        functools.partial(pack_kernel, reach, own_rows),
        out_shape=jax.ShapeDtypeStruct((slots, tile_rows, width), jnp.bfloat16),
        in_specs=[SMEM, SMEM, VMEM],
        out_specs=VMEM,
        scratch_shapes=[pltpu.VMEM((2 * reach + order + tile_rows + SUBLANES, width), jnp.float32)],
        compiler_params=pltpu.CompilerParams(vmem_limit_bytes=16 * 2**20),
        cost_estimate=pl.CostEstimate(flops=0, bytes_accessed=3 * 2**20, transcendentals=0),
        name="pack",
    )(dealing, rows, term)


def place_kernel(order, dealing, cols, blocks, owners, terms, empty, out, totals, sems):
    del empty
    slots, tile_rows = terms.shape[0], terms.shape[1]
    count = (order + LANES) // LANES
    totals[...] = jnp.zeros_like(totals)
    lane = lax.broadcasted_iota(jnp.int32, (tile_rows, LANES), 1)
    nothing = jnp.zeros((tile_rows, LANES), jnp.float32)

    @pl.loop(0, slots, unroll=4)
    def _(slot):
        _, offset = window_start(cols[dealing[slot]], order, out.shape[2])
        shift = lax.rem(offset, LANES)
        for part in range(2):
            turned = []
            for b in range(count - 1):
                first = part * order + b * LANES
                turned.append(pltpu.roll(terms[slot, :, first : first + LANES], shift, 1).astype(jnp.float32))
            for b in range(count):
                before = turned[b - 1] if b else nothing
                after = turned[b] if b < count - 1 else nothing
                owner = owners[slot * count + b]
                totals[owner, part] += jnp.where(lane < offset, before, after)

    def copy(number):
        place = pl.multiple_of(blocks[number] * LANES, LANES)
        return pltpu.make_async_copy(totals.at[number], out.at[:, :, pl.ds(place, LANES)], sems.at[number])

    @pl.loop(0, slots * count)
    def _(number):
        @pl.when(owners[number] == number)
        def _():
            copy(number).start()

    @pl.loop(0, slots * count)
    def _(number):
        @pl.when(owners[number] == number)
        def _():
            copy(number).wait()


def place_windows(terms, empty, blocks, owners, dealing, cols, order):
    slots, tile_rows = terms.shape[0], terms.shape[1]
    count = (order + LANES) // LANES
    return pl.pallas_call(
        functools.partial(place_kernel, order),
        out_shape=jax.ShapeDtypeStruct(empty.shape, empty.dtype),
        in_specs=[SMEM, SMEM, SMEM, SMEM, VMEM, ANY],
        out_specs=ANY,
        scratch_shapes=[
            pltpu.VMEM((slots * count, 2, tile_rows, LANES), jnp.float32),
            pltpu.SemaphoreType.DMA((slots * count,)),
        ],
        input_output_aliases={5: 0},
        compiler_params=pltpu.CompilerParams(vmem_limit_bytes=24 * 2**20),
        cost_estimate=pl.CostEstimate(flops=0, bytes_accessed=6 * 2**20, transcendentals=0),
        name="place",
    )(dealing, cols, blocks, owners, terms, empty)


def strides(devices):
    steps, stride = [], 1
    while stride < devices:
        radix = 4 if len(steps) >= 2 and (devices // stride) % 4 == 0 else 2
        steps.append((stride, radix))
        stride *= radix
    return steps


def swap(x, distance, devices):
    return lax.ppermute(x, "row", [(d, d ^ distance) for d in range(devices)])


def sum_probe(kept, sent, devices):
    chips = devices // 2
    total = (kept + swap(sent, 1, devices).astype(jnp.float32)).astype(jnp.bfloat16)
    groups = [list(range(core, devices, 2)) for core in range(2)]
    count = total.shape[0] // chips
    shares = lax.all_to_all(
        total.reshape(chips, count, -1), "row", split_axis=0, concat_axis=0, tiled=True, axis_index_groups=groups
    )
    return jnp.sum(shares.astype(jnp.float32), axis=0)


def join(whole, devices):
    me = lax.axis_index("row")
    rows, width = whole.shape
    steps = strides(devices)
    axes = [*range(len(steps) - 1), 0]
    for axis, (stride, radix) in zip(axes, reversed(steps)):
        digit = me // stride % radix
        shares = [whole] + [swap(whole, k * stride, devices) for k in range(1, radix)]
        pieces = []
        for j in range(radix):
            piece = shares[0]
            for k in range(1, radix):
                piece = jnp.where(lax.bitwise_xor(digit, k) == j, shares[k], piece)
            pieces.append(piece)
        whole = jnp.stack(pieces, axis=axis)
    return whole.reshape(devices * rows, width)


def body(object_field, probe, amplitude, row_offsets, col_offsets, dealing):
    order = probe.shape[1]
    devices = lax.axis_size("row")
    own_rows, tile_cols = object_field.shape[1], object_field.shape[2]
    total_rows = devices * own_rows
    tile_rows = -(-own_rows // SUBLANES) * SUBLANES
    spare = tile_rows - own_rows
    if spare:
        object_field = jnp.pad(object_field, ((0, 0), (0, spare), (0, 0)))
    pieces, token = fetch_windows(object_field, dealing, col_offsets, order)
    strips = lax.all_to_all(pieces, "row", split_axis=0, concat_axis=0, tiled=True)
    cells = strips[:, :own_rows].reshape(total_rows, 2 * order)
    empty, blocks, owners, stock = prepare(
        dealing, col_offsets, token, probe, amplitude, object_field.shape
    )
    term, kept, sent = slot_terms(cells, stock, dealing, row_offsets, owners, order)
    total = sum_probe(kept, sent, devices)
    terms = pack_rows(term, dealing, row_offsets, devices, own_rows, tile_rows)
    terms, total = lax.optimization_barrier((terms, total))
    arrived = lax.all_to_all(terms, "row", split_axis=0, concat_axis=0, tiled=True)
    share = (total * (1.0 / dealing.shape[0])).astype(jnp.bfloat16)
    whole = join(share, devices).astype(jnp.float32)
    probe_grad = jnp.stack([whole[:, :order], whole[:, order:]])
    object_grad = place_windows(arrived, empty, blocks, owners, dealing, col_offsets, order)
    if spare:
        object_grad = object_grad[:, :own_rows]
    return (object_grad, probe_grad)


def solution(mesh):
    return jax.shard_map(
        body,
        mesh=mesh,
        in_specs=(
            P(None, ("groups", "row"), None),
            P("groups", None, None),
            P(("groups", "row"), None, None),
            P("groups"),
            P("groups"),
            P("groups"),
        ),
        out_specs=(P(None, ("groups", "row"), None), P("groups", None, None)),
        check_vma=False,
    )
```

```python
import functools
import math

import jax
import jax.numpy as jnp
import numpy as np
from jax import lax
from jax.experimental import pallas as pl
from jax.experimental.pallas import tpu as pltpu
from jax.sharding import PartitionSpec as P

MAG_FLOOR = 0.25
LANES = 128
SUBLANES = 8
SMEM = pl.BlockSpec(memory_space=pltpu.SMEM)
VMEM = pl.BlockSpec(memory_space=pltpu.VMEM)
ANY = pl.BlockSpec(memory_space=pl.ANY)


def dft_tables(order):
    indices = np.arange(order, dtype=np.int32)
    phases = indices[:, None] * indices[None, :] % order
    angles = phases.astype(np.float32) * np.float32(2.0 * math.pi / order)
    factor = np.float32(1.0 / math.sqrt(order))
    real_part = np.cos(angles) * factor
    imag_part = -np.sin(angles) * factor
    right_table = np.block([[real_part, imag_part], [-imag_part, real_part]])
    left_table = np.block([[real_part, -imag_part], [imag_part, real_part]])
    return right_table.astype(jnp.bfloat16), left_table.astype(jnp.bfloat16)


def window_start(column, order, tile_cols):
    span = order + LANES
    base = jnp.minimum(column // LANES, (tile_cols - span) // LANES) * LANES
    return pl.multiple_of(base, LANES), column - base


def rows_from(ref, start, count):
    aligned = pl.multiple_of(start // SUBLANES * SUBLANES, SUBLANES)
    rest = start - aligned
    width = ref.shape[-1]
    blocks = ref[pl.ds(aligned, count + SUBLANES), :].reshape(-1, SUBLANES, width)
    turned = pltpu.roll(blocks, lax.rem(SUBLANES - rest, SUBLANES), 1)
    sub = lax.broadcasted_iota(jnp.int32, (1, SUBLANES, width), 1)
    picked = jnp.where(sub < SUBLANES - rest, turned[:-1], turned[1:])
    return picked.reshape(count, width)


def fetch_kernel(order, dealing, cols, tile, out, token, held, sems):
    token[0] = dealing[0]
    slots, tile_rows = out.shape[0], out.shape[1]
    tile_cols = tile.shape[2]
    span = order + LANES

    def copy(slot):
        base, _ = window_start(cols[dealing[slot]], order, tile_cols)
        return pltpu.make_async_copy(tile.at[:, :, pl.ds(base, span)], held.at[slot], sems.at[slot])

    @pl.loop(0, slots)
    def _(slot):
        copy(slot).start()

    lane = lax.broadcasted_iota(jnp.int32, (tile_rows, LANES), 1)

    @pl.loop(0, slots, unroll=4)
    def _(slot):
        copy(slot).wait()
        _, offset = window_start(cols[dealing[slot]], order, tile_cols)
        shift = lax.rem(LANES - lax.rem(offset, LANES), LANES)
        for part in range(2):
            turned = [
                pltpu.roll(held[slot, part, :, b * LANES : (b + 1) * LANES].astype(out.dtype), shift, 1)
                for b in range(span // LANES)
            ]
            for b in range(order // LANES):
                first = part * order + b * LANES
                cells = jnp.where(lane < LANES - offset, turned[b], turned[b + 1])
                out[slot, :, first : first + LANES] = cells


def fetch_windows(tile, dealing, cols, order):
    slots, tile_rows, tile_cols = dealing.shape[0], tile.shape[1], tile.shape[2]
    span = order + LANES

    return pl.pallas_call(
        functools.partial(fetch_kernel, order),
        out_shape=(
            jax.ShapeDtypeStruct((slots, tile_rows, 2 * order), jnp.bfloat16),
            jax.ShapeDtypeStruct((1,), jnp.int32),
        ),
        in_specs=[SMEM, SMEM, ANY],
        out_specs=(VMEM, SMEM),
        scratch_shapes=[
            pltpu.VMEM((slots, 2, tile_rows, span), jnp.float32),
            pltpu.SemaphoreType.DMA((slots,)),
        ],
        compiler_params=pltpu.CompilerParams(vmem_limit_bytes=56 * 2**20),
        cost_estimate=pl.CostEstimate(flops=0, bytes_accessed=6 * 2**20, transcendentals=0),
        name="fetch",
    )(dealing, cols, tile)


def stock_places(stock, order):
    return (
        stock.at[0:order, 0:order],
        stock.at[0:order, order : 2 * order],
        stock.at[order : 3 * order, :],
        stock.at[3 * order : 4 * order, 0:order],
        stock.at[4 * order : 6 * order, :],
    )


def prepare_kernel(
    order, dealing, cols, token, right, left, probe, measured,
    empty, blocks, owners, stock,
    table, zeros, sems, stock_sems,
):
    del token
    places = stock_places(stock, order)
    sources = (probe.at[0], probe.at[1], right, measured.at[0], left)
    fills = []
    for k, (source, place) in enumerate(zip(sources, places)):
        fill = pltpu.make_async_copy(source, place, stock_sems.at[k])
        fill.start()
        fills.append(fill)
    count = (order + LANES) // LANES
    slots = dealing.shape[0]
    tile_cols = empty.shape[2]
    width = zeros.shape[2]
    zeros[...] = jnp.zeros_like(zeros)
    for b in range(tile_cols // width):
        fill = pltpu.make_async_copy(zeros, empty.at[:, :, b * width : (b + 1) * width], sems.at[b])
        fill.start()
        fills.append(fill)

    @pl.loop(0, tile_cols // LANES)
    def _(block):
        table[block] = -1

    @pl.loop(0, slots)
    def _(slot):
        base, _ = window_start(cols[dealing[slot]], order, tile_cols)
        for b in range(count):
            number = slot * count + b
            block = base // LANES + b
            blocks[number] = block
            known = table[block]
            owner = jnp.where(known < 0, number, known)
            owners[number] = owner
            table[block] = owner

    for fill in fills:
        fill.wait()


def prepare(dealing, cols, token, probe, measured, tile_shape):
    order = probe.shape[1]
    right, left = dft_tables(order)
    slots = dealing.shape[0]
    numbers = slots * (order + LANES) // LANES
    fill_cols = 2048
    return pl.pallas_call(
        functools.partial(prepare_kernel, order),
        out_shape=(
            jax.ShapeDtypeStruct(tile_shape, jnp.float32),
            jax.ShapeDtypeStruct((numbers,), jnp.int32),
            jax.ShapeDtypeStruct((numbers,), jnp.int32),
            jax.ShapeDtypeStruct((28 * order, 2 * order), jnp.bfloat16),
        ),
        in_specs=[SMEM, SMEM, SMEM, ANY, ANY, ANY, ANY],
        out_specs=(ANY, SMEM, SMEM, ANY),
        scratch_shapes=[
            pltpu.SMEM((tile_shape[2] // LANES,), jnp.int32),
            pltpu.VMEM(tile_shape[:2] + (fill_cols,), jnp.float32),
            pltpu.SemaphoreType.DMA((tile_shape[2] // fill_cols,)),
            pltpu.SemaphoreType.DMA((5,)),
        ],
        compiler_params=pltpu.CompilerParams(vmem_limit_bytes=8 * 2**20),
        cost_estimate=pl.CostEstimate(flops=0, bytes_accessed=110 * 2**20, transcendentals=0),
        name="prepare",
    )(dealing, cols, token, jnp.asarray(right), jnp.asarray(left), probe, measured)


def slot_kernel(
    dealing, rows, owners, cells, stock,
    term, kept, sent,
    wide, patch, wave, half, resid, turned, mine, probe, right, measured, left, sems,
):
    del owners
    order = term.shape[0]
    targets = (probe.at[0], probe.at[1], right, measured, left)
    loads = [
        pltpu.make_async_copy(source, target, sems.at[k])
        for k, (source, target) in enumerate(zip(stock_places(stock, order), targets))
    ]
    for load in loads:
        load.start()
    total_rows = cells.shape[0]
    me = lax.axis_index("row")
    first_row = rows[dealing[me]]
    step = 64
    tile = 256

    wide[0:total_rows, :] = cells[...].astype(jnp.float32)
    wide[total_rows:, :] = jnp.zeros((SUBLANES, 2 * order), jnp.float32)
    loads[0].wait()
    loads[1].wait()

    @pl.loop(0, order // step)
    def _(i):
        place = pl.ds(pl.multiple_of(i * step, step), step)
        found = rows_from(wide, first_row + i * step, step)
        patch[place, :] = found.astype(patch.dtype)
        real, imag = found[:, :order], found[:, order:]
        probe_real = probe[0, place, :].astype(jnp.float32)
        probe_imag = probe[1, place, :].astype(jnp.float32)
        wave[place, :order] = (probe_real * real - probe_imag * imag).astype(wave.dtype)
        wave[place, order:] = (probe_real * imag + probe_imag * real).astype(wave.dtype)

    def dot(a, b):
        return jnp.dot(a, b, preferred_element_type=jnp.float32)

    loads[2].wait()
    for first in range(0, order, tile):
        here = slice(first, first + tile)
        there = slice(order + first, order + first + tile)
        half[:order, here] = dot(wave[...], right[:, here]).astype(half.dtype)
        half[order:, here] = dot(wave[...], right[:, there]).astype(half.dtype)
    loads[3].wait()
    loads[4].wait()
    for first in range(0, order, tile):
        here = slice(first, first + tile)
        there = slice(order + first, order + first + tile)
        for top in range(0, order, tile):
            line = slice(top, top + tile)
            real = dot(left[line, :], half[:, here])
            imag = dot(left[order + top : order + top + tile, :], half[:, here])
            inverse = jnp.minimum(lax.rsqrt(real * real + imag * imag), 1.0 / MAG_FLOOR)
            shrink = 1.0 - measured[line, here].astype(jnp.float32) * inverse
            resid[line, here] = (real * shrink).astype(resid.dtype)
            resid[line, there] = (imag * shrink).astype(resid.dtype)
    for first in range(0, order, tile):
        here = slice(first, first + tile)
        there = slice(order + first, order + first + tile)
        turned[:order, here] = dot(resid[...], left[:, here]).astype(turned.dtype)
        turned[order:, here] = dot(resid[...], left[:, there]).astype(turned.dtype)
    for first in range(0, order, tile):
        here = slice(first, first + tile)
        there = slice(order + first, order + first + tile)
        for top in range(0, order, tile):
            line = slice(top, top + tile)
            real = dot(right[line, :], turned[:, here])
            imag = dot(right[order + top : order + top + tile, :], turned[:, here])
            probe_real = probe[0, line, here].astype(jnp.float32)
            probe_imag = probe[1, line, here].astype(jnp.float32)
            term[line, here] = (probe_real * real + probe_imag * imag).astype(term.dtype)
            term[line, there] = (probe_real * imag - probe_imag * real).astype(term.dtype)
            patch_real = patch[line, here].astype(jnp.float32)
            patch_imag = patch[line, there].astype(jnp.float32)
            mine[line, here] = patch_real * real + patch_imag * imag
            mine[line, there] = patch_real * imag - patch_imag * real

    count = kept.shape[0]
    side = lax.rem(me, 2)
    kept[...] = mine[pl.ds(pl.multiple_of(side * count, count), count), :]
    sent[...] = mine[pl.ds(pl.multiple_of((1 - side) * count, count), count), :].astype(sent.dtype)

def slot_terms(cells, stock, dealing, rows, owners, order):
    total_rows = cells.shape[0]
    wide_cols = 2 * order
    bf16, f32 = jnp.bfloat16, jnp.float32
    return pl.pallas_call(
        slot_kernel,
        out_shape=(
            jax.ShapeDtypeStruct((order, wide_cols), bf16),
            jax.ShapeDtypeStruct((order // 2, wide_cols), f32),
            jax.ShapeDtypeStruct((order // 2, wide_cols), bf16),
        ),
        in_specs=[SMEM, SMEM, SMEM, VMEM, ANY],
        out_specs=(VMEM,) * 3,
        scratch_shapes=[
            pltpu.VMEM((total_rows + SUBLANES, wide_cols), f32),
            pltpu.VMEM((order, wide_cols), bf16),
            pltpu.VMEM((order, wide_cols), bf16),
            pltpu.VMEM((wide_cols, order), bf16),
            pltpu.VMEM((order, wide_cols), bf16),
            pltpu.VMEM((wide_cols, order), bf16),
            pltpu.VMEM((order, wide_cols), f32),
            pltpu.VMEM((2, order, order), bf16),
            pltpu.VMEM((wide_cols, wide_cols), bf16),
            pltpu.VMEM((order, order), bf16),
            pltpu.VMEM((wide_cols, wide_cols), bf16),
            pltpu.SemaphoreType.DMA((5,)),
        ],
        compiler_params=pltpu.CompilerParams(vmem_limit_bytes=40 * 2**20),
        cost_estimate=pl.CostEstimate(
            flops=8 * 2 * order**3 * 2, bytes_accessed=8 * 2**20, transcendentals=order * order
        ),
        name="slot",
    )(dealing, rows, owners, cells, stock)


def pack_kernel(reach, own_rows, dealing, rows, term, out, padded):
    order = term.shape[0]
    first_row = rows[dealing[lax.axis_index("row")]]
    below = padded.shape[0] - reach - order
    padded[0:reach, :] = jnp.zeros((reach, padded.shape[1]), jnp.float32)
    padded[reach : reach + order, :] = term[...].astype(jnp.float32)
    padded[reach + order :, :] = jnp.zeros((below, padded.shape[1]), jnp.float32)

    @pl.loop(0, out.shape[0], unroll=2)
    def _(k):
        out[k] = rows_from(padded, reach - first_row + k * own_rows, out.shape[1]).astype(out.dtype)


def pack_rows(term, dealing, rows, slots, own_rows, tile_rows):
    order, width = term.shape
    reach = slots * own_rows - order
    return pl.pallas_call(
        functools.partial(pack_kernel, reach, own_rows),
        out_shape=jax.ShapeDtypeStruct((slots, tile_rows, width), jnp.bfloat16),
        in_specs=[SMEM, SMEM, VMEM],
        out_specs=VMEM,
        scratch_shapes=[pltpu.VMEM((2 * reach + order + tile_rows + SUBLANES, width), jnp.float32)],
        compiler_params=pltpu.CompilerParams(vmem_limit_bytes=16 * 2**20),
        cost_estimate=pl.CostEstimate(flops=0, bytes_accessed=3 * 2**20, transcendentals=0),
        name="pack",
    )(dealing, rows, term)


def place_kernel(order, dealing, cols, blocks, owners, terms, empty, out, totals, sems):
    del empty
    slots, tile_rows = terms.shape[0], terms.shape[1]
    count = (order + LANES) // LANES
    totals[...] = jnp.zeros_like(totals)
    lane = lax.broadcasted_iota(jnp.int32, (tile_rows, LANES), 1)
    nothing = jnp.zeros((tile_rows, LANES), jnp.float32)

    @pl.loop(0, slots, unroll=4)
    def _(slot):
        _, offset = window_start(cols[dealing[slot]], order, out.shape[2])
        shift = lax.rem(offset, LANES)
        for part in range(2):
            turned = []
            for b in range(count - 1):
                first = part * order + b * LANES
                turned.append(pltpu.roll(terms[slot, :, first : first + LANES], shift, 1).astype(jnp.float32))
            for b in range(count):
                before = turned[b - 1] if b else nothing
                after = turned[b] if b < count - 1 else nothing
                owner = owners[slot * count + b]
                totals[owner, part] += jnp.where(lane < offset, before, after)

    def copy(number):
        place = pl.multiple_of(blocks[number] * LANES, LANES)
        return pltpu.make_async_copy(totals.at[number], out.at[:, :, pl.ds(place, LANES)], sems.at[number])

    @pl.loop(0, slots * count)
    def _(number):
        @pl.when(owners[number] == number)
        def _():
            copy(number).start()

    @pl.loop(0, slots * count)
    def _(number):
        @pl.when(owners[number] == number)
        def _():
            copy(number).wait()


def place_windows(terms, empty, blocks, owners, dealing, cols, order):
    slots, tile_rows = terms.shape[0], terms.shape[1]
    count = (order + LANES) // LANES
    return pl.pallas_call(
        functools.partial(place_kernel, order),
        out_shape=jax.ShapeDtypeStruct(empty.shape, empty.dtype),
        in_specs=[SMEM, SMEM, SMEM, SMEM, VMEM, ANY],
        out_specs=ANY,
        scratch_shapes=[
            pltpu.VMEM((slots * count, 2, tile_rows, LANES), jnp.float32),
            pltpu.SemaphoreType.DMA((slots * count,)),
        ],
        input_output_aliases={5: 0},
        compiler_params=pltpu.CompilerParams(vmem_limit_bytes=24 * 2**20),
        cost_estimate=pl.CostEstimate(flops=0, bytes_accessed=6 * 2**20, transcendentals=0),
        name="place",
    )(dealing, cols, blocks, owners, terms, empty)


def strides(devices):
    steps, stride = [], 1
    while stride < devices:
        radix = 4 if len(steps) >= 2 and (devices // stride) % 4 == 0 else 2
        steps.append((stride, radix))
        stride *= radix
    return steps


def swap(x, distance, devices):
    return lax.ppermute(x, "row", [(d, d ^ distance) for d in range(devices)])


def sum_probe(kept, sent, devices):
    me = lax.axis_index("row")
    total = kept + swap(sent, 1, devices).astype(jnp.float32)
    for stride, radix in strides(devices)[1:]:
        digit = me // stride % radix
        count = total.shape[0] // radix
        own = lax.dynamic_slice_in_dim(total, digit * count, count)
        for k in range(1, radix):
            share = lax.dynamic_slice_in_dim(total, lax.bitwise_xor(digit, k) * count, count)
            own = own + swap(share.astype(jnp.bfloat16), k * stride, devices).astype(jnp.float32)
        total = own
    return total


def join(whole, devices):
    me = lax.axis_index("row")
    for stride, radix in reversed(strides(devices)):
        digit = me // stride % radix
        shares = [whole] + [swap(whole, k * stride, devices) for k in range(1, radix)]
        pieces = []
        for j in range(radix):
            piece = shares[0]
            for k in range(1, radix):
                piece = jnp.where(lax.bitwise_xor(digit, k) == j, shares[k], piece)
            pieces.append(piece)
        whole = jnp.concatenate(pieces, axis=0)
    return whole


def body(object_field, probe, amplitude, row_offsets, col_offsets, dealing):
    order = probe.shape[1]
    devices = lax.axis_size("row")
    own_rows, tile_cols = object_field.shape[1], object_field.shape[2]
    total_rows = devices * own_rows
    tile_rows = -(-own_rows // SUBLANES) * SUBLANES
    spare = tile_rows - own_rows
    if spare:
        object_field = jnp.pad(object_field, ((0, 0), (0, spare), (0, 0)))
    pieces, token = fetch_windows(object_field, dealing, col_offsets, order)
    strips = lax.all_to_all(pieces, "row", split_axis=0, concat_axis=0, tiled=True)
    cells = strips[:, :own_rows].reshape(total_rows, 2 * order)
    empty, blocks, owners, stock = prepare(
        dealing, col_offsets, token, probe, amplitude, object_field.shape
    )
    term, kept, sent = slot_terms(cells, stock, dealing, row_offsets, owners, order)
    total = sum_probe(kept, sent, devices)
    terms = pack_rows(term, dealing, row_offsets, devices, own_rows, tile_rows)
    terms, total = lax.optimization_barrier((terms, total))
    arrived = lax.all_to_all(terms, "row", split_axis=0, concat_axis=0, tiled=True)
    share = (total * (1.0 / dealing.shape[0])).astype(jnp.bfloat16)
    whole = join(share, devices).astype(jnp.float32)
    probe_grad = jnp.stack([whole[:, :order], whole[:, order:]])
    object_grad = place_windows(arrived, empty, blocks, owners, dealing, col_offsets, order)
    if spare:
        object_grad = object_grad[:, :own_rows]
    return (object_grad, probe_grad)


def solution(mesh):
    return jax.shard_map(
        body,
        mesh=mesh,
        in_specs=(
            P(None, ("groups", "row"), None),
            P("groups", None, None),
            P(("groups", "row"), None, None),
            P("groups"),
            P("groups"),
            P("groups"),
        ),
        out_specs=(P(None, ("groups", "row"), None), P("groups", None, None)),
        check_vma=False,
    )
```

```python
import functools
import math

import jax
import jax.numpy as jnp
import numpy as np
from jax import lax
from jax.experimental import pallas as pl
from jax.experimental.pallas import tpu as pltpu
from jax.sharding import PartitionSpec as P

MAG_FLOOR = 0.25
LANES = 128
SUBLANES = 8
SMEM = pl.BlockSpec(memory_space=pltpu.SMEM)
VMEM = pl.BlockSpec(memory_space=pltpu.VMEM)
ANY = pl.BlockSpec(memory_space=pl.ANY)


def dft_tables(order):
    indices = np.arange(order, dtype=np.int32)
    phases = indices[:, None] * indices[None, :] % order
    angles = phases.astype(np.float32) * np.float32(2.0 * math.pi / order)
    factor = np.float32(1.0 / math.sqrt(order))
    real_part = np.cos(angles) * factor
    imag_part = -np.sin(angles) * factor
    right_table = np.block([[real_part, imag_part], [-imag_part, real_part]])
    left_table = np.block([[real_part, -imag_part], [imag_part, real_part]])
    return right_table.astype(jnp.bfloat16), left_table.astype(jnp.bfloat16)


def window_start(column, order, tile_cols):
    span = order + LANES
    base = jnp.minimum(column // LANES, (tile_cols - span) // LANES) * LANES
    return pl.multiple_of(base, LANES), column - base


def rows_from(ref, start, count):
    aligned = pl.multiple_of(start // SUBLANES * SUBLANES, SUBLANES)
    rest = start - aligned
    width = ref.shape[-1]
    blocks = ref[pl.ds(aligned, count + SUBLANES), :].reshape(-1, SUBLANES, width)
    turned = pltpu.roll(blocks, lax.rem(SUBLANES - rest, SUBLANES), 1)
    sub = lax.broadcasted_iota(jnp.int32, (1, SUBLANES, width), 1)
    picked = jnp.where(sub < SUBLANES - rest, turned[:-1], turned[1:])
    return picked.reshape(count, width)


def fetch_kernel(order, dealing, cols, tile, out, token, held, cut, sems, out_sems):
    token[0] = dealing[0]
    slots, tile_rows = out.shape[0], out.shape[1]
    tile_cols = tile.shape[2]
    span = order + LANES

    def copy(slot):
        base, _ = window_start(cols[dealing[slot]], order, tile_cols)
        return pltpu.make_async_copy(tile.at[:, :, pl.ds(base, span)], held.at[slot], sems.at[slot])

    @pl.loop(0, slots)
    def _(slot):
        copy(slot).start()

    lane = lax.broadcasted_iota(jnp.int32, (tile_rows, LANES), 1)

    def send(slot):
        return pltpu.make_async_copy(cut.at[slot], out.at[slot], out_sems.at[slot])

    @pl.loop(0, slots, unroll=4)
    def _(slot):
        copy(slot).wait()
        _, offset = window_start(cols[dealing[slot]], order, tile_cols)
        shift = lax.rem(LANES - lax.rem(offset, LANES), LANES)
        for part in range(2):
            turned = [
                pltpu.roll(held[slot, part, :, b * LANES : (b + 1) * LANES].astype(out.dtype), shift, 1)
                for b in range(span // LANES)
            ]
            for b in range(order // LANES):
                first = part * order + b * LANES
                cells = jnp.where(lane < LANES - offset, turned[b], turned[b + 1])
                cut[slot, :, first : first + LANES] = cells
        send(slot).start()

    @pl.loop(0, slots)
    def _(slot):
        send(slot).wait()


def fetch_windows(tile, dealing, cols, order):
    slots, tile_rows, tile_cols = dealing.shape[0], tile.shape[1], tile.shape[2]
    span = order + LANES

    return pl.pallas_call(
        functools.partial(fetch_kernel, order),
        out_shape=(
            jax.ShapeDtypeStruct((slots, tile_rows, 2 * order), jnp.bfloat16),
            jax.ShapeDtypeStruct((1,), jnp.int32),
        ),
        in_specs=[SMEM, SMEM, ANY],
        out_specs=(ANY, SMEM),
        scratch_shapes=[
            pltpu.VMEM((slots, 2, tile_rows, span), jnp.float32),
            pltpu.VMEM((slots, tile_rows, 2 * order), jnp.bfloat16),
            pltpu.SemaphoreType.DMA((slots,)),
            pltpu.SemaphoreType.DMA((slots,)),
        ],
        compiler_params=pltpu.CompilerParams(vmem_limit_bytes=56 * 2**20),
        cost_estimate=pl.CostEstimate(flops=0, bytes_accessed=6 * 2**20, transcendentals=0),
        name="fetch",
    )(dealing, cols, tile)


def stock_places(stock, order):
    return (
        stock.at[0:order, 0:order],
        stock.at[0:order, order : 2 * order],
        stock.at[order : 3 * order, :],
        stock.at[3 * order : 4 * order, 0:order],
        stock.at[4 * order : 6 * order, :],
    )


def prepare_kernel(
    order, dealing, cols, token, right, left, probe, measured,
    empty, blocks, owners, single, stock,
    table, shared, zeros, sems, stock_sems,
):
    del token
    places = stock_places(stock, order)
    sources = (probe.at[0], probe.at[1], right, measured.at[0], left)
    fills = []
    for k, (source, place) in enumerate(zip(sources, places)):
        fill = pltpu.make_async_copy(source, place, stock_sems.at[k])
        fill.start()
        fills.append(fill)
    count = (order + LANES) // LANES
    slots = dealing.shape[0]
    tile_cols = empty.shape[2]
    width = zeros.shape[2]
    zeros[...] = jnp.zeros_like(zeros)
    for b in range(tile_cols // width):
        fill = pltpu.make_async_copy(zeros, empty.at[:, :, b * width : (b + 1) * width], sems.at[b])
        fill.start()
        fills.append(fill)

    @pl.loop(0, tile_cols // LANES)
    def _(block):
        table[block] = -1

    @pl.loop(0, slots)
    def _(slot):
        base, _ = window_start(cols[dealing[slot]], order, tile_cols)
        for b in range(count):
            number = slot * count + b
            block = base // LANES + b
            blocks[number] = block
            known = table[block]
            owner = jnp.where(known < 0, number, known)
            owners[number] = owner
            table[block] = owner
            shared[number] = jnp.where(known < 0, 0, 1)
            shared[owner] = jnp.where(known < 0, 0, 1)

    @pl.loop(0, slots)
    def _(slot):
        total = shared[slot * count]
        for b in range(1, count):
            total += shared[slot * count + b]
        single[slot] = jnp.where(total == 0, 1, 0)

    for fill in fills:
        fill.wait()


def prepare(dealing, cols, token, probe, measured, tile_shape):
    order = probe.shape[1]
    right, left = dft_tables(order)
    slots = dealing.shape[0]
    numbers = slots * (order + LANES) // LANES
    fill_cols = 2048
    return pl.pallas_call(
        functools.partial(prepare_kernel, order),
        out_shape=(
            jax.ShapeDtypeStruct(tile_shape, jnp.float32),
            jax.ShapeDtypeStruct((numbers,), jnp.int32),
            jax.ShapeDtypeStruct((numbers,), jnp.int32),
            jax.ShapeDtypeStruct((slots,), jnp.int32),
            jax.ShapeDtypeStruct((28 * order, 2 * order), jnp.bfloat16),
        ),
        in_specs=[SMEM, SMEM, SMEM, ANY, ANY, ANY, ANY],
        out_specs=(ANY, SMEM, SMEM, SMEM, ANY),
        scratch_shapes=[
            pltpu.SMEM((tile_shape[2] // LANES,), jnp.int32),
            pltpu.SMEM((numbers,), jnp.int32),
            pltpu.VMEM(tile_shape[:2] + (fill_cols,), jnp.float32),
            pltpu.SemaphoreType.DMA((tile_shape[2] // fill_cols,)),
            pltpu.SemaphoreType.DMA((5,)),
        ],
        compiler_params=pltpu.CompilerParams(vmem_limit_bytes=8 * 2**20),
        cost_estimate=pl.CostEstimate(flops=0, bytes_accessed=110 * 2**20, transcendentals=0),
        name="prepare",
    )(dealing, cols, token, jnp.asarray(right), jnp.asarray(left), probe, measured)


def slot_kernel(
    dealing, rows, owners, cells, stock,
    term, kept, sent,
    wide, patch, wave, half, resid, turned, mine, probe, right, measured, left, sems,
):
    del owners
    order = term.shape[0]
    targets = (probe.at[0], probe.at[1], right, measured, left)
    loads = [
        pltpu.make_async_copy(source, target, sems.at[k])
        for k, (source, target) in enumerate(zip(stock_places(stock, order), targets))
    ]
    for load in loads:
        load.start()
    total_rows = cells.shape[0]
    me = lax.axis_index("row")
    first_row = rows[dealing[me]]
    step = 64
    tile = 256

    wide[0:total_rows, :] = cells[...].astype(jnp.float32)
    wide[total_rows:, :] = jnp.zeros((SUBLANES, 2 * order), jnp.float32)
    loads[0].wait()
    loads[1].wait()
    loads[2].wait()

    def dot(a, b):
        return jnp.dot(a, b, preferred_element_type=jnp.float32)

    for top in range(0, order, tile):
        for start in range(top, top + tile, step):
            line = slice(start, start + step)
            found = rows_from(wide, first_row + start, step)
            patch[line, :] = found.astype(patch.dtype)
            real, imag = found[:, :order], found[:, order:]
            probe_real = probe[0, line, :].astype(jnp.float32)
            probe_imag = probe[1, line, :].astype(jnp.float32)
            wave[line, :order] = (probe_real * real - probe_imag * imag).astype(wave.dtype)
            wave[line, order:] = (probe_real * imag + probe_imag * real).astype(wave.dtype)
        line = slice(top, top + tile)
        for first in range(0, order, tile):
            here = slice(first, first + tile)
            there = slice(order + first, order + first + tile)
            half[line, here] = dot(wave[line, :], right[:, here]).astype(half.dtype)
            half[order + top : order + top + tile, here] = dot(wave[line, :], right[:, there]).astype(half.dtype)
    loads[3].wait()
    loads[4].wait()
    for first in range(0, order, tile):
        here = slice(first, first + tile)
        there = slice(order + first, order + first + tile)
        for top in range(0, order, tile):
            line = slice(top, top + tile)
            real = dot(left[line, :], half[:, here])
            imag = dot(left[order + top : order + top + tile, :], half[:, here])
            inverse = jnp.minimum(lax.rsqrt(real * real + imag * imag), 1.0 / MAG_FLOOR)
            shrink = 1.0 - measured[line, here].astype(jnp.float32) * inverse
            resid[line, here] = (real * shrink).astype(resid.dtype)
            resid[line, there] = (imag * shrink).astype(resid.dtype)
    for first in range(0, order, tile):
        here = slice(first, first + tile)
        there = slice(order + first, order + first + tile)
        turned[:order, here] = dot(resid[...], left[:, here]).astype(turned.dtype)
        turned[order:, here] = dot(resid[...], left[:, there]).astype(turned.dtype)
    for first in range(0, order, tile):
        here = slice(first, first + tile)
        there = slice(order + first, order + first + tile)
        for top in range(0, order, tile):
            line = slice(top, top + tile)
            real = dot(right[line, :], turned[:, here])
            imag = dot(right[order + top : order + top + tile, :], turned[:, here])
            probe_real = probe[0, line, here].astype(jnp.float32)
            probe_imag = probe[1, line, here].astype(jnp.float32)
            term[line, here] = (probe_real * real + probe_imag * imag).astype(term.dtype)
            term[line, there] = (probe_real * imag - probe_imag * real).astype(term.dtype)
            patch_real = patch[line, here].astype(jnp.float32)
            patch_imag = patch[line, there].astype(jnp.float32)
            mine[line, here] = patch_real * real + patch_imag * imag
            mine[line, there] = patch_real * imag - patch_imag * real

    count = kept.shape[0]
    side = lax.rem(me, 2)
    kept[...] = mine[pl.ds(pl.multiple_of(side * count, count), count), :]
    sent[...] = mine[pl.ds(pl.multiple_of((1 - side) * count, count), count), :].astype(sent.dtype)

def slot_terms(cells, stock, dealing, rows, owners, order):
    total_rows = cells.shape[0]
    wide_cols = 2 * order
    bf16, f32 = jnp.bfloat16, jnp.float32
    return pl.pallas_call(
        slot_kernel,
        out_shape=(
            jax.ShapeDtypeStruct((order, wide_cols), bf16),
            jax.ShapeDtypeStruct((order // 2, wide_cols), f32),
            jax.ShapeDtypeStruct((order // 2, wide_cols), bf16),
        ),
        in_specs=[SMEM, SMEM, SMEM, VMEM, ANY],
        out_specs=(VMEM,) * 3,
        scratch_shapes=[
            pltpu.VMEM((total_rows + SUBLANES, wide_cols), f32),
            pltpu.VMEM((order, wide_cols), bf16),
            pltpu.VMEM((order, wide_cols), bf16),
            pltpu.VMEM((wide_cols, order), bf16),
            pltpu.VMEM((order, wide_cols), bf16),
            pltpu.VMEM((wide_cols, order), bf16),
            pltpu.VMEM((order, wide_cols), f32),
            pltpu.VMEM((2, order, order), bf16),
            pltpu.VMEM((wide_cols, wide_cols), bf16),
            pltpu.VMEM((order, order), bf16),
            pltpu.VMEM((wide_cols, wide_cols), bf16),
            pltpu.SemaphoreType.DMA((5,)),
        ],
        compiler_params=pltpu.CompilerParams(vmem_limit_bytes=40 * 2**20),
        cost_estimate=pl.CostEstimate(
            flops=8 * 2 * order**3 * 2, bytes_accessed=8 * 2**20, transcendentals=order * order
        ),
        name="slot",
    )(dealing, rows, owners, cells, stock)


def pack_kernel(reach, own_rows, dealing, rows, term, out, padded):
    order = term.shape[0]
    first_row = rows[dealing[lax.axis_index("row")]]
    below = padded.shape[0] - reach - order
    padded[0:reach, :] = jnp.zeros((reach, padded.shape[1]), jnp.float32)
    padded[reach : reach + order, :] = term[...].astype(jnp.float32)
    padded[reach + order :, :] = jnp.zeros((below, padded.shape[1]), jnp.float32)

    @pl.loop(0, out.shape[0], unroll=2)
    def _(k):
        out[k] = rows_from(padded, reach - first_row + k * own_rows, out.shape[1]).astype(out.dtype)


def pack_rows(term, dealing, rows, slots, own_rows, tile_rows):
    order, width = term.shape
    reach = slots * own_rows - order
    return pl.pallas_call(
        functools.partial(pack_kernel, reach, own_rows),
        out_shape=jax.ShapeDtypeStruct((slots, tile_rows, width), jnp.bfloat16),
        in_specs=[SMEM, SMEM, VMEM],
        out_specs=VMEM,
        scratch_shapes=[pltpu.VMEM((2 * reach + order + tile_rows + SUBLANES, width), jnp.float32)],
        compiler_params=pltpu.CompilerParams(vmem_limit_bytes=16 * 2**20),
        cost_estimate=pl.CostEstimate(flops=0, bytes_accessed=3 * 2**20, transcendentals=0),
        name="pack",
    )(dealing, rows, term)


def place_kernel(order, dealing, cols, blocks, owners, single, terms, empty, out, totals, sems):
    del empty
    slots, tile_rows = terms.shape[0], terms.shape[1]
    count = (order + LANES) // LANES
    lane = lax.broadcasted_iota(jnp.int32, (tile_rows, LANES), 1)
    nothing = jnp.zeros((tile_rows, LANES), jnp.float32)

    def whole(slot):
        place = pl.multiple_of(blocks[slot * count] * LANES, LANES)
        window = out.at[:, :, pl.ds(place, count * LANES)]
        return pltpu.make_async_copy(totals.at[slot], window, sems.at[slot * count])

    def part_of(slot, b):
        number = slot * count + b
        place = pl.multiple_of(blocks[number] * LANES, LANES)
        held = totals.at[slot, :, :, b * LANES : (b + 1) * LANES]
        return pltpu.make_async_copy(held, out.at[:, :, pl.ds(place, LANES)], sems.at[number])

    def add(slot):
        _, offset = window_start(cols[dealing[slot]], order, out.shape[2])
        shift = lax.rem(offset, LANES)
        for part in range(2):
            turned = []
            for b in range(count - 1):
                first = part * order + b * LANES
                turned.append(pltpu.roll(terms[slot, :, first : first + LANES], shift, 1).astype(jnp.float32))
            for b in range(count):
                before = turned[b - 1] if b else nothing
                after = turned[b] if b < count - 1 else nothing
                term = jnp.where(lane < offset, before, after)
                owner = owners[slot * count + b]
                holder = lax.div(owner, count)
                here = pl.ds(pl.multiple_of((owner - holder * count) * LANES, LANES), LANES)
                held = totals[holder, part, :, here]
                totals[holder, part, :, here] = jnp.where(owner == slot * count + b, term, held + term)

    half = slots // 2
    for low, high in ((0, half), (half, slots)):

        @pl.loop(low, high, unroll=4)
        def _(slot):
            add(slot)

        @pl.loop(low, high)
        def _(slot):
            @pl.when(single[slot] == 1)
            def _():
                whole(slot).start()

    def finish(slot, act):
        @pl.when(single[slot] == 0)
        def _():
            for b in range(count):

                @pl.when(owners[slot * count + b] == slot * count + b)
                def _():
                    act(part_of(slot, b))

    @pl.loop(0, slots)
    def _(slot):
        finish(slot, lambda copy: copy.start())

    @pl.loop(0, slots)
    def _(slot):
        @pl.when(single[slot] == 1)
        def _():
            whole(slot).wait()

        finish(slot, lambda copy: copy.wait())


def place_windows(terms, empty, blocks, owners, single, dealing, cols, order):
    slots, tile_rows = terms.shape[0], terms.shape[1]
    count = (order + LANES) // LANES
    return pl.pallas_call(
        functools.partial(place_kernel, order),
        out_shape=jax.ShapeDtypeStruct(empty.shape, empty.dtype),
        in_specs=[SMEM, SMEM, SMEM, SMEM, SMEM, VMEM, ANY],
        out_specs=ANY,
        scratch_shapes=[
            pltpu.VMEM((slots, 2, tile_rows, count * LANES), jnp.float32),
            pltpu.SemaphoreType.DMA((slots * count,)),
        ],
        input_output_aliases={6: 0},
        compiler_params=pltpu.CompilerParams(vmem_limit_bytes=24 * 2**20),
        cost_estimate=pl.CostEstimate(flops=0, bytes_accessed=6 * 2**20, transcendentals=0),
        name="place",
    )(dealing, cols, blocks, owners, single, terms, empty)


def strides(devices):
    steps, stride = [], 1
    while stride < devices:
        radix = 4 if len(steps) >= 2 and (devices // stride) % 4 == 0 else 2
        steps.append((stride, radix))
        stride *= radix
    return steps


def swap(x, distance, devices):
    return lax.ppermute(x, "row", [(d, d ^ distance) for d in range(devices)])


def sum_probe(kept, sent, devices):
    me = lax.axis_index("row")
    total = kept + swap(sent, 1, devices).astype(jnp.float32)
    for stride, radix in strides(devices)[1:]:
        digit = me // stride % radix
        count = total.shape[0] // radix
        own = lax.dynamic_slice_in_dim(total, digit * count, count)
        for k in range(1, radix):
            share = lax.dynamic_slice_in_dim(total, lax.bitwise_xor(digit, k) * count, count)
            own = own + swap(share.astype(jnp.bfloat16), k * stride, devices).astype(jnp.float32)
        total = own
    return total


def join(whole, devices):
    me = lax.axis_index("row")
    for stride, radix in reversed(strides(devices)):
        digit = me // stride % radix
        shares = [whole] + [swap(whole, k * stride, devices) for k in range(1, radix)]
        pieces = []
        for j in range(radix):
            piece = shares[0]
            for k in range(1, radix):
                piece = jnp.where(lax.bitwise_xor(digit, k) == j, shares[k], piece)
            pieces.append(piece)
        whole = jnp.concatenate(pieces, axis=0)
    return whole


def body(object_field, probe, amplitude, row_offsets, col_offsets, dealing):
    order = probe.shape[1]
    devices = lax.axis_size("row")
    own_rows, tile_cols = object_field.shape[1], object_field.shape[2]
    total_rows = devices * own_rows
    tile_rows = -(-own_rows // SUBLANES) * SUBLANES
    spare = tile_rows - own_rows
    if spare:
        object_field = jnp.pad(object_field, ((0, 0), (0, spare), (0, 0)))
    pieces, token = fetch_windows(object_field, dealing, col_offsets, order)
    strips = lax.all_to_all(pieces, "row", split_axis=0, concat_axis=0, tiled=True)
    cells = strips[:, :own_rows].reshape(total_rows, 2 * order)
    empty, blocks, owners, single, stock = prepare(
        dealing, col_offsets, token, probe, amplitude, object_field.shape
    )
    term, kept, sent = slot_terms(cells, stock, dealing, row_offsets, owners, order)
    total = sum_probe(kept, sent, devices)
    terms = pack_rows(term, dealing, row_offsets, devices, own_rows, tile_rows)
    terms, total = lax.optimization_barrier((terms, total))
    arrived = lax.all_to_all(terms, "row", split_axis=0, concat_axis=0, tiled=True)
    share = (total * (1.0 / dealing.shape[0])).astype(jnp.bfloat16)
    whole = join(share, devices).astype(jnp.float32)
    probe_grad = jnp.stack([whole[:, :order], whole[:, order:]])
    object_grad = place_windows(arrived, empty, blocks, owners, single, dealing, col_offsets, order)
    if spare:
        object_grad = object_grad[:, :own_rows]
    return (object_grad, probe_grad)


def solution(mesh):
    return jax.shard_map(
        body,
        mesh=mesh,
        in_specs=(
            P(None, ("groups", "row"), None),
            P("groups", None, None),
            P(("groups", "row"), None, None),
            P("groups"),
            P("groups"),
            P("groups"),
        ),
        out_specs=(P(None, ("groups", "row"), None), P("groups", None, None)),
        check_vma=False,
    )
```

```python
import functools
import math

import jax
import jax.numpy as jnp
import numpy as np
from jax import lax
from jax.experimental import pallas as pl
from jax.experimental.pallas import tpu as pltpu
from jax.sharding import PartitionSpec as P

MAG_FLOOR = 0.25
LANES = 128
SUBLANES = 8
SMEM = pl.BlockSpec(memory_space=pltpu.SMEM)
VMEM = pl.BlockSpec(memory_space=pltpu.VMEM)
ANY = pl.BlockSpec(memory_space=pl.ANY)


def dft_tables(order):
    indices = np.arange(order, dtype=np.int32)
    phases = indices[:, None] * indices[None, :] % order
    angles = phases.astype(np.float32) * np.float32(2.0 * math.pi / order)
    factor = np.float32(1.0 / math.sqrt(order))
    real_part = np.cos(angles) * factor
    imag_part = -np.sin(angles) * factor
    right_table = np.block([[real_part, imag_part], [-imag_part, real_part]])
    left_table = np.block([[real_part, -imag_part], [imag_part, real_part]])
    return right_table.astype(jnp.bfloat16), left_table.astype(jnp.bfloat16)


def window_start(column, order, tile_cols):
    span = order + LANES
    base = jnp.minimum(column // LANES, (tile_cols - span) // LANES) * LANES
    return pl.multiple_of(base, LANES), column - base


def rows_from(ref, start, count):
    aligned = pl.multiple_of(start // SUBLANES * SUBLANES, SUBLANES)
    rest = start - aligned
    width = ref.shape[-1]
    blocks = ref[pl.ds(aligned, count + SUBLANES), :].reshape(-1, SUBLANES, width)
    turned = pltpu.roll(blocks, lax.rem(SUBLANES - rest, SUBLANES), 1)
    sub = lax.broadcasted_iota(jnp.int32, (1, SUBLANES, width), 1)
    picked = jnp.where(sub < SUBLANES - rest, turned[:-1], turned[1:])
    return picked.reshape(count, width)


def fetch_kernel(order, dealing, cols, tile, out, token, held, cut, sems, out_sems):
    token[0] = dealing[0]
    slots, tile_rows = out.shape[0], out.shape[1]
    tile_cols = tile.shape[2]
    span = order + LANES

    def copy(slot, part):
        base, _ = window_start(cols[dealing[slot]], order, tile_cols)
        return pltpu.make_async_copy(
            tile.at[part, :, pl.ds(base, span)], held.at[slot, part], sems.at[slot, part]
        )

    @pl.loop(0, slots)
    def _(slot):
        copy(slot, 0).start()
        copy(slot, 1).start()

    lane = lax.broadcasted_iota(jnp.int32, (tile_rows, LANES), 1)

    def send(slot):
        return pltpu.make_async_copy(cut.at[slot], out.at[slot], out_sems.at[slot])

    @pl.loop(0, slots, unroll=4)
    def _(slot):
        _, offset = window_start(cols[dealing[slot]], order, tile_cols)
        shift = lax.rem(LANES - lax.rem(offset, LANES), LANES)
        for part in range(2):
            copy(slot, part).wait()
            turned = [
                pltpu.roll(held[slot, part, :, b * LANES : (b + 1) * LANES].astype(out.dtype), shift, 1)
                for b in range(span // LANES)
            ]
            for b in range(order // LANES):
                first = part * order + b * LANES
                cells = jnp.where(lane < LANES - offset, turned[b], turned[b + 1])
                cut[slot, :, first : first + LANES] = cells
        send(slot).start()

    @pl.loop(0, slots)
    def _(slot):
        send(slot).wait()


def fetch_windows(tile, dealing, cols, order):
    slots, tile_rows, tile_cols = dealing.shape[0], tile.shape[1], tile.shape[2]
    span = order + LANES

    return pl.pallas_call(
        functools.partial(fetch_kernel, order),
        out_shape=(
            jax.ShapeDtypeStruct((slots, tile_rows, 2 * order), jnp.bfloat16),
            jax.ShapeDtypeStruct((1,), jnp.int32),
        ),
        in_specs=[SMEM, SMEM, ANY],
        out_specs=(ANY, SMEM),
        scratch_shapes=[
            pltpu.VMEM((slots, 2, tile_rows, span), jnp.float32),
            pltpu.VMEM((slots, tile_rows, 2 * order), jnp.bfloat16),
            pltpu.SemaphoreType.DMA((slots, 2)),
            pltpu.SemaphoreType.DMA((slots,)),
        ],
        compiler_params=pltpu.CompilerParams(vmem_limit_bytes=56 * 2**20),
        cost_estimate=pl.CostEstimate(flops=0, bytes_accessed=6 * 2**20, transcendentals=0),
        name="fetch",
    )(dealing, cols, tile)


def stock_places(stock, order):
    return (
        stock.at[0:order, 0:order],
        stock.at[0:order, order : 2 * order],
        stock.at[order : 3 * order, :],
        stock.at[3 * order : 4 * order, 0:order],
        stock.at[4 * order : 6 * order, :],
    )


def prepare_kernel(
    order, dealing, cols, token, right, left, probe, measured,
    empty, blocks, owners, single, stock,
    table, shared, zeros, sems, stock_sems,
):
    del token
    places = stock_places(stock, order)
    sources = (probe.at[0], probe.at[1], right, measured.at[0], left)
    fills = []
    for k, (source, place) in enumerate(zip(sources, places)):
        fill = pltpu.make_async_copy(source, place, stock_sems.at[k])
        fill.start()
        fills.append(fill)
    count = (order + LANES) // LANES
    slots = dealing.shape[0]
    tile_cols = empty.shape[2]
    width = zeros.shape[2]
    zeros[...] = jnp.zeros_like(zeros)
    for b in range(tile_cols // width):
        fill = pltpu.make_async_copy(zeros, empty.at[:, :, b * width : (b + 1) * width], sems.at[b])
        fill.start()
        fills.append(fill)

    @pl.loop(0, tile_cols // LANES)
    def _(block):
        table[block] = -1

    @pl.loop(0, slots)
    def _(slot):
        base, _ = window_start(cols[dealing[slot]], order, tile_cols)
        for b in range(count):
            number = slot * count + b
            block = base // LANES + b
            blocks[number] = block
            known = table[block]
            owner = jnp.where(known < 0, number, known)
            owners[number] = owner
            table[block] = owner
            shared[number] = jnp.where(known < 0, 0, 1)
            shared[owner] = jnp.where(known < 0, 0, 1)

    @pl.loop(0, slots)
    def _(slot):
        total = shared[slot * count]
        for b in range(1, count):
            total += shared[slot * count + b]
        single[slot] = jnp.where(total == 0, 1, 0)

    for fill in fills:
        fill.wait()


def prepare(dealing, cols, token, probe, measured, tile_shape):
    order = probe.shape[1]
    right, left = dft_tables(order)
    slots = dealing.shape[0]
    numbers = slots * (order + LANES) // LANES
    fill_cols = 2048
    return pl.pallas_call(
        functools.partial(prepare_kernel, order),
        out_shape=(
            jax.ShapeDtypeStruct(tile_shape, jnp.float32),
            jax.ShapeDtypeStruct((numbers,), jnp.int32),
            jax.ShapeDtypeStruct((numbers,), jnp.int32),
            jax.ShapeDtypeStruct((slots,), jnp.int32),
            jax.ShapeDtypeStruct((28 * order, 2 * order), jnp.bfloat16),
        ),
        in_specs=[SMEM, SMEM, SMEM, ANY, ANY, ANY, ANY],
        out_specs=(ANY, SMEM, SMEM, SMEM, ANY),
        scratch_shapes=[
            pltpu.SMEM((tile_shape[2] // LANES,), jnp.int32),
            pltpu.SMEM((numbers,), jnp.int32),
            pltpu.VMEM(tile_shape[:2] + (fill_cols,), jnp.float32),
            pltpu.SemaphoreType.DMA((tile_shape[2] // fill_cols,)),
            pltpu.SemaphoreType.DMA((5,)),
        ],
        compiler_params=pltpu.CompilerParams(vmem_limit_bytes=8 * 2**20),
        cost_estimate=pl.CostEstimate(flops=0, bytes_accessed=110 * 2**20, transcendentals=0),
        name="prepare",
    )(dealing, cols, token, jnp.asarray(right), jnp.asarray(left), probe, measured)


def slot_kernel(
    dealing, rows, owners, cells, stock,
    term, kept, sent,
    wide, patch, wave, half, resid, turned, mine, probe, right, measured, left, sems,
):
    del owners
    order = term.shape[0]
    targets = (probe.at[0], probe.at[1], right, measured, left)
    loads = [
        pltpu.make_async_copy(source, target, sems.at[k])
        for k, (source, target) in enumerate(zip(stock_places(stock, order), targets))
    ]
    for load in loads:
        load.start()
    total_rows = cells.shape[0]
    me = lax.axis_index("row")
    first_row = rows[dealing[me]]
    step = 64
    tile = 256

    wide[0:total_rows, :] = cells[...].astype(jnp.float32)
    wide[total_rows:, :] = jnp.zeros((SUBLANES, 2 * order), jnp.float32)
    loads[0].wait()
    loads[1].wait()

    @pl.loop(0, order // step)
    def _(i):
        place = pl.ds(pl.multiple_of(i * step, step), step)
        found = rows_from(wide, first_row + i * step, step)
        patch[place, :] = found.astype(patch.dtype)
        real, imag = found[:, :order], found[:, order:]
        probe_real = probe[0, place, :].astype(jnp.float32)
        probe_imag = probe[1, place, :].astype(jnp.float32)
        wave[place, :order] = (probe_real * real - probe_imag * imag).astype(wave.dtype)
        wave[place, order:] = (probe_real * imag + probe_imag * real).astype(wave.dtype)

    def dot(a, b):
        return jnp.dot(a, b, preferred_element_type=jnp.float32)

    loads[2].wait()
    for first in range(0, order, tile):
        here = slice(first, first + tile)
        there = slice(order + first, order + first + tile)
        half[:order, here] = dot(wave[...], right[:, here]).astype(half.dtype)
        half[order:, here] = dot(wave[...], right[:, there]).astype(half.dtype)
    loads[3].wait()
    loads[4].wait()
    for first in range(0, order, tile):
        here = slice(first, first + tile)
        there = slice(order + first, order + first + tile)
        far = dot(left[...], half[:, here])
        real, imag = far[:order], far[order:]
        inverse = jnp.minimum(lax.rsqrt(real * real + imag * imag), 1.0 / MAG_FLOOR)
        shrink = 1.0 - measured[:, here].astype(jnp.float32) * inverse
        resid[:, here] = (real * shrink).astype(resid.dtype)
        resid[:, there] = (imag * shrink).astype(resid.dtype)
    for first in range(0, order, tile):
        here = slice(first, first + tile)
        there = slice(order + first, order + first + tile)
        turned[:order, here] = dot(resid[...], left[:, here]).astype(turned.dtype)
        turned[order:, here] = dot(resid[...], left[:, there]).astype(turned.dtype)
    for first in range(0, order, tile):
        here = slice(first, first + tile)
        there = slice(order + first, order + first + tile)
        back = dot(right[...], turned[:, here])
        real, imag = back[:order], back[order:]
        probe_real = probe[0, :, here].astype(jnp.float32)
        probe_imag = probe[1, :, here].astype(jnp.float32)
        term[:, here] = (probe_real * real + probe_imag * imag).astype(term.dtype)
        term[:, there] = (probe_real * imag - probe_imag * real).astype(term.dtype)
        patch_real = patch[:, here].astype(jnp.float32)
        patch_imag = patch[:, there].astype(jnp.float32)
        mine[:, here] = patch_real * real + patch_imag * imag
        mine[:, there] = patch_real * imag - patch_imag * real

    count = kept.shape[0]
    side = lax.rem(me, 2)
    kept[...] = mine[pl.ds(pl.multiple_of(side * count, count), count), :]
    sent[...] = mine[pl.ds(pl.multiple_of((1 - side) * count, count), count), :].astype(sent.dtype)

def slot_terms(cells, stock, dealing, rows, owners, order):
    total_rows = cells.shape[0]
    wide_cols = 2 * order
    bf16, f32 = jnp.bfloat16, jnp.float32
    return pl.pallas_call(
        slot_kernel,
        out_shape=(
            jax.ShapeDtypeStruct((order, wide_cols), bf16),
            jax.ShapeDtypeStruct((order // 2, wide_cols), f32),
            jax.ShapeDtypeStruct((order // 2, wide_cols), bf16),
        ),
        in_specs=[SMEM, SMEM, SMEM, VMEM, ANY],
        out_specs=(VMEM,) * 3,
        scratch_shapes=[
            pltpu.VMEM((total_rows + SUBLANES, wide_cols), f32),
            pltpu.VMEM((order, wide_cols), bf16),
            pltpu.VMEM((order, wide_cols), bf16),
            pltpu.VMEM((wide_cols, order), bf16),
            pltpu.VMEM((order, wide_cols), bf16),
            pltpu.VMEM((wide_cols, order), bf16),
            pltpu.VMEM((order, wide_cols), f32),
            pltpu.VMEM((2, order, order), bf16),
            pltpu.VMEM((wide_cols, wide_cols), bf16),
            pltpu.VMEM((order, order), bf16),
            pltpu.VMEM((wide_cols, wide_cols), bf16),
            pltpu.SemaphoreType.DMA((5,)),
        ],
        compiler_params=pltpu.CompilerParams(vmem_limit_bytes=40 * 2**20),
        cost_estimate=pl.CostEstimate(
            flops=8 * 2 * order**3 * 2, bytes_accessed=8 * 2**20, transcendentals=order * order
        ),
        name="slot",
    )(dealing, rows, owners, cells, stock)


def pack_kernel(reach, own_rows, dealing, rows, term, out, padded):
    order = term.shape[0]
    first_row = rows[dealing[lax.axis_index("row")]]
    below = padded.shape[0] - reach - order
    padded[0:reach, :] = jnp.zeros((reach, padded.shape[1]), jnp.float32)
    padded[reach : reach + order, :] = term[...].astype(jnp.float32)
    padded[reach + order :, :] = jnp.zeros((below, padded.shape[1]), jnp.float32)

    @pl.loop(0, out.shape[0], unroll=2)
    def _(k):
        out[k] = rows_from(padded, reach - first_row + k * own_rows, out.shape[1]).astype(out.dtype)


def pack_rows(term, dealing, rows, slots, own_rows, tile_rows):
    order, width = term.shape
    reach = slots * own_rows - order
    return pl.pallas_call(
        functools.partial(pack_kernel, reach, own_rows),
        out_shape=jax.ShapeDtypeStruct((slots, tile_rows, width), jnp.bfloat16),
        in_specs=[SMEM, SMEM, VMEM],
        out_specs=VMEM,
        scratch_shapes=[pltpu.VMEM((2 * reach + order + tile_rows + SUBLANES, width), jnp.float32)],
        compiler_params=pltpu.CompilerParams(vmem_limit_bytes=16 * 2**20),
        cost_estimate=pl.CostEstimate(flops=0, bytes_accessed=3 * 2**20, transcendentals=0),
        name="pack",
    )(dealing, rows, term)


def place_kernel(order, dealing, cols, blocks, owners, single, terms, empty, out, totals, sems):
    del empty
    slots, tile_rows = terms.shape[0], terms.shape[1]
    count = (order + LANES) // LANES
    lane = lax.broadcasted_iota(jnp.int32, (tile_rows, LANES), 1)
    nothing = jnp.zeros((tile_rows, LANES), jnp.float32)

    def whole(slot):
        place = pl.multiple_of(blocks[slot * count] * LANES, LANES)
        window = out.at[:, :, pl.ds(place, count * LANES)]
        return pltpu.make_async_copy(totals.at[slot], window, sems.at[slot * count])

    def part_of(slot, b):
        number = slot * count + b
        place = pl.multiple_of(blocks[number] * LANES, LANES)
        held = totals.at[slot, :, :, b * LANES : (b + 1) * LANES]
        return pltpu.make_async_copy(held, out.at[:, :, pl.ds(place, LANES)], sems.at[number])

    def add(slot):
        _, offset = window_start(cols[dealing[slot]], order, out.shape[2])
        shift = lax.rem(offset, LANES)
        for part in range(2):
            turned = []
            for b in range(count - 1):
                first = part * order + b * LANES
                turned.append(pltpu.roll(terms[slot, :, first : first + LANES], shift, 1).astype(jnp.float32))
            for b in range(count):
                before = turned[b - 1] if b else nothing
                after = turned[b] if b < count - 1 else nothing
                term = jnp.where(lane < offset, before, after)
                owner = owners[slot * count + b]
                holder = lax.div(owner, count)
                here = pl.ds(pl.multiple_of((owner - holder * count) * LANES, LANES), LANES)
                held = totals[holder, part, :, here]
                totals[holder, part, :, here] = jnp.where(owner == slot * count + b, term, held + term)

    half = slots // 2
    for low, high in ((0, half), (half, slots)):

        @pl.loop(low, high, unroll=4)
        def _(slot):
            add(slot)

        @pl.loop(low, high)
        def _(slot):
            @pl.when(single[slot] == 1)
            def _():
                whole(slot).start()

    def finish(slot, act):
        @pl.when(single[slot] == 0)
        def _():
            for b in range(count):

                @pl.when(owners[slot * count + b] == slot * count + b)
                def _():
                    act(part_of(slot, b))

    @pl.loop(0, slots)
    def _(slot):
        finish(slot, lambda copy: copy.start())

    @pl.loop(0, slots)
    def _(slot):
        @pl.when(single[slot] == 1)
        def _():
            whole(slot).wait()

        finish(slot, lambda copy: copy.wait())


def place_windows(terms, empty, blocks, owners, single, dealing, cols, order):
    slots, tile_rows = terms.shape[0], terms.shape[1]
    count = (order + LANES) // LANES
    return pl.pallas_call(
        functools.partial(place_kernel, order),
        out_shape=jax.ShapeDtypeStruct(empty.shape, empty.dtype),
        in_specs=[SMEM, SMEM, SMEM, SMEM, SMEM, VMEM, ANY],
        out_specs=ANY,
        scratch_shapes=[
            pltpu.VMEM((slots, 2, tile_rows, count * LANES), jnp.float32),
            pltpu.SemaphoreType.DMA((slots * count,)),
        ],
        input_output_aliases={6: 0},
        compiler_params=pltpu.CompilerParams(vmem_limit_bytes=24 * 2**20),
        cost_estimate=pl.CostEstimate(flops=0, bytes_accessed=6 * 2**20, transcendentals=0),
        name="place",
    )(dealing, cols, blocks, owners, single, terms, empty)


def strides(devices):
    steps, stride = [], 1
    while stride < devices:
        radix = 4 if len(steps) >= 2 and (devices // stride) % 4 == 0 else 2
        steps.append((stride, radix))
        stride *= radix
    return steps


def swap(x, distance, devices):
    return lax.ppermute(x, "row", [(d, d ^ distance) for d in range(devices)])


def sum_probe(kept, sent, devices):
    me = lax.axis_index("row")
    total = kept + swap(sent, 1, devices).astype(jnp.float32)
    for stride, radix in strides(devices)[1:]:
        digit = me // stride % radix
        count = total.shape[0] // radix
        own = lax.dynamic_slice_in_dim(total, digit * count, count)
        for k in range(1, radix):
            share = lax.dynamic_slice_in_dim(total, lax.bitwise_xor(digit, k) * count, count)
            own = own + swap(share.astype(jnp.bfloat16), k * stride, devices).astype(jnp.float32)
        total = own
    return total


def join(whole, devices):
    me = lax.axis_index("row")
    for stride, radix in reversed(strides(devices)):
        digit = me // stride % radix
        shares = [whole] + [swap(whole, k * stride, devices) for k in range(1, radix)]
        pieces = []
        for j in range(radix):
            piece = shares[0]
            for k in range(1, radix):
                piece = jnp.where(lax.bitwise_xor(digit, k) == j, shares[k], piece)
            pieces.append(piece)
        whole = jnp.concatenate(pieces, axis=0)
    return whole


def body(object_field, probe, amplitude, row_offsets, col_offsets, dealing):
    order = probe.shape[1]
    devices = lax.axis_size("row")
    own_rows, tile_cols = object_field.shape[1], object_field.shape[2]
    total_rows = devices * own_rows
    tile_rows = -(-own_rows // SUBLANES) * SUBLANES
    spare = tile_rows - own_rows
    if spare:
        object_field = jnp.pad(object_field, ((0, 0), (0, spare), (0, 0)))
    pieces, token = fetch_windows(object_field, dealing, col_offsets, order)
    strips = lax.all_to_all(pieces, "row", split_axis=0, concat_axis=0, tiled=True)
    cells = strips[:, :own_rows].reshape(total_rows, 2 * order)
    empty, blocks, owners, single, stock = prepare(
        dealing, col_offsets, token, probe, amplitude, object_field.shape
    )
    term, kept, sent = slot_terms(cells, stock, dealing, row_offsets, owners, order)
    total = sum_probe(kept, sent, devices)
    terms = pack_rows(term, dealing, row_offsets, devices, own_rows, tile_rows)
    terms, total = lax.optimization_barrier((terms, total))
    arrived = lax.all_to_all(terms, "row", split_axis=0, concat_axis=0, tiled=True)
    share = (total * (1.0 / dealing.shape[0])).astype(jnp.bfloat16)
    whole = join(share, devices).astype(jnp.float32)
    probe_grad = jnp.stack([whole[:, :order], whole[:, order:]])
    object_grad = place_windows(arrived, empty, blocks, owners, single, dealing, col_offsets, order)
    if spare:
        object_grad = object_grad[:, :own_rows]
    return (object_grad, probe_grad)


def solution(mesh):
    return jax.shard_map(
        body,
        mesh=mesh,
        in_specs=(
            P(None, ("groups", "row"), None),
            P("groups", None, None),
            P(("groups", "row"), None, None),
            P("groups"),
            P("groups"),
            P("groups"),
        ),
        out_specs=(P(None, ("groups", "row"), None), P("groups", None, None)),
        check_vma=False,
    )
```

```python
import functools
import math

import jax
import jax.numpy as jnp
import numpy as np
from jax import lax
from jax.experimental import pallas as pl
from jax.experimental.pallas import tpu as pltpu
from jax.sharding import PartitionSpec as P

MAG_FLOOR = 0.25
LANES = 128
SUBLANES = 8
SMEM = pl.BlockSpec(memory_space=pltpu.SMEM)
VMEM = pl.BlockSpec(memory_space=pltpu.VMEM)
ANY = pl.BlockSpec(memory_space=pl.ANY)


def dft_table(order):
    indices = np.arange(order, dtype=np.int32)
    phases = indices[:, None] * indices[None, :] % order
    angles = phases.astype(np.float32) * np.float32(2.0 * math.pi / order)
    factor = np.float32(1.0 / math.sqrt(order))
    return np.concatenate([np.cos(angles) * factor, -np.sin(angles) * factor], axis=1).astype(jnp.bfloat16)


def window_start(column, order, tile_cols):
    span = order + LANES
    base = jnp.minimum(column // LANES, (tile_cols - span) // LANES) * LANES
    return pl.multiple_of(base, LANES), column - base


def rows_from(ref, start, count):
    aligned = pl.multiple_of(start // SUBLANES * SUBLANES, SUBLANES)
    rest = start - aligned
    width = ref.shape[-1]
    blocks = ref[pl.ds(aligned, count + SUBLANES), :].reshape(-1, SUBLANES, width)
    turned = pltpu.roll(blocks, lax.rem(SUBLANES - rest, SUBLANES), 1)
    sub = lax.broadcasted_iota(jnp.int32, (1, SUBLANES, width), 1)
    picked = jnp.where(sub < SUBLANES - rest, turned[:-1], turned[1:])
    return picked.reshape(count, width)


def fetch_kernel(order, dealing, cols, tile, out, token, held, sems):
    token[0] = dealing[0]
    slots, tile_rows = out.shape[0], out.shape[1]
    tile_cols = tile.shape[2]
    span = order + LANES

    def copy(slot):
        base, _ = window_start(cols[dealing[slot]], order, tile_cols)
        return pltpu.make_async_copy(tile.at[:, :, pl.ds(base, span)], held.at[slot], sems.at[slot])

    @pl.loop(0, slots)
    def _(slot):
        copy(slot).start()

    lane = lax.broadcasted_iota(jnp.int32, (tile_rows, LANES), 1)

    @pl.loop(0, slots, unroll=4)
    def _(slot):
        copy(slot).wait()
        _, offset = window_start(cols[dealing[slot]], order, tile_cols)
        shift = lax.rem(LANES - lax.rem(offset, LANES), LANES)
        for part in range(2):
            turned = [
                pltpu.roll(held[slot, part, :, b * LANES : (b + 1) * LANES].astype(out.dtype), shift, 1)
                for b in range(span // LANES)
            ]
            for b in range(order // LANES):
                first = part * order + b * LANES
                cells = jnp.where(lane < LANES - offset, turned[b], turned[b + 1])
                out[slot, :, first : first + LANES] = cells


def fetch_windows(tile, dealing, cols, order):
    slots, tile_rows, tile_cols = dealing.shape[0], tile.shape[1], tile.shape[2]
    span = order + LANES

    return pl.pallas_call(
        functools.partial(fetch_kernel, order),
        out_shape=(
            jax.ShapeDtypeStruct((slots, tile_rows, 2 * order), jnp.bfloat16),
            jax.ShapeDtypeStruct((1,), jnp.int32),
        ),
        in_specs=[SMEM, SMEM, ANY],
        out_specs=(VMEM, SMEM),
        scratch_shapes=[
            pltpu.VMEM((slots, 2, tile_rows, span), jnp.float32),
            pltpu.SemaphoreType.DMA((slots,)),
        ],
        compiler_params=pltpu.CompilerParams(vmem_limit_bytes=56 * 2**20),
        cost_estimate=pl.CostEstimate(flops=0, bytes_accessed=6 * 2**20, transcendentals=0),
        name="fetch",
    )(dealing, cols, tile)


def stock_places(stock, order):
    return (
        stock.at[0:order, 0:order],
        stock.at[0:order, order : 2 * order],
        stock.at[order : 2 * order, :],
        stock.at[2 * order : 3 * order, 0:order],
    )


def prepare_kernel(
    order, dealing, cols, token, table_in, probe, measured,
    empty, blocks, owners, stock,
    table, zeros, sems, stock_sems,
):
    del token
    places = stock_places(stock, order)
    sources = (probe.at[0], probe.at[1], table_in, measured.at[0])
    fills = []
    for k, (source, place) in enumerate(zip(sources, places)):
        fill = pltpu.make_async_copy(source, place, stock_sems.at[k])
        fill.start()
        fills.append(fill)
    count = (order + LANES) // LANES
    slots = dealing.shape[0]
    tile_cols = empty.shape[2]
    width = zeros.shape[2]
    zeros[...] = jnp.zeros_like(zeros)
    for b in range(tile_cols // width):
        fill = pltpu.make_async_copy(zeros, empty.at[:, :, b * width : (b + 1) * width], sems.at[b])
        fill.start()
        fills.append(fill)

    @pl.loop(0, tile_cols // LANES)
    def _(block):
        table[block] = -1

    @pl.loop(0, slots)
    def _(slot):
        base, _ = window_start(cols[dealing[slot]], order, tile_cols)
        for b in range(count):
            number = slot * count + b
            block = base // LANES + b
            blocks[number] = block
            known = table[block]
            owner = jnp.where(known < 0, number, known)
            owners[number] = owner
            table[block] = owner

    for fill in fills:
        fill.wait()


def prepare(dealing, cols, token, probe, measured, tile_shape):
    order = probe.shape[1]
    slots = dealing.shape[0]
    numbers = slots * (order + LANES) // LANES
    fill_cols = 2048
    return pl.pallas_call(
        functools.partial(prepare_kernel, order),
        out_shape=(
            jax.ShapeDtypeStruct(tile_shape, jnp.float32),
            jax.ShapeDtypeStruct((numbers,), jnp.int32),
            jax.ShapeDtypeStruct((numbers,), jnp.int32),
            jax.ShapeDtypeStruct((28 * order, 2 * order), jnp.bfloat16),
        ),
        in_specs=[SMEM, SMEM, SMEM, ANY, ANY, ANY],
        out_specs=(ANY, SMEM, SMEM, ANY),
        scratch_shapes=[
            pltpu.SMEM((tile_shape[2] // LANES,), jnp.int32),
            pltpu.VMEM(tile_shape[:2] + (fill_cols,), jnp.float32),
            pltpu.SemaphoreType.DMA((tile_shape[2] // fill_cols,)),
            pltpu.SemaphoreType.DMA((4,)),
        ],
        compiler_params=pltpu.CompilerParams(vmem_limit_bytes=8 * 2**20),
        cost_estimate=pl.CostEstimate(flops=0, bytes_accessed=110 * 2**20, transcendentals=0),
        name="prepare",
    )(dealing, cols, token, jnp.asarray(dft_table(order)), probe, measured)


def slot_kernel(
    dealing, rows, owners, cells, stock,
    term, kept, sent,
    wide, patch, wave, half, resid, turned, mine, probe, table, minus, measured, sems,
):
    del owners
    order = term.shape[0]
    places = stock_places(stock, order)
    targets = (probe.at[0], probe.at[1], table, measured)
    loads = [
        pltpu.make_async_copy(source, target, sems.at[k])
        for k, (source, target) in enumerate(zip(places, targets))
    ]
    for load in loads:
        load.start()
    total_rows = cells.shape[0]
    me = lax.axis_index("row")
    first_row = rows[dealing[me]]
    step = 64
    tile = 256

    wide[0:total_rows, :] = cells[...].astype(jnp.float32)
    wide[total_rows:, :] = jnp.zeros((SUBLANES, 2 * order), jnp.float32)
    loads[0].wait()
    loads[1].wait()

    @pl.loop(0, order // step)
    def _(i):
        place = pl.ds(pl.multiple_of(i * step, step), step)
        found = rows_from(wide, first_row + i * step, step)
        patch[place, :] = found.astype(patch.dtype)
        real, imag = found[:, :order], found[:, order:]
        probe_real = probe[0, place, :].astype(jnp.float32)
        probe_imag = probe[1, place, :].astype(jnp.float32)
        wave[place, :order] = (probe_real * real - probe_imag * imag).astype(wave.dtype)
        wave[place, order:] = (probe_real * imag + probe_imag * real).astype(wave.dtype)

    loads[2].wait()
    minus[...] = -table[:, order:]
    cos, sin = table.at[:, :order], table.at[:, order:]
    first_half, second_half = slice(0, order), slice(order, 2 * order)

    def dots(a, b, c, d):
        one = jnp.dot(a, b, preferred_element_type=jnp.float32)
        return one + jnp.dot(c, d, preferred_element_type=jnp.float32)

    for first in range(0, order, tile):
        here = slice(first, first + tile)
        real, imag = wave[:, first_half], wave[:, second_half]
        half[first_half, here] = dots(real, cos[:, here], imag, minus[:, here]).astype(half.dtype)
        half[second_half, here] = dots(real, sin[:, here], imag, cos[:, here]).astype(half.dtype)
    loads[3].wait()
    for first in range(0, order, tile):
        here = slice(first, first + tile)
        there = slice(order + first, order + first + tile)
        for top in range(0, order, tile):
            line = slice(top, top + tile)
            half_real, half_imag = half[first_half, here], half[second_half, here]
            real = dots(cos[line, :], half_real, minus[line, :], half_imag)
            imag = dots(sin[line, :], half_real, cos[line, :], half_imag)
            inverse = jnp.minimum(lax.rsqrt(real * real + imag * imag), 1.0 / MAG_FLOOR)
            shrink = 1.0 - measured[line, here].astype(jnp.float32) * inverse
            resid[line, here] = (real * shrink).astype(resid.dtype)
            resid[line, there] = (imag * shrink).astype(resid.dtype)
    for first in range(0, order, tile):
        here = slice(first, first + tile)
        real, imag = resid[:, first_half], resid[:, second_half]
        turned[first_half, here] = dots(real, cos[:, here], imag, sin[:, here]).astype(turned.dtype)
        turned[second_half, here] = dots(real, minus[:, here], imag, cos[:, here]).astype(turned.dtype)
    for first in range(0, order, tile):
        here = slice(first, first + tile)
        there = slice(order + first, order + first + tile)
        for top in range(0, order, tile):
            line = slice(top, top + tile)
            turned_real, turned_imag = turned[first_half, here], turned[second_half, here]
            real = dots(cos[line, :], turned_real, sin[line, :], turned_imag)
            imag = dots(minus[line, :], turned_real, cos[line, :], turned_imag)
            probe_real = probe[0, line, here].astype(jnp.float32)
            probe_imag = probe[1, line, here].astype(jnp.float32)
            term[line, here] = (probe_real * real + probe_imag * imag).astype(term.dtype)
            term[line, there] = (probe_real * imag - probe_imag * real).astype(term.dtype)
            patch_real = patch[line, here].astype(jnp.float32)
            patch_imag = patch[line, there].astype(jnp.float32)
            mine[line, here] = patch_real * real + patch_imag * imag
            mine[line, there] = patch_real * imag - patch_imag * real

    count = kept.shape[0]
    side = lax.rem(me, 2)
    kept[...] = mine[pl.ds(pl.multiple_of(side * count, count), count), :]
    sent[...] = mine[pl.ds(pl.multiple_of((1 - side) * count, count), count), :].astype(sent.dtype)

def slot_terms(cells, stock, dealing, rows, owners, order):
    total_rows = cells.shape[0]
    wide_cols = 2 * order
    bf16, f32 = jnp.bfloat16, jnp.float32
    return pl.pallas_call(
        slot_kernel,
        out_shape=(
            jax.ShapeDtypeStruct((order, wide_cols), bf16),
            jax.ShapeDtypeStruct((order // 2, wide_cols), f32),
            jax.ShapeDtypeStruct((order // 2, wide_cols), bf16),
        ),
        in_specs=[SMEM, SMEM, SMEM, VMEM, ANY],
        out_specs=(VMEM,) * 3,
        scratch_shapes=[
            pltpu.VMEM((total_rows + SUBLANES, wide_cols), f32),
            pltpu.VMEM((order, wide_cols), bf16),
            pltpu.VMEM((order, wide_cols), bf16),
            pltpu.VMEM((wide_cols, order), bf16),
            pltpu.VMEM((order, wide_cols), bf16),
            pltpu.VMEM((wide_cols, order), bf16),
            pltpu.VMEM((order, wide_cols), f32),
            pltpu.VMEM((2, order, order), bf16),
            pltpu.VMEM((order, wide_cols), bf16),
            pltpu.VMEM((order, order), bf16),
            pltpu.VMEM((order, order), bf16),
            pltpu.SemaphoreType.DMA((4,)),
        ],
        compiler_params=pltpu.CompilerParams(vmem_limit_bytes=40 * 2**20),
        cost_estimate=pl.CostEstimate(
            flops=8 * 2 * order**3 * 2, bytes_accessed=8 * 2**20, transcendentals=order * order
        ),
        name="slot",
    )(dealing, rows, owners, cells, stock)


def pack_kernel(reach, own_rows, dealing, rows, term, out, padded):
    order = term.shape[0]
    first_row = rows[dealing[lax.axis_index("row")]]
    below = padded.shape[0] - reach - order
    padded[0:reach, :] = jnp.zeros((reach, padded.shape[1]), jnp.float32)
    padded[reach : reach + order, :] = term[...].astype(jnp.float32)
    padded[reach + order :, :] = jnp.zeros((below, padded.shape[1]), jnp.float32)

    @pl.loop(0, out.shape[0], unroll=2)
    def _(k):
        out[k] = rows_from(padded, reach - first_row + k * own_rows, out.shape[1]).astype(out.dtype)


def pack_rows(term, dealing, rows, slots, own_rows, tile_rows):
    order, width = term.shape
    reach = slots * own_rows - order
    return pl.pallas_call(
        functools.partial(pack_kernel, reach, own_rows),
        out_shape=jax.ShapeDtypeStruct((slots, tile_rows, width), jnp.bfloat16),
        in_specs=[SMEM, SMEM, VMEM],
        out_specs=VMEM,
        scratch_shapes=[pltpu.VMEM((2 * reach + order + tile_rows + SUBLANES, width), jnp.float32)],
        compiler_params=pltpu.CompilerParams(vmem_limit_bytes=16 * 2**20),
        cost_estimate=pl.CostEstimate(flops=0, bytes_accessed=3 * 2**20, transcendentals=0),
        name="pack",
    )(dealing, rows, term)


def place_kernel(order, dealing, cols, blocks, owners, terms, empty, out, totals, sems):
    del empty
    slots, tile_rows = terms.shape[0], terms.shape[1]
    count = (order + LANES) // LANES
    totals[...] = jnp.zeros_like(totals)
    lane = lax.broadcasted_iota(jnp.int32, (tile_rows, LANES), 1)
    nothing = jnp.zeros((tile_rows, LANES), jnp.float32)

    @pl.loop(0, slots, unroll=4)
    def _(slot):
        _, offset = window_start(cols[dealing[slot]], order, out.shape[2])
        shift = lax.rem(offset, LANES)
        for part in range(2):
            turned = []
            for b in range(count - 1):
                first = part * order + b * LANES
                turned.append(pltpu.roll(terms[slot, :, first : first + LANES], shift, 1).astype(jnp.float32))
            for b in range(count):
                before = turned[b - 1] if b else nothing
                after = turned[b] if b < count - 1 else nothing
                owner = owners[slot * count + b]
                totals[owner, part] += jnp.where(lane < offset, before, after)

    def copy(number):
        place = pl.multiple_of(blocks[number] * LANES, LANES)
        return pltpu.make_async_copy(totals.at[number], out.at[:, :, pl.ds(place, LANES)], sems.at[number])

    @pl.loop(0, slots * count)
    def _(number):
        @pl.when(owners[number] == number)
        def _():
            copy(number).start()

    @pl.loop(0, slots * count)
    def _(number):
        @pl.when(owners[number] == number)
        def _():
            copy(number).wait()


def place_windows(terms, empty, blocks, owners, dealing, cols, order):
    slots, tile_rows = terms.shape[0], terms.shape[1]
    count = (order + LANES) // LANES
    return pl.pallas_call(
        functools.partial(place_kernel, order),
        out_shape=jax.ShapeDtypeStruct(empty.shape, empty.dtype),
        in_specs=[SMEM, SMEM, SMEM, SMEM, VMEM, ANY],
        out_specs=ANY,
        scratch_shapes=[
            pltpu.VMEM((slots * count, 2, tile_rows, LANES), jnp.float32),
            pltpu.SemaphoreType.DMA((slots * count,)),
        ],
        input_output_aliases={5: 0},
        compiler_params=pltpu.CompilerParams(vmem_limit_bytes=24 * 2**20),
        cost_estimate=pl.CostEstimate(flops=0, bytes_accessed=6 * 2**20, transcendentals=0),
        name="place",
    )(dealing, cols, blocks, owners, terms, empty)


def strides(devices):
    steps, stride = [], 1
    while stride < devices:
        radix = 4 if len(steps) >= 2 and (devices // stride) % 4 == 0 else 2
        steps.append((stride, radix))
        stride *= radix
    return steps


def swap(x, distance, devices):
    return lax.ppermute(x, "row", [(d, d ^ distance) for d in range(devices)])


def sum_probe(kept, sent, devices):
    me = lax.axis_index("row")
    total = kept + swap(sent, 1, devices).astype(jnp.float32)
    for stride, radix in strides(devices)[1:]:
        digit = me // stride % radix
        count = total.shape[0] // radix
        own = lax.dynamic_slice_in_dim(total, digit * count, count)
        for k in range(1, radix):
            share = lax.dynamic_slice_in_dim(total, lax.bitwise_xor(digit, k) * count, count)
            own = own + swap(share.astype(jnp.bfloat16), k * stride, devices).astype(jnp.float32)
        total = own
    return total


def join(whole, devices):
    me = lax.axis_index("row")
    for stride, radix in reversed(strides(devices)):
        digit = me // stride % radix
        shares = [whole] + [swap(whole, k * stride, devices) for k in range(1, radix)]
        pieces = []
        for j in range(radix):
            piece = shares[0]
            for k in range(1, radix):
                piece = jnp.where(lax.bitwise_xor(digit, k) == j, shares[k], piece)
            pieces.append(piece)
        whole = jnp.concatenate(pieces, axis=0)
    return whole


def body(object_field, probe, amplitude, row_offsets, col_offsets, dealing):
    order = probe.shape[1]
    devices = lax.axis_size("row")
    own_rows, tile_cols = object_field.shape[1], object_field.shape[2]
    total_rows = devices * own_rows
    tile_rows = -(-own_rows // SUBLANES) * SUBLANES
    spare = tile_rows - own_rows
    if spare:
        object_field = jnp.pad(object_field, ((0, 0), (0, spare), (0, 0)))
    pieces, token = fetch_windows(object_field, dealing, col_offsets, order)
    strips = lax.all_to_all(pieces, "row", split_axis=0, concat_axis=0, tiled=True)
    cells = strips[:, :own_rows].reshape(total_rows, 2 * order)
    empty, blocks, owners, stock = prepare(
        dealing, col_offsets, token, probe, amplitude, object_field.shape
    )
    term, kept, sent = slot_terms(cells, stock, dealing, row_offsets, owners, order)
    total = sum_probe(kept, sent, devices)
    terms = pack_rows(term, dealing, row_offsets, devices, own_rows, tile_rows)
    terms, total = lax.optimization_barrier((terms, total))
    arrived = lax.all_to_all(terms, "row", split_axis=0, concat_axis=0, tiled=True)
    share = (total * (1.0 / dealing.shape[0])).astype(jnp.bfloat16)
    whole = join(share, devices).astype(jnp.float32)
    probe_grad = jnp.stack([whole[:, :order], whole[:, order:]])
    object_grad = place_windows(arrived, empty, blocks, owners, dealing, col_offsets, order)
    if spare:
        object_grad = object_grad[:, :own_rows]
    return (object_grad, probe_grad)


def solution(mesh):
    return jax.shard_map(
        body,
        mesh=mesh,
        in_specs=(
            P(None, ("groups", "row"), None),
            P("groups", None, None),
            P(("groups", "row"), None, None),
            P("groups"),
            P("groups"),
            P("groups"),
        ),
        out_specs=(P(None, ("groups", "row"), None), P("groups", None, None)),
        check_vma=False,
    )
```

```python
import functools
import math

import jax
import jax.numpy as jnp
import numpy as np
from jax import lax
from jax.experimental import pallas as pl
from jax.experimental.pallas import tpu as pltpu
from jax.sharding import PartitionSpec as P

MAG_FLOOR = 0.25
LANES = 128
SUBLANES = 8
SMEM = pl.BlockSpec(memory_space=pltpu.SMEM)
VMEM = pl.BlockSpec(memory_space=pltpu.VMEM)
ANY = pl.BlockSpec(memory_space=pl.ANY)


def dft_table(order):
    indices = np.arange(order, dtype=np.int32)
    phases = indices[:, None] * indices[None, :] % order
    angles = phases.astype(np.float32) * np.float32(2.0 * math.pi / order)
    factor = np.float32(1.0 / math.sqrt(order))
    return np.concatenate([np.cos(angles) * factor, -np.sin(angles) * factor], axis=1).astype(jnp.bfloat16)


def window_start(column, order, tile_cols):
    span = order + LANES
    base = jnp.minimum(column // LANES, (tile_cols - span) // LANES) * LANES
    return pl.multiple_of(base, LANES), column - base


def rows_from(ref, start, count):
    aligned = pl.multiple_of(start // SUBLANES * SUBLANES, SUBLANES)
    rest = start - aligned
    width = ref.shape[-1]
    blocks = ref[pl.ds(aligned, count + SUBLANES), :].reshape(-1, SUBLANES, width)
    turned = pltpu.roll(blocks, lax.rem(SUBLANES - rest, SUBLANES), 1)
    sub = lax.broadcasted_iota(jnp.int32, (1, SUBLANES, width), 1)
    picked = jnp.where(sub < SUBLANES - rest, turned[:-1], turned[1:])
    return picked.reshape(count, width)


def fetch_kernel(order, dealing, cols, tile, out, token, held, sems):
    token[0] = dealing[0]
    slots, tile_rows = out.shape[0], out.shape[1]
    tile_cols = tile.shape[2]
    span = order + LANES

    def copy(slot):
        base, _ = window_start(cols[dealing[slot]], order, tile_cols)
        return pltpu.make_async_copy(tile.at[:, :, pl.ds(base, span)], held.at[slot], sems.at[slot])

    @pl.loop(0, slots)
    def _(slot):
        copy(slot).start()

    lane = lax.broadcasted_iota(jnp.int32, (tile_rows, LANES), 1)

    @pl.loop(0, slots, unroll=4)
    def _(slot):
        copy(slot).wait()
        _, offset = window_start(cols[dealing[slot]], order, tile_cols)
        shift = lax.rem(LANES - lax.rem(offset, LANES), LANES)
        for part in range(2):
            turned = [
                pltpu.roll(held[slot, part, :, b * LANES : (b + 1) * LANES].astype(out.dtype), shift, 1)
                for b in range(span // LANES)
            ]
            for b in range(order // LANES):
                first = part * order + b * LANES
                cells = jnp.where(lane < LANES - offset, turned[b], turned[b + 1])
                out[slot, :, first : first + LANES] = cells


def fetch_windows(tile, dealing, cols, order):
    slots, tile_rows, tile_cols = dealing.shape[0], tile.shape[1], tile.shape[2]
    span = order + LANES

    return pl.pallas_call(
        functools.partial(fetch_kernel, order),
        out_shape=(
            jax.ShapeDtypeStruct((slots, tile_rows, 2 * order), jnp.bfloat16),
            jax.ShapeDtypeStruct((1,), jnp.int32),
        ),
        in_specs=[SMEM, SMEM, ANY],
        out_specs=(VMEM, SMEM),
        scratch_shapes=[
            pltpu.VMEM((slots, 2, tile_rows, span), jnp.float32),
            pltpu.SemaphoreType.DMA((slots,)),
        ],
        compiler_params=pltpu.CompilerParams(vmem_limit_bytes=56 * 2**20),
        cost_estimate=pl.CostEstimate(flops=0, bytes_accessed=6 * 2**20, transcendentals=0),
        name="fetch",
    )(dealing, cols, tile)


def stock_places(stock, order):
    return (
        stock.at[0:order, 0:order],
        stock.at[0:order, order : 2 * order],
        stock.at[order : 2 * order, :],
        stock.at[2 * order : 3 * order, 0:order],
    )


def prepare_kernel(
    order, dealing, cols, token, table_in, probe, measured,
    empty, blocks, owners, stock,
    table, zeros, sems, stock_sems,
):
    del token
    places = stock_places(stock, order)
    sources = (probe.at[0], probe.at[1], table_in, measured.at[0])
    fills = []
    for k, (source, place) in enumerate(zip(sources, places)):
        fill = pltpu.make_async_copy(source, place, stock_sems.at[k])
        fill.start()
        fills.append(fill)
    count = (order + LANES) // LANES
    slots = dealing.shape[0]
    tile_cols = empty.shape[2]
    width = zeros.shape[2]
    zeros[...] = jnp.zeros_like(zeros)
    for b in range(tile_cols // width):
        fill = pltpu.make_async_copy(zeros, empty.at[:, :, b * width : (b + 1) * width], sems.at[b])
        fill.start()
        fills.append(fill)

    @pl.loop(0, tile_cols // LANES)
    def _(block):
        table[block] = -1

    @pl.loop(0, slots)
    def _(slot):
        base, _ = window_start(cols[dealing[slot]], order, tile_cols)
        for b in range(count):
            number = slot * count + b
            block = base // LANES + b
            blocks[number] = block
            known = table[block]
            owner = jnp.where(known < 0, number, known)
            owners[number] = owner
            table[block] = owner

    for fill in fills:
        fill.wait()


def prepare(dealing, cols, token, probe, measured, tile_shape):
    order = probe.shape[1]
    slots = dealing.shape[0]
    numbers = slots * (order + LANES) // LANES
    fill_cols = 2048
    return pl.pallas_call(
        functools.partial(prepare_kernel, order),
        out_shape=(
            jax.ShapeDtypeStruct(tile_shape, jnp.float32),
            jax.ShapeDtypeStruct((numbers,), jnp.int32),
            jax.ShapeDtypeStruct((numbers,), jnp.int32),
            jax.ShapeDtypeStruct((48 * order, 2 * order), jnp.bfloat16),
        ),
        in_specs=[SMEM, SMEM, SMEM, ANY, ANY, ANY],
        out_specs=(ANY, SMEM, SMEM, ANY),
        scratch_shapes=[
            pltpu.SMEM((tile_shape[2] // LANES,), jnp.int32),
            pltpu.VMEM(tile_shape[:2] + (fill_cols,), jnp.float32),
            pltpu.SemaphoreType.DMA((tile_shape[2] // fill_cols,)),
            pltpu.SemaphoreType.DMA((4,)),
        ],
        compiler_params=pltpu.CompilerParams(vmem_limit_bytes=8 * 2**20),
        cost_estimate=pl.CostEstimate(flops=0, bytes_accessed=110 * 2**20, transcendentals=0),
        name="prepare",
    )(dealing, cols, token, jnp.asarray(dft_table(order)), probe, measured)


def slot_kernel(
    dealing, rows, owners, cells, stock,
    term, kept, sent,
    wide, patch, wave, half, resid, turned, mine, probe, table, minus, measured, sems,
):
    del owners
    order = term.shape[0]
    places = stock_places(stock, order)
    targets = (probe.at[0], probe.at[1], table, measured)
    loads = [
        pltpu.make_async_copy(source, target, sems.at[k])
        for k, (source, target) in enumerate(zip(places, targets))
    ]
    for load in loads:
        load.start()
    total_rows = cells.shape[0]
    me = lax.axis_index("row")
    first_row = rows[dealing[me]]
    step = 64
    tile = 256

    wide[0:total_rows, :] = cells[...].astype(jnp.float32)
    wide[total_rows:, :] = jnp.zeros((SUBLANES, 2 * order), jnp.float32)

    @pl.loop(0, order // step, unroll=2)
    def _(i):
        place = pl.ds(pl.multiple_of(i * step, step), step)
        patch[place, :] = rows_from(wide, first_row + i * step, step).astype(patch.dtype)

    loads[0].wait()
    loads[1].wait()

    @pl.loop(0, order // step, unroll=2)
    def _(i):
        place = pl.ds(pl.multiple_of(i * step, step), step)
        found = patch[place, :].astype(jnp.float32)
        real, imag = found[:, :order], found[:, order:]
        probe_real = probe[0, place, :].astype(jnp.float32)
        probe_imag = probe[1, place, :].astype(jnp.float32)
        wave[place, :order] = (probe_real * real - probe_imag * imag).astype(wave.dtype)
        wave[place, order:] = (probe_real * imag + probe_imag * real).astype(wave.dtype)

    loads[2].wait()
    minus[...] = -table[:, order:]
    cos, sin = table.at[:, :order], table.at[:, order:]
    first_half, second_half = slice(0, order), slice(order, 2 * order)

    def dots(a, b, c, d):
        one = jnp.dot(a, b, preferred_element_type=jnp.float32)
        return one + jnp.dot(c, d, preferred_element_type=jnp.float32)

    for first in range(0, order, tile):
        here = slice(first, first + tile)
        real, imag = wave[:, first_half], wave[:, second_half]
        half[first_half, here] = dots(real, cos[:, here], imag, minus[:, here]).astype(half.dtype)
        half[second_half, here] = dots(real, sin[:, here], imag, cos[:, here]).astype(half.dtype)
    loads[3].wait()
    for first in range(0, order, tile):
        here = slice(first, first + tile)
        there = slice(order + first, order + first + tile)
        for top in range(0, order, tile):
            line = slice(top, top + tile)
            half_real, half_imag = half[first_half, here], half[second_half, here]
            real = dots(cos[line, :], half_real, minus[line, :], half_imag)
            imag = dots(sin[line, :], half_real, cos[line, :], half_imag)
            inverse = jnp.minimum(lax.rsqrt(real * real + imag * imag), 1.0 / MAG_FLOOR)
            shrink = 1.0 - measured[line, here].astype(jnp.float32) * inverse
            resid[line, here] = (real * shrink).astype(resid.dtype)
            resid[line, there] = (imag * shrink).astype(resid.dtype)
    for first in range(0, order, tile):
        here = slice(first, first + tile)
        real, imag = resid[:, first_half], resid[:, second_half]
        turned[first_half, here] = dots(real, cos[:, here], imag, sin[:, here]).astype(turned.dtype)
        turned[second_half, here] = dots(real, minus[:, here], imag, cos[:, here]).astype(turned.dtype)
    for first in range(0, order, tile):
        here = slice(first, first + tile)
        there = slice(order + first, order + first + tile)
        for top in range(0, order, tile):
            line = slice(top, top + tile)
            turned_real, turned_imag = turned[first_half, here], turned[second_half, here]
            real = dots(cos[line, :], turned_real, sin[line, :], turned_imag)
            imag = dots(minus[line, :], turned_real, cos[line, :], turned_imag)
            probe_real = probe[0, line, here].astype(jnp.float32)
            probe_imag = probe[1, line, here].astype(jnp.float32)
            term[line, here] = (probe_real * real + probe_imag * imag).astype(term.dtype)
            term[line, there] = (probe_real * imag - probe_imag * real).astype(term.dtype)
            patch_real = patch[line, here].astype(jnp.float32)
            patch_imag = patch[line, there].astype(jnp.float32)
            mine[line, here] = patch_real * real + patch_imag * imag
            mine[line, there] = patch_real * imag - patch_imag * real

    count = kept.shape[0]
    side = lax.rem(me, 2)
    kept[...] = mine[pl.ds(pl.multiple_of(side * count, count), count), :]
    sent[...] = mine[pl.ds(pl.multiple_of((1 - side) * count, count), count), :].astype(sent.dtype)

def slot_terms(cells, stock, dealing, rows, owners, order):
    total_rows = cells.shape[0]
    wide_cols = 2 * order
    bf16, f32 = jnp.bfloat16, jnp.float32
    return pl.pallas_call(
        slot_kernel,
        out_shape=(
            jax.ShapeDtypeStruct((order, wide_cols), bf16),
            jax.ShapeDtypeStruct((order // 2, wide_cols), f32),
            jax.ShapeDtypeStruct((order // 2, wide_cols), bf16),
        ),
        in_specs=[SMEM, SMEM, SMEM, VMEM, ANY],
        out_specs=(VMEM,) * 3,
        scratch_shapes=[
            pltpu.VMEM((total_rows + SUBLANES, wide_cols), f32),
            pltpu.VMEM((order, wide_cols), bf16),
            pltpu.VMEM((order, wide_cols), bf16),
            pltpu.VMEM((wide_cols, order), bf16),
            pltpu.VMEM((order, wide_cols), bf16),
            pltpu.VMEM((wide_cols, order), bf16),
            pltpu.VMEM((order, wide_cols), f32),
            pltpu.VMEM((2, order, order), bf16),
            pltpu.VMEM((order, wide_cols), bf16),
            pltpu.VMEM((order, order), bf16),
            pltpu.VMEM((order, order), bf16),
            pltpu.SemaphoreType.DMA((4,)),
        ],
        compiler_params=pltpu.CompilerParams(vmem_limit_bytes=24 * 2**20),
        cost_estimate=pl.CostEstimate(
            flops=8 * 2 * order**3 * 2, bytes_accessed=8 * 2**20, transcendentals=order * order
        ),
        name="slot",
    )(dealing, rows, owners, cells, stock)


def pack_kernel(reach, own_rows, dealing, rows, term, out, padded):
    order = term.shape[0]
    first_row = rows[dealing[lax.axis_index("row")]]
    below = padded.shape[0] - reach - order
    padded[0:reach, :] = jnp.zeros((reach, padded.shape[1]), jnp.float32)
    padded[reach : reach + order, :] = term[...].astype(jnp.float32)
    padded[reach + order :, :] = jnp.zeros((below, padded.shape[1]), jnp.float32)

    @pl.loop(0, out.shape[0], unroll=2)
    def _(k):
        out[k] = rows_from(padded, reach - first_row + k * own_rows, out.shape[1]).astype(out.dtype)


def pack_rows(term, dealing, rows, slots, own_rows, tile_rows):
    order, width = term.shape
    reach = slots * own_rows - order
    return pl.pallas_call(
        functools.partial(pack_kernel, reach, own_rows),
        out_shape=jax.ShapeDtypeStruct((slots, tile_rows, width), jnp.bfloat16),
        in_specs=[SMEM, SMEM, VMEM],
        out_specs=VMEM,
        scratch_shapes=[pltpu.VMEM((2 * reach + order + tile_rows + SUBLANES, width), jnp.float32)],
        compiler_params=pltpu.CompilerParams(vmem_limit_bytes=8 * 2**20),
        cost_estimate=pl.CostEstimate(flops=0, bytes_accessed=3 * 2**20, transcendentals=0),
        name="pack",
    )(dealing, rows, term)


def place_kernel(order, dealing, cols, blocks, owners, terms, empty, out, totals, sems):
    del empty
    slots, tile_rows = terms.shape[0], terms.shape[1]
    count = (order + LANES) // LANES
    totals[...] = jnp.zeros_like(totals)
    lane = lax.broadcasted_iota(jnp.int32, (tile_rows, LANES), 1)
    nothing = jnp.zeros((tile_rows, LANES), jnp.float32)

    @pl.loop(0, slots, unroll=4)
    def _(slot):
        _, offset = window_start(cols[dealing[slot]], order, out.shape[2])
        shift = lax.rem(offset, LANES)
        for part in range(2):
            turned = []
            for b in range(count - 1):
                first = part * order + b * LANES
                turned.append(pltpu.roll(terms[slot, :, first : first + LANES], shift, 1).astype(jnp.float32))
            for b in range(count):
                before = turned[b - 1] if b else nothing
                after = turned[b] if b < count - 1 else nothing
                owner = owners[slot * count + b]
                totals[owner, part] += jnp.where(lane < offset, before, after)

    def copy(number):
        place = pl.multiple_of(blocks[number] * LANES, LANES)
        return pltpu.make_async_copy(totals.at[number], out.at[:, :, pl.ds(place, LANES)], sems.at[number])

    @pl.loop(0, slots * count)
    def _(number):
        @pl.when(owners[number] == number)
        def _():
            copy(number).start()

    @pl.loop(0, slots * count)
    def _(number):
        @pl.when(owners[number] == number)
        def _():
            copy(number).wait()


def place_windows(terms, empty, blocks, owners, dealing, cols, order):
    slots, tile_rows = terms.shape[0], terms.shape[1]
    count = (order + LANES) // LANES
    return pl.pallas_call(
        functools.partial(place_kernel, order),
        out_shape=jax.ShapeDtypeStruct(empty.shape, empty.dtype),
        in_specs=[SMEM, SMEM, SMEM, SMEM, VMEM, ANY],
        out_specs=ANY,
        scratch_shapes=[
            pltpu.VMEM((slots * count, 2, tile_rows, LANES), jnp.float32),
            pltpu.SemaphoreType.DMA((slots * count,)),
        ],
        input_output_aliases={5: 0},
        compiler_params=pltpu.CompilerParams(vmem_limit_bytes=12 * 2**20),
        cost_estimate=pl.CostEstimate(flops=0, bytes_accessed=6 * 2**20, transcendentals=0),
        name="place",
    )(dealing, cols, blocks, owners, terms, empty)


def strides(devices):
    steps, stride = [], 1
    while stride < devices:
        radix = 4 if len(steps) >= 2 and (devices // stride) % 4 == 0 else 2
        steps.append((stride, radix))
        stride *= radix
    return steps


def swap(x, distance, devices):
    return lax.ppermute(x, "row", [(d, d ^ distance) for d in range(devices)])


def sum_probe(kept, sent, devices):
    me = lax.axis_index("row")
    total = kept + swap(sent, 1, devices).astype(jnp.float32)
    for stride, radix in strides(devices)[1:]:
        digit = me // stride % radix
        count = total.shape[0] // radix
        own = lax.dynamic_slice_in_dim(total, digit * count, count)
        for k in range(1, radix):
            share = lax.dynamic_slice_in_dim(total, lax.bitwise_xor(digit, k) * count, count)
            own = own + swap(share.astype(jnp.bfloat16), k * stride, devices).astype(jnp.float32)
        total = own
    return total


def join(whole, devices):
    me = lax.axis_index("row")
    for stride, radix in reversed(strides(devices)):
        digit = me // stride % radix
        shares = [whole] + [swap(whole, k * stride, devices) for k in range(1, radix)]
        pieces = []
        for j in range(radix):
            piece = shares[0]
            for k in range(1, radix):
                piece = jnp.where(lax.bitwise_xor(digit, k) == j, shares[k], piece)
            pieces.append(piece)
        whole = jnp.concatenate(pieces, axis=0)
    return whole


def body(object_field, probe, amplitude, row_offsets, col_offsets, dealing):
    order = probe.shape[1]
    devices = lax.axis_size("row")
    own_rows, tile_cols = object_field.shape[1], object_field.shape[2]
    total_rows = devices * own_rows
    tile_rows = -(-own_rows // SUBLANES) * SUBLANES
    spare = tile_rows - own_rows
    if spare:
        object_field = jnp.pad(object_field, ((0, 0), (0, spare), (0, 0)))
    pieces, token = fetch_windows(object_field, dealing, col_offsets, order)
    strips = lax.all_to_all(pieces, "row", split_axis=0, concat_axis=0, tiled=True)
    cells = strips[:, :own_rows].reshape(total_rows, 2 * order)
    empty, blocks, owners, stock = prepare(
        dealing, col_offsets, token, probe, amplitude, object_field.shape
    )
    term, kept, sent = slot_terms(cells, stock, dealing, row_offsets, owners, order)
    total = sum_probe(kept, sent, devices)
    terms = pack_rows(term, dealing, row_offsets, devices, own_rows, tile_rows)
    terms, total = lax.optimization_barrier((terms, total))
    arrived = lax.all_to_all(terms, "row", split_axis=0, concat_axis=0, tiled=True)
    share = (total * (1.0 / dealing.shape[0])).astype(jnp.bfloat16)
    whole = join(share, devices).astype(jnp.float32)
    probe_grad = jnp.stack([whole[:, :order], whole[:, order:]])
    object_grad = place_windows(arrived, empty, blocks, owners, dealing, col_offsets, order)
    if spare:
        object_grad = object_grad[:, :own_rows]
    return (object_grad, probe_grad)


def solution(mesh):
    return jax.shard_map(
        body,
        mesh=mesh,
        in_specs=(
            P(None, ("groups", "row"), None),
            P("groups", None, None),
            P(("groups", "row"), None, None),
            P("groups"),
            P("groups"),
            P("groups"),
        ),
        out_specs=(P(None, ("groups", "row"), None), P("groups", None, None)),
        check_vma=False,
    )
```

```python
import functools
import math

import jax
import jax.numpy as jnp
import numpy as np
from jax import lax
from jax.experimental import pallas as pl
from jax.experimental.pallas import tpu as pltpu
from jax.sharding import PartitionSpec as P

MAG_FLOOR = 0.25
LANES = 128
SUBLANES = 8
SMEM = pl.BlockSpec(memory_space=pltpu.SMEM)
VMEM = pl.BlockSpec(memory_space=pltpu.VMEM)
ANY = pl.BlockSpec(memory_space=pl.ANY)


def dft_table(order):
    indices = np.arange(order, dtype=np.int32)
    phases = indices[:, None] * indices[None, :] % order
    angles = phases.astype(np.float32) * np.float32(2.0 * math.pi / order)
    factor = np.float32(1.0 / math.sqrt(order))
    return np.concatenate([np.cos(angles) * factor, -np.sin(angles) * factor], axis=1).astype(jnp.bfloat16)


def window_start(column, order, tile_cols):
    span = order + LANES
    base = jnp.minimum(column // LANES, (tile_cols - span) // LANES) * LANES
    return pl.multiple_of(base, LANES), column - base


def rows_from(ref, start, count):
    aligned = pl.multiple_of(start // SUBLANES * SUBLANES, SUBLANES)
    rest = start - aligned
    width = ref.shape[-1]
    blocks = ref[pl.ds(aligned, count + SUBLANES), :].reshape(-1, SUBLANES, width)
    turned = pltpu.roll(blocks, lax.rem(SUBLANES - rest, SUBLANES), 1)
    sub = lax.broadcasted_iota(jnp.int32, (1, SUBLANES, width), 1)
    picked = jnp.where(sub < SUBLANES - rest, turned[:-1], turned[1:])
    return picked.reshape(count, width)


def fetch_kernel(order, dealing, cols, tile, out, token, held, cut, sems, out_sems):
    token[0] = dealing[0]
    slots, tile_rows = out.shape[0], out.shape[1]
    tile_cols = tile.shape[2]
    span = order + LANES

    def copy(slot):
        base, _ = window_start(cols[dealing[slot]], order, tile_cols)
        return pltpu.make_async_copy(tile.at[:, :, pl.ds(base, span)], held.at[slot], sems.at[slot])

    @pl.loop(0, slots)
    def _(slot):
        copy(slot).start()

    lane = lax.broadcasted_iota(jnp.int32, (tile_rows, LANES), 1)

    def cut_slot(slot):
        copy(slot).wait()
        _, offset = window_start(cols[dealing[slot]], order, tile_cols)
        shift = lax.rem(LANES - lax.rem(offset, LANES), LANES)
        for part in range(2):
            turned = [
                pltpu.roll(held[slot, part, :, b * LANES : (b + 1) * LANES].astype(out.dtype), shift, 1)
                for b in range(span // LANES)
            ]
            for b in range(order // LANES):
                first = part * order + b * LANES
                cut[slot, :, first : first + LANES] = jnp.where(lane < LANES - offset, turned[b], turned[b + 1])

    group = slots // out_sems.shape[0]
    sends = []
    for g in range(out_sems.shape[0]):

        @pl.loop(g * group, (g + 1) * group, unroll=4)
        def _(slot):
            cut_slot(slot)

        here = slice(g * group, (g + 1) * group)
        send = pltpu.make_async_copy(cut.at[here], out.at[here], out_sems.at[g])
        send.start()
        sends.append(send)
    for send in sends:
        send.wait()


def fetch_windows(tile, dealing, cols, order):
    slots, tile_rows, tile_cols = dealing.shape[0], tile.shape[1], tile.shape[2]
    span = order + LANES

    return pl.pallas_call(
        functools.partial(fetch_kernel, order),
        out_shape=(
            jax.ShapeDtypeStruct((slots, tile_rows, 2 * order), jnp.bfloat16),
            jax.ShapeDtypeStruct((1,), jnp.int32),
        ),
        in_specs=[SMEM, SMEM, ANY],
        out_specs=(ANY, SMEM),
        scratch_shapes=[
            pltpu.VMEM((slots, 2, tile_rows, span), jnp.float32),
            pltpu.VMEM((slots, tile_rows, 2 * order), jnp.bfloat16),
            pltpu.SemaphoreType.DMA((slots,)),
            pltpu.SemaphoreType.DMA((4,)),
        ],
        compiler_params=pltpu.CompilerParams(vmem_limit_bytes=56 * 2**20),
        cost_estimate=pl.CostEstimate(flops=0, bytes_accessed=6 * 2**20, transcendentals=0),
        name="fetch",
    )(dealing, cols, tile)


def stock_places(stock, order):
    return (
        stock.at[0:order, 0:order],
        stock.at[0:order, order : 2 * order],
        stock.at[order : 2 * order, :],
        stock.at[2 * order : 3 * order, 0:order],
    )


def prepare_kernel(
    order, dealing, cols, token, table_in, probe, measured,
    empty, blocks, owners, stock,
    table, zeros, sems, stock_sems,
):
    del token
    places = stock_places(stock, order)
    sources = (probe.at[0], probe.at[1], table_in, measured.at[0])
    fills = []
    for k, (source, place) in enumerate(zip(sources, places)):
        fill = pltpu.make_async_copy(source, place, stock_sems.at[k])
        fill.start()
        fills.append(fill)
    count = (order + LANES) // LANES
    slots = dealing.shape[0]
    tile_cols = empty.shape[2]
    width = zeros.shape[2]
    zeros[...] = jnp.zeros_like(zeros)
    for b in range(tile_cols // width):
        fill = pltpu.make_async_copy(zeros, empty.at[:, :, b * width : (b + 1) * width], sems.at[b])
        fill.start()
        fills.append(fill)

    @pl.loop(0, tile_cols // LANES)
    def _(block):
        table[block] = -1

    @pl.loop(0, slots)
    def _(slot):
        base, _ = window_start(cols[dealing[slot]], order, tile_cols)
        for b in range(count):
            number = slot * count + b
            block = base // LANES + b
            blocks[number] = block
            known = table[block]
            owner = jnp.where(known < 0, number, known)
            owners[number] = owner
            table[block] = owner

    for fill in fills:
        fill.wait()


def prepare(dealing, cols, token, probe, measured, tile_shape):
    order = probe.shape[1]
    slots = dealing.shape[0]
    numbers = slots * (order + LANES) // LANES
    fill_cols = 2048
    return pl.pallas_call(
        functools.partial(prepare_kernel, order),
        out_shape=(
            jax.ShapeDtypeStruct(tile_shape, jnp.float32),
            jax.ShapeDtypeStruct((numbers,), jnp.int32),
            jax.ShapeDtypeStruct((numbers,), jnp.int32),
            jax.ShapeDtypeStruct((48 * order, 2 * order), jnp.bfloat16),
        ),
        in_specs=[SMEM, SMEM, SMEM, ANY, ANY, ANY],
        out_specs=(ANY, SMEM, SMEM, ANY),
        scratch_shapes=[
            pltpu.SMEM((tile_shape[2] // LANES,), jnp.int32),
            pltpu.VMEM(tile_shape[:2] + (fill_cols,), jnp.float32),
            pltpu.SemaphoreType.DMA((tile_shape[2] // fill_cols,)),
            pltpu.SemaphoreType.DMA((4,)),
        ],
        compiler_params=pltpu.CompilerParams(vmem_limit_bytes=8 * 2**20),
        cost_estimate=pl.CostEstimate(flops=0, bytes_accessed=110 * 2**20, transcendentals=0),
        name="prepare",
    )(dealing, cols, token, jnp.asarray(dft_table(order)), probe, measured)


def slot_kernel(
    dealing, rows, owners, cells, stock,
    term, kept, sent,
    wide, patch, wave, half, resid, turned, mine, probe, table, minus, measured, sems,
):
    del owners
    order = term.shape[0]
    places = (stock.at[0:order, :],) + stock_places(stock, order)[2:]
    targets = (probe, table, measured)
    loads = [
        pltpu.make_async_copy(source, target, sems.at[k])
        for k, (source, target) in enumerate(zip(places, targets))
    ]
    for load in loads:
        load.start()
    total_rows = cells.shape[0]
    me = lax.axis_index("row")
    first_row = rows[dealing[me]]
    step = 64
    tile = 256

    wide[0:total_rows, :] = cells[...].astype(jnp.float32)
    wide[total_rows:, :] = jnp.zeros((SUBLANES, 2 * order), jnp.float32)

    @pl.loop(0, order // step, unroll=2)
    def _(i):
        place = pl.ds(pl.multiple_of(i * step, step), step)
        patch[place, :] = rows_from(wide, first_row + i * step, step).astype(patch.dtype)

    loads[0].wait()

    @pl.loop(0, order // step, unroll=2)
    def _(i):
        place = pl.ds(pl.multiple_of(i * step, step), step)
        found = patch[place, :].astype(jnp.float32)
        real, imag = found[:, :order], found[:, order:]
        probe_real = probe[place, :order].astype(jnp.float32)
        probe_imag = probe[place, order:].astype(jnp.float32)
        wave[place, :order] = (probe_real * real - probe_imag * imag).astype(wave.dtype)
        wave[place, order:] = (probe_real * imag + probe_imag * real).astype(wave.dtype)

    loads[1].wait()
    minus[...] = -table[:, order:]
    cos, sin = table.at[:, :order], table.at[:, order:]
    first_half, second_half = slice(0, order), slice(order, 2 * order)

    def dots(a, b, c, d):
        one = jnp.dot(a, b, preferred_element_type=jnp.float32)
        return one + jnp.dot(c, d, preferred_element_type=jnp.float32)

    for first in range(0, order, tile):
        here = slice(first, first + tile)
        real, imag = wave[:, first_half], wave[:, second_half]
        half[first_half, here] = dots(real, cos[:, here], imag, minus[:, here]).astype(half.dtype)
        half[second_half, here] = dots(real, sin[:, here], imag, cos[:, here]).astype(half.dtype)
    loads[2].wait()
    for first in range(0, order, tile):
        here = slice(first, first + tile)
        there = slice(order + first, order + first + tile)
        for top in range(0, order, tile):
            line = slice(top, top + tile)
            half_real, half_imag = half[first_half, here], half[second_half, here]
            real = dots(cos[line, :], half_real, minus[line, :], half_imag)
            imag = dots(sin[line, :], half_real, cos[line, :], half_imag)
            inverse = jnp.minimum(lax.rsqrt(real * real + imag * imag), 1.0 / MAG_FLOOR)
            shrink = 1.0 - measured[line, here].astype(jnp.float32) * inverse
            resid[line, here] = (real * shrink).astype(resid.dtype)
            resid[line, there] = (imag * shrink).astype(resid.dtype)
    for first in range(0, order, tile):
        here = slice(first, first + tile)
        real, imag = resid[:, first_half], resid[:, second_half]
        turned[first_half, here] = dots(real, cos[:, here], imag, sin[:, here]).astype(turned.dtype)
        turned[second_half, here] = dots(real, minus[:, here], imag, cos[:, here]).astype(turned.dtype)
    for first in range(0, order, tile):
        here = slice(first, first + tile)
        there = slice(order + first, order + first + tile)
        for top in range(0, order, tile):
            line = slice(top, top + tile)
            turned_real, turned_imag = turned[first_half, here], turned[second_half, here]
            real = dots(cos[line, :], turned_real, sin[line, :], turned_imag)
            imag = dots(minus[line, :], turned_real, cos[line, :], turned_imag)
            probe_real = probe[line, here].astype(jnp.float32)
            probe_imag = probe[line, there].astype(jnp.float32)
            term[line, here] = (probe_real * real + probe_imag * imag).astype(term.dtype)
            term[line, there] = (probe_real * imag - probe_imag * real).astype(term.dtype)
            patch_real = patch[line, here].astype(jnp.float32)
            patch_imag = patch[line, there].astype(jnp.float32)
            mine[line, here] = patch_real * real + patch_imag * imag
            mine[line, there] = patch_real * imag - patch_imag * real

    count = kept.shape[0]
    side = lax.rem(me, 2)
    kept[...] = mine[pl.ds(pl.multiple_of(side * count, count), count), :]
    sent[...] = mine[pl.ds(pl.multiple_of((1 - side) * count, count), count), :].astype(sent.dtype)

def slot_terms(cells, stock, dealing, rows, owners, order):
    total_rows = cells.shape[0]
    wide_cols = 2 * order
    bf16, f32 = jnp.bfloat16, jnp.float32
    return pl.pallas_call(
        slot_kernel,
        out_shape=(
            jax.ShapeDtypeStruct((order, wide_cols), bf16),
            jax.ShapeDtypeStruct((order // 2, wide_cols), f32),
            jax.ShapeDtypeStruct((order // 2, wide_cols), bf16),
        ),
        in_specs=[SMEM, SMEM, SMEM, VMEM, ANY],
        out_specs=(VMEM,) * 3,
        scratch_shapes=[
            pltpu.VMEM((total_rows + SUBLANES, wide_cols), f32),
            pltpu.VMEM((order, wide_cols), bf16),
            pltpu.VMEM((order, wide_cols), bf16),
            pltpu.VMEM((wide_cols, order), bf16),
            pltpu.VMEM((order, wide_cols), bf16),
            pltpu.VMEM((wide_cols, order), bf16),
            pltpu.VMEM((order, wide_cols), f32),
            pltpu.VMEM((order, wide_cols), bf16),
            pltpu.VMEM((order, wide_cols), bf16),
            pltpu.VMEM((order, order), bf16),
            pltpu.VMEM((order, order), bf16),
            pltpu.SemaphoreType.DMA((3,)),
        ],
        compiler_params=pltpu.CompilerParams(vmem_limit_bytes=24 * 2**20),
        cost_estimate=pl.CostEstimate(
            flops=8 * 2 * order**3 * 2, bytes_accessed=8 * 2**20, transcendentals=order * order
        ),
        name="slot",
    )(dealing, rows, owners, cells, stock)


def pack_kernel(reach, own_rows, dealing, rows, term, out, padded):
    order = term.shape[0]
    first_row = rows[dealing[lax.axis_index("row")]]
    below = padded.shape[0] - reach - order
    padded[0:reach, :] = jnp.zeros((reach, padded.shape[1]), jnp.float32)
    padded[reach : reach + order, :] = term[...].astype(jnp.float32)
    padded[reach + order :, :] = jnp.zeros((below, padded.shape[1]), jnp.float32)

    @pl.loop(0, out.shape[0], unroll=2)
    def _(k):
        out[k] = rows_from(padded, reach - first_row + k * own_rows, out.shape[1]).astype(out.dtype)


def pack_rows(term, dealing, rows, slots, own_rows, tile_rows):
    order, width = term.shape
    reach = slots * own_rows - order
    return pl.pallas_call(
        functools.partial(pack_kernel, reach, own_rows),
        out_shape=jax.ShapeDtypeStruct((slots, tile_rows, width), jnp.bfloat16),
        in_specs=[SMEM, SMEM, VMEM],
        out_specs=VMEM,
        scratch_shapes=[pltpu.VMEM((2 * reach + order + tile_rows + SUBLANES, width), jnp.float32)],
        compiler_params=pltpu.CompilerParams(vmem_limit_bytes=8 * 2**20),
        cost_estimate=pl.CostEstimate(flops=0, bytes_accessed=3 * 2**20, transcendentals=0),
        name="pack",
    )(dealing, rows, term)


def place_kernel(order, dealing, cols, blocks, owners, terms, empty, out, totals, sems):
    del empty
    slots, tile_rows = terms.shape[0], terms.shape[1]
    count = (order + LANES) // LANES
    totals[...] = jnp.zeros_like(totals)
    lane = lax.broadcasted_iota(jnp.int32, (tile_rows, LANES), 1)
    nothing = jnp.zeros((tile_rows, LANES), jnp.float32)

    @pl.loop(0, slots, unroll=4)
    def _(slot):
        _, offset = window_start(cols[dealing[slot]], order, out.shape[2])
        shift = lax.rem(offset, LANES)
        for part in range(2):
            turned = []
            for b in range(count - 1):
                first = part * order + b * LANES
                turned.append(pltpu.roll(terms[slot, :, first : first + LANES], shift, 1).astype(jnp.float32))
            for b in range(count):
                before = turned[b - 1] if b else nothing
                after = turned[b] if b < count - 1 else nothing
                owner = owners[slot * count + b]
                totals[owner, part] += jnp.where(lane < offset, before, after)

    def copy(number):
        place = pl.multiple_of(blocks[number] * LANES, LANES)
        return pltpu.make_async_copy(totals.at[number], out.at[:, :, pl.ds(place, LANES)], sems.at[number])

    @pl.loop(0, slots * count)
    def _(number):
        @pl.when(owners[number] == number)
        def _():
            copy(number).start()

    @pl.loop(0, slots * count)
    def _(number):
        @pl.when(owners[number] == number)
        def _():
            copy(number).wait()


def place_windows(terms, empty, blocks, owners, dealing, cols, order):
    slots, tile_rows = terms.shape[0], terms.shape[1]
    count = (order + LANES) // LANES
    return pl.pallas_call(
        functools.partial(place_kernel, order),
        out_shape=jax.ShapeDtypeStruct(empty.shape, empty.dtype),
        in_specs=[SMEM, SMEM, SMEM, SMEM, VMEM, ANY],
        out_specs=ANY,
        scratch_shapes=[
            pltpu.VMEM((slots * count, 2, tile_rows, LANES), jnp.float32),
            pltpu.SemaphoreType.DMA((slots * count,)),
        ],
        input_output_aliases={5: 0},
        compiler_params=pltpu.CompilerParams(vmem_limit_bytes=12 * 2**20),
        cost_estimate=pl.CostEstimate(flops=0, bytes_accessed=6 * 2**20, transcendentals=0),
        name="place",
    )(dealing, cols, blocks, owners, terms, empty)


def strides(devices):
    steps, stride = [], 1
    while stride < devices:
        radix = 4 if len(steps) >= 2 and (devices // stride) % 4 == 0 else 2
        steps.append((stride, radix))
        stride *= radix
    return steps


def swap(x, distance, devices):
    return lax.ppermute(x, "row", [(d, d ^ distance) for d in range(devices)])


def sum_probe(kept, sent, devices):
    me = lax.axis_index("row")
    addends = [kept, swap(sent, 1, devices)]

    def rows(index, count):
        found = [lax.dynamic_slice_in_dim(x, index * count, count).astype(jnp.float32) for x in addends]
        return found[0] + found[1]

    for stride, radix in strides(devices)[1:]:
        digit = me // stride % radix
        count = addends[0].shape[0] // radix
        met = []
        for k in range(1, radix):
            share = rows(lax.bitwise_xor(digit, k), count).astype(jnp.bfloat16)
            met.append(swap(share, k * stride, devices))
        own = rows(digit, count)
        for one in met[:-1]:
            own = own + one.astype(jnp.float32)
        addends = [own, met[-1]]
    return addends[0] + addends[1].astype(jnp.float32)


def join(whole, devices):
    me = lax.axis_index("row")
    for stride, radix in reversed(strides(devices)):
        digit = me // stride % radix
        shares = [whole] + [swap(whole, k * stride, devices) for k in range(1, radix)]
        pieces = []
        for j in range(radix):
            piece = shares[0]
            for k in range(1, radix):
                piece = jnp.where(lax.bitwise_xor(digit, k) == j, shares[k], piece)
            pieces.append(piece)
        whole = jnp.concatenate(pieces, axis=0)
    return whole


def body(object_field, probe, amplitude, row_offsets, col_offsets, dealing):
    order = probe.shape[1]
    devices = lax.axis_size("row")
    own_rows, tile_cols = object_field.shape[1], object_field.shape[2]
    total_rows = devices * own_rows
    tile_rows = -(-own_rows // SUBLANES) * SUBLANES
    spare = tile_rows - own_rows
    if spare:
        object_field = jnp.pad(object_field, ((0, 0), (0, spare), (0, 0)))
    pieces, token = fetch_windows(object_field, dealing, col_offsets, order)
    strips = lax.all_to_all(pieces, "row", split_axis=0, concat_axis=0, tiled=True)
    cells = strips[:, :own_rows].reshape(total_rows, 2 * order)
    empty, blocks, owners, stock = prepare(
        dealing, col_offsets, token, probe, amplitude, object_field.shape
    )
    term, kept, sent = slot_terms(cells, stock, dealing, row_offsets, owners, order)
    total = sum_probe(kept, sent, devices)
    terms = pack_rows(term, dealing, row_offsets, devices, own_rows, tile_rows)
    terms, total = lax.optimization_barrier((terms, total))
    arrived = lax.all_to_all(terms, "row", split_axis=0, concat_axis=0, tiled=True)
    share = (total * (1.0 / dealing.shape[0])).astype(jnp.bfloat16)
    whole = join(share, devices).astype(jnp.float32)
    probe_grad = jnp.stack([whole[:, :order], whole[:, order:]])
    object_grad = place_windows(arrived, empty, blocks, owners, dealing, col_offsets, order)
    if spare:
        object_grad = object_grad[:, :own_rows]
    return (object_grad, probe_grad)


def solution(mesh):
    return jax.shard_map(
        body,
        mesh=mesh,
        in_specs=(
            P(None, ("groups", "row"), None),
            P("groups", None, None),
            P(("groups", "row"), None, None),
            P("groups"),
            P("groups"),
            P("groups"),
        ),
        out_specs=(P(None, ("groups", "row"), None), P("groups", None, None)),
        check_vma=False,
    )
```

```python
import functools
import math

import jax
import jax.numpy as jnp
import numpy as np
from jax import lax
from jax.experimental import pallas as pl
from jax.experimental.pallas import tpu as pltpu
from jax.sharding import PartitionSpec as P

MAG_FLOOR = 0.25
LANES = 128
SUBLANES = 8
SMEM = pl.BlockSpec(memory_space=pltpu.SMEM)
VMEM = pl.BlockSpec(memory_space=pltpu.VMEM)
ANY = pl.BlockSpec(memory_space=pl.ANY)


def dft_table(order):
    indices = np.arange(order, dtype=np.int32)
    phases = indices[:, None] * indices[None, :] % order
    angles = phases.astype(np.float32) * np.float32(2.0 * math.pi / order)
    factor = np.float32(1.0 / math.sqrt(order))
    return np.concatenate([np.cos(angles) * factor, -np.sin(angles) * factor], axis=1).astype(jnp.bfloat16)


def window_start(column, order, tile_cols):
    span = order + LANES
    base = jnp.minimum(column // LANES, (tile_cols - span) // LANES) * LANES
    return pl.multiple_of(base, LANES), column - base


def rows_from(ref, start, count):
    aligned = pl.multiple_of(start // SUBLANES * SUBLANES, SUBLANES)
    rest = start - aligned
    width = ref.shape[-1]
    blocks = ref[pl.ds(aligned, count + SUBLANES), :].reshape(-1, SUBLANES, width)
    turned = pltpu.roll(blocks, lax.rem(SUBLANES - rest, SUBLANES), 1)
    sub = lax.broadcasted_iota(jnp.int32, (1, SUBLANES, width), 1)
    picked = jnp.where(sub < SUBLANES - rest, turned[:-1], turned[1:])
    return picked.reshape(count, width)


def fetch_kernel(order, dealing, cols, tile, out, token, held, sems):
    token[0] = dealing[0]
    slots, tile_rows = out.shape[0], out.shape[1]
    tile_cols = tile.shape[2]
    span = order + LANES

    def copy(slot):
        base, _ = window_start(cols[dealing[slot]], order, tile_cols)
        return pltpu.make_async_copy(tile.at[:, :, pl.ds(base, span)], held.at[slot], sems.at[slot])

    @pl.loop(0, slots)
    def _(slot):
        copy(slot).start()

    lane = lax.broadcasted_iota(jnp.int32, (tile_rows, LANES), 1)

    @pl.loop(0, slots, unroll=4)
    def _(slot):
        copy(slot).wait()
        _, offset = window_start(cols[dealing[slot]], order, tile_cols)
        shift = lax.rem(LANES - lax.rem(offset, LANES), LANES)
        for part in range(2):
            turned = [
                pltpu.roll(held[slot, part, :, b * LANES : (b + 1) * LANES].astype(out.dtype), shift, 1)
                for b in range(span // LANES)
            ]
            for b in range(order // LANES):
                first = part * order + b * LANES
                cells = jnp.where(lane < LANES - offset, turned[b], turned[b + 1])
                out[slot, :, first : first + LANES] = cells


def fetch_windows(tile, dealing, cols, order):
    slots, tile_rows, tile_cols = dealing.shape[0], tile.shape[1], tile.shape[2]
    span = order + LANES

    return pl.pallas_call(
        functools.partial(fetch_kernel, order),
        out_shape=(
            jax.ShapeDtypeStruct((slots, tile_rows, 2 * order), jnp.bfloat16),
            jax.ShapeDtypeStruct((1,), jnp.int32),
        ),
        in_specs=[SMEM, SMEM, ANY],
        out_specs=(VMEM, SMEM),
        scratch_shapes=[
            pltpu.VMEM((slots, 2, tile_rows, span), jnp.float32),
            pltpu.SemaphoreType.DMA((slots,)),
        ],
        compiler_params=pltpu.CompilerParams(vmem_limit_bytes=56 * 2**20),
        cost_estimate=pl.CostEstimate(flops=0, bytes_accessed=6 * 2**20, transcendentals=0),
        name="fetch",
    )(dealing, cols, tile)


def stock_places(stock, order):
    return (
        stock.at[0:order, 0:order],
        stock.at[0:order, order : 2 * order],
        stock.at[order : 2 * order, :],
        stock.at[2 * order : 3 * order, 0:order],
    )


def prepare_kernel(
    order, dealing, cols, token, table_in, probe, measured,
    empty, blocks, owners, stock,
    table, zeros, sems, stock_sems,
):
    del token
    places = stock_places(stock, order)
    sources = (probe.at[0], probe.at[1], table_in, measured.at[0])
    fills = []
    for k, (source, place) in enumerate(zip(sources, places)):
        fill = pltpu.make_async_copy(source, place, stock_sems.at[k])
        fill.start()
        fills.append(fill)
    count = (order + LANES) // LANES
    slots = dealing.shape[0]
    tile_cols = empty.shape[2]
    width = zeros.shape[2]
    zeros[...] = jnp.zeros_like(zeros)
    for b in range(tile_cols // width):
        fill = pltpu.make_async_copy(zeros, empty.at[:, :, b * width : (b + 1) * width], sems.at[b])
        fill.start()
        fills.append(fill)

    @pl.loop(0, tile_cols // LANES)
    def _(block):
        table[block] = -1

    @pl.loop(0, slots)
    def _(slot):
        base, _ = window_start(cols[dealing[slot]], order, tile_cols)
        for b in range(count):
            number = slot * count + b
            block = base // LANES + b
            blocks[number] = block
            known = table[block]
            owner = jnp.where(known < 0, number, known)
            owners[number] = owner
            table[block] = owner

    for fill in fills:
        fill.wait()


def prepare(dealing, cols, token, probe, measured, tile_shape):
    order = probe.shape[1]
    slots = dealing.shape[0]
    numbers = slots * (order + LANES) // LANES
    fill_cols = 2048
    return pl.pallas_call(
        functools.partial(prepare_kernel, order),
        out_shape=(
            jax.ShapeDtypeStruct(tile_shape, jnp.float32),
            jax.ShapeDtypeStruct((numbers,), jnp.int32),
            jax.ShapeDtypeStruct((numbers,), jnp.int32),
            jax.ShapeDtypeStruct((48 * order, 2 * order), jnp.bfloat16),
        ),
        in_specs=[SMEM, SMEM, SMEM, ANY, ANY, ANY],
        out_specs=(ANY, SMEM, SMEM, ANY),
        scratch_shapes=[
            pltpu.SMEM((tile_shape[2] // LANES,), jnp.int32),
            pltpu.VMEM(tile_shape[:2] + (fill_cols,), jnp.float32),
            pltpu.SemaphoreType.DMA((tile_shape[2] // fill_cols,)),
            pltpu.SemaphoreType.DMA((4,)),
        ],
        compiler_params=pltpu.CompilerParams(vmem_limit_bytes=8 * 2**20),
        cost_estimate=pl.CostEstimate(flops=0, bytes_accessed=110 * 2**20, transcendentals=0),
        name="prepare",
    )(dealing, cols, token, jnp.asarray(dft_table(order)), probe, measured)


def slot_kernel(
    dealing, rows, owners, cells, stock,
    term, kept, sent,
    wide, patch, wave, half, resid, turned, leaving, probe, table, minus, measured, sems, leave_sem,
):
    del owners
    order = term.shape[0]
    places = (stock.at[0:order, :],) + stock_places(stock, order)[2:]
    targets = (probe, table, measured)
    loads = [
        pltpu.make_async_copy(source, target, sems.at[k])
        for k, (source, target) in enumerate(zip(places, targets))
    ]
    for load in loads:
        load.start()
    total_rows = cells.shape[0]
    me = lax.axis_index("row")
    first_row = rows[dealing[me]]
    step = 64
    tile = 256

    wide[0:total_rows, :] = cells[...].astype(jnp.float32)
    wide[total_rows:, :] = jnp.zeros((SUBLANES, 2 * order), jnp.float32)

    @pl.loop(0, order // step, unroll=2)
    def _(i):
        place = pl.ds(pl.multiple_of(i * step, step), step)
        patch[place, :] = rows_from(wide, first_row + i * step, step).astype(patch.dtype)

    loads[0].wait()

    @pl.loop(0, order // step, unroll=2)
    def _(i):
        place = pl.ds(pl.multiple_of(i * step, step), step)
        found = patch[place, :].astype(jnp.float32)
        real, imag = found[:, :order], found[:, order:]
        probe_real = probe[place, :order].astype(jnp.float32)
        probe_imag = probe[place, order:].astype(jnp.float32)
        wave[place, :order] = (probe_real * real - probe_imag * imag).astype(wave.dtype)
        wave[place, order:] = (probe_real * imag + probe_imag * real).astype(wave.dtype)

    loads[1].wait()
    minus[...] = -table[:, order:]
    cos, sin = table.at[:, :order], table.at[:, order:]
    first_half, second_half = slice(0, order), slice(order, 2 * order)

    def dots(a, b, c, d):
        one = jnp.dot(a, b, preferred_element_type=jnp.float32)
        return one + jnp.dot(c, d, preferred_element_type=jnp.float32)

    for first in range(0, order, tile):
        here = slice(first, first + tile)
        real, imag = wave[:, first_half], wave[:, second_half]
        half[first_half, here] = dots(real, cos[:, here], imag, minus[:, here]).astype(half.dtype)
        half[second_half, here] = dots(real, sin[:, here], imag, cos[:, here]).astype(half.dtype)
    loads[2].wait()
    for first in range(0, order, tile):
        here = slice(first, first + tile)
        there = slice(order + first, order + first + tile)
        for top in range(0, order, tile):
            line = slice(top, top + tile)
            half_real, half_imag = half[first_half, here], half[second_half, here]
            real = dots(cos[line, :], half_real, minus[line, :], half_imag)
            imag = dots(sin[line, :], half_real, cos[line, :], half_imag)
            inverse = jnp.minimum(lax.rsqrt(real * real + imag * imag), 1.0 / MAG_FLOOR)
            shrink = 1.0 - measured[line, here].astype(jnp.float32) * inverse
            resid[line, here] = (real * shrink).astype(resid.dtype)
            resid[line, there] = (imag * shrink).astype(resid.dtype)
    for first in range(0, order, tile):
        here = slice(first, first + tile)
        real, imag = resid[:, first_half], resid[:, second_half]
        turned[first_half, here] = dots(real, cos[:, here], imag, sin[:, here]).astype(turned.dtype)
        turned[second_half, here] = dots(real, minus[:, here], imag, cos[:, here]).astype(turned.dtype)
    count = order // 2
    side = lax.rem(me, 2)
    for number, target in ((1 - side, leaving), (side, kept)):
        line = pl.ds(pl.multiple_of(number * count, count), count)
        for first in range(0, order, tile):
            here = slice(first, first + tile)
            there = slice(order + first, order + first + tile)
            turned_real, turned_imag = turned[first_half, here], turned[second_half, here]
            real = dots(cos[line, :], turned_real, sin[line, :], turned_imag)
            imag = dots(minus[line, :], turned_real, cos[line, :], turned_imag)
            patch_real = patch[line, here].astype(jnp.float32)
            patch_imag = patch[line, there].astype(jnp.float32)
            target[:, here] = (patch_real * real + patch_imag * imag).astype(target.dtype)
            target[:, there] = (patch_real * imag - patch_imag * real).astype(target.dtype)
            probe_real = probe[line, here].astype(jnp.float32)
            probe_imag = probe[line, there].astype(jnp.float32)
            term[line, here] = (probe_real * real + probe_imag * imag).astype(term.dtype)
            term[line, there] = (probe_real * imag - probe_imag * real).astype(term.dtype)
        if target is leaving:
            leave = pltpu.make_async_copy(leaving, sent, leave_sem.at[0])
            leave.start()
    leave.wait()


def slot_terms(cells, stock, dealing, rows, owners, order):
    total_rows = cells.shape[0]
    wide_cols = 2 * order
    bf16, f32 = jnp.bfloat16, jnp.float32
    return pl.pallas_call(
        slot_kernel,
        out_shape=(
            jax.ShapeDtypeStruct((order, wide_cols), bf16),
            jax.ShapeDtypeStruct((order // 2, wide_cols), f32),
            jax.ShapeDtypeStruct((order // 2, wide_cols), bf16),
        ),
        in_specs=[SMEM, SMEM, SMEM, VMEM, ANY],
        out_specs=(VMEM, VMEM, ANY),
        scratch_shapes=[
            pltpu.VMEM((total_rows + SUBLANES, wide_cols), f32),
            pltpu.VMEM((order, wide_cols), bf16),
            pltpu.VMEM((order, wide_cols), bf16),
            pltpu.VMEM((wide_cols, order), bf16),
            pltpu.VMEM((order, wide_cols), bf16),
            pltpu.VMEM((wide_cols, order), bf16),
            pltpu.VMEM((order // 2, wide_cols), bf16),
            pltpu.VMEM((order, wide_cols), bf16),
            pltpu.VMEM((order, wide_cols), bf16),
            pltpu.VMEM((order, order), bf16),
            pltpu.VMEM((order, order), bf16),
            pltpu.SemaphoreType.DMA((3,)),
            pltpu.SemaphoreType.DMA((1,)),
        ],
        compiler_params=pltpu.CompilerParams(vmem_limit_bytes=24 * 2**20),
        cost_estimate=pl.CostEstimate(
            flops=8 * 2 * order**3 * 2, bytes_accessed=8 * 2**20, transcendentals=order * order
        ),
        name="slot",
    )(dealing, rows, owners, cells, stock)


def pack_kernel(reach, own_rows, dealing, rows, term, out, padded):
    order = term.shape[0]
    first_row = rows[dealing[lax.axis_index("row")]]
    below = padded.shape[0] - reach - order
    padded[0:reach, :] = jnp.zeros((reach, padded.shape[1]), jnp.float32)
    padded[reach : reach + order, :] = term[...].astype(jnp.float32)
    padded[reach + order :, :] = jnp.zeros((below, padded.shape[1]), jnp.float32)

    @pl.loop(0, out.shape[0], unroll=2)
    def _(k):
        out[k] = rows_from(padded, reach - first_row + k * own_rows, out.shape[1]).astype(out.dtype)


def pack_rows(term, dealing, rows, slots, own_rows, tile_rows):
    order, width = term.shape
    reach = slots * own_rows - order
    return pl.pallas_call(
        functools.partial(pack_kernel, reach, own_rows),
        out_shape=jax.ShapeDtypeStruct((slots, tile_rows, width), jnp.bfloat16),
        in_specs=[SMEM, SMEM, VMEM],
        out_specs=VMEM,
        scratch_shapes=[pltpu.VMEM((2 * reach + order + tile_rows + SUBLANES, width), jnp.float32)],
        compiler_params=pltpu.CompilerParams(vmem_limit_bytes=8 * 2**20),
        cost_estimate=pl.CostEstimate(flops=0, bytes_accessed=3 * 2**20, transcendentals=0),
        name="pack",
    )(dealing, rows, term)


def place_kernel(order, dealing, cols, blocks, owners, terms, empty, out, totals, sems):
    del empty
    slots, tile_rows = terms.shape[0], terms.shape[1]
    count = (order + LANES) // LANES
    totals[...] = jnp.zeros_like(totals)
    lane = lax.broadcasted_iota(jnp.int32, (tile_rows, LANES), 1)
    nothing = jnp.zeros((tile_rows, LANES), jnp.float32)

    @pl.loop(0, slots, unroll=4)
    def _(slot):
        _, offset = window_start(cols[dealing[slot]], order, out.shape[2])
        shift = lax.rem(offset, LANES)
        for part in range(2):
            turned = []
            for b in range(count - 1):
                first = part * order + b * LANES
                turned.append(pltpu.roll(terms[slot, :, first : first + LANES], shift, 1).astype(jnp.float32))
            for b in range(count):
                before = turned[b - 1] if b else nothing
                after = turned[b] if b < count - 1 else nothing
                owner = owners[slot * count + b]
                totals[owner, part] += jnp.where(lane < offset, before, after)

    def copy(number):
        place = pl.multiple_of(blocks[number] * LANES, LANES)
        return pltpu.make_async_copy(totals.at[number], out.at[:, :, pl.ds(place, LANES)], sems.at[number])

    @pl.loop(0, slots * count)
    def _(number):
        @pl.when(owners[number] == number)
        def _():
            copy(number).start()

    @pl.loop(0, slots * count)
    def _(number):
        @pl.when(owners[number] == number)
        def _():
            copy(number).wait()


def place_windows(terms, empty, blocks, owners, dealing, cols, order):
    slots, tile_rows = terms.shape[0], terms.shape[1]
    count = (order + LANES) // LANES
    return pl.pallas_call(
        functools.partial(place_kernel, order),
        out_shape=jax.ShapeDtypeStruct(empty.shape, empty.dtype),
        in_specs=[SMEM, SMEM, SMEM, SMEM, VMEM, ANY],
        out_specs=ANY,
        scratch_shapes=[
            pltpu.VMEM((slots * count, 2, tile_rows, LANES), jnp.float32),
            pltpu.SemaphoreType.DMA((slots * count,)),
        ],
        input_output_aliases={5: 0},
        compiler_params=pltpu.CompilerParams(vmem_limit_bytes=12 * 2**20),
        cost_estimate=pl.CostEstimate(flops=0, bytes_accessed=6 * 2**20, transcendentals=0),
        name="place",
    )(dealing, cols, blocks, owners, terms, empty)


def strides(devices):
    steps, stride = [], 1
    while stride < devices:
        radix = 4 if len(steps) >= 2 and (devices // stride) % 4 == 0 else 2
        steps.append((stride, radix))
        stride *= radix
    return steps


def swap(x, distance, devices):
    return lax.ppermute(x, "row", [(d, d ^ distance) for d in range(devices)])


def sum_probe(kept, sent, devices):
    me = lax.axis_index("row")
    addends = [kept, swap(sent, 1, devices)]

    def rows(index, count):
        found = [lax.dynamic_slice_in_dim(x, index * count, count).astype(jnp.float32) for x in addends]
        return found[0] + found[1]

    for stride, radix in strides(devices)[1:]:
        digit = me // stride % radix
        count = addends[0].shape[0] // radix
        met = []
        for k in range(1, radix):
            share = rows(lax.bitwise_xor(digit, k), count).astype(jnp.bfloat16)
            met.append(swap(share, k * stride, devices))
        own = rows(digit, count)
        for one in met[:-1]:
            own = own + one.astype(jnp.float32)
        addends = [own, met[-1]]
    return addends[0] + addends[1].astype(jnp.float32)


def join(whole, devices):
    me = lax.axis_index("row")
    for stride, radix in reversed(strides(devices)):
        digit = me // stride % radix
        shares = [whole] + [swap(whole, k * stride, devices) for k in range(1, radix)]
        pieces = []
        for j in range(radix):
            piece = shares[0]
            for k in range(1, radix):
                piece = jnp.where(lax.bitwise_xor(digit, k) == j, shares[k], piece)
            pieces.append(piece)
        whole = jnp.concatenate(pieces, axis=0)
    return whole


def body(object_field, probe, amplitude, row_offsets, col_offsets, dealing):
    order = probe.shape[1]
    devices = lax.axis_size("row")
    own_rows, tile_cols = object_field.shape[1], object_field.shape[2]
    total_rows = devices * own_rows
    tile_rows = -(-own_rows // SUBLANES) * SUBLANES
    spare = tile_rows - own_rows
    if spare:
        object_field = jnp.pad(object_field, ((0, 0), (0, spare), (0, 0)))
    pieces, token = fetch_windows(object_field, dealing, col_offsets, order)
    strips = lax.all_to_all(pieces, "row", split_axis=0, concat_axis=0, tiled=True)
    cells = strips[:, :own_rows].reshape(total_rows, 2 * order)
    empty, blocks, owners, stock = prepare(
        dealing, col_offsets, token, probe, amplitude, object_field.shape
    )
    term, kept, sent = slot_terms(cells, stock, dealing, row_offsets, owners, order)
    total = sum_probe(kept, sent, devices)
    terms = pack_rows(term, dealing, row_offsets, devices, own_rows, tile_rows)
    terms, total = lax.optimization_barrier((terms, total))
    arrived = lax.all_to_all(terms, "row", split_axis=0, concat_axis=0, tiled=True)
    share = (total * (1.0 / dealing.shape[0])).astype(jnp.bfloat16)
    whole = join(share, devices).astype(jnp.float32)
    probe_grad = jnp.stack([whole[:, :order], whole[:, order:]])
    object_grad = place_windows(arrived, empty, blocks, owners, dealing, col_offsets, order)
    if spare:
        object_grad = object_grad[:, :own_rows]
    return (object_grad, probe_grad)


def solution(mesh):
    return jax.shard_map(
        body,
        mesh=mesh,
        in_specs=(
            P(None, ("groups", "row"), None),
            P("groups", None, None),
            P(("groups", "row"), None, None),
            P("groups"),
            P("groups"),
            P("groups"),
        ),
        out_specs=(P(None, ("groups", "row"), None), P("groups", None, None)),
        check_vma=False,
    )
```

```python
import functools
import math

import jax
import jax.numpy as jnp
import numpy as np
from jax import lax
from jax.experimental import pallas as pl
from jax.experimental.pallas import tpu as pltpu
from jax.sharding import PartitionSpec as P

MAG_FLOOR = 0.25
LANES = 128
SUBLANES = 8
SMEM = pl.BlockSpec(memory_space=pltpu.SMEM)
VMEM = pl.BlockSpec(memory_space=pltpu.VMEM)
ANY = pl.BlockSpec(memory_space=pl.ANY)


def dft_table(order):
    indices = np.arange(order, dtype=np.int32)
    phases = indices[:, None] * indices[None, :] % order
    angles = phases.astype(np.float32) * np.float32(2.0 * math.pi / order)
    factor = np.float32(1.0 / math.sqrt(order))
    return np.concatenate([np.cos(angles) * factor, -np.sin(angles) * factor], axis=1).astype(jnp.bfloat16)


def window_start(column, order, tile_cols):
    span = order + LANES
    base = jnp.minimum(column // LANES, (tile_cols - span) // LANES) * LANES
    return pl.multiple_of(base, LANES), column - base


def rows_from(ref, start, count):
    aligned = pl.multiple_of(start // SUBLANES * SUBLANES, SUBLANES)
    rest = start - aligned
    width = ref.shape[-1]
    blocks = ref[pl.ds(aligned, count + SUBLANES), :].reshape(-1, SUBLANES, width)
    turned = pltpu.roll(blocks, lax.rem(SUBLANES - rest, SUBLANES), 1)
    sub = lax.broadcasted_iota(jnp.int32, (1, SUBLANES, width), 1)
    picked = jnp.where(sub < SUBLANES - rest, turned[:-1], turned[1:])
    return picked.reshape(count, width)


def fetch_kernel(order, dealing, cols, tile, out, token, held, sems):
    token[0] = dealing[0]
    slots, tile_rows = out.shape[0], out.shape[1]
    tile_cols = tile.shape[2]
    span = order + LANES

    def copy(slot):
        base, _ = window_start(cols[dealing[slot]], order, tile_cols)
        return pltpu.make_async_copy(tile.at[:, :, pl.ds(base, span)], held.at[slot], sems.at[slot])

    @pl.loop(0, slots)
    def _(slot):
        copy(slot).start()

    lane = lax.broadcasted_iota(jnp.int32, (tile_rows, LANES), 1)

    @pl.loop(0, slots, unroll=4)
    def _(slot):
        copy(slot).wait()
        _, offset = window_start(cols[dealing[slot]], order, tile_cols)
        shift = lax.rem(LANES - lax.rem(offset, LANES), LANES)
        for part in range(2):
            turned = [
                pltpu.roll(held[slot, part, :, b * LANES : (b + 1) * LANES].astype(out.dtype), shift, 1)
                for b in range(span // LANES)
            ]
            for b in range(order // LANES):
                first = part * order + b * LANES
                cells = jnp.where(lane < LANES - offset, turned[b], turned[b + 1])
                out[slot, :, first : first + LANES] = cells


def fetch_windows(tile, dealing, cols, order):
    slots, tile_rows, tile_cols = dealing.shape[0], tile.shape[1], tile.shape[2]
    span = order + LANES

    return pl.pallas_call(
        functools.partial(fetch_kernel, order),
        out_shape=(
            jax.ShapeDtypeStruct((slots, tile_rows, 2 * order), jnp.bfloat16),
            jax.ShapeDtypeStruct((1,), jnp.int32),
        ),
        in_specs=[SMEM, SMEM, ANY],
        out_specs=(VMEM, SMEM),
        scratch_shapes=[
            pltpu.VMEM((slots, 2, tile_rows, span), jnp.float32),
            pltpu.SemaphoreType.DMA((slots,)),
        ],
        compiler_params=pltpu.CompilerParams(vmem_limit_bytes=56 * 2**20),
        cost_estimate=pl.CostEstimate(flops=0, bytes_accessed=6 * 2**20, transcendentals=0),
        name="fetch",
    )(dealing, cols, tile)


def stock_places(stock, order):
    return (
        stock.at[0:order, 0:order],
        stock.at[0:order, order : 2 * order],
        stock.at[order : 2 * order, :],
        stock.at[2 * order : 3 * order, 0:order],
    )


def prepare_kernel(
    order, dealing, cols, token, table_in, probe, measured,
    empty, blocks, owners, stock,
    table, zeros, sems, stock_sems,
):
    del token
    places = stock_places(stock, order)
    sources = (probe.at[0], probe.at[1], table_in, measured.at[0])
    fills = []
    for k, (source, place) in enumerate(zip(sources, places)):
        fill = pltpu.make_async_copy(source, place, stock_sems.at[k])
        fill.start()
        fills.append(fill)
    count = (order + LANES) // LANES
    slots = dealing.shape[0]
    tile_cols = empty.shape[2]
    width = zeros.shape[2]
    zeros[...] = jnp.zeros_like(zeros)
    for b in range(tile_cols // width):
        fill = pltpu.make_async_copy(zeros, empty.at[:, :, b * width : (b + 1) * width], sems.at[b])
        fill.start()
        fills.append(fill)

    @pl.loop(0, tile_cols // LANES)
    def _(block):
        table[block] = -1

    @pl.loop(0, slots)
    def _(slot):
        base, _ = window_start(cols[dealing[slot]], order, tile_cols)
        for b in range(count):
            number = slot * count + b
            block = base // LANES + b
            blocks[number] = block
            known = table[block]
            owner = jnp.where(known < 0, number, known)
            owners[number] = owner
            table[block] = owner

    for fill in fills:
        fill.wait()


def prepare(dealing, cols, token, probe, measured, tile_shape):
    order = probe.shape[1]
    slots = dealing.shape[0]
    numbers = slots * (order + LANES) // LANES
    fill_cols = 2048
    return pl.pallas_call(
        functools.partial(prepare_kernel, order),
        out_shape=(
            jax.ShapeDtypeStruct(tile_shape, jnp.float32),
            jax.ShapeDtypeStruct((numbers,), jnp.int32),
            jax.ShapeDtypeStruct((numbers,), jnp.int32),
            jax.ShapeDtypeStruct((48 * order, 2 * order), jnp.bfloat16),
        ),
        in_specs=[SMEM, SMEM, SMEM, ANY, ANY, ANY],
        out_specs=(ANY, SMEM, SMEM, ANY),
        scratch_shapes=[
            pltpu.SMEM((tile_shape[2] // LANES,), jnp.int32),
            pltpu.VMEM(tile_shape[:2] + (fill_cols,), jnp.float32),
            pltpu.SemaphoreType.DMA((tile_shape[2] // fill_cols,)),
            pltpu.SemaphoreType.DMA((4,)),
        ],
        compiler_params=pltpu.CompilerParams(vmem_limit_bytes=8 * 2**20),
        cost_estimate=pl.CostEstimate(flops=0, bytes_accessed=110 * 2**20, transcendentals=0),
        name="prepare",
    )(dealing, cols, token, jnp.asarray(dft_table(order)), probe, measured)


def slot_kernel(
    dealing, rows, owners, cells, stock,
    term, kept, sent,
    wide, patch, wave, half, resid, turned, leaving, probe, table, minus, measured, sems, leave_sem,
):
    del owners
    order = term.shape[0]
    places = (stock.at[0:order, :],) + stock_places(stock, order)[2:]
    targets = (probe, table, measured)
    loads = [
        pltpu.make_async_copy(source, target, sems.at[k])
        for k, (source, target) in enumerate(zip(places, targets))
    ]
    for load in loads:
        load.start()
    total_rows = cells.shape[0]
    me = lax.axis_index("row")
    first_row = rows[dealing[me]]
    step = 64
    tile = 256

    wide[0:total_rows, :] = cells[...].astype(jnp.float32)
    wide[total_rows:, :] = jnp.zeros((SUBLANES, 2 * order), jnp.float32)

    @pl.loop(0, order // step, unroll=2)
    def _(i):
        place = pl.ds(pl.multiple_of(i * step, step), step)
        patch[place, :] = rows_from(wide, first_row + i * step, step).astype(patch.dtype)

    loads[0].wait()

    @pl.loop(0, order // step, unroll=2)
    def _(i):
        place = pl.ds(pl.multiple_of(i * step, step), step)
        found = patch[place, :].astype(jnp.float32)
        real, imag = found[:, :order], found[:, order:]
        probe_real = probe[place, :order].astype(jnp.float32)
        probe_imag = probe[place, order:].astype(jnp.float32)
        wave[place, :order] = (probe_real * real - probe_imag * imag).astype(wave.dtype)
        wave[place, order:] = (probe_real * imag + probe_imag * real).astype(wave.dtype)

    loads[1].wait()
    minus[...] = -table[:, order:]
    cos, sin = table.at[:, :order], table.at[:, order:]
    first_half, second_half = slice(0, order), slice(order, 2 * order)

    def dots(a, b, c, d):
        one = jnp.dot(a, b, preferred_element_type=jnp.float32)
        return one + jnp.dot(c, d, preferred_element_type=jnp.float32)

    for first in range(0, order, tile):
        here = slice(first, first + tile)
        real, imag = wave[:, first_half], wave[:, second_half]
        half[first_half, here] = dots(real, cos[:, here], imag, minus[:, here]).astype(half.dtype)
        half[second_half, here] = dots(real, sin[:, here], imag, cos[:, here]).astype(half.dtype)
    loads[2].wait()
    for first in range(0, order, tile):
        here = slice(first, first + tile)
        there = slice(order + first, order + first + tile)
        for top in range(0, order, tile):
            line = slice(top, top + tile)
            half_real, half_imag = half[first_half, here], half[second_half, here]
            real = dots(cos[line, :], half_real, minus[line, :], half_imag)
            imag = dots(sin[line, :], half_real, cos[line, :], half_imag)
            inverse = jnp.minimum(lax.rsqrt(real * real + imag * imag), 1.0 / MAG_FLOOR)
            shrink = 1.0 - measured[line, here].astype(jnp.float32) * inverse
            resid[line, here] = (real * shrink).astype(resid.dtype)
            resid[line, there] = (imag * shrink).astype(resid.dtype)
    for first in range(0, order, tile):
        here = slice(first, first + tile)
        real, imag = resid[:, first_half], resid[:, second_half]
        turned[first_half, here] = dots(real, cos[:, here], imag, sin[:, here]).astype(turned.dtype)
        turned[second_half, here] = dots(real, minus[:, here], imag, cos[:, here]).astype(turned.dtype)
    count = order // 2
    side = lax.rem(me, 2)
    for number, target in ((1 - side, leaving), (side, kept)):
        line = pl.ds(pl.multiple_of(number * count, count), count)
        for first in range(0, order, tile):
            here = slice(first, first + tile)
            there = slice(order + first, order + first + tile)
            turned_real, turned_imag = turned[first_half, here], turned[second_half, here]
            real = dots(cos[line, :], turned_real, sin[line, :], turned_imag)
            imag = dots(minus[line, :], turned_real, cos[line, :], turned_imag)
            patch_real = patch[line, here].astype(jnp.float32)
            patch_imag = patch[line, there].astype(jnp.float32)
            target[:, here] = (patch_real * real + patch_imag * imag).astype(target.dtype)
            target[:, there] = (patch_real * imag - patch_imag * real).astype(target.dtype)
            probe_real = probe[line, here].astype(jnp.float32)
            probe_imag = probe[line, there].astype(jnp.float32)
            term[line, here] = (probe_real * real + probe_imag * imag).astype(term.dtype)
            term[line, there] = (probe_real * imag - probe_imag * real).astype(term.dtype)
        if target is leaving:
            leave = pltpu.make_async_copy(leaving, sent, leave_sem.at[0])
            leave.start()
    leave.wait()


def slot_terms(cells, stock, dealing, rows, owners, order):
    total_rows = cells.shape[0]
    wide_cols = 2 * order
    bf16, f32 = jnp.bfloat16, jnp.float32
    return pl.pallas_call(
        slot_kernel,
        out_shape=(
            jax.ShapeDtypeStruct((order, wide_cols), bf16),
            jax.ShapeDtypeStruct((order // 2, wide_cols), f32),
            jax.ShapeDtypeStruct((order // 2, wide_cols), bf16),
        ),
        in_specs=[SMEM, SMEM, SMEM, VMEM, ANY],
        out_specs=(VMEM, VMEM, ANY),
        scratch_shapes=[
            pltpu.VMEM((total_rows + SUBLANES, wide_cols), f32),
            pltpu.VMEM((order, wide_cols), bf16),
            pltpu.VMEM((order, wide_cols), bf16),
            pltpu.VMEM((wide_cols, order), bf16),
            pltpu.VMEM((order, wide_cols), bf16),
            pltpu.VMEM((wide_cols, order), bf16),
            pltpu.VMEM((order // 2, wide_cols), bf16),
            pltpu.VMEM((order, wide_cols), bf16),
            pltpu.VMEM((order, wide_cols), bf16),
            pltpu.VMEM((order, order), bf16),
            pltpu.VMEM((order, order), bf16),
            pltpu.SemaphoreType.DMA((3,)),
            pltpu.SemaphoreType.DMA((1,)),
        ],
        compiler_params=pltpu.CompilerParams(vmem_limit_bytes=24 * 2**20),
        cost_estimate=pl.CostEstimate(
            flops=8 * 2 * order**3 * 2, bytes_accessed=8 * 2**20, transcendentals=order * order
        ),
        name="slot",
    )(dealing, rows, owners, cells, stock)


def pack_kernel(reach, own_rows, dealing, rows, term, out, padded):
    order = term.shape[0]
    first_row = rows[dealing[lax.axis_index("row")]]
    below = padded.shape[0] - reach - order
    padded[0:reach, :] = jnp.zeros((reach, padded.shape[1]), jnp.float32)
    padded[reach : reach + order, :] = term[...].astype(jnp.float32)
    padded[reach + order :, :] = jnp.zeros((below, padded.shape[1]), jnp.float32)

    @pl.loop(0, out.shape[0], unroll=2)
    def _(k):
        out[k] = rows_from(padded, reach - first_row + k * own_rows, out.shape[1]).astype(out.dtype)


def pack_rows(term, dealing, rows, slots, own_rows, tile_rows):
    order, width = term.shape
    reach = slots * own_rows - order
    return pl.pallas_call(
        functools.partial(pack_kernel, reach, own_rows),
        out_shape=jax.ShapeDtypeStruct((slots, tile_rows, width), jnp.bfloat16),
        in_specs=[SMEM, SMEM, VMEM],
        out_specs=VMEM,
        scratch_shapes=[pltpu.VMEM((2 * reach + order + tile_rows + SUBLANES, width), jnp.float32)],
        compiler_params=pltpu.CompilerParams(vmem_limit_bytes=8 * 2**20),
        cost_estimate=pl.CostEstimate(flops=0, bytes_accessed=3 * 2**20, transcendentals=0),
        name="pack",
    )(dealing, rows, term)


def place_kernel(order, dealing, cols, blocks, owners, terms, empty, out, totals, sems):
    del empty
    slots, tile_rows = terms.shape[0], terms.shape[1]
    count = (order + LANES) // LANES
    lane = lax.broadcasted_iota(jnp.int32, (tile_rows, LANES), 1)
    nothing = jnp.zeros((tile_rows, LANES), jnp.float32)

    @pl.loop(0, slots, unroll=4)
    def _(slot):
        _, offset = window_start(cols[dealing[slot]], order, out.shape[2])
        shift = lax.rem(offset, LANES)
        for part in range(2):
            turned = []
            for b in range(count - 1):
                first = part * order + b * LANES
                turned.append(pltpu.roll(terms[slot, :, first : first + LANES], shift, 1).astype(jnp.float32))
            holders = [owners[slot * count + b] for b in range(count)]
            held = [totals[holder, part] for holder in holders]
            for b in range(count):
                before = turned[b - 1] if b else nothing
                after = turned[b] if b < count - 1 else nothing
                term = jnp.where(lane < offset, before, after)
                first_one = holders[b] == slot * count + b
                totals[holders[b], part] = jnp.where(first_one, term, held[b] + term)

    def copy(number):
        place = pl.multiple_of(blocks[number] * LANES, LANES)
        return pltpu.make_async_copy(totals.at[number], out.at[:, :, pl.ds(place, LANES)], sems.at[number])

    @pl.loop(0, slots * count)
    def _(number):
        @pl.when(owners[number] == number)
        def _():
            copy(number).start()

    @pl.loop(0, slots * count)
    def _(number):
        @pl.when(owners[number] == number)
        def _():
            copy(number).wait()


def place_windows(terms, empty, blocks, owners, dealing, cols, order):
    slots, tile_rows = terms.shape[0], terms.shape[1]
    count = (order + LANES) // LANES
    return pl.pallas_call(
        functools.partial(place_kernel, order),
        out_shape=jax.ShapeDtypeStruct(empty.shape, empty.dtype),
        in_specs=[SMEM, SMEM, SMEM, SMEM, VMEM, ANY],
        out_specs=ANY,
        scratch_shapes=[
            pltpu.VMEM((slots * count, 2, tile_rows, LANES), jnp.float32),
            pltpu.SemaphoreType.DMA((slots * count,)),
        ],
        input_output_aliases={5: 0},
        compiler_params=pltpu.CompilerParams(vmem_limit_bytes=12 * 2**20),
        cost_estimate=pl.CostEstimate(flops=0, bytes_accessed=6 * 2**20, transcendentals=0),
        name="place",
    )(dealing, cols, blocks, owners, terms, empty)


def strides(devices):
    steps, stride = [], 1
    while stride < devices:
        radix = 4 if len(steps) >= 2 and (devices // stride) % 4 == 0 else 2
        steps.append((stride, radix))
        stride *= radix
    return steps


def swap(x, distance, devices):
    return lax.ppermute(x, "row", [(d, d ^ distance) for d in range(devices)])


def sum_probe(kept, sent, devices):
    me = lax.axis_index("row")

    def rows(addends, first, count):
        found = [lax.dynamic_slice_in_dim(x, first, count).astype(jnp.float32) for x in addends]
        return found[0] + found[1]

    halves = [kept, swap(sent, 1, devices)]
    (stride, radix), *later = strides(devices)[1:]
    digit = me // stride % radix
    count = kept.shape[0] // (2 * radix)
    other = lax.rem(digit + 1, 2)
    met = [
        swap(rows(halves, (other * 2 + number) * count, count).astype(jnp.bfloat16), stride, devices)
        for number in range(2)
    ]
    totals = []
    for number in range(2):
        addends = [rows(halves, (digit * 2 + number) * count, count), met[number]]
        for stride, radix in later:
            digit_here = me // stride % radix
            share_rows = addends[0].shape[0] // radix
            arrived = []
            for k in range(1, radix):
                share = rows(addends, lax.bitwise_xor(digit_here, k) * share_rows, share_rows)
                arrived.append(swap(share.astype(jnp.bfloat16), k * stride, devices))
            own = rows(addends, digit_here * share_rows, share_rows)
            for one in arrived[:-1]:
                own = own + one.astype(jnp.float32)
            addends = [own, arrived[-1]]
        totals.append(addends[0] + addends[1].astype(jnp.float32))
    return jnp.concatenate(totals)


def join(whole, devices):
    me = lax.axis_index("row")
    rows, width = whole.shape
    steps = strides(devices)
    for stride, radix in reversed(steps):
        if stride == steps[1][0]:
            sets = whole.reshape(-1, 2, rows // 2, width)
            whole = jnp.concatenate([sets[:, 0].reshape(-1, width), sets[:, 1].reshape(-1, width)])
        digit = me // stride % radix
        shares = [whole] + [swap(whole, k * stride, devices) for k in range(1, radix)]
        pieces = []
        for j in range(radix):
            piece = shares[0]
            for k in range(1, radix):
                piece = jnp.where(lax.bitwise_xor(digit, k) == j, shares[k], piece)
            pieces.append(piece)
        whole = jnp.concatenate(pieces, axis=0)
    return whole


def body(object_field, probe, amplitude, row_offsets, col_offsets, dealing):
    order = probe.shape[1]
    devices = lax.axis_size("row")
    own_rows, tile_cols = object_field.shape[1], object_field.shape[2]
    total_rows = devices * own_rows
    tile_rows = -(-own_rows // SUBLANES) * SUBLANES
    spare = tile_rows - own_rows
    if spare:
        object_field = jnp.pad(object_field, ((0, 0), (0, spare), (0, 0)))
    pieces, token = fetch_windows(object_field, dealing, col_offsets, order)
    strips = lax.all_to_all(pieces, "row", split_axis=0, concat_axis=0, tiled=True)
    cells = strips[:, :own_rows].reshape(total_rows, 2 * order)
    empty, blocks, owners, stock = prepare(
        dealing, col_offsets, token, probe, amplitude, object_field.shape
    )
    term, kept, sent = slot_terms(cells, stock, dealing, row_offsets, owners, order)
    total = sum_probe(kept, sent, devices)
    terms = pack_rows(term, dealing, row_offsets, devices, own_rows, tile_rows)
    terms, total = lax.optimization_barrier((terms, total))
    arrived = lax.all_to_all(terms, "row", split_axis=0, concat_axis=0, tiled=True)
    share = (total * (1.0 / dealing.shape[0])).astype(jnp.bfloat16)
    whole = join(share, devices).astype(jnp.float32)
    probe_grad = jnp.stack([whole[:, :order], whole[:, order:]])
    object_grad = place_windows(arrived, empty, blocks, owners, dealing, col_offsets, order)
    if spare:
        object_grad = object_grad[:, :own_rows]
    return (object_grad, probe_grad)


def solution(mesh):
    return jax.shard_map(
        body,
        mesh=mesh,
        in_specs=(
            P(None, ("groups", "row"), None),
            P("groups", None, None),
            P(("groups", "row"), None, None),
            P("groups"),
            P("groups"),
            P("groups"),
        ),
        out_specs=(P(None, ("groups", "row"), None), P("groups", None, None)),
        check_vma=False,
    )
```

```python
import functools
import math

import jax
import jax.numpy as jnp
import numpy as np
from jax import lax
from jax.experimental import pallas as pl
from jax.experimental.pallas import tpu as pltpu
from jax.sharding import PartitionSpec as P

MAG_FLOOR = 0.25
LANES = 128
SUBLANES = 8
SMEM = pl.BlockSpec(memory_space=pltpu.SMEM)
VMEM = pl.BlockSpec(memory_space=pltpu.VMEM)
ANY = pl.BlockSpec(memory_space=pl.ANY)


def dft_table(order):
    indices = np.arange(order, dtype=np.int32)
    phases = indices[:, None] * indices[None, :] % order
    angles = phases.astype(np.float32) * np.float32(2.0 * math.pi / order)
    factor = np.float32(1.0 / math.sqrt(order))
    return np.concatenate([np.cos(angles) * factor, -np.sin(angles) * factor], axis=1).astype(jnp.bfloat16)


def window_start(column, order, tile_cols):
    span = order + LANES
    base = jnp.minimum(column // LANES, (tile_cols - span) // LANES) * LANES
    return pl.multiple_of(base, LANES), column - base


def rows_from(ref, start, count):
    aligned = pl.multiple_of(start // SUBLANES * SUBLANES, SUBLANES)
    rest = start - aligned
    width = ref.shape[-1]
    blocks = ref[pl.ds(aligned, count + SUBLANES), :].reshape(-1, SUBLANES, width)
    turned = pltpu.roll(blocks, lax.rem(SUBLANES - rest, SUBLANES), 1)
    sub = lax.broadcasted_iota(jnp.int32, (1, SUBLANES, width), 1)
    picked = jnp.where(sub < SUBLANES - rest, turned[:-1], turned[1:])
    return picked.reshape(count, width)


def fetch_kernel(order, dealing, cols, tile, out, token, held, sems):
    token[0] = dealing[0]
    slots, tile_rows = out.shape[0], out.shape[1]
    tile_cols = tile.shape[2]
    span = order + LANES

    def copy(slot):
        base, _ = window_start(cols[dealing[slot]], order, tile_cols)
        return pltpu.make_async_copy(tile.at[:, :, pl.ds(base, span)], held.at[slot], sems.at[slot])

    @pl.loop(0, slots)
    def _(slot):
        copy(slot).start()

    lane = lax.broadcasted_iota(jnp.int32, (tile_rows, LANES), 1)

    @pl.loop(0, slots, unroll=4)
    def _(slot):
        copy(slot).wait()
        _, offset = window_start(cols[dealing[slot]], order, tile_cols)
        shift = lax.rem(LANES - lax.rem(offset, LANES), LANES)
        for part in range(2):
            turned = [
                pltpu.roll(held[slot, part, :, b * LANES : (b + 1) * LANES].astype(out.dtype), shift, 1)
                for b in range(span // LANES)
            ]
            for b in range(order // LANES):
                first = part * order + b * LANES
                cells = jnp.where(lane < LANES - offset, turned[b], turned[b + 1])
                out[slot, :, first : first + LANES] = cells


def fetch_windows(tile, dealing, cols, order):
    slots, tile_rows, tile_cols = dealing.shape[0], tile.shape[1], tile.shape[2]
    span = order + LANES

    return pl.pallas_call(
        functools.partial(fetch_kernel, order),
        out_shape=(
            jax.ShapeDtypeStruct((slots, tile_rows, 2 * order), jnp.bfloat16),
            jax.ShapeDtypeStruct((1,), jnp.int32),
        ),
        in_specs=[SMEM, SMEM, ANY],
        out_specs=(VMEM, SMEM),
        scratch_shapes=[
            pltpu.VMEM((slots, 2, tile_rows, span), jnp.float32),
            pltpu.SemaphoreType.DMA((slots,)),
        ],
        compiler_params=pltpu.CompilerParams(vmem_limit_bytes=56 * 2**20),
        cost_estimate=pl.CostEstimate(flops=0, bytes_accessed=6 * 2**20, transcendentals=0),
        name="fetch",
    )(dealing, cols, tile)


def stock_places(stock, order):
    return (
        stock.at[0:order, 0:order],
        stock.at[0:order, order : 2 * order],
        stock.at[order : 2 * order, :],
        stock.at[2 * order : 3 * order, 0:order],
    )


def prepare_kernel(
    order, dealing, cols, token, table_in, probe, measured,
    empty, blocks, owners, stock,
    table, zeros, sems, stock_sems,
):
    del token
    places = stock_places(stock, order)
    sources = (probe.at[0], probe.at[1], table_in, measured.at[0])
    fills = []
    for k, (source, place) in enumerate(zip(sources, places)):
        fill = pltpu.make_async_copy(source, place, stock_sems.at[k])
        fill.start()
        fills.append(fill)
    count = (order + LANES) // LANES
    slots = dealing.shape[0]
    tile_cols = empty.shape[2]
    width = zeros.shape[2]
    zeros[...] = jnp.zeros_like(zeros)
    for b in range(tile_cols // width):
        fill = pltpu.make_async_copy(zeros, empty.at[:, :, b * width : (b + 1) * width], sems.at[b])
        fill.start()
        fills.append(fill)

    @pl.loop(0, tile_cols // LANES)
    def _(block):
        table[block] = -1

    @pl.loop(0, slots)
    def _(slot):
        base, _ = window_start(cols[dealing[slot]], order, tile_cols)
        for b in range(count):
            number = slot * count + b
            block = base // LANES + b
            blocks[number] = block
            known = table[block]
            owner = jnp.where(known < 0, number, known)
            owners[number] = owner
            table[block] = owner

    for fill in fills:
        fill.wait()


def prepare(dealing, cols, token, probe, measured, tile_shape):
    order = probe.shape[1]
    slots = dealing.shape[0]
    numbers = slots * (order + LANES) // LANES
    fill_cols = 2048
    return pl.pallas_call(
        functools.partial(prepare_kernel, order),
        out_shape=(
            jax.ShapeDtypeStruct(tile_shape, jnp.float32),
            jax.ShapeDtypeStruct((numbers,), jnp.int32),
            jax.ShapeDtypeStruct((numbers,), jnp.int32),
            jax.ShapeDtypeStruct((48 * order, 2 * order), jnp.bfloat16),
        ),
        in_specs=[SMEM, SMEM, SMEM, ANY, ANY, ANY],
        out_specs=(ANY, SMEM, SMEM, ANY),
        scratch_shapes=[
            pltpu.SMEM((tile_shape[2] // LANES,), jnp.int32),
            pltpu.VMEM(tile_shape[:2] + (fill_cols,), jnp.float32),
            pltpu.SemaphoreType.DMA((tile_shape[2] // fill_cols,)),
            pltpu.SemaphoreType.DMA((4,)),
        ],
        compiler_params=pltpu.CompilerParams(vmem_limit_bytes=8 * 2**20),
        cost_estimate=pl.CostEstimate(flops=0, bytes_accessed=110 * 2**20, transcendentals=0),
        name="prepare",
    )(dealing, cols, token, jnp.asarray(dft_table(order)), probe, measured)


def slot_kernel(
    dealing, rows, owners, cells, stock,
    term, kept, sent,
    wide, patch, wave, half, resid, turned, leaving, probe, table, minus, measured, sems, leave_sem,
):
    del owners
    order = term.shape[0]
    places = (stock.at[0:order, :],) + stock_places(stock, order)[2:]
    targets = (probe, table, measured)
    loads = [
        pltpu.make_async_copy(source, target, sems.at[k])
        for k, (source, target) in enumerate(zip(places, targets))
    ]
    for load in loads:
        load.start()
    total_rows = cells.shape[0]
    me = lax.axis_index("row")
    first_row = rows[dealing[me]]
    step = 64
    tile = 256

    wide[0:total_rows, :] = cells[...].astype(jnp.float32)
    wide[total_rows:, :] = jnp.zeros((SUBLANES, 2 * order), jnp.float32)

    @pl.loop(0, order // step, unroll=2)
    def _(i):
        place = pl.ds(pl.multiple_of(i * step, step), step)
        patch[place, :] = rows_from(wide, first_row + i * step, step).astype(patch.dtype)

    loads[0].wait()

    @pl.loop(0, order // step, unroll=2)
    def _(i):
        place = pl.ds(pl.multiple_of(i * step, step), step)
        found = patch[place, :].astype(jnp.float32)
        real, imag = found[:, :order], found[:, order:]
        probe_real = probe[place, :order].astype(jnp.float32)
        probe_imag = probe[place, order:].astype(jnp.float32)
        wave[place, :order] = (probe_real * real - probe_imag * imag).astype(wave.dtype)
        wave[place, order:] = (probe_real * imag + probe_imag * real).astype(wave.dtype)

    loads[1].wait()
    minus[...] = -table[:, order:]
    cos, sin = table.at[:, :order], table.at[:, order:]
    first_half, second_half = slice(0, order), slice(order, 2 * order)

    def dots(a, b, c, d):
        one = jnp.dot(a, b, preferred_element_type=jnp.float32)
        return one + jnp.dot(c, d, preferred_element_type=jnp.float32)

    for first in range(0, order, tile):
        here = slice(first, first + tile)
        real, imag = wave[:, first_half], wave[:, second_half]
        half[first_half, here] = dots(real, cos[:, here], imag, minus[:, here]).astype(half.dtype)
        half[second_half, here] = dots(real, sin[:, here], imag, cos[:, here]).astype(half.dtype)
    loads[2].wait()
    for first in range(0, order, tile):
        here = slice(first, first + tile)
        there = slice(order + first, order + first + tile)
        for top in range(0, order, tile):
            line = slice(top, top + tile)
            half_real, half_imag = half[first_half, here], half[second_half, here]
            real = dots(cos[line, :], half_real, minus[line, :], half_imag)
            imag = dots(sin[line, :], half_real, cos[line, :], half_imag)
            inverse = jnp.minimum(lax.rsqrt(real * real + imag * imag), 1.0 / MAG_FLOOR)
            shrink = 1.0 - measured[line, here].astype(jnp.float32) * inverse
            resid[line, here] = (real * shrink).astype(resid.dtype)
            resid[line, there] = (imag * shrink).astype(resid.dtype)
    for first in range(0, order, tile):
        here = slice(first, first + tile)
        real, imag = resid[:, first_half], resid[:, second_half]
        turned[first_half, here] = dots(real, cos[:, here], imag, sin[:, here]).astype(turned.dtype)
        turned[second_half, here] = dots(real, minus[:, here], imag, cos[:, here]).astype(turned.dtype)
    count = order // 2
    side = lax.rem(me, 2)
    for number, target in ((1 - side, leaving), (side, kept)):
        line = pl.ds(pl.multiple_of(number * count, count), count)
        for first in range(0, order, tile):
            here = slice(first, first + tile)
            there = slice(order + first, order + first + tile)
            turned_real, turned_imag = turned[first_half, here], turned[second_half, here]
            real = dots(cos[line, :], turned_real, sin[line, :], turned_imag)
            imag = dots(minus[line, :], turned_real, cos[line, :], turned_imag)
            patch_real = patch[line, here].astype(jnp.float32)
            patch_imag = patch[line, there].astype(jnp.float32)
            target[:, here] = (patch_real * real + patch_imag * imag).astype(target.dtype)
            target[:, there] = (patch_real * imag - patch_imag * real).astype(target.dtype)
            probe_real = probe[line, here].astype(jnp.float32)
            probe_imag = probe[line, there].astype(jnp.float32)
            term[line, here] = (probe_real * real + probe_imag * imag).astype(term.dtype)
            term[line, there] = (probe_real * imag - probe_imag * real).astype(term.dtype)
        if target is leaving:
            leave = pltpu.make_async_copy(leaving, sent, leave_sem.at[0])
            leave.start()
    leave.wait()


def slot_terms(cells, stock, dealing, rows, owners, order):
    total_rows = cells.shape[0]
    wide_cols = 2 * order
    bf16, f32 = jnp.bfloat16, jnp.float32
    return pl.pallas_call(
        slot_kernel,
        out_shape=(
            jax.ShapeDtypeStruct((order, wide_cols), bf16),
            jax.ShapeDtypeStruct((order // 2, wide_cols), f32),
            jax.ShapeDtypeStruct((order // 2, wide_cols), bf16),
        ),
        in_specs=[SMEM, SMEM, SMEM, VMEM, ANY],
        out_specs=(VMEM, VMEM, ANY),
        scratch_shapes=[
            pltpu.VMEM((total_rows + SUBLANES, wide_cols), f32),
            pltpu.VMEM((order, wide_cols), bf16),
            pltpu.VMEM((order, wide_cols), bf16),
            pltpu.VMEM((wide_cols, order), bf16),
            pltpu.VMEM((order, wide_cols), bf16),
            pltpu.VMEM((wide_cols, order), bf16),
            pltpu.VMEM((order // 2, wide_cols), bf16),
            pltpu.VMEM((order, wide_cols), bf16),
            pltpu.VMEM((order, wide_cols), bf16),
            pltpu.VMEM((order, order), bf16),
            pltpu.VMEM((order, order), bf16),
            pltpu.SemaphoreType.DMA((3,)),
            pltpu.SemaphoreType.DMA((1,)),
        ],
        compiler_params=pltpu.CompilerParams(vmem_limit_bytes=24 * 2**20),
        cost_estimate=pl.CostEstimate(
            flops=8 * 2 * order**3 * 2, bytes_accessed=8 * 2**20, transcendentals=order * order
        ),
        name="slot",
    )(dealing, rows, owners, cells, stock)


def pack_kernel(reach, own_rows, dealing, rows, term, out, padded):
    order = term.shape[0]
    first_row = rows[dealing[lax.axis_index("row")]]
    below = padded.shape[0] - reach - order
    padded[0:reach, :] = jnp.zeros((reach, padded.shape[1]), jnp.float32)
    padded[reach : reach + order, :] = term[...].astype(jnp.float32)
    padded[reach + order :, :] = jnp.zeros((below, padded.shape[1]), jnp.float32)

    @pl.loop(0, out.shape[0], unroll=2)
    def _(k):
        out[k] = rows_from(padded, reach - first_row + k * own_rows, out.shape[1]).astype(out.dtype)


def pack_rows(term, dealing, rows, slots, own_rows, tile_rows):
    order, width = term.shape
    reach = slots * own_rows - order
    return pl.pallas_call(
        functools.partial(pack_kernel, reach, own_rows),
        out_shape=jax.ShapeDtypeStruct((slots, tile_rows, width), jnp.bfloat16),
        in_specs=[SMEM, SMEM, VMEM],
        out_specs=VMEM,
        scratch_shapes=[pltpu.VMEM((2 * reach + order + tile_rows + SUBLANES, width), jnp.float32)],
        compiler_params=pltpu.CompilerParams(vmem_limit_bytes=8 * 2**20),
        cost_estimate=pl.CostEstimate(flops=0, bytes_accessed=3 * 2**20, transcendentals=0),
        name="pack",
    )(dealing, rows, term)


def place_kernel(order, dealing, cols, blocks, owners, terms, empty, out, totals, sems):
    del empty
    slots, tile_rows = terms.shape[0], terms.shape[1]
    count = (order + LANES) // LANES
    lane = lax.broadcasted_iota(jnp.int32, (tile_rows, LANES), 1)
    nothing = jnp.zeros((tile_rows, LANES), jnp.float32)

    @pl.loop(0, slots, unroll=4)
    def _(slot):
        _, offset = window_start(cols[dealing[slot]], order, out.shape[2])
        shift = lax.rem(offset, LANES)
        for part in range(2):
            turned = []
            for b in range(count - 1):
                first = part * order + b * LANES
                turned.append(pltpu.roll(terms[slot, :, first : first + LANES], shift, 1).astype(jnp.float32))
            holders = [owners[slot * count + b] for b in range(count)]
            held = [totals[holder, part] for holder in holders]
            for b in range(count):
                before = turned[b - 1] if b else nothing
                after = turned[b] if b < count - 1 else nothing
                term = jnp.where(lane < offset, before, after)
                first_one = holders[b] == slot * count + b
                totals[holders[b], part] = jnp.where(first_one, term, held[b] + term)

    def copy(number):
        place = pl.multiple_of(blocks[number] * LANES, LANES)
        return pltpu.make_async_copy(totals.at[number], out.at[:, :, pl.ds(place, LANES)], sems.at[number])

    @pl.loop(0, slots * count)
    def _(number):
        @pl.when(owners[number] == number)
        def _():
            copy(number).start()

    @pl.loop(0, slots * count)
    def _(number):
        @pl.when(owners[number] == number)
        def _():
            copy(number).wait()


def place_windows(terms, empty, blocks, owners, dealing, cols, order):
    slots, tile_rows = terms.shape[0], terms.shape[1]
    count = (order + LANES) // LANES
    return pl.pallas_call(
        functools.partial(place_kernel, order),
        out_shape=jax.ShapeDtypeStruct(empty.shape, empty.dtype),
        in_specs=[SMEM, SMEM, SMEM, SMEM, VMEM, ANY],
        out_specs=ANY,
        scratch_shapes=[
            pltpu.VMEM((slots * count, 2, tile_rows, LANES), jnp.float32),
            pltpu.SemaphoreType.DMA((slots * count,)),
        ],
        input_output_aliases={5: 0},
        compiler_params=pltpu.CompilerParams(vmem_limit_bytes=12 * 2**20),
        cost_estimate=pl.CostEstimate(flops=0, bytes_accessed=6 * 2**20, transcendentals=0),
        name="place",
    )(dealing, cols, blocks, owners, terms, empty)


def strides(devices):
    steps, stride = [], 1
    while stride < devices:
        radix = 4 if len(steps) >= 2 and (devices // stride) % 4 == 0 else 2
        steps.append((stride, radix))
        stride *= radix
    return steps


def swap(x, distance, devices):
    return lax.ppermute(x, "row", [(d, d ^ distance) for d in range(devices)])


def sum_probe(kept, sent, devices):
    me = lax.axis_index("row")
    addends = [kept, swap(sent, 1, devices)]

    def rows(index, count):
        found = [lax.dynamic_slice_in_dim(x, index * count, count).astype(jnp.float32) for x in addends]
        return found[0] + found[1]

    for stride, radix in strides(devices)[1:]:
        digit = me // stride % radix
        count = addends[0].shape[0] // radix
        met = []
        for k in range(radix - 1, 0, -1):
            share = rows(lax.bitwise_xor(digit, k), count).astype(jnp.bfloat16)
            met.append(swap(share, k * stride, devices))
        own = rows(digit, count)
        for one in met[:-1]:
            own = own + one.astype(jnp.float32)
        addends = [own, met[-1]]
    return addends[0] + addends[1].astype(jnp.float32)


def join(whole, devices):
    me = lax.axis_index("row")
    for stride, radix in reversed(strides(devices)):
        digit = me // stride % radix
        shares = {k: swap(whole, k * stride, devices) for k in range(radix - 1, 0, -1)}
        pieces = []
        for j in range(radix):
            piece = whole
            for k in range(1, radix):
                piece = jnp.where(lax.bitwise_xor(digit, k) == j, shares[k], piece)
            pieces.append(piece)
        whole = jnp.concatenate(pieces, axis=0)
    return whole


def body(object_field, probe, amplitude, row_offsets, col_offsets, dealing):
    order = probe.shape[1]
    devices = lax.axis_size("row")
    own_rows, tile_cols = object_field.shape[1], object_field.shape[2]
    total_rows = devices * own_rows
    tile_rows = -(-own_rows // SUBLANES) * SUBLANES
    spare = tile_rows - own_rows
    if spare:
        object_field = jnp.pad(object_field, ((0, 0), (0, spare), (0, 0)))
    pieces, token = fetch_windows(object_field, dealing, col_offsets, order)
    strips = lax.all_to_all(pieces, "row", split_axis=0, concat_axis=0, tiled=True)
    cells = strips[:, :own_rows].reshape(total_rows, 2 * order)
    empty, blocks, owners, stock = prepare(
        dealing, col_offsets, token, probe, amplitude, object_field.shape
    )
    term, kept, sent = slot_terms(cells, stock, dealing, row_offsets, owners, order)
    total = sum_probe(kept, sent, devices)
    terms = pack_rows(term, dealing, row_offsets, devices, own_rows, tile_rows)
    terms, total = lax.optimization_barrier((terms, total))
    arrived = lax.all_to_all(terms, "row", split_axis=0, concat_axis=0, tiled=True)
    share = (total * (1.0 / dealing.shape[0])).astype(jnp.bfloat16)
    whole = join(share, devices).astype(jnp.float32)
    probe_grad = jnp.stack([whole[:, :order], whole[:, order:]])
    object_grad = place_windows(arrived, empty, blocks, owners, dealing, col_offsets, order)
    if spare:
        object_grad = object_grad[:, :own_rows]
    return (object_grad, probe_grad)


def solution(mesh):
    return jax.shard_map(
        body,
        mesh=mesh,
        in_specs=(
            P(None, ("groups", "row"), None),
            P("groups", None, None),
            P(("groups", "row"), None, None),
            P("groups"),
            P("groups"),
            P("groups"),
        ),
        out_specs=(P(None, ("groups", "row"), None), P("groups", None, None)),
        check_vma=False,
    )
```

```python
import functools
import math

import jax
import jax.numpy as jnp
import numpy as np
from jax import lax
from jax.experimental import pallas as pl
from jax.experimental.pallas import tpu as pltpu
from jax.sharding import PartitionSpec as P

MAG_FLOOR = 0.25
LANES = 128
SUBLANES = 8
SMEM = pl.BlockSpec(memory_space=pltpu.SMEM)
VMEM = pl.BlockSpec(memory_space=pltpu.VMEM)
ANY = pl.BlockSpec(memory_space=pl.ANY)


def dft_table(order):
    indices = np.arange(order, dtype=np.int32)
    phases = indices[:, None] * indices[None, :] % order
    angles = phases.astype(np.float32) * np.float32(2.0 * math.pi / order)
    factor = np.float32(1.0 / math.sqrt(order))
    return np.concatenate([np.cos(angles) * factor, -np.sin(angles) * factor], axis=1).astype(jnp.bfloat16)


def window_start(column, order, tile_cols):
    span = order + LANES
    base = jnp.minimum(column // LANES, (tile_cols - span) // LANES) * LANES
    return pl.multiple_of(base, LANES), column - base


def rows_from(ref, start, count):
    aligned = pl.multiple_of(start // SUBLANES * SUBLANES, SUBLANES)
    rest = start - aligned
    width = ref.shape[-1]
    blocks = ref[pl.ds(aligned, count + SUBLANES), :].reshape(-1, SUBLANES, width)
    turned = pltpu.roll(blocks, lax.rem(SUBLANES - rest, SUBLANES), 1)
    sub = lax.broadcasted_iota(jnp.int32, (1, SUBLANES, width), 1)
    picked = jnp.where(sub < SUBLANES - rest, turned[:-1], turned[1:])
    return picked.reshape(count, width)


def fetch_kernel(order, dealing, cols, tile, out, token, held, sems):
    token[0] = dealing[0]
    slots, tile_rows = out.shape[0], out.shape[1]
    tile_cols = tile.shape[2]
    span = order + LANES

    def copy(slot):
        base, _ = window_start(cols[dealing[slot]], order, tile_cols)
        return pltpu.make_async_copy(tile.at[:, :, pl.ds(base, span)], held.at[slot], sems.at[slot])

    @pl.loop(0, slots)
    def _(slot):
        copy(slot).start()

    lane = lax.broadcasted_iota(jnp.int32, (tile_rows, LANES), 1)

    @pl.loop(0, slots, unroll=4)
    def _(slot):
        copy(slot).wait()
        _, offset = window_start(cols[dealing[slot]], order, tile_cols)
        shift = lax.rem(LANES - lax.rem(offset, LANES), LANES)
        for part in range(2):
            turned = [
                pltpu.roll(held[slot, part, :, b * LANES : (b + 1) * LANES].astype(out.dtype), shift, 1)
                for b in range(span // LANES)
            ]
            for b in range(order // LANES):
                first = part * order + b * LANES
                cells = jnp.where(lane < LANES - offset, turned[b], turned[b + 1])
                out[slot, :, first : first + LANES] = cells


def fetch_windows(tile, dealing, cols, order):
    slots, tile_rows, tile_cols = dealing.shape[0], tile.shape[1], tile.shape[2]
    span = order + LANES

    return pl.pallas_call(
        functools.partial(fetch_kernel, order),
        out_shape=(
            jax.ShapeDtypeStruct((slots, tile_rows, 2 * order), jnp.bfloat16),
            jax.ShapeDtypeStruct((1,), jnp.int32),
        ),
        in_specs=[SMEM, SMEM, ANY],
        out_specs=(VMEM, SMEM),
        scratch_shapes=[
            pltpu.VMEM((slots, 2, tile_rows, span), jnp.float32),
            pltpu.SemaphoreType.DMA((slots,)),
        ],
        compiler_params=pltpu.CompilerParams(vmem_limit_bytes=56 * 2**20),
        cost_estimate=pl.CostEstimate(flops=0, bytes_accessed=6 * 2**20, transcendentals=0),
        name="fetch",
    )(dealing, cols, tile)


def stock_places(stock, order):
    return (
        stock.at[0:order, 0:order],
        stock.at[0:order, order : 2 * order],
        stock.at[order : 2 * order, :],
        stock.at[2 * order : 3 * order, 0:order],
    )


def prepare_kernel(
    order, dealing, cols, token, table_in, probe, measured,
    empty, blocks, owners, stock,
    table, zeros, sems, stock_sems,
):
    del token
    places = stock_places(stock, order)
    sources = (probe.at[0], probe.at[1], table_in, measured.at[0])
    fills = []
    for k, (source, place) in enumerate(zip(sources, places)):
        fill = pltpu.make_async_copy(source, place, stock_sems.at[k])
        fill.start()
        fills.append(fill)
    count = (order + LANES) // LANES
    slots = dealing.shape[0]
    tile_cols = empty.shape[2]
    width = zeros.shape[2]
    zeros[...] = jnp.zeros_like(zeros)
    for b in range(tile_cols // width):
        fill = pltpu.make_async_copy(zeros, empty.at[:, :, b * width : (b + 1) * width], sems.at[b])
        fill.start()
        fills.append(fill)

    @pl.loop(0, tile_cols // LANES)
    def _(block):
        table[block] = -1

    @pl.loop(0, slots)
    def _(slot):
        base, _ = window_start(cols[dealing[slot]], order, tile_cols)
        for b in range(count):
            number = slot * count + b
            block = base // LANES + b
            blocks[number] = block
            known = table[block]
            owner = jnp.where(known < 0, number, known)
            owners[number] = owner
            table[block] = owner

    for fill in fills:
        fill.wait()


def prepare(dealing, cols, token, probe, measured, tile_shape):
    order = probe.shape[1]
    slots = dealing.shape[0]
    numbers = slots * (order + LANES) // LANES
    fill_cols = 2048
    return pl.pallas_call(
        functools.partial(prepare_kernel, order),
        out_shape=(
            jax.ShapeDtypeStruct(tile_shape, jnp.float32),
            jax.ShapeDtypeStruct((numbers,), jnp.int32),
            jax.ShapeDtypeStruct((numbers,), jnp.int32),
            jax.ShapeDtypeStruct((48 * order, 2 * order), jnp.bfloat16),
        ),
        in_specs=[SMEM, SMEM, SMEM, ANY, ANY, ANY],
        out_specs=(ANY, SMEM, SMEM, ANY),
        scratch_shapes=[
            pltpu.SMEM((tile_shape[2] // LANES,), jnp.int32),
            pltpu.VMEM(tile_shape[:2] + (fill_cols,), jnp.float32),
            pltpu.SemaphoreType.DMA((tile_shape[2] // fill_cols,)),
            pltpu.SemaphoreType.DMA((4,)),
        ],
        compiler_params=pltpu.CompilerParams(vmem_limit_bytes=8 * 2**20),
        cost_estimate=pl.CostEstimate(flops=0, bytes_accessed=110 * 2**20, transcendentals=0),
        name="prepare",
    )(dealing, cols, token, jnp.asarray(dft_table(order)), probe, measured)


def slot_kernel(
    dealing, rows, owners, cells, stock,
    term, kept, sent,
    wide, patch, wave, half, resid, turned, leaving, probe, table, minus, measured, sems, leave_sem,
):
    del owners
    order = term.shape[0]
    places = (stock.at[0:order, :],) + stock_places(stock, order)[2:]
    targets = (probe, table, measured)
    loads = [
        pltpu.make_async_copy(source, target, sems.at[k])
        for k, (source, target) in enumerate(zip(places, targets))
    ]
    for load in loads:
        load.start()
    total_rows = cells.shape[0]
    me = lax.axis_index("row")
    first_row = rows[dealing[me]]
    step = 64
    tile = 256

    wide[0:total_rows, :] = cells[...].astype(jnp.float32)
    wide[total_rows:, :] = jnp.zeros((SUBLANES, 2 * order), jnp.float32)

    @pl.loop(0, order // step, unroll=2)
    def _(i):
        place = pl.ds(pl.multiple_of(i * step, step), step)
        patch[place, :] = rows_from(wide, first_row + i * step, step).astype(patch.dtype)

    loads[0].wait()

    @pl.loop(0, order // step, unroll=2)
    def _(i):
        place = pl.ds(pl.multiple_of(i * step, step), step)
        found = patch[place, :].astype(jnp.float32)
        real, imag = found[:, :order], found[:, order:]
        probe_real = probe[place, :order].astype(jnp.float32)
        probe_imag = probe[place, order:].astype(jnp.float32)
        wave[place, :order] = (probe_real * real - probe_imag * imag).astype(wave.dtype)
        wave[place, order:] = (probe_real * imag + probe_imag * real).astype(wave.dtype)

    loads[1].wait()
    minus[...] = -table[:, order:]
    cos, sin = table.at[:, :order], table.at[:, order:]
    first_half, second_half = slice(0, order), slice(order, 2 * order)

    def dots(a, b, c, d):
        one = jnp.dot(a, b, preferred_element_type=jnp.float32)
        return one + jnp.dot(c, d, preferred_element_type=jnp.float32)

    real, imag = wave[:, first_half], wave[:, second_half]
    half[first_half, :] = dots(real, cos[...], imag, minus[...]).astype(half.dtype)
    half[second_half, :] = dots(real, sin[...], imag, cos[...]).astype(half.dtype)
    loads[2].wait()
    for first in range(0, order, tile):
        here = slice(first, first + tile)
        there = slice(order + first, order + first + tile)
        for top in range(0, order, tile):
            line = slice(top, top + tile)
            half_real, half_imag = half[first_half, here], half[second_half, here]
            real = dots(cos[line, :], half_real, minus[line, :], half_imag)
            imag = dots(sin[line, :], half_real, cos[line, :], half_imag)
            inverse = jnp.minimum(lax.rsqrt(real * real + imag * imag), 1.0 / MAG_FLOOR)
            shrink = 1.0 - measured[line, here].astype(jnp.float32) * inverse
            resid[line, here] = (real * shrink).astype(resid.dtype)
            resid[line, there] = (imag * shrink).astype(resid.dtype)
    real, imag = resid[:, first_half], resid[:, second_half]
    turned[first_half, :] = dots(real, cos[...], imag, sin[...]).astype(turned.dtype)
    turned[second_half, :] = dots(real, minus[...], imag, cos[...]).astype(turned.dtype)
    count = order // 2
    side = lax.rem(me, 2)
    for number, target in ((1 - side, leaving), (side, kept)):
        line = pl.ds(pl.multiple_of(number * count, count), count)
        for first in range(0, order, tile):
            here = slice(first, first + tile)
            there = slice(order + first, order + first + tile)
            turned_real, turned_imag = turned[first_half, here], turned[second_half, here]
            real = dots(cos[line, :], turned_real, sin[line, :], turned_imag)
            imag = dots(minus[line, :], turned_real, cos[line, :], turned_imag)
            patch_real = patch[line, here].astype(jnp.float32)
            patch_imag = patch[line, there].astype(jnp.float32)
            target[:, here] = (patch_real * real + patch_imag * imag).astype(target.dtype)
            target[:, there] = (patch_real * imag - patch_imag * real).astype(target.dtype)
            probe_real = probe[line, here].astype(jnp.float32)
            probe_imag = probe[line, there].astype(jnp.float32)
            term[line, here] = (probe_real * real + probe_imag * imag).astype(term.dtype)
            term[line, there] = (probe_real * imag - probe_imag * real).astype(term.dtype)
        if target is leaving:
            leave = pltpu.make_async_copy(leaving, sent, leave_sem.at[0])
            leave.start()
    leave.wait()


def slot_terms(cells, stock, dealing, rows, owners, order):
    total_rows = cells.shape[0]
    wide_cols = 2 * order
    bf16, f32 = jnp.bfloat16, jnp.float32
    return pl.pallas_call(
        slot_kernel,
        out_shape=(
            jax.ShapeDtypeStruct((order, wide_cols), bf16),
            jax.ShapeDtypeStruct((order // 2, wide_cols), f32),
            jax.ShapeDtypeStruct((order // 2, wide_cols), bf16),
        ),
        in_specs=[SMEM, SMEM, SMEM, VMEM, ANY],
        out_specs=(VMEM, VMEM, ANY),
        scratch_shapes=[
            pltpu.VMEM((total_rows + SUBLANES, wide_cols), f32),
            pltpu.VMEM((order, wide_cols), bf16),
            pltpu.VMEM((order, wide_cols), bf16),
            pltpu.VMEM((wide_cols, order), bf16),
            pltpu.VMEM((order, wide_cols), bf16),
            pltpu.VMEM((wide_cols, order), bf16),
            pltpu.VMEM((order // 2, wide_cols), bf16),
            pltpu.VMEM((order, wide_cols), bf16),
            pltpu.VMEM((order, wide_cols), bf16),
            pltpu.VMEM((order, order), bf16),
            pltpu.VMEM((order, order), bf16),
            pltpu.SemaphoreType.DMA((3,)),
            pltpu.SemaphoreType.DMA((1,)),
        ],
        compiler_params=pltpu.CompilerParams(vmem_limit_bytes=24 * 2**20),
        cost_estimate=pl.CostEstimate(
            flops=8 * 2 * order**3 * 2, bytes_accessed=8 * 2**20, transcendentals=order * order
        ),
        name="slot",
    )(dealing, rows, owners, cells, stock)


def pack_kernel(reach, own_rows, dealing, rows, term, out, padded):
    order = term.shape[0]
    first_row = rows[dealing[lax.axis_index("row")]]
    below = padded.shape[0] - reach - order
    padded[0:reach, :] = jnp.zeros((reach, padded.shape[1]), jnp.float32)
    padded[reach : reach + order, :] = term[...].astype(jnp.float32)
    padded[reach + order :, :] = jnp.zeros((below, padded.shape[1]), jnp.float32)

    @pl.loop(0, out.shape[0], unroll=2)
    def _(k):
        out[k] = rows_from(padded, reach - first_row + k * own_rows, out.shape[1]).astype(out.dtype)


def pack_rows(term, dealing, rows, slots, own_rows, tile_rows):
    order, width = term.shape
    reach = slots * own_rows - order
    return pl.pallas_call(
        functools.partial(pack_kernel, reach, own_rows),
        out_shape=jax.ShapeDtypeStruct((slots, tile_rows, width), jnp.bfloat16),
        in_specs=[SMEM, SMEM, VMEM],
        out_specs=VMEM,
        scratch_shapes=[pltpu.VMEM((2 * reach + order + tile_rows + SUBLANES, width), jnp.float32)],
        compiler_params=pltpu.CompilerParams(vmem_limit_bytes=8 * 2**20),
        cost_estimate=pl.CostEstimate(flops=0, bytes_accessed=3 * 2**20, transcendentals=0),
        name="pack",
    )(dealing, rows, term)


def place_kernel(order, dealing, cols, blocks, owners, terms, empty, out, totals, sems):
    del empty
    slots, tile_rows = terms.shape[0], terms.shape[1]
    count = (order + LANES) // LANES
    lane = lax.broadcasted_iota(jnp.int32, (tile_rows, LANES), 1)
    nothing = jnp.zeros((tile_rows, LANES), jnp.float32)

    @pl.loop(0, slots, unroll=4)
    def _(slot):
        _, offset = window_start(cols[dealing[slot]], order, out.shape[2])
        shift = lax.rem(offset, LANES)
        for part in range(2):
            turned = []
            for b in range(count - 1):
                first = part * order + b * LANES
                turned.append(pltpu.roll(terms[slot, :, first : first + LANES], shift, 1).astype(jnp.float32))
            holders = [owners[slot * count + b] for b in range(count)]
            held = [totals[holder, part] for holder in holders]
            for b in range(count):
                before = turned[b - 1] if b else nothing
                after = turned[b] if b < count - 1 else nothing
                term = jnp.where(lane < offset, before, after)
                first_one = holders[b] == slot * count + b
                totals[holders[b], part] = jnp.where(first_one, term, held[b] + term)

    def copy(number):
        place = pl.multiple_of(blocks[number] * LANES, LANES)
        return pltpu.make_async_copy(totals.at[number], out.at[:, :, pl.ds(place, LANES)], sems.at[number])

    @pl.loop(0, slots * count)
    def _(number):
        @pl.when(owners[number] == number)
        def _():
            copy(number).start()

    @pl.loop(0, slots * count)
    def _(number):
        @pl.when(owners[number] == number)
        def _():
            copy(number).wait()


def place_windows(terms, empty, blocks, owners, dealing, cols, order):
    slots, tile_rows = terms.shape[0], terms.shape[1]
    count = (order + LANES) // LANES
    return pl.pallas_call(
        functools.partial(place_kernel, order),
        out_shape=jax.ShapeDtypeStruct(empty.shape, empty.dtype),
        in_specs=[SMEM, SMEM, SMEM, SMEM, VMEM, ANY],
        out_specs=ANY,
        scratch_shapes=[
            pltpu.VMEM((slots * count, 2, tile_rows, LANES), jnp.float32),
            pltpu.SemaphoreType.DMA((slots * count,)),
        ],
        input_output_aliases={5: 0},
        compiler_params=pltpu.CompilerParams(vmem_limit_bytes=12 * 2**20),
        cost_estimate=pl.CostEstimate(flops=0, bytes_accessed=6 * 2**20, transcendentals=0),
        name="place",
    )(dealing, cols, blocks, owners, terms, empty)


def strides(devices):
    steps, stride = [], 1
    while stride < devices:
        radix = 4 if len(steps) >= 2 and (devices // stride) % 4 == 0 else 2
        steps.append((stride, radix))
        stride *= radix
    return steps


def swap(x, distance, devices):
    return lax.ppermute(x, "row", [(d, d ^ distance) for d in range(devices)])


def sum_probe(kept, sent, devices):
    me = lax.axis_index("row")
    addends = [kept, swap(sent, 1, devices)]

    def rows(index, count):
        found = [lax.dynamic_slice_in_dim(x, index * count, count).astype(jnp.float32) for x in addends]
        return found[0] + found[1]

    for stride, radix in strides(devices)[1:]:
        digit = me // stride % radix
        count = addends[0].shape[0] // radix
        met = []
        for k in range(1, radix):
            share = rows(lax.bitwise_xor(digit, k), count).astype(jnp.bfloat16)
            met.append(swap(share, k * stride, devices))
        own = rows(digit, count)
        for one in met[:-1]:
            own = own + one.astype(jnp.float32)
        addends = [own, met[-1]]
    return addends[0] + addends[1].astype(jnp.float32)


def join(whole, devices):
    me = lax.axis_index("row")
    for stride, radix in reversed(strides(devices)):
        digit = me // stride % radix
        shares = [whole] + [swap(whole, k * stride, devices) for k in range(1, radix)]
        pieces = []
        for j in range(radix):
            piece = shares[0]
            for k in range(1, radix):
                piece = jnp.where(lax.bitwise_xor(digit, k) == j, shares[k], piece)
            pieces.append(piece)
        whole = jnp.concatenate(pieces, axis=0)
    return whole


def body(object_field, probe, amplitude, row_offsets, col_offsets, dealing):
    order = probe.shape[1]
    devices = lax.axis_size("row")
    own_rows, tile_cols = object_field.shape[1], object_field.shape[2]
    total_rows = devices * own_rows
    tile_rows = -(-own_rows // SUBLANES) * SUBLANES
    spare = tile_rows - own_rows
    if spare:
        object_field = jnp.pad(object_field, ((0, 0), (0, spare), (0, 0)))
    pieces, token = fetch_windows(object_field, dealing, col_offsets, order)
    strips = lax.all_to_all(pieces, "row", split_axis=0, concat_axis=0, tiled=True)
    cells = strips[:, :own_rows].reshape(total_rows, 2 * order)
    empty, blocks, owners, stock = prepare(
        dealing, col_offsets, token, probe, amplitude, object_field.shape
    )
    term, kept, sent = slot_terms(cells, stock, dealing, row_offsets, owners, order)
    total = sum_probe(kept, sent, devices)
    terms = pack_rows(term, dealing, row_offsets, devices, own_rows, tile_rows)
    terms, total = lax.optimization_barrier((terms, total))
    arrived = lax.all_to_all(terms, "row", split_axis=0, concat_axis=0, tiled=True)
    share = (total * (1.0 / dealing.shape[0])).astype(jnp.bfloat16)
    whole = join(share, devices).astype(jnp.float32)
    probe_grad = jnp.stack([whole[:, :order], whole[:, order:]])
    object_grad = place_windows(arrived, empty, blocks, owners, dealing, col_offsets, order)
    if spare:
        object_grad = object_grad[:, :own_rows]
    return (object_grad, probe_grad)


def solution(mesh):
    return jax.shard_map(
        body,
        mesh=mesh,
        in_specs=(
            P(None, ("groups", "row"), None),
            P("groups", None, None),
            P(("groups", "row"), None, None),
            P("groups"),
            P("groups"),
            P("groups"),
        ),
        out_specs=(P(None, ("groups", "row"), None), P("groups", None, None)),
        check_vma=False,
    )
```

```python
import functools
import math

import jax
import jax.numpy as jnp
import numpy as np
from jax import lax
from jax.experimental import pallas as pl
from jax.experimental.pallas import tpu as pltpu
from jax.sharding import PartitionSpec as P

MAG_FLOOR = 0.25
LANES = 128
SUBLANES = 8
SMEM = pl.BlockSpec(memory_space=pltpu.SMEM)
VMEM = pl.BlockSpec(memory_space=pltpu.VMEM)
ANY = pl.BlockSpec(memory_space=pl.ANY)


def dft_table(order):
    indices = np.arange(order, dtype=np.int32)
    phases = indices[:, None] * indices[None, :] % order
    angles = phases.astype(np.float32) * np.float32(2.0 * math.pi / order)
    factor = np.float32(1.0 / math.sqrt(order))
    return np.concatenate([np.cos(angles) * factor, -np.sin(angles) * factor], axis=1).astype(jnp.bfloat16)


def window_start(column, order, tile_cols):
    span = order + LANES
    base = jnp.minimum(column // LANES, (tile_cols - span) // LANES) * LANES
    return pl.multiple_of(base, LANES), column - base


def rows_from(ref, start, count):
    aligned = pl.multiple_of(start // SUBLANES * SUBLANES, SUBLANES)
    rest = start - aligned
    width = ref.shape[-1]
    blocks = ref[pl.ds(aligned, count + SUBLANES), :].reshape(-1, SUBLANES, width)
    turned = pltpu.roll(blocks, lax.rem(SUBLANES - rest, SUBLANES), 1)
    sub = lax.broadcasted_iota(jnp.int32, (1, SUBLANES, width), 1)
    picked = jnp.where(sub < SUBLANES - rest, turned[:-1], turned[1:])
    return picked.reshape(count, width)


def fetch_kernel(order, dealing, cols, tile, out, token, held, sems):
    token[0] = dealing[0]
    slots, tile_rows = out.shape[0], out.shape[1]
    tile_cols = tile.shape[2]
    span = order + LANES

    def copy(slot):
        base, _ = window_start(cols[dealing[slot]], order, tile_cols)
        return pltpu.make_async_copy(tile.at[:, :, pl.ds(base, span)], held.at[slot], sems.at[slot])

    @pl.loop(0, slots)
    def _(slot):
        copy(slot).start()

    lane = lax.broadcasted_iota(jnp.int32, (tile_rows, LANES), 1)

    @pl.loop(0, slots, unroll=4)
    def _(slot):
        copy(slot).wait()
        _, offset = window_start(cols[dealing[slot]], order, tile_cols)
        shift = lax.rem(LANES - lax.rem(offset, LANES), LANES)
        for part in range(2):
            turned = [
                pltpu.roll(held[slot, part, :, b * LANES : (b + 1) * LANES].astype(out.dtype), shift, 1)
                for b in range(span // LANES)
            ]
            for b in range(order // LANES):
                first = part * order + b * LANES
                cells = jnp.where(lane < LANES - offset, turned[b], turned[b + 1])
                out[slot, :, first : first + LANES] = cells


def fetch_windows(tile, dealing, cols, order):
    slots, tile_rows, tile_cols = dealing.shape[0], tile.shape[1], tile.shape[2]
    span = order + LANES

    return pl.pallas_call(
        functools.partial(fetch_kernel, order),
        out_shape=(
            jax.ShapeDtypeStruct((slots, tile_rows, 2 * order), jnp.bfloat16),
            jax.ShapeDtypeStruct((1,), jnp.int32),
        ),
        in_specs=[SMEM, SMEM, ANY],
        out_specs=(VMEM, SMEM),
        scratch_shapes=[
            pltpu.VMEM((slots, 2, tile_rows, span), jnp.float32),
            pltpu.SemaphoreType.DMA((slots,)),
        ],
        compiler_params=pltpu.CompilerParams(vmem_limit_bytes=56 * 2**20),
        cost_estimate=pl.CostEstimate(flops=0, bytes_accessed=6 * 2**20, transcendentals=0),
        name="fetch",
    )(dealing, cols, tile)


def stock_places(stock, order):
    return (
        stock.at[0:order, 0:order],
        stock.at[0:order, order : 2 * order],
        stock.at[order : 2 * order, :],
        stock.at[2 * order : 3 * order, 0:order],
    )


def prepare_kernel(
    order, dealing, rows, cols, token, table_in, probe, measured,
    empty, starts, info, stock,
    table, zeros, sems, stock_sems,
):
    del token
    places = stock_places(stock, order)
    sources = (probe.at[0], probe.at[1], table_in, measured.at[0])
    fills = []
    for k, (source, place) in enumerate(zip(sources, places)):
        fill = pltpu.make_async_copy(source, place, stock_sems.at[k])
        fill.start()
        fills.append(fill)
    count = (order + LANES) // LANES
    slots = dealing.shape[0]
    tile_cols = empty.shape[2]
    width = zeros.shape[2]
    zeros[...] = jnp.zeros_like(zeros)
    for b in range(tile_cols // width):
        fill = pltpu.make_async_copy(zeros, empty.at[:, :, b * width : (b + 1) * width], sems.at[b])
        fill.start()
        fills.append(fill)

    @pl.loop(0, tile_cols // LANES)
    def _(block):
        table[block] = -1

    @pl.loop(0, slots)
    def _(slot):
        base, offset = window_start(cols[dealing[slot]], order, tile_cols)
        starts[slot] = rows[dealing[slot]]
        info[2 * slots * count + slot] = offset
        for b in range(count):
            number = slot * count + b
            block = base // LANES + b
            info[number] = block
            known = table[block]
            owner = jnp.where(known < 0, number, known)
            info[slots * count + number] = owner
            table[block] = owner

    for fill in fills:
        fill.wait()


def prepare(dealing, rows, cols, token, probe, measured, tile_shape):
    order = probe.shape[1]
    slots = dealing.shape[0]
    numbers = slots * (order + LANES) // LANES
    fill_cols = 2048
    return pl.pallas_call(
        functools.partial(prepare_kernel, order),
        out_shape=(
            jax.ShapeDtypeStruct(tile_shape, jnp.float32),
            jax.ShapeDtypeStruct((slots,), jnp.int32),
            jax.ShapeDtypeStruct((2 * numbers + slots,), jnp.int32),
            jax.ShapeDtypeStruct((48 * order, 2 * order), jnp.bfloat16),
        ),
        in_specs=[SMEM, SMEM, SMEM, SMEM, ANY, ANY, ANY],
        out_specs=(ANY, SMEM, SMEM, ANY),
        scratch_shapes=[
            pltpu.SMEM((tile_shape[2] // LANES,), jnp.int32),
            pltpu.VMEM(tile_shape[:2] + (fill_cols,), jnp.float32),
            pltpu.SemaphoreType.DMA((tile_shape[2] // fill_cols,)),
            pltpu.SemaphoreType.DMA((4,)),
        ],
        compiler_params=pltpu.CompilerParams(vmem_limit_bytes=8 * 2**20),
        cost_estimate=pl.CostEstimate(flops=0, bytes_accessed=110 * 2**20, transcendentals=0),
        name="prepare",
    )(dealing, rows, cols, token, jnp.asarray(dft_table(order)), probe, measured)


def slot_kernel(
    starts, cells, stock,
    term, kept, sent,
    wide, patch, wave, half, resid, turned, leaving, probe, table, minus, measured, sems, leave_sem,
):
    order = term.shape[0]
    places = (stock.at[0:order, :],) + stock_places(stock, order)[2:]
    targets = (probe, table, measured)
    loads = [
        pltpu.make_async_copy(source, target, sems.at[k])
        for k, (source, target) in enumerate(zip(places, targets))
    ]
    for load in loads:
        load.start()
    total_rows = cells.shape[0]
    me = lax.axis_index("row")
    first_row = starts[me]
    step = 64
    tile = 256

    wide[0:total_rows, :] = cells[...].astype(jnp.float32)
    wide[total_rows:, :] = jnp.zeros((SUBLANES, 2 * order), jnp.float32)

    @pl.loop(0, order // step, unroll=2)
    def _(i):
        place = pl.ds(pl.multiple_of(i * step, step), step)
        patch[place, :] = rows_from(wide, first_row + i * step, step).astype(patch.dtype)

    loads[0].wait()

    @pl.loop(0, order // step, unroll=2)
    def _(i):
        place = pl.ds(pl.multiple_of(i * step, step), step)
        found = patch[place, :].astype(jnp.float32)
        real, imag = found[:, :order], found[:, order:]
        probe_real = probe[place, :order].astype(jnp.float32)
        probe_imag = probe[place, order:].astype(jnp.float32)
        wave[place, :order] = (probe_real * real - probe_imag * imag).astype(wave.dtype)
        wave[place, order:] = (probe_real * imag + probe_imag * real).astype(wave.dtype)

    loads[1].wait()
    minus[...] = -table[:, order:]
    cos, sin = table.at[:, :order], table.at[:, order:]
    first_half, second_half = slice(0, order), slice(order, 2 * order)

    def dots(a, b, c, d):
        one = jnp.dot(a, b, preferred_element_type=jnp.float32)
        return one + jnp.dot(c, d, preferred_element_type=jnp.float32)

    real, imag = wave[:, first_half], wave[:, second_half]
    half[first_half, :] = dots(real, cos[...], imag, minus[...]).astype(half.dtype)
    half[second_half, :] = dots(real, sin[...], imag, cos[...]).astype(half.dtype)
    loads[2].wait()
    for first in range(0, order, tile):
        here = slice(first, first + tile)
        there = slice(order + first, order + first + tile)
        for top in range(0, order, tile):
            line = slice(top, top + tile)
            half_real, half_imag = half[first_half, here], half[second_half, here]
            real = dots(cos[line, :], half_real, minus[line, :], half_imag)
            imag = dots(sin[line, :], half_real, cos[line, :], half_imag)
            inverse = jnp.minimum(lax.rsqrt(real * real + imag * imag), 1.0 / MAG_FLOOR)
            shrink = 1.0 - measured[line, here].astype(jnp.float32) * inverse
            resid[line, here] = (real * shrink).astype(resid.dtype)
            resid[line, there] = (imag * shrink).astype(resid.dtype)
    real, imag = resid[:, first_half], resid[:, second_half]
    turned[first_half, :] = dots(real, cos[...], imag, sin[...]).astype(turned.dtype)
    turned[second_half, :] = dots(real, minus[...], imag, cos[...]).astype(turned.dtype)
    count = order // 2
    side = lax.rem(me, 2)
    for number, target in ((1 - side, leaving), (side, kept)):
        line = pl.ds(pl.multiple_of(number * count, count), count)
        for first in range(0, order, tile):
            here = slice(first, first + tile)
            there = slice(order + first, order + first + tile)
            turned_real, turned_imag = turned[first_half, here], turned[second_half, here]
            real = dots(cos[line, :], turned_real, sin[line, :], turned_imag)
            imag = dots(minus[line, :], turned_real, cos[line, :], turned_imag)
            patch_real = patch[line, here].astype(jnp.float32)
            patch_imag = patch[line, there].astype(jnp.float32)
            target[:, here] = (patch_real * real + patch_imag * imag).astype(target.dtype)
            target[:, there] = (patch_real * imag - patch_imag * real).astype(target.dtype)
            probe_real = probe[line, here].astype(jnp.float32)
            probe_imag = probe[line, there].astype(jnp.float32)
            term[line, here] = (probe_real * real + probe_imag * imag).astype(term.dtype)
            term[line, there] = (probe_real * imag - probe_imag * real).astype(term.dtype)
        if target is leaving:
            leave = pltpu.make_async_copy(leaving, sent, leave_sem.at[0])
            leave.start()
    leave.wait()


def slot_terms(cells, stock, starts, order):
    total_rows = cells.shape[0]
    wide_cols = 2 * order
    bf16, f32 = jnp.bfloat16, jnp.float32
    return pl.pallas_call(
        slot_kernel,
        out_shape=(
            jax.ShapeDtypeStruct((order, wide_cols), bf16),
            jax.ShapeDtypeStruct((order // 2, wide_cols), f32),
            jax.ShapeDtypeStruct((order // 2, wide_cols), bf16),
        ),
        in_specs=[SMEM, VMEM, ANY],
        out_specs=(VMEM, VMEM, ANY),
        scratch_shapes=[
            pltpu.VMEM((total_rows + SUBLANES, wide_cols), f32),
            pltpu.VMEM((order, wide_cols), bf16),
            pltpu.VMEM((order, wide_cols), bf16),
            pltpu.VMEM((wide_cols, order), bf16),
            pltpu.VMEM((order, wide_cols), bf16),
            pltpu.VMEM((wide_cols, order), bf16),
            pltpu.VMEM((order // 2, wide_cols), bf16),
            pltpu.VMEM((order, wide_cols), bf16),
            pltpu.VMEM((order, wide_cols), bf16),
            pltpu.VMEM((order, order), bf16),
            pltpu.VMEM((order, order), bf16),
            pltpu.SemaphoreType.DMA((3,)),
            pltpu.SemaphoreType.DMA((1,)),
        ],
        compiler_params=pltpu.CompilerParams(vmem_limit_bytes=24 * 2**20),
        cost_estimate=pl.CostEstimate(
            flops=8 * 2 * order**3 * 2, bytes_accessed=8 * 2**20, transcendentals=order * order
        ),
        name="slot",
    )(starts, cells, stock)


def pack_kernel(reach, own_rows, starts, term, out, padded):
    order = term.shape[0]
    first_row = starts[lax.axis_index("row")]
    below = padded.shape[0] - reach - order
    padded[0:reach, :] = jnp.zeros((reach, padded.shape[1]), jnp.float32)
    padded[reach : reach + order, :] = term[...].astype(jnp.float32)
    padded[reach + order :, :] = jnp.zeros((below, padded.shape[1]), jnp.float32)

    @pl.loop(0, out.shape[0], unroll=2)
    def _(k):
        out[k] = rows_from(padded, reach - first_row + k * own_rows, out.shape[1]).astype(out.dtype)


def pack_rows(term, starts, slots, own_rows, tile_rows):
    order, width = term.shape
    reach = slots * own_rows - order
    return pl.pallas_call(
        functools.partial(pack_kernel, reach, own_rows),
        out_shape=jax.ShapeDtypeStruct((slots, tile_rows, width), jnp.bfloat16),
        in_specs=[SMEM, VMEM],
        out_specs=VMEM,
        scratch_shapes=[pltpu.VMEM((2 * reach + order + tile_rows + SUBLANES, width), jnp.float32)],
        compiler_params=pltpu.CompilerParams(vmem_limit_bytes=8 * 2**20),
        cost_estimate=pl.CostEstimate(flops=0, bytes_accessed=3 * 2**20, transcendentals=0),
        name="pack",
    )(starts, term)


def place_kernel(order, info, terms, empty, out, totals, sems):
    del empty
    slots, tile_rows = terms.shape[0], terms.shape[1]
    count = (order + LANES) // LANES
    lane = lax.broadcasted_iota(jnp.int32, (tile_rows, LANES), 1)
    nothing = jnp.zeros((tile_rows, LANES), jnp.float32)

    @pl.loop(0, slots, unroll=4)
    def _(slot):
        offset = info[2 * slots * count + slot]
        shift = lax.rem(offset, LANES)
        for part in range(2):
            turned = []
            for b in range(count - 1):
                first = part * order + b * LANES
                turned.append(pltpu.roll(terms[slot, :, first : first + LANES], shift, 1).astype(jnp.float32))
            holders = [info[slots * count + slot * count + b] for b in range(count)]
            held = [totals[holder, part] for holder in holders]
            for b in range(count):
                before = turned[b - 1] if b else nothing
                after = turned[b] if b < count - 1 else nothing
                term = jnp.where(lane < offset, before, after)
                first_one = holders[b] == slot * count + b
                totals[holders[b], part] = jnp.where(first_one, term, held[b] + term)

    def copy(number):
        place = pl.multiple_of(info[number] * LANES, LANES)
        return pltpu.make_async_copy(totals.at[number], out.at[:, :, pl.ds(place, LANES)], sems.at[number])

    @pl.loop(0, slots * count)
    def _(number):
        @pl.when(info[slots * count + number] == number)
        def _():
            copy(number).start()

    @pl.loop(0, slots * count)
    def _(number):
        @pl.when(info[slots * count + number] == number)
        def _():
            copy(number).wait()


def place_windows(terms, empty, info, order):
    slots, tile_rows = terms.shape[0], terms.shape[1]
    count = (order + LANES) // LANES
    return pl.pallas_call(
        functools.partial(place_kernel, order),
        out_shape=jax.ShapeDtypeStruct(empty.shape, empty.dtype),
        in_specs=[SMEM, VMEM, ANY],
        out_specs=ANY,
        scratch_shapes=[
            pltpu.VMEM((slots * count, 2, tile_rows, LANES), jnp.float32),
            pltpu.SemaphoreType.DMA((slots * count,)),
        ],
        input_output_aliases={2: 0},
        compiler_params=pltpu.CompilerParams(vmem_limit_bytes=12 * 2**20),
        cost_estimate=pl.CostEstimate(flops=0, bytes_accessed=6 * 2**20, transcendentals=0),
        name="place",
    )(info, terms, empty)


def strides(devices):
    steps, stride = [], 1
    while stride < devices:
        radix = 4 if len(steps) >= 2 and (devices // stride) % 4 == 0 else 2
        steps.append((stride, radix))
        stride *= radix
    return steps


def swap(x, distance, devices):
    return lax.ppermute(x, "row", [(d, d ^ distance) for d in range(devices)])


def sum_probe(kept, sent, devices):
    me = lax.axis_index("row")
    addends = [kept, swap(sent, 1, devices)]

    def rows(index, count):
        found = [lax.dynamic_slice_in_dim(x, index * count, count).astype(jnp.float32) for x in addends]
        return found[0] + found[1]

    for stride, radix in strides(devices)[1:]:
        digit = me // stride % radix
        count = addends[0].shape[0] // radix
        met = []
        for k in range(1, radix):
            share = rows(lax.bitwise_xor(digit, k), count).astype(jnp.bfloat16)
            met.append(swap(share, k * stride, devices))
        own = rows(digit, count)
        for one in met[:-1]:
            own = own + one.astype(jnp.float32)
        addends = [own, met[-1]]
    return addends[0] + addends[1].astype(jnp.float32)


def join(whole, devices):
    me = lax.axis_index("row")
    for stride, radix in reversed(strides(devices)):
        digit = me // stride % radix
        shares = [whole] + [swap(whole, k * stride, devices) for k in range(1, radix)]
        pieces = []
        for j in range(radix):
            piece = shares[0]
            for k in range(1, radix):
                piece = jnp.where(lax.bitwise_xor(digit, k) == j, shares[k], piece)
            pieces.append(piece)
        whole = jnp.concatenate(pieces, axis=0)
    return whole


def body(object_field, probe, amplitude, row_offsets, col_offsets, dealing):
    order = probe.shape[1]
    devices = lax.axis_size("row")
    own_rows, tile_cols = object_field.shape[1], object_field.shape[2]
    total_rows = devices * own_rows
    tile_rows = -(-own_rows // SUBLANES) * SUBLANES
    spare = tile_rows - own_rows
    if spare:
        object_field = jnp.pad(object_field, ((0, 0), (0, spare), (0, 0)))
    pieces, token = fetch_windows(object_field, dealing, col_offsets, order)
    strips = lax.all_to_all(pieces, "row", split_axis=0, concat_axis=0, tiled=True)
    cells = strips[:, :own_rows].reshape(total_rows, 2 * order)
    empty, starts, info, stock = prepare(
        dealing, row_offsets, col_offsets, token, probe, amplitude, object_field.shape
    )
    term, kept, sent = slot_terms(cells, stock, starts, order)
    total = sum_probe(kept, sent, devices)
    terms = pack_rows(term, starts, devices, own_rows, tile_rows)
    terms, total = lax.optimization_barrier((terms, total))
    arrived = lax.all_to_all(terms, "row", split_axis=0, concat_axis=0, tiled=True)
    share = (total * (1.0 / dealing.shape[0])).astype(jnp.bfloat16)
    whole = join(share, devices).astype(jnp.float32)
    probe_grad = jnp.stack([whole[:, :order], whole[:, order:]])
    object_grad = place_windows(arrived, empty, info, order)
    if spare:
        object_grad = object_grad[:, :own_rows]
    return (object_grad, probe_grad)


def solution(mesh):
    return jax.shard_map(
        body,
        mesh=mesh,
        in_specs=(
            P(None, ("groups", "row"), None),
            P("groups", None, None),
            P(("groups", "row"), None, None),
            P("groups"),
            P("groups"),
            P("groups"),
        ),
        out_specs=(P(None, ("groups", "row"), None), P("groups", None, None)),
        check_vma=False,
    )
```

```python
import functools
import math

import jax
import jax.numpy as jnp
import numpy as np
from jax import lax
from jax.experimental import pallas as pl
from jax.experimental.pallas import tpu as pltpu
from jax.sharding import PartitionSpec as P

MAG_FLOOR = 0.25
LANES = 128
SUBLANES = 8
SMEM = pl.BlockSpec(memory_space=pltpu.SMEM)
VMEM = pl.BlockSpec(memory_space=pltpu.VMEM)
ANY = pl.BlockSpec(memory_space=pl.ANY)


def dft_table(order):
    indices = np.arange(order, dtype=np.int32)
    phases = indices[:, None] * indices[None, :] % order
    angles = phases.astype(np.float32) * np.float32(2.0 * math.pi / order)
    factor = np.float32(1.0 / math.sqrt(order))
    return np.concatenate([np.cos(angles) * factor, -np.sin(angles) * factor], axis=1).astype(jnp.bfloat16)


def window_start(column, order, tile_cols):
    span = order + LANES
    base = jnp.minimum(column // LANES, (tile_cols - span) // LANES) * LANES
    return pl.multiple_of(base, LANES), column - base


def rows_from(ref, start, count):
    aligned = pl.multiple_of(start // SUBLANES * SUBLANES, SUBLANES)
    rest = start - aligned
    width = ref.shape[-1]
    blocks = ref[pl.ds(aligned, count + SUBLANES), :].reshape(-1, SUBLANES, width)
    turned = pltpu.roll(blocks, lax.rem(SUBLANES - rest, SUBLANES), 1)
    sub = lax.broadcasted_iota(jnp.int32, (1, SUBLANES, width), 1)
    picked = jnp.where(sub < SUBLANES - rest, turned[:-1], turned[1:])
    return picked.reshape(count, width)


def fetch_kernel(order, dealing, cols, tile, out, token, held, sems):
    token[0] = dealing[0]
    slots, tile_rows = out.shape[0], out.shape[1]
    tile_cols = tile.shape[2]
    span = order + LANES

    def copy(slot):
        base, _ = window_start(cols[dealing[slot]], order, tile_cols)
        return pltpu.make_async_copy(tile.at[:, :, pl.ds(base, span)], held.at[slot], sems.at[slot])

    @pl.loop(0, slots, unroll=8)
    def _(slot):
        copy(slot).start()

    lane = lax.broadcasted_iota(jnp.int32, (tile_rows, LANES), 1)

    @pl.loop(0, slots, unroll=8)
    def _(slot):
        copy(slot).wait()
        _, offset = window_start(cols[dealing[slot]], order, tile_cols)
        shift = lax.rem(LANES - lax.rem(offset, LANES), LANES)
        for part in range(2):
            turned = [
                pltpu.roll(held[slot, part, :, b * LANES : (b + 1) * LANES].astype(out.dtype), shift, 1)
                for b in range(span // LANES)
            ]
            for b in range(order // LANES):
                first = part * order + b * LANES
                cells = jnp.where(lane < LANES - offset, turned[b], turned[b + 1])
                out[slot, :, first : first + LANES] = cells


def fetch_windows(tile, dealing, cols, order):
    slots, tile_rows, tile_cols = dealing.shape[0], tile.shape[1], tile.shape[2]
    span = order + LANES

    return pl.pallas_call(
        functools.partial(fetch_kernel, order),
        out_shape=(
            jax.ShapeDtypeStruct((slots, tile_rows, 2 * order), jnp.bfloat16),
            jax.ShapeDtypeStruct((1,), jnp.int32),
        ),
        in_specs=[SMEM, SMEM, ANY],
        out_specs=(VMEM, SMEM),
        scratch_shapes=[
            pltpu.VMEM((slots, 2, tile_rows, span), jnp.float32),
            pltpu.SemaphoreType.DMA((slots,)),
        ],
        compiler_params=pltpu.CompilerParams(vmem_limit_bytes=56 * 2**20),
        cost_estimate=pl.CostEstimate(flops=0, bytes_accessed=6 * 2**20, transcendentals=0),
        name="fetch",
    )(dealing, cols, tile)


def stock_places(stock, order):
    return (
        stock.at[0:order, 0:order],
        stock.at[0:order, order : 2 * order],
        stock.at[order : 2 * order, :],
        stock.at[2 * order : 3 * order, 0:order],
    )


def prepare_kernel(
    order, dealing, rows, cols, token, table_in, probe, measured,
    empty, starts, info, stock,
    table, zeros, sems, stock_sems,
):
    del token
    places = stock_places(stock, order)
    sources = (probe.at[0], probe.at[1], table_in, measured.at[0])
    fills = []
    for k, (source, place) in enumerate(zip(sources, places)):
        fill = pltpu.make_async_copy(source, place, stock_sems.at[k])
        fill.start()
        fills.append(fill)
    count = (order + LANES) // LANES
    slots = dealing.shape[0]
    tile_cols = empty.shape[2]
    width = zeros.shape[2]
    zeros[...] = jnp.zeros_like(zeros)
    for b in range(tile_cols // width):
        fill = pltpu.make_async_copy(zeros, empty.at[:, :, b * width : (b + 1) * width], sems.at[b])
        fill.start()
        fills.append(fill)

    @pl.loop(0, tile_cols // LANES)
    def _(block):
        table[block] = -1

    @pl.loop(0, slots)
    def _(slot):
        base, offset = window_start(cols[dealing[slot]], order, tile_cols)
        starts[slot] = rows[dealing[slot]]
        info[2 * slots * count + slot] = offset
        for b in range(count):
            number = slot * count + b
            block = base // LANES + b
            info[number] = block
            known = table[block]
            owner = jnp.where(known < 0, number, known)
            info[slots * count + number] = owner
            table[block] = owner

    for fill in fills:
        fill.wait()


def prepare(dealing, rows, cols, token, probe, measured, tile_shape):
    order = probe.shape[1]
    slots = dealing.shape[0]
    numbers = slots * (order + LANES) // LANES
    fill_cols = 2048
    return pl.pallas_call(
        functools.partial(prepare_kernel, order),
        out_shape=(
            jax.ShapeDtypeStruct(tile_shape, jnp.float32),
            jax.ShapeDtypeStruct((slots,), jnp.int32),
            jax.ShapeDtypeStruct((2 * numbers + slots,), jnp.int32),
            jax.ShapeDtypeStruct((48 * order, 2 * order), jnp.bfloat16),
        ),
        in_specs=[SMEM, SMEM, SMEM, SMEM, ANY, ANY, ANY],
        out_specs=(ANY, SMEM, SMEM, ANY),
        scratch_shapes=[
            pltpu.SMEM((tile_shape[2] // LANES,), jnp.int32),
            pltpu.VMEM(tile_shape[:2] + (fill_cols,), jnp.float32),
            pltpu.SemaphoreType.DMA((tile_shape[2] // fill_cols,)),
            pltpu.SemaphoreType.DMA((4,)),
        ],
        compiler_params=pltpu.CompilerParams(vmem_limit_bytes=8 * 2**20),
        cost_estimate=pl.CostEstimate(flops=0, bytes_accessed=110 * 2**20, transcendentals=0),
        name="prepare",
    )(dealing, rows, cols, token, jnp.asarray(dft_table(order)), probe, measured)


def slot_kernel(
    starts, cells, stock,
    term, kept, sent,
    wide, patch, wave, half, resid, turned, leaving, probe, table, minus, measured, sems, leave_sem,
):
    order = term.shape[0]
    places = (stock.at[0:order, :],) + stock_places(stock, order)[2:]
    targets = (probe, table, measured)
    loads = [
        pltpu.make_async_copy(source, target, sems.at[k])
        for k, (source, target) in enumerate(zip(places, targets))
    ]
    for load in loads:
        load.start()
    total_rows = cells.shape[0]
    me = lax.axis_index("row")
    first_row = starts[me]
    step = 64
    tile = 256

    wide[0:total_rows, :] = cells[...].astype(jnp.float32)
    wide[total_rows:, :] = jnp.zeros((SUBLANES, 2 * order), jnp.float32)

    @pl.loop(0, order // step, unroll=2)
    def _(i):
        place = pl.ds(pl.multiple_of(i * step, step), step)
        patch[place, :] = rows_from(wide, first_row + i * step, step).astype(patch.dtype)

    loads[0].wait()

    @pl.loop(0, order // step, unroll=2)
    def _(i):
        place = pl.ds(pl.multiple_of(i * step, step), step)
        found = patch[place, :].astype(jnp.float32)
        real, imag = found[:, :order], found[:, order:]
        probe_real = probe[place, :order].astype(jnp.float32)
        probe_imag = probe[place, order:].astype(jnp.float32)
        wave[place, :order] = (probe_real * real - probe_imag * imag).astype(wave.dtype)
        wave[place, order:] = (probe_real * imag + probe_imag * real).astype(wave.dtype)

    loads[1].wait()
    minus[...] = -table[:, order:]
    cos, sin = table.at[:, :order], table.at[:, order:]
    first_half, second_half = slice(0, order), slice(order, 2 * order)

    def dots(a, b, c, d):
        one = jnp.dot(a, b, preferred_element_type=jnp.float32)
        return one + jnp.dot(c, d, preferred_element_type=jnp.float32)

    real, imag = wave[:, first_half], wave[:, second_half]
    half[first_half, :] = dots(real, cos[...], imag, minus[...]).astype(half.dtype)
    half[second_half, :] = dots(real, sin[...], imag, cos[...]).astype(half.dtype)
    loads[2].wait()
    for first in range(0, order, tile):
        here = slice(first, first + tile)
        there = slice(order + first, order + first + tile)
        for top in range(0, order, tile):
            line = slice(top, top + tile)
            half_real, half_imag = half[first_half, here], half[second_half, here]
            real = dots(cos[line, :], half_real, minus[line, :], half_imag)
            imag = dots(sin[line, :], half_real, cos[line, :], half_imag)
            inverse = jnp.minimum(lax.rsqrt(real * real + imag * imag), 1.0 / MAG_FLOOR)
            shrink = 1.0 - measured[line, here].astype(jnp.float32) * inverse
            resid[line, here] = (real * shrink).astype(resid.dtype)
            resid[line, there] = (imag * shrink).astype(resid.dtype)
    real, imag = resid[:, first_half], resid[:, second_half]
    turned[first_half, :] = dots(real, cos[...], imag, sin[...]).astype(turned.dtype)
    turned[second_half, :] = dots(real, minus[...], imag, cos[...]).astype(turned.dtype)
    count = order // 2
    side = lax.rem(me, 2)
    for number, target in ((1 - side, leaving), (side, kept)):
        line = pl.ds(pl.multiple_of(number * count, count), count)
        for first in range(0, order, tile):
            here = slice(first, first + tile)
            there = slice(order + first, order + first + tile)
            turned_real, turned_imag = turned[first_half, here], turned[second_half, here]
            real = dots(cos[line, :], turned_real, sin[line, :], turned_imag)
            imag = dots(minus[line, :], turned_real, cos[line, :], turned_imag)
            patch_real = patch[line, here].astype(jnp.float32)
            patch_imag = patch[line, there].astype(jnp.float32)
            target[:, here] = (patch_real * real + patch_imag * imag).astype(target.dtype)
            target[:, there] = (patch_real * imag - patch_imag * real).astype(target.dtype)
            probe_real = probe[line, here].astype(jnp.float32)
            probe_imag = probe[line, there].astype(jnp.float32)
            term[line, here] = (probe_real * real + probe_imag * imag).astype(term.dtype)
            term[line, there] = (probe_real * imag - probe_imag * real).astype(term.dtype)
        if target is leaving:
            leave = pltpu.make_async_copy(leaving, sent, leave_sem.at[0])
            leave.start()
    leave.wait()


def slot_terms(cells, stock, starts, order):
    total_rows = cells.shape[0]
    wide_cols = 2 * order
    bf16, f32 = jnp.bfloat16, jnp.float32
    return pl.pallas_call(
        slot_kernel,
        out_shape=(
            jax.ShapeDtypeStruct((order, wide_cols), bf16),
            jax.ShapeDtypeStruct((order // 2, wide_cols), f32),
            jax.ShapeDtypeStruct((order // 2, wide_cols), bf16),
        ),
        in_specs=[SMEM, VMEM, ANY],
        out_specs=(VMEM, VMEM, ANY),
        scratch_shapes=[
            pltpu.VMEM((total_rows + SUBLANES, wide_cols), f32),
            pltpu.VMEM((order, wide_cols), bf16),
            pltpu.VMEM((order, wide_cols), bf16),
            pltpu.VMEM((wide_cols, order), bf16),
            pltpu.VMEM((order, wide_cols), bf16),
            pltpu.VMEM((wide_cols, order), bf16),
            pltpu.VMEM((order // 2, wide_cols), bf16),
            pltpu.VMEM((order, wide_cols), bf16),
            pltpu.VMEM((order, wide_cols), bf16),
            pltpu.VMEM((order, order), bf16),
            pltpu.VMEM((order, order), bf16),
            pltpu.SemaphoreType.DMA((3,)),
            pltpu.SemaphoreType.DMA((1,)),
        ],
        compiler_params=pltpu.CompilerParams(vmem_limit_bytes=24 * 2**20),
        cost_estimate=pl.CostEstimate(
            flops=8 * 2 * order**3 * 2, bytes_accessed=8 * 2**20, transcendentals=order * order
        ),
        name="slot",
    )(starts, cells, stock)


def pack_kernel(reach, own_rows, starts, term, out, padded):
    order = term.shape[0]
    first_row = starts[lax.axis_index("row")]
    below = padded.shape[0] - reach - order
    padded[0:reach, :] = jnp.zeros((reach, padded.shape[1]), jnp.float32)
    padded[reach : reach + order, :] = term[...].astype(jnp.float32)
    padded[reach + order :, :] = jnp.zeros((below, padded.shape[1]), jnp.float32)

    @pl.loop(0, out.shape[0], unroll=2)
    def _(k):
        out[k] = rows_from(padded, reach - first_row + k * own_rows, out.shape[1]).astype(out.dtype)


def pack_rows(term, starts, slots, own_rows, tile_rows):
    order, width = term.shape
    reach = slots * own_rows - order
    return pl.pallas_call(
        functools.partial(pack_kernel, reach, own_rows),
        out_shape=jax.ShapeDtypeStruct((slots, tile_rows, width), jnp.bfloat16),
        in_specs=[SMEM, VMEM],
        out_specs=VMEM,
        scratch_shapes=[pltpu.VMEM((2 * reach + order + tile_rows + SUBLANES, width), jnp.float32)],
        compiler_params=pltpu.CompilerParams(vmem_limit_bytes=8 * 2**20),
        cost_estimate=pl.CostEstimate(flops=0, bytes_accessed=3 * 2**20, transcendentals=0),
        name="pack",
    )(starts, term)


def place_kernel(order, info, terms, empty, out, totals, sems):
    del empty
    slots, tile_rows = terms.shape[0], terms.shape[1]
    count = (order + LANES) // LANES
    lane = lax.broadcasted_iota(jnp.int32, (tile_rows, LANES), 1)
    nothing = jnp.zeros((tile_rows, LANES), jnp.float32)

    @pl.loop(0, slots, unroll=8)
    def _(slot):
        offset = info[2 * slots * count + slot]
        shift = lax.rem(offset, LANES)
        for part in range(2):
            turned = []
            for b in range(count - 1):
                first = part * order + b * LANES
                turned.append(pltpu.roll(terms[slot, :, first : first + LANES], shift, 1).astype(jnp.float32))
            holders = [info[slots * count + slot * count + b] for b in range(count)]
            held = [totals[holder, part] for holder in holders]
            for b in range(count):
                before = turned[b - 1] if b else nothing
                after = turned[b] if b < count - 1 else nothing
                term = jnp.where(lane < offset, before, after)
                first_one = holders[b] == slot * count + b
                totals[holders[b], part] = jnp.where(first_one, term, held[b] + term)

    def copy(number):
        place = pl.multiple_of(info[number] * LANES, LANES)
        return pltpu.make_async_copy(totals.at[number], out.at[:, :, pl.ds(place, LANES)], sems.at[number])

    @pl.loop(0, slots * count)
    def _(number):
        @pl.when(info[slots * count + number] == number)
        def _():
            copy(number).start()

    @pl.loop(0, slots * count)
    def _(number):
        @pl.when(info[slots * count + number] == number)
        def _():
            copy(number).wait()


def place_windows(terms, empty, info, order):
    slots, tile_rows = terms.shape[0], terms.shape[1]
    count = (order + LANES) // LANES
    return pl.pallas_call(
        functools.partial(place_kernel, order),
        out_shape=jax.ShapeDtypeStruct(empty.shape, empty.dtype),
        in_specs=[SMEM, VMEM, ANY],
        out_specs=ANY,
        scratch_shapes=[
            pltpu.VMEM((slots * count, 2, tile_rows, LANES), jnp.float32),
            pltpu.SemaphoreType.DMA((slots * count,)),
        ],
        input_output_aliases={2: 0},
        compiler_params=pltpu.CompilerParams(vmem_limit_bytes=12 * 2**20),
        cost_estimate=pl.CostEstimate(flops=0, bytes_accessed=6 * 2**20, transcendentals=0),
        name="place",
    )(info, terms, empty)


def strides(devices):
    steps, stride = [], 1
    while stride < devices:
        radix = 4 if len(steps) >= 2 and (devices // stride) % 4 == 0 else 2
        steps.append((stride, radix))
        stride *= radix
    return steps


def swap(x, distance, devices):
    return lax.ppermute(x, "row", [(d, d ^ distance) for d in range(devices)])


def sum_probe(kept, sent, devices):
    me = lax.axis_index("row")
    addends = [kept, swap(sent, 1, devices)]

    def rows(index, count):
        found = [lax.dynamic_slice_in_dim(x, index * count, count).astype(jnp.float32) for x in addends]
        return found[0] + found[1]

    for stride, radix in strides(devices)[1:]:
        digit = me // stride % radix
        count = addends[0].shape[0] // radix
        met = []
        for k in range(1, radix):
            share = rows(lax.bitwise_xor(digit, k), count).astype(jnp.bfloat16)
            met.append(swap(share, k * stride, devices))
        own = rows(digit, count)
        for one in met[:-1]:
            own = own + one.astype(jnp.float32)
        addends = [own, met[-1]]
    return addends[0] + addends[1].astype(jnp.float32)


def join(whole, devices):
    me = lax.axis_index("row")
    for stride, radix in reversed(strides(devices)):
        digit = me // stride % radix
        shares = [whole] + [swap(whole, k * stride, devices) for k in range(1, radix)]
        pieces = []
        for j in range(radix):
            piece = shares[0]
            for k in range(1, radix):
                piece = jnp.where(lax.bitwise_xor(digit, k) == j, shares[k], piece)
            pieces.append(piece)
        whole = jnp.concatenate(pieces, axis=0)
    return whole


def body(object_field, probe, amplitude, row_offsets, col_offsets, dealing):
    order = probe.shape[1]
    devices = lax.axis_size("row")
    own_rows, tile_cols = object_field.shape[1], object_field.shape[2]
    total_rows = devices * own_rows
    tile_rows = -(-own_rows // SUBLANES) * SUBLANES
    spare = tile_rows - own_rows
    if spare:
        object_field = jnp.pad(object_field, ((0, 0), (0, spare), (0, 0)))
    pieces, token = fetch_windows(object_field, dealing, col_offsets, order)
    strips = lax.all_to_all(pieces, "row", split_axis=0, concat_axis=0, tiled=True)
    cells = strips[:, :own_rows].reshape(total_rows, 2 * order)
    empty, starts, info, stock = prepare(
        dealing, row_offsets, col_offsets, token, probe, amplitude, object_field.shape
    )
    term, kept, sent = slot_terms(cells, stock, starts, order)
    total = sum_probe(kept, sent, devices)
    terms = pack_rows(term, starts, devices, own_rows, tile_rows)
    terms, total = lax.optimization_barrier((terms, total))
    arrived = lax.all_to_all(terms, "row", split_axis=0, concat_axis=0, tiled=True)
    share = (total * (1.0 / dealing.shape[0])).astype(jnp.bfloat16)
    whole = join(share, devices).astype(jnp.float32)
    probe_grad = jnp.stack([whole[:, :order], whole[:, order:]])
    object_grad = place_windows(arrived, empty, info, order)
    if spare:
        object_grad = object_grad[:, :own_rows]
    return (object_grad, probe_grad)


def solution(mesh):
    return jax.shard_map(
        body,
        mesh=mesh,
        in_specs=(
            P(None, ("groups", "row"), None),
            P("groups", None, None),
            P(("groups", "row"), None, None),
            P("groups"),
            P("groups"),
            P("groups"),
        ),
        out_specs=(P(None, ("groups", "row"), None), P("groups", None, None)),
        check_vma=False,
    )
```

```python
import functools
import math

import jax
import jax.numpy as jnp
import numpy as np
from jax import lax
from jax.experimental import pallas as pl
from jax.experimental.pallas import tpu as pltpu
from jax.sharding import PartitionSpec as P

MAG_FLOOR = 0.25
LANES = 128
SUBLANES = 8
SMEM = pl.BlockSpec(memory_space=pltpu.SMEM)
VMEM = pl.BlockSpec(memory_space=pltpu.VMEM)
ANY = pl.BlockSpec(memory_space=pl.ANY)


def dft_table(order):
    indices = np.arange(order, dtype=np.int32)
    phases = indices[:, None] * indices[None, :] % order
    angles = phases.astype(np.float32) * np.float32(2.0 * math.pi / order)
    factor = np.float32(1.0 / math.sqrt(order))
    return np.concatenate([np.cos(angles) * factor, -np.sin(angles) * factor], axis=1).astype(jnp.bfloat16)


def window_start(column, order, tile_cols):
    span = order + LANES
    base = jnp.minimum(column // LANES, (tile_cols - span) // LANES) * LANES
    return pl.multiple_of(base, LANES), column - base


def rows_from(ref, start, count):
    aligned = pl.multiple_of(start // SUBLANES * SUBLANES, SUBLANES)
    rest = start - aligned
    width = ref.shape[-1]
    blocks = ref[pl.ds(aligned, count + SUBLANES), :].reshape(-1, SUBLANES, width)
    turned = pltpu.roll(blocks, lax.rem(SUBLANES - rest, SUBLANES), 1)
    sub = lax.broadcasted_iota(jnp.int32, (1, SUBLANES, width), 1)
    picked = jnp.where(sub < SUBLANES - rest, turned[:-1], turned[1:])
    return picked.reshape(count, width)


def fetch_kernel(order, dealing, cols, tile, out, token, held, sems):
    token[0] = dealing[0]
    slots, tile_rows = out.shape[0], out.shape[1]
    tile_cols = tile.shape[2]
    span = order + LANES

    def copy(slot):
        base, _ = window_start(cols[dealing[slot]], order, tile_cols)
        return pltpu.make_async_copy(tile.at[:, :, pl.ds(base, span)], held.at[slot], sems.at[slot])

    @pl.loop(0, slots)
    def _(slot):
        copy(slot).start()

    lane = lax.broadcasted_iota(jnp.int32, (tile_rows, LANES), 1)

    @pl.loop(0, slots, unroll=4)
    def _(slot):
        copy(slot).wait()
        _, offset = window_start(cols[dealing[slot]], order, tile_cols)
        shift = lax.rem(LANES - lax.rem(offset, LANES), LANES)
        for part in range(2):
            turned = [
                pltpu.roll(held[slot, part, :, b * LANES : (b + 1) * LANES].astype(out.dtype), shift, 1)
                for b in range(span // LANES)
            ]
            for b in range(order // LANES):
                first = part * order + b * LANES
                cells = jnp.where(lane < LANES - offset, turned[b], turned[b + 1])
                out[slot, :, first : first + LANES] = cells


def fetch_windows(tile, dealing, cols, order):
    slots, tile_rows, tile_cols = dealing.shape[0], tile.shape[1], tile.shape[2]
    span = order + LANES

    return pl.pallas_call(
        functools.partial(fetch_kernel, order),
        out_shape=(
            jax.ShapeDtypeStruct((slots, tile_rows, 2 * order), jnp.bfloat16),
            jax.ShapeDtypeStruct((1,), jnp.int32),
        ),
        in_specs=[SMEM, SMEM, ANY],
        out_specs=(VMEM, SMEM),
        scratch_shapes=[
            pltpu.VMEM((slots, 2, tile_rows, span), jnp.float32),
            pltpu.SemaphoreType.DMA((slots,)),
        ],
        compiler_params=pltpu.CompilerParams(vmem_limit_bytes=56 * 2**20),
        cost_estimate=pl.CostEstimate(flops=0, bytes_accessed=6 * 2**20, transcendentals=0),
        name="fetch",
    )(dealing, cols, tile)


def stock_places(stock, order):
    return (
        stock.at[0:order, 0:order],
        stock.at[0:order, order : 2 * order],
        stock.at[order : 2 * order, :],
        stock.at[2 * order : 3 * order, 0:order],
    )


def prepare_kernel(
    order, dealing, cols, token, table_in, probe, measured,
    empty, blocks, owners, stock,
    table, zeros, sems, stock_sems,
):
    del token
    places = stock_places(stock, order)
    sources = (probe.at[0], probe.at[1], table_in, measured.at[0])
    fills = []
    for k, (source, place) in enumerate(zip(sources, places)):
        fill = pltpu.make_async_copy(source, place, stock_sems.at[k])
        fill.start()
        fills.append(fill)
    count = (order + LANES) // LANES
    slots = dealing.shape[0]
    tile_cols = empty.shape[2]
    width = zeros.shape[2]
    zeros[...] = jnp.zeros_like(zeros)
    for b in range(tile_cols // width):
        fill = pltpu.make_async_copy(zeros, empty.at[:, :, b * width : (b + 1) * width], sems.at[b])
        fill.start()
        fills.append(fill)

    @pl.loop(0, tile_cols // LANES)
    def _(block):
        table[block] = -1

    @pl.loop(0, slots)
    def _(slot):
        base, _ = window_start(cols[dealing[slot]], order, tile_cols)
        for b in range(count):
            number = slot * count + b
            block = base // LANES + b
            blocks[number] = block
            known = table[block]
            owner = jnp.where(known < 0, number, known)
            owners[number] = owner
            table[block] = owner

    for fill in fills:
        fill.wait()


def prepare(dealing, cols, token, probe, measured, tile_shape):
    order = probe.shape[1]
    slots = dealing.shape[0]
    numbers = slots * (order + LANES) // LANES
    fill_cols = 2048
    return pl.pallas_call(
        functools.partial(prepare_kernel, order),
        out_shape=(
            jax.ShapeDtypeStruct(tile_shape, jnp.float32),
            jax.ShapeDtypeStruct((numbers,), jnp.int32),
            jax.ShapeDtypeStruct((numbers,), jnp.int32),
            jax.ShapeDtypeStruct((48 * order, 2 * order), jnp.bfloat16),
        ),
        in_specs=[SMEM, SMEM, SMEM, ANY, ANY, ANY],
        out_specs=(ANY, SMEM, SMEM, ANY),
        scratch_shapes=[
            pltpu.SMEM((tile_shape[2] // LANES,), jnp.int32),
            pltpu.VMEM(tile_shape[:2] + (fill_cols,), jnp.float32),
            pltpu.SemaphoreType.DMA((tile_shape[2] // fill_cols,)),
            pltpu.SemaphoreType.DMA((4,)),
        ],
        compiler_params=pltpu.CompilerParams(vmem_limit_bytes=8 * 2**20),
        cost_estimate=pl.CostEstimate(flops=0, bytes_accessed=110 * 2**20, transcendentals=0),
        name="prepare",
    )(dealing, cols, token, jnp.asarray(dft_table(order)), probe, measured)


def slot_kernel(
    dealing, rows, owners, cells, stock,
    term, kept, sent,
    wide, patch, wave, half, resid, turned, leaving, probe, table, minus, measured, sems, leave_sem,
):
    del owners
    order = term.shape[0]
    places = (stock.at[0:order, :],) + stock_places(stock, order)[2:]
    targets = (probe, table, measured)
    loads = [
        pltpu.make_async_copy(source, target, sems.at[k])
        for k, (source, target) in enumerate(zip(places, targets))
    ]
    for load in loads:
        load.start()
    total_rows = cells.shape[0]
    me = lax.axis_index("row")
    first_row = rows[dealing[me]]
    step = 64
    tile = 256

    wide[0:total_rows, :] = cells[...].astype(jnp.float32)
    wide[total_rows:, :] = jnp.zeros((SUBLANES, 2 * order), jnp.float32)

    @pl.loop(0, order // step, unroll=2)
    def _(i):
        place = pl.ds(pl.multiple_of(i * step, step), step)
        patch[place, :] = rows_from(wide, first_row + i * step, step).astype(patch.dtype)

    loads[0].wait()

    @pl.loop(0, order // step, unroll=2)
    def _(i):
        place = pl.ds(pl.multiple_of(i * step, step), step)
        found = patch[place, :].astype(jnp.float32)
        real, imag = found[:, :order], found[:, order:]
        probe_real = probe[place, :order].astype(jnp.float32)
        probe_imag = probe[place, order:].astype(jnp.float32)
        wave[place, :order] = (probe_real * real - probe_imag * imag).astype(wave.dtype)
        wave[place, order:] = (probe_real * imag + probe_imag * real).astype(wave.dtype)

    loads[1].wait()
    minus[...] = -table[:, order:]
    cos, sin = table.at[:, :order], table.at[:, order:]
    first_half, second_half = slice(0, order), slice(order, 2 * order)

    def dots(a, b, c, d):
        one = jnp.dot(a, b, preferred_element_type=jnp.float32)
        return one + jnp.dot(c, d, preferred_element_type=jnp.float32)

    real, imag = wave[:, first_half], wave[:, second_half]
    half[first_half, :] = dots(real, cos[...], imag, minus[...]).astype(half.dtype)
    half[second_half, :] = dots(real, sin[...], imag, cos[...]).astype(half.dtype)
    loads[2].wait()
    for first in range(0, order, tile):
        here = slice(first, first + tile)
        there = slice(order + first, order + first + tile)
        for top in range(0, order, tile):
            line = slice(top, top + tile)
            half_real, half_imag = half[first_half, here], half[second_half, here]
            real = dots(cos[line, :], half_real, minus[line, :], half_imag)
            imag = dots(sin[line, :], half_real, cos[line, :], half_imag)
            inverse = jnp.minimum(lax.rsqrt(real * real + imag * imag), 1.0 / MAG_FLOOR)
            shrink = 1.0 - measured[line, here].astype(jnp.float32) * inverse
            resid[line, here] = (real * shrink).astype(resid.dtype)
            resid[line, there] = (imag * shrink).astype(resid.dtype)
    real, imag = resid[:, first_half], resid[:, second_half]
    turned[first_half, :] = dots(real, cos[...], imag, sin[...]).astype(turned.dtype)
    turned[second_half, :] = dots(real, minus[...], imag, cos[...]).astype(turned.dtype)
    count = order // 2
    side = lax.rem(me, 2)
    for number, target in ((1 - side, leaving), (side, kept)):
        line = pl.ds(pl.multiple_of(number * count, count), count)
        for first in range(0, order, tile):
            here = slice(first, first + tile)
            there = slice(order + first, order + first + tile)
            turned_real, turned_imag = turned[first_half, here], turned[second_half, here]
            real = dots(cos[line, :], turned_real, sin[line, :], turned_imag)
            imag = dots(minus[line, :], turned_real, cos[line, :], turned_imag)
            patch_real = patch[line, here].astype(jnp.float32)
            patch_imag = patch[line, there].astype(jnp.float32)
            target[:, here] = (patch_real * real + patch_imag * imag).astype(target.dtype)
            target[:, there] = (patch_real * imag - patch_imag * real).astype(target.dtype)
            probe_real = probe[line, here].astype(jnp.float32)
            probe_imag = probe[line, there].astype(jnp.float32)
            term[line, here] = (probe_real * real + probe_imag * imag).astype(term.dtype)
            term[line, there] = (probe_real * imag - probe_imag * real).astype(term.dtype)
        if target is leaving:
            leave = pltpu.make_async_copy(leaving, sent, leave_sem.at[0])
            leave.start()
    leave.wait()


def slot_terms(cells, stock, dealing, rows, owners, order):
    total_rows = cells.shape[0]
    wide_cols = 2 * order
    bf16, f32 = jnp.bfloat16, jnp.float32
    return pl.pallas_call(
        slot_kernel,
        out_shape=(
            jax.ShapeDtypeStruct((order, wide_cols), bf16),
            jax.ShapeDtypeStruct((order // 2, wide_cols), f32),
            jax.ShapeDtypeStruct((order // 2, wide_cols), bf16),
        ),
        in_specs=[SMEM, SMEM, SMEM, VMEM, ANY],
        out_specs=(VMEM, VMEM, ANY),
        scratch_shapes=[
            pltpu.VMEM((total_rows + SUBLANES, wide_cols), f32),
            pltpu.VMEM((order, wide_cols), bf16),
            pltpu.VMEM((order, wide_cols), bf16),
            pltpu.VMEM((wide_cols, order), bf16),
            pltpu.VMEM((order, wide_cols), bf16),
            pltpu.VMEM((wide_cols, order), bf16),
            pltpu.VMEM((order // 2, wide_cols), bf16),
            pltpu.VMEM((order, wide_cols), bf16),
            pltpu.VMEM((order, wide_cols), bf16),
            pltpu.VMEM((order, order), bf16),
            pltpu.VMEM((order, order), bf16),
            pltpu.SemaphoreType.DMA((3,)),
            pltpu.SemaphoreType.DMA((1,)),
        ],
        compiler_params=pltpu.CompilerParams(vmem_limit_bytes=24 * 2**20),
        cost_estimate=pl.CostEstimate(
            flops=8 * 2 * order**3 * 2, bytes_accessed=8 * 2**20, transcendentals=order * order
        ),
        name="slot",
    )(dealing, rows, owners, cells, stock)


def pack_kernel(reach, own_rows, dealing, rows, term, out, padded):
    order = term.shape[0]
    first_row = rows[dealing[lax.axis_index("row")]]
    below = padded.shape[0] - reach - order
    padded[0:reach, :] = jnp.zeros((reach, padded.shape[1]), jnp.float32)
    padded[reach : reach + order, :] = term[...].astype(jnp.float32)
    padded[reach + order :, :] = jnp.zeros((below, padded.shape[1]), jnp.float32)

    @pl.loop(0, out.shape[0], unroll=2)
    def _(k):
        out[k] = rows_from(padded, reach - first_row + k * own_rows, out.shape[1]).astype(out.dtype)


def pack_rows(term, dealing, rows, slots, own_rows, tile_rows):
    order, width = term.shape
    reach = slots * own_rows - order
    return pl.pallas_call(
        functools.partial(pack_kernel, reach, own_rows),
        out_shape=jax.ShapeDtypeStruct((slots, tile_rows, width), jnp.bfloat16),
        in_specs=[SMEM, SMEM, VMEM],
        out_specs=VMEM,
        scratch_shapes=[pltpu.VMEM((2 * reach + order + tile_rows + SUBLANES, width), jnp.float32)],
        compiler_params=pltpu.CompilerParams(vmem_limit_bytes=8 * 2**20),
        cost_estimate=pl.CostEstimate(flops=0, bytes_accessed=3 * 2**20, transcendentals=0),
        name="pack",
    )(dealing, rows, term)


def place_kernel(order, dealing, cols, blocks, owners, terms, empty, out, totals, sems):
    del empty
    slots, tile_rows = terms.shape[0], terms.shape[1]
    count = (order + LANES) // LANES
    lane = lax.broadcasted_iota(jnp.int32, (tile_rows, LANES), 1)
    nothing = jnp.zeros((tile_rows, LANES), jnp.float32)

    @pl.loop(0, slots, unroll=4)
    def _(slot):
        _, offset = window_start(cols[dealing[slot]], order, out.shape[2])
        shift = lax.rem(offset, LANES)
        for part in range(2):
            turned = []
            for b in range(count - 1):
                first = part * order + b * LANES
                turned.append(pltpu.roll(terms[slot, :, first : first + LANES], shift, 1).astype(jnp.float32))
            holders = [owners[slot * count + b] for b in range(count)]
            held = [totals[holder, part] for holder in holders]
            for b in range(count):
                before = turned[b - 1] if b else nothing
                after = turned[b] if b < count - 1 else nothing
                term = jnp.where(lane < offset, before, after)
                first_one = holders[b] == slot * count + b
                totals[holders[b], part] = jnp.where(first_one, term, held[b] + term)

    def copy(number):
        place = pl.multiple_of(blocks[number] * LANES, LANES)
        return pltpu.make_async_copy(totals.at[number], out.at[:, :, pl.ds(place, LANES)], sems.at[number])

    @pl.loop(0, slots * count)
    def _(number):
        @pl.when(owners[number] == number)
        def _():
            copy(number).start()

    @pl.loop(0, slots * count)
    def _(number):
        @pl.when(owners[number] == number)
        def _():
            copy(number).wait()


def place_windows(terms, empty, blocks, owners, dealing, cols, order):
    slots, tile_rows = terms.shape[0], terms.shape[1]
    count = (order + LANES) // LANES
    return pl.pallas_call(
        functools.partial(place_kernel, order),
        out_shape=jax.ShapeDtypeStruct(empty.shape, empty.dtype),
        in_specs=[SMEM, SMEM, SMEM, SMEM, VMEM, ANY],
        out_specs=ANY,
        scratch_shapes=[
            pltpu.VMEM((slots * count, 2, tile_rows, LANES), jnp.float32),
            pltpu.SemaphoreType.DMA((slots * count,)),
        ],
        input_output_aliases={5: 0},
        compiler_params=pltpu.CompilerParams(vmem_limit_bytes=12 * 2**20),
        cost_estimate=pl.CostEstimate(flops=0, bytes_accessed=6 * 2**20, transcendentals=0),
        name="place",
    )(dealing, cols, blocks, owners, terms, empty)


def strides(devices):
    steps, stride = [], 1
    while stride < devices:
        radix = 4 if len(steps) >= 2 and (devices // stride) % 4 == 0 else 2
        steps.append((stride, radix))
        stride *= radix
    return steps


def swap(x, distance, devices):
    return lax.ppermute(x, "row", [(d, d ^ distance) for d in range(devices)])


def sum_probe(kept, sent, devices):
    me = lax.axis_index("row")
    addends = [kept, swap(sent, 1, devices)]

    def rows(index, count):
        found = [lax.dynamic_slice_in_dim(x, index * count, count).astype(jnp.float32) for x in addends]
        return found[0] + found[1]

    for stride, radix in strides(devices)[1:]:
        digit = me // stride % radix
        count = addends[0].shape[0] // radix
        met = []
        for k in range(1, radix):
            share = rows(lax.bitwise_xor(digit, k), count).astype(jnp.bfloat16)
            met.append(swap(share, k * stride, devices))
        own = rows(digit, count)
        for one in met[:-1]:
            own = own + one.astype(jnp.float32)
        addends = [own, met[-1]]
    return addends[0] + addends[1].astype(jnp.float32)


def join(whole, devices):
    me = lax.axis_index("row")
    rows, width = whole.shape
    places = []
    for stride, radix in strides(devices):
        places += [2 * stride, stride] if radix == 4 else [stride]
    far = max(places)
    order = [far] + places[1:2] + [part for part in places[2:] if part != far] + places[:1]
    done = []
    for part in order:
        met = swap(whole, part, devices)
        high = me // part % 2 == 1
        axis = sum(places.index(one) < places.index(part) for one in done)
        whole = jnp.stack([jnp.where(high, met, whole), jnp.where(high, whole, met)], axis=axis)
        done.append(part)
    return whole.reshape(devices * rows, width)


def body(object_field, probe, amplitude, row_offsets, col_offsets, dealing):
    order = probe.shape[1]
    devices = lax.axis_size("row")
    own_rows, tile_cols = object_field.shape[1], object_field.shape[2]
    total_rows = devices * own_rows
    tile_rows = -(-own_rows // SUBLANES) * SUBLANES
    spare = tile_rows - own_rows
    if spare:
        object_field = jnp.pad(object_field, ((0, 0), (0, spare), (0, 0)))
    pieces, token = fetch_windows(object_field, dealing, col_offsets, order)
    strips = lax.all_to_all(pieces, "row", split_axis=0, concat_axis=0, tiled=True)
    cells = strips[:, :own_rows].reshape(total_rows, 2 * order)
    empty, blocks, owners, stock = prepare(
        dealing, col_offsets, token, probe, amplitude, object_field.shape
    )
    term, kept, sent = slot_terms(cells, stock, dealing, row_offsets, owners, order)
    total = sum_probe(kept, sent, devices)
    terms = pack_rows(term, dealing, row_offsets, devices, own_rows, tile_rows)
    terms, total = lax.optimization_barrier((terms, total))
    arrived = lax.all_to_all(terms, "row", split_axis=0, concat_axis=0, tiled=True)
    share = (total * (1.0 / dealing.shape[0])).astype(jnp.bfloat16)
    whole = join(share, devices).astype(jnp.float32)
    probe_grad = jnp.stack([whole[:, :order], whole[:, order:]])
    object_grad = place_windows(arrived, empty, blocks, owners, dealing, col_offsets, order)
    if spare:
        object_grad = object_grad[:, :own_rows]
    return (object_grad, probe_grad)


def solution(mesh):
    return jax.shard_map(
        body,
        mesh=mesh,
        in_specs=(
            P(None, ("groups", "row"), None),
            P("groups", None, None),
            P(("groups", "row"), None, None),
            P("groups"),
            P("groups"),
            P("groups"),
        ),
        out_specs=(P(None, ("groups", "row"), None), P("groups", None, None)),
        check_vma=False,
    )
```

```python
import functools
import math

import jax
import jax.numpy as jnp
import numpy as np
from jax import lax
from jax.experimental import pallas as pl
from jax.experimental.pallas import tpu as pltpu
from jax.sharding import PartitionSpec as P

MAG_FLOOR = 0.25
LANES = 128
SUBLANES = 8
SMEM = pl.BlockSpec(memory_space=pltpu.SMEM)
VMEM = pl.BlockSpec(memory_space=pltpu.VMEM)
ANY = pl.BlockSpec(memory_space=pl.ANY)


def dft_table(order):
    indices = np.arange(order, dtype=np.int32)
    phases = indices[:, None] * indices[None, :] % order
    angles = phases.astype(np.float32) * np.float32(2.0 * math.pi / order)
    factor = np.float32(1.0 / math.sqrt(order))
    return np.concatenate([np.cos(angles) * factor, -np.sin(angles) * factor], axis=1).astype(jnp.bfloat16)


def window_start(column, order, tile_cols):
    span = order + LANES
    base = jnp.minimum(column // LANES, (tile_cols - span) // LANES) * LANES
    return pl.multiple_of(base, LANES), column - base


def rows_from(ref, start, count):
    aligned = pl.multiple_of(start // SUBLANES * SUBLANES, SUBLANES)
    rest = start - aligned
    width = ref.shape[-1]
    blocks = ref[pl.ds(aligned, count + SUBLANES), :].reshape(-1, SUBLANES, width)
    turned = pltpu.roll(blocks, lax.rem(SUBLANES - rest, SUBLANES), 1)
    sub = lax.broadcasted_iota(jnp.int32, (1, SUBLANES, width), 1)
    picked = jnp.where(sub < SUBLANES - rest, turned[:-1], turned[1:])
    return picked.reshape(count, width)


def fetch_kernel(order, dealing, cols, tile, out, token, held, sems):
    token[0] = dealing[0]
    slots, tile_rows = out.shape[0], out.shape[1]
    tile_cols = tile.shape[2]
    span = order + LANES

    def copy(slot):
        base, _ = window_start(cols[dealing[slot]], order, tile_cols)
        return pltpu.make_async_copy(tile.at[:, :, pl.ds(base, span)], held.at[slot], sems.at[slot])

    @pl.loop(0, slots)
    def _(slot):
        copy(slot).start()

    lane = lax.broadcasted_iota(jnp.int32, (tile_rows, LANES), 1)

    @pl.loop(0, slots, unroll=4)
    def _(slot):
        copy(slot).wait()
        _, offset = window_start(cols[dealing[slot]], order, tile_cols)
        shift = lax.rem(LANES - lax.rem(offset, LANES), LANES)
        for part in range(2):
            turned = [
                pltpu.roll(held[slot, part, :, b * LANES : (b + 1) * LANES], shift, 1)
                for b in range(span // LANES)
            ]
            for b in range(order // LANES):
                first = part * order + b * LANES
                cells = jnp.where(lane < LANES - offset, turned[b], turned[b + 1])
                out[slot, :, first : first + LANES] = cells.astype(out.dtype)


def fetch_windows(tile, dealing, cols, order):
    slots, tile_rows, tile_cols = dealing.shape[0], tile.shape[1], tile.shape[2]
    span = order + LANES

    return pl.pallas_call(
        functools.partial(fetch_kernel, order),
        out_shape=(
            jax.ShapeDtypeStruct((slots, tile_rows, 2 * order), jnp.bfloat16),
            jax.ShapeDtypeStruct((1,), jnp.int32),
        ),
        in_specs=[SMEM, SMEM, ANY],
        out_specs=(VMEM, SMEM),
        scratch_shapes=[
            pltpu.VMEM((slots, 2, tile_rows, span), jnp.float32),
            pltpu.SemaphoreType.DMA((slots,)),
        ],
        compiler_params=pltpu.CompilerParams(vmem_limit_bytes=56 * 2**20),
        cost_estimate=pl.CostEstimate(flops=0, bytes_accessed=6 * 2**20, transcendentals=0),
        name="fetch",
    )(dealing, cols, tile)


def stock_places(stock, order):
    return (
        stock.at[0:order, 0:order],
        stock.at[0:order, order : 2 * order],
        stock.at[order : 2 * order, :],
        stock.at[2 * order : 3 * order, 0:order],
    )


def prepare_kernel(
    order, dealing, cols, token, table_in, probe, measured,
    empty, blocks, owners, stock,
    table, zeros, sems, stock_sems,
):
    del token
    places = stock_places(stock, order)
    sources = (probe.at[0], probe.at[1], table_in, measured.at[0])
    fills = []
    for k, (source, place) in enumerate(zip(sources, places)):
        fill = pltpu.make_async_copy(source, place, stock_sems.at[k])
        fill.start()
        fills.append(fill)
    count = (order + LANES) // LANES
    slots = dealing.shape[0]
    tile_cols = empty.shape[2]
    width = zeros.shape[2]
    zeros[...] = jnp.zeros_like(zeros)
    for b in range(tile_cols // width):
        fill = pltpu.make_async_copy(zeros, empty.at[:, :, b * width : (b + 1) * width], sems.at[b])
        fill.start()
        fills.append(fill)

    @pl.loop(0, tile_cols // LANES)
    def _(block):
        table[block] = -1

    @pl.loop(0, slots)
    def _(slot):
        base, _ = window_start(cols[dealing[slot]], order, tile_cols)
        for b in range(count):
            number = slot * count + b
            block = base // LANES + b
            blocks[number] = block
            known = table[block]
            owner = jnp.where(known < 0, number, known)
            owners[number] = owner
            table[block] = owner

    for fill in fills:
        fill.wait()


def prepare(dealing, cols, token, probe, measured, tile_shape):
    order = probe.shape[1]
    slots = dealing.shape[0]
    numbers = slots * (order + LANES) // LANES
    fill_cols = 2048
    return pl.pallas_call(
        functools.partial(prepare_kernel, order),
        out_shape=(
            jax.ShapeDtypeStruct(tile_shape, jnp.float32),
            jax.ShapeDtypeStruct((numbers,), jnp.int32),
            jax.ShapeDtypeStruct((numbers,), jnp.int32),
            jax.ShapeDtypeStruct((48 * order, 2 * order), jnp.bfloat16),
        ),
        in_specs=[SMEM, SMEM, SMEM, ANY, ANY, ANY],
        out_specs=(ANY, SMEM, SMEM, ANY),
        scratch_shapes=[
            pltpu.SMEM((tile_shape[2] // LANES,), jnp.int32),
            pltpu.VMEM(tile_shape[:2] + (fill_cols,), jnp.float32),
            pltpu.SemaphoreType.DMA((tile_shape[2] // fill_cols,)),
            pltpu.SemaphoreType.DMA((4,)),
        ],
        compiler_params=pltpu.CompilerParams(vmem_limit_bytes=8 * 2**20),
        cost_estimate=pl.CostEstimate(flops=0, bytes_accessed=110 * 2**20, transcendentals=0),
        name="prepare",
    )(dealing, cols, token, jnp.asarray(dft_table(order)), probe, measured)


def slot_kernel(
    dealing, rows, owners, cells, stock,
    term, kept, sent,
    wide, patch, wave, half, resid, turned, leaving, probe, table, minus, measured, sems, leave_sem,
):
    del owners
    order = term.shape[0]
    places = (stock.at[0:order, :],) + stock_places(stock, order)[2:]
    targets = (probe, table, measured)
    loads = [
        pltpu.make_async_copy(source, target, sems.at[k])
        for k, (source, target) in enumerate(zip(places, targets))
    ]
    for load in loads:
        load.start()
    total_rows = cells.shape[0]
    me = lax.axis_index("row")
    first_row = rows[dealing[me]]
    step = 64
    tile = 256

    wide[0:total_rows, :] = cells[...].astype(jnp.float32)
    wide[total_rows:, :] = jnp.zeros((SUBLANES, 2 * order), jnp.float32)

    @pl.loop(0, order // step, unroll=4)
    def _(i):
        place = pl.ds(pl.multiple_of(i * step, step), step)
        patch[place, :] = rows_from(wide, first_row + i * step, step).astype(patch.dtype)

    loads[0].wait()

    @pl.loop(0, order // step, unroll=4)
    def _(i):
        place = pl.ds(pl.multiple_of(i * step, step), step)
        found = patch[place, :].astype(jnp.float32)
        real, imag = found[:, :order], found[:, order:]
        probe_real = probe[place, :order].astype(jnp.float32)
        probe_imag = probe[place, order:].astype(jnp.float32)
        wave[place, :order] = (probe_real * real - probe_imag * imag).astype(wave.dtype)
        wave[place, order:] = (probe_real * imag + probe_imag * real).astype(wave.dtype)

    loads[1].wait()
    minus[...] = -table[:, order:]
    cos, sin = table.at[:, :order], table.at[:, order:]
    first_half, second_half = slice(0, order), slice(order, 2 * order)

    def dots(a, b, c, d):
        one = jnp.dot(a, b, preferred_element_type=jnp.float32)
        return one + jnp.dot(c, d, preferred_element_type=jnp.float32)

    real, imag = wave[:, first_half], wave[:, second_half]
    half[first_half, :] = dots(real, cos[...], imag, minus[...]).astype(half.dtype)
    half[second_half, :] = dots(real, sin[...], imag, cos[...]).astype(half.dtype)
    loads[2].wait()
    for first in range(0, order, tile):
        here = slice(first, first + tile)
        there = slice(order + first, order + first + tile)
        for top in range(0, order, tile):
            line = slice(top, top + tile)
            half_real, half_imag = half[first_half, here], half[second_half, here]
            real = dots(cos[line, :], half_real, minus[line, :], half_imag)
            imag = dots(sin[line, :], half_real, cos[line, :], half_imag)
            inverse = jnp.minimum(lax.rsqrt(real * real + imag * imag), 1.0 / MAG_FLOOR)
            shrink = 1.0 - measured[line, here].astype(jnp.float32) * inverse
            resid[line, here] = (real * shrink).astype(resid.dtype)
            resid[line, there] = (imag * shrink).astype(resid.dtype)
    real, imag = resid[:, first_half], resid[:, second_half]
    turned[first_half, :] = dots(real, cos[...], imag, sin[...]).astype(turned.dtype)
    turned[second_half, :] = dots(real, minus[...], imag, cos[...]).astype(turned.dtype)
    count = order // 2
    side = lax.rem(me, 2)
    for number, target in ((1 - side, leaving), (side, kept)):
        line = pl.ds(pl.multiple_of(number * count, count), count)
        for first in range(0, order, tile):
            here = slice(first, first + tile)
            there = slice(order + first, order + first + tile)
            turned_real, turned_imag = turned[first_half, here], turned[second_half, here]
            real = dots(cos[line, :], turned_real, sin[line, :], turned_imag)
            imag = dots(minus[line, :], turned_real, cos[line, :], turned_imag)
            patch_real = patch[line, here].astype(jnp.float32)
            patch_imag = patch[line, there].astype(jnp.float32)
            target[:, here] = (patch_real * real + patch_imag * imag).astype(target.dtype)
            target[:, there] = (patch_real * imag - patch_imag * real).astype(target.dtype)
            probe_real = probe[line, here].astype(jnp.float32)
            probe_imag = probe[line, there].astype(jnp.float32)
            term[line, here] = (probe_real * real + probe_imag * imag).astype(term.dtype)
            term[line, there] = (probe_real * imag - probe_imag * real).astype(term.dtype)
        if target is leaving:
            leave = pltpu.make_async_copy(leaving, sent, leave_sem.at[0])
            leave.start()
    leave.wait()


def slot_terms(cells, stock, dealing, rows, owners, order):
    total_rows = cells.shape[0]
    wide_cols = 2 * order
    bf16, f32 = jnp.bfloat16, jnp.float32
    return pl.pallas_call(
        slot_kernel,
        out_shape=(
            jax.ShapeDtypeStruct((order, wide_cols), bf16),
            jax.ShapeDtypeStruct((order // 2, wide_cols), f32),
            jax.ShapeDtypeStruct((order // 2, wide_cols), bf16),
        ),
        in_specs=[SMEM, SMEM, SMEM, VMEM, ANY],
        out_specs=(VMEM, VMEM, ANY),
        scratch_shapes=[
            pltpu.VMEM((total_rows + SUBLANES, wide_cols), f32),
            pltpu.VMEM((order, wide_cols), bf16),
            pltpu.VMEM((order, wide_cols), bf16),
            pltpu.VMEM((wide_cols, order), bf16),
            pltpu.VMEM((order, wide_cols), bf16),
            pltpu.VMEM((wide_cols, order), bf16),
            pltpu.VMEM((order // 2, wide_cols), bf16),
            pltpu.VMEM((order, wide_cols), bf16),
            pltpu.VMEM((order, wide_cols), bf16),
            pltpu.VMEM((order, order), bf16),
            pltpu.VMEM((order, order), bf16),
            pltpu.SemaphoreType.DMA((3,)),
            pltpu.SemaphoreType.DMA((1,)),
        ],
        compiler_params=pltpu.CompilerParams(vmem_limit_bytes=24 * 2**20),
        cost_estimate=pl.CostEstimate(
            flops=8 * 2 * order**3 * 2, bytes_accessed=8 * 2**20, transcendentals=order * order
        ),
        name="slot",
    )(dealing, rows, owners, cells, stock)


def pack_kernel(reach, own_rows, dealing, rows, term, out, padded):
    order = term.shape[0]
    first_row = rows[dealing[lax.axis_index("row")]]
    below = padded.shape[0] - reach - order
    padded[0:reach, :] = jnp.zeros((reach, padded.shape[1]), jnp.float32)
    padded[reach : reach + order, :] = term[...].astype(jnp.float32)
    padded[reach + order :, :] = jnp.zeros((below, padded.shape[1]), jnp.float32)

    @pl.loop(0, out.shape[0], unroll=2)
    def _(k):
        out[k] = rows_from(padded, reach - first_row + k * own_rows, out.shape[1]).astype(out.dtype)


def pack_rows(term, dealing, rows, slots, own_rows, tile_rows):
    order, width = term.shape
    reach = slots * own_rows - order
    return pl.pallas_call(
        functools.partial(pack_kernel, reach, own_rows),
        out_shape=jax.ShapeDtypeStruct((slots, tile_rows, width), jnp.bfloat16),
        in_specs=[SMEM, SMEM, VMEM],
        out_specs=VMEM,
        scratch_shapes=[pltpu.VMEM((2 * reach + order + tile_rows + SUBLANES, width), jnp.float32)],
        compiler_params=pltpu.CompilerParams(vmem_limit_bytes=8 * 2**20),
        cost_estimate=pl.CostEstimate(flops=0, bytes_accessed=3 * 2**20, transcendentals=0),
        name="pack",
    )(dealing, rows, term)


def place_kernel(order, dealing, cols, blocks, owners, terms, empty, out, totals, sems):
    del empty
    slots, tile_rows = terms.shape[0], terms.shape[1]
    count = (order + LANES) // LANES
    lane = lax.broadcasted_iota(jnp.int32, (tile_rows, LANES), 1)
    nothing = jnp.zeros((tile_rows, LANES), jnp.float32)

    @pl.loop(0, slots, unroll=4)
    def _(slot):
        _, offset = window_start(cols[dealing[slot]], order, out.shape[2])
        shift = lax.rem(offset, LANES)
        for part in range(2):
            turned = []
            for b in range(count - 1):
                first = part * order + b * LANES
                turned.append(pltpu.roll(terms[slot, :, first : first + LANES], shift, 1).astype(jnp.float32))
            holders = [owners[slot * count + b] for b in range(count)]
            held = [totals[holder, part] for holder in holders]
            for b in range(count):
                before = turned[b - 1] if b else nothing
                after = turned[b] if b < count - 1 else nothing
                term = jnp.where(lane < offset, before, after)
                first_one = holders[b] == slot * count + b
                totals[holders[b], part] = jnp.where(first_one, term, held[b] + term)

    def copy(number):
        place = pl.multiple_of(blocks[number] * LANES, LANES)
        return pltpu.make_async_copy(totals.at[number], out.at[:, :, pl.ds(place, LANES)], sems.at[number])

    @pl.loop(0, slots * count)
    def _(number):
        @pl.when(owners[number] == number)
        def _():
            copy(number).start()

    @pl.loop(0, slots * count)
    def _(number):
        @pl.when(owners[number] == number)
        def _():
            copy(number).wait()


def place_windows(terms, empty, blocks, owners, dealing, cols, order):
    slots, tile_rows = terms.shape[0], terms.shape[1]
    count = (order + LANES) // LANES
    return pl.pallas_call(
        functools.partial(place_kernel, order),
        out_shape=jax.ShapeDtypeStruct(empty.shape, empty.dtype),
        in_specs=[SMEM, SMEM, SMEM, SMEM, VMEM, ANY],
        out_specs=ANY,
        scratch_shapes=[
            pltpu.VMEM((slots * count, 2, tile_rows, LANES), jnp.float32),
            pltpu.SemaphoreType.DMA((slots * count,)),
        ],
        input_output_aliases={5: 0},
        compiler_params=pltpu.CompilerParams(vmem_limit_bytes=12 * 2**20),
        cost_estimate=pl.CostEstimate(flops=0, bytes_accessed=6 * 2**20, transcendentals=0),
        name="place",
    )(dealing, cols, blocks, owners, terms, empty)


def strides(devices):
    steps, stride = [], 1
    while stride < devices:
        radix = 4 if len(steps) >= 2 and (devices // stride) % 4 == 0 else 2
        steps.append((stride, radix))
        stride *= radix
    return steps


def swap(x, distance, devices):
    return lax.ppermute(x, "row", [(d, d ^ distance) for d in range(devices)])


def sum_probe(kept, sent, devices):
    me = lax.axis_index("row")
    addends = [kept, swap(sent, 1, devices)]

    def rows(index, count):
        found = [lax.dynamic_slice_in_dim(x, index * count, count).astype(jnp.float32) for x in addends]
        return found[0] + found[1]

    for stride, radix in strides(devices)[1:]:
        digit = me // stride % radix
        count = addends[0].shape[0] // radix
        met = []
        for k in range(1, radix):
            share = rows(lax.bitwise_xor(digit, k), count).astype(jnp.bfloat16)
            met.append(swap(share, k * stride, devices))
        own = rows(digit, count)
        for one in met[:-1]:
            own = own + one.astype(jnp.float32)
        addends = [own, met[-1]]
    return addends[0] + addends[1].astype(jnp.float32)


def join(whole, devices):
    me = lax.axis_index("row")
    for stride, radix in reversed(strides(devices)):
        digit = me // stride % radix
        shares = [whole] + [swap(whole, k * stride, devices) for k in range(1, radix)]
        pieces = []
        for j in range(radix):
            piece = shares[0]
            for k in range(1, radix):
                piece = jnp.where(lax.bitwise_xor(digit, k) == j, shares[k], piece)
            pieces.append(piece)
        whole = jnp.concatenate(pieces, axis=0)
    return whole


def body(object_field, probe, amplitude, row_offsets, col_offsets, dealing):
    order = probe.shape[1]
    devices = lax.axis_size("row")
    own_rows, tile_cols = object_field.shape[1], object_field.shape[2]
    total_rows = devices * own_rows
    tile_rows = -(-own_rows // SUBLANES) * SUBLANES
    spare = tile_rows - own_rows
    if spare:
        object_field = jnp.pad(object_field, ((0, 0), (0, spare), (0, 0)))
    pieces, token = fetch_windows(object_field, dealing, col_offsets, order)
    strips = lax.all_to_all(pieces, "row", split_axis=0, concat_axis=0, tiled=True)
    cells = strips[:, :own_rows].reshape(total_rows, 2 * order)
    empty, blocks, owners, stock = prepare(
        dealing, col_offsets, token, probe, amplitude, object_field.shape
    )
    term, kept, sent = slot_terms(cells, stock, dealing, row_offsets, owners, order)
    total = sum_probe(kept, sent, devices)
    terms = pack_rows(term, dealing, row_offsets, devices, own_rows, tile_rows)
    terms, total = lax.optimization_barrier((terms, total))
    arrived = lax.all_to_all(terms, "row", split_axis=0, concat_axis=0, tiled=True)
    share = (total * (1.0 / dealing.shape[0])).astype(jnp.bfloat16)
    whole = join(share, devices).astype(jnp.float32)
    probe_grad = jnp.stack([whole[:, :order], whole[:, order:]])
    object_grad = place_windows(arrived, empty, blocks, owners, dealing, col_offsets, order)
    if spare:
        object_grad = object_grad[:, :own_rows]
    return (object_grad, probe_grad)


def solution(mesh):
    return jax.shard_map(
        body,
        mesh=mesh,
        in_specs=(
            P(None, ("groups", "row"), None),
            P("groups", None, None),
            P(("groups", "row"), None, None),
            P("groups"),
            P("groups"),
            P("groups"),
        ),
        out_specs=(P(None, ("groups", "row"), None), P("groups", None, None)),
        check_vma=False,
    )
```
